32 devices in a mesh: section: 2 (over core), seq: 4 (over z), fsdp: 4 (over y, x).
Axes of the slice: x: 2, y: 2, z: 4, core: 2. Of those that a mesh axis runs over, the one named last changes fastest.
Arguments:
- tokens: bfloat16 [2, 4, 1024, 1024], P(None, 'fsdp', 'seq'), may hold values from -0.1875 to 0.1875
- cotangent: bfloat16 [2, 4, 1024, 1024], P(None, 'fsdp', 'seq'), may hold values from -6 to 6
- lengths: int32 [2, 4, 4], P(None, 'fsdp'), may hold values from 1 to 896, 1024 in all within a row
- valid_mask: int32 [2, 4, 1024], P(None, 'fsdp', 'seq'), may hold values 0 or 1
- w_qkv: bfloat16 [2, 1024, 3072], P('section', 'fsdp'), may hold values from -0.1875 to 0.1875
- w_out: bfloat16 [2, 1024, 1024], P('section', 'fsdp'), may hold values from -0.1875 to 0.1875
- w_in: bfloat16 [2, 1024, 8192], P('section', 'fsdp'), may hold values from -0.1875 to 0.1875
- w_down: bfloat16 [2, 4096, 1024], P('section', 'fsdp'), may hold values from -0.09375 to 0.09375
- qk_scale: bfloat16 [2, 1024], P('section', 'fsdp'), may hold values from 0.099609375 to 1.8984375
- mlp_scale: bfloat16 [2, 8192], P('section', 'fsdp'), may hold values from 0.099609375 to 1.8984375
- alphas: bfloat16 [2, 2048], P('section', 'fsdp'), may hold values from 0.099609375 to 0.5
Outputs:
- hidden_out: bfloat16 [2, 2, 4, 1024, 1024], P('section', None, 'fsdp', 'seq')
- grad_in: float32 [2, 2, 4, 1024, 1024], P('section', None, 'fsdp', 'seq')
- grad_qkv: float32 [2, 1024, 3072], P('section', 'fsdp')
- grad_out_proj: float32 [2, 1024, 1024], P('section', 'fsdp')
- grad_in_proj: float32 [2, 1024, 8192], P('section', 'fsdp')
- grad_down: float32 [2, 4096, 1024], P('section', 'fsdp')
- grad_qk_scale: float32 [2, 1024], P('section', 'fsdp')
- grad_mlp_scale: float32 [2, 8192], P('section', 'fsdp')
- grad_alphas: float32 [2, 2048], P('section', 'fsdp')
- rms_stats: float32 [2], P('section')
The draws below stay inside these ranges and needn't reach their ends.
Inputs may be any that keep to these rules, and one draw needn't show every extreme that they name: The 4 lengths of a row add up to 1024; the longest of each row is exactly 896.
All inputs are finite; a program needn't handle non-finite values. No bound on the sum of `valid_mask` on one device may be relied on, other than what follows from the above.
Results may differ from the reference program's by a relative error of at most 0.025.
Values may be sent and summed in bfloat16 or wider, within the bound.
A program may use at most 640 MiB of HBM per device.

```python
import math
import jax
import jax.numpy as jnp
import numpy as np
from jax import lax

D = 1024
HEAD = 64
FF = 4096
MICRO = 2
SEQ_LEN = 1024
NDOC = 4
ROWS = 4
GROUP = 256
TOKENS = 8192


def touch_ends(result, own_key, least, top_value):
    longest = result.shape.index(max(result.shape))
    spots = []
    for shift in (0, 1):
        where = [jax.random.randint(jax.random.fold_in(own_key, axis), (), 0, length) for axis, length in enumerate(result.shape)]
        where[longest] = (where[longest] + shift) % result.shape[longest]
        spots.append(tuple(where))
    return result.at[spots[0]].set(least).at[spots[1]].set(top_value)


def block_scale(own_key, extent, split, smallest, high):
    level, own = 1.0, jax.random.fold_in(own_key, 6)
    for dim, parts in split:
        heights = jnp.exp(jax.random.uniform(jax.random.fold_in(own, dim), (parts,), jnp.float32, smallest / len(split), high / len(split)))
        level = level * jnp.repeat(heights, extent[dim] // parts).reshape([-1 if axis == dim else 1 for axis in range(len(extent))])
    return level


def profile(number_of, total, reach, lean):
    weights = [(1 << 20) // math.isqrt(rank ** lean) + 1 for rank in range(2, number_of + 1)]
    rest, holding = total - reach - (number_of - 1), [1] * (number_of - 1)
    while rest > 0:
        movable = [i for i in range(number_of - 1) if holding[i] < reach]
        pool, left = sum([weights[i] for i in movable]), rest
        for i in movable:
            extra = min(reach - holding[i], max(1, left * weights[i] // pool), rest)
            holding[i] = holding[i] + extra
            rest = rest - extra
    return np.array([reach] + holding)


def uneven_parts(stream_key, amount, total, most, slope):
    if amount == 2:
        one = jax.random.randint(stream_key, (), max(1, total - most), min(most, total - 1) + 1)
        return jnp.stack([one, total - one])
    tallies = jnp.asarray(profile(amount, total, most, slope), jnp.int32)
    twos = (amount - 1) // 2
    source_of, sink = tallies[1:1 + 2 * twos:2], tallies[2:2 + 2 * twos:2]
    margin = jnp.minimum(source_of - 1, most - sink)
    shifted = jax.random.randint(jax.random.fold_in(stream_key, 1), (twos,), 0, 1 << 20) % (margin + 1)
    tallies = tallies.at[1:1 + 2 * twos:2].set(source_of - shifted).at[2:2 + 2 * twos:2].set(sink + shifted)
    return tallies[jax.random.permutation(jax.random.fold_in(stream_key, 2), amount)]


def normal_values(rng, extent, scale, bound, split=(), held_as=jnp.bfloat16):
    array = jax.random.normal(rng, extent, jnp.float32) * scale
    if len(split) > 0:
        array = block_scale(rng, extent, split, -0.22, 0.18) * array
    return jnp.clip(array, min=-bound, max=bound).astype(held_as)


def setup_inputs(seed: int = 0) -> dict:
    key_list = jax.random.split(jax.random.key(seed), 12)
    return {
        "tokens": normal_values(key_list[0], (MICRO, ROWS, SEQ_LEN, D), (D ** -0.5), 0.1875, ((1, 4), (2, 4))),
        "cotangent": normal_values(key_list[1], (MICRO, ROWS, SEQ_LEN, D), 1.0, 6.0, ((1, 4), (2, 4))),
        "lengths": jax.vmap(lambda own: uneven_parts(own, NDOC, SEQ_LEN, SEQ_LEN - GROUP // 2, 0))(jax.random.split(key_list[2], MICRO * ROWS)).reshape((MICRO, ROWS, NDOC)).astype(jnp.int32),
        "valid_mask": touch_ends((jax.random.randint(key_list[3], (MICRO, ROWS, SEQ_LEN), 0, 4) < 1).astype(jnp.int32), jax.random.fold_in(key_list[3], 1), 0, 1),
        "w_qkv": normal_values(key_list[4], (2, D, 3 * D), D ** -0.5, 0.1875, ((0, 2), (1, 4))),
        "w_out": normal_values(key_list[5], (2, D, D), D ** -0.5, 0.1875, ((0, 2), (1, 4))),
        "w_in": normal_values(key_list[6], (2, D, 2 * FF), D ** -0.5, 0.1875, ((0, 2), (1, 4))),
        "w_down": normal_values(key_list[7], (2, FF, D), FF ** -0.5, 0.09375, ((0, 2), (1, 4))),
        "qk_scale": jnp.clip(1.0 + 0.18 * jax.random.normal(key_list[8], (2, D), jnp.float32), 0.099609375, 1.8984375).astype(jnp.bfloat16),
        "mlp_scale": jnp.clip(1.0 + 0.18 * jax.random.normal(key_list[9], (2, 2 * FF), jnp.float32), 0.099609375, 1.8984375).astype(jnp.bfloat16),
        "alphas": jnp.clip(0.099609375 + 0.40039062 * jax.random.uniform(key_list[10], (2, 2 * D), jnp.float32) ** block_scale(key_list[10], (2, 2 * D), ((0, 2), (1, 4)), -0.2, 0.2), 0.099609375, 0.5).astype(jnp.bfloat16),
    }


@jax.custom_vjp
def low(v):
    return lax.optimization_barrier(v.astype(jnp.bfloat16)).astype(jnp.float32)

@jax.custom_vjp
def low_back(v):
    return v

def low_keep(v):
    return (low(v), None)

def low_pass(kept, grad):
    return (grad,)

def back_keep(v):
    return (v, None)

def back_low(kept, grad):
    return (low(grad),)
low.defvjp(low_keep, low_pass)
low_back.defvjp(back_keep, back_low)
epsilon = 1e-06

def product(left, right):
    return jnp.dot(left, right, precision=lax.Precision.HIGHEST, preferred_element_type=jnp.float32)

def unit(values):
    return values * lax.rsqrt(lax.optimization_barrier(jnp.sum(values * values, axis=-1, keepdims=True)) + epsilon)

def allowed_pairs(row_lengths):
    ends = jnp.cumsum(row_lengths)[:-1]
    position = jnp.arange(SEQ_LEN, dtype=jnp.int32)
    segment = lax.optimization_barrier(jnp.sum((position[:, None] >= ends[None, :]).astype(jnp.int32), axis=1))
    return (segment[:, None] == segment[None, :]) & (position[None, :] <= position[:, None])

def layer(hidden, w_qkv, w_out, w_in, w_down, qk_scale, mlp_scale, alphas, allowed, valid):
    count = hidden.shape[0]
    heads = D // HEAD
    mixed = low_back(product(hidden, w_qkv))
    head_scale = qk_scale.reshape(heads, HEAD)
    queries = low(unit(mixed[:, :D].reshape(count, heads, HEAD)) * head_scale)
    keys = low(unit(mixed[:, D:2 * D].reshape(count, heads, HEAD)) * head_scale)
    values = low(mixed[:, 2 * D:].reshape(count, heads, HEAD))
    scores = low_back(math.sqrt(HEAD) * jnp.einsum('qhd,khd->hqk', queries, keys, precision=lax.Precision.HIGHEST))
    scores = jnp.where(allowed[None], scores, -1e+30)
    weights = jnp.exp(scores - lax.optimization_barrier(jnp.max(scores, axis=-1, keepdims=True)))
    weights = weights / lax.optimization_barrier(jnp.sum(weights, axis=-1, keepdims=True))
    attended = jnp.einsum('hqk,khd->qhd', low(weights), values, precision=lax.Precision.HIGHEST)
    attended = low(low_back(attended.reshape(count, D)))
    branch = low_back(product(attended, w_out))
    statistic = jnp.sum(valid * lax.optimization_barrier(jnp.sum(branch * branch, axis=-1)))
    middle = unit(hidden + alphas[:D] * (unit(branch) - hidden))
    lifted = low_back(product(low(middle), w_in))
    upward = lifted[:, :FF] * mlp_scale[:FF]
    gating = lifted[:, FF:] * mlp_scale[FF:] * math.sqrt(D)
    inner = low(upward * jax.nn.silu(gating))
    output = low_back(product(inner, w_down))
    final = unit(middle + alphas[D:] * (unit(output) - middle))
    return (final, statistic)

def reference(tokens, cotangent, lengths, valid_mask, w_qkv, w_out, w_in, w_down, qk_scale, mlp_scale, alphas):
    params = tuple((piece.astype(jnp.float32) for piece in (w_qkv, w_out, w_in, w_down, qk_scale, mlp_scale, alphas)))
    total_rows = MICRO * ROWS
    flat_tokens = tokens.reshape(total_rows, SEQ_LEN, D)
    flat_cotangent = cotangent.reshape(total_rows, SEQ_LEN, D)
    flat_lengths = lengths.reshape(total_rows, NDOC)
    flat_valid = valid_mask.reshape(total_rows, SEQ_LEN)

    def per_row(carry, item):
        row_tokens, row_cotangent, row_lengths, row_valid = item
        allowed = allowed_pairs(row_lengths)
        valid = row_valid.astype(jnp.float32)
        first = tuple((piece[0] for piece in params))
        second = tuple((piece[1] for piece in params))

        def section_one(hidden, *weights):
            final, statistic = layer(hidden, *weights, allowed, valid)
            return (low_back(low(final)), statistic)

        def section_two(hidden, *weights):
            final, statistic = layer(hidden, *weights, allowed, valid)
            return (low(final), statistic)
        middle, pull_one, stat_one = jax.vjp(section_one, row_tokens.astype(jnp.float32), *first, has_aux=True)
        final, pull_two, stat_two = jax.vjp(section_two, middle, *second, has_aux=True)
        grads_two = pull_two(row_cotangent.astype(jnp.float32))
        grads_one = pull_one(grads_two[0])
        sums, stats = carry
        sums = tuple((total + jnp.stack([one, two]) for total, one, two in zip(sums, grads_one[1:], grads_two[1:])))
        stats = stats + jnp.stack([stat_one, stat_two])
        return ((sums, stats), (middle, final, grads_one[0], grads_two[0]))
    zeros = tuple((jnp.zeros(piece.shape, jnp.float32) for piece in params))
    start = (zeros, jnp.zeros((2,), jnp.float32))
    (sums, stats), (middles, finals, grad_first, grad_second) = lax.scan(per_row, start, (flat_tokens, flat_cotangent, flat_lengths, flat_valid))
    shape = (MICRO, ROWS, SEQ_LEN, D)
    hidden_out = jnp.stack([middles.reshape(shape), finals.reshape(shape)]).astype(jnp.bfloat16)
    grad_in = jnp.stack([grad_first.reshape(shape), grad_second.reshape(shape)])
    rms_stats = jnp.sqrt(stats / TOKENS + epsilon)
    return (hidden_out, grad_in, sums[0], sums[1], sums[2], sums[3], sums[4], sums[5], sums[6], rms_stats)
```

```python
import math

import jax
import jax.numpy as jnp
from jax import lax
from jax.experimental import pallas as pl
from jax.experimental.pallas import tpu as pltpu
from jax.sharding import PartitionSpec as P

HEAD = 64


epsilon = 1e-06


def shifted(block, axis, distance):
    devices = range(lax.axis_size(axis))
    route = [(i - distance, i) for i in devices if i - distance in devices]
    return lax.ppermute(block, axis, route)


def for_sending(x):
    return jax.tree.map(lambda a: a.astype(jnp.bfloat16) if a.dtype == jnp.float32 else a, x)


def unit(values):
    return values * lax.rsqrt(jnp.sum(values * values, axis=-1, keepdims=True) + epsilon)


def unit_back(values, grad):
    factor = lax.rsqrt(jnp.sum(values * values, axis=-1, keepdims=True) + epsilon)
    normed = values * factor
    return factor * (grad - normed * jnp.sum(normed * grad, axis=-1, keepdims=True))


def contract_rows(left, right):
    return lax.dot_general(
        left, right, (((0,), (0,)), ((), ())), preferred_element_type=jnp.float32
    )


def contract_cols(left, right):
    return lax.dot_general(
        left, right, (((1,), (1,)), ((), ())), preferred_element_type=jnp.float32
    )


def segments_of(row_lengths, seq_len):
    ends = jnp.cumsum(row_lengths)[:-1]
    place = jnp.arange(seq_len, dtype=jnp.int32)
    return (place, jnp.sum((place[:, None] >= ends[None, :]).astype(jnp.int32), axis=1))


def allowed_pairs(row_lengths, offset, group, seq_len):
    key_place, key_segment = segments_of(row_lengths, seq_len)
    query_place = offset + jnp.arange(group, dtype=jnp.int32)
    query_segment = lax.dynamic_slice_in_dim(key_segment, offset, group)
    return (query_segment[:, None] == key_segment[None, :]) & (
        key_place[None, :] <= query_place[:, None]
    )


def masked_scores(queries, key_heads, allowed):
    scores = jnp.einsum(
        "qhd,khd->hqk", queries, key_heads, preferred_element_type=jnp.float32
    ) * math.sqrt(HEAD)
    return jnp.where(allowed[None], scores, -1e30)


def forward_layer(hidden_b, params, allowed, valid):
    w_qkv, w_out, w_in, w_down, qk_scale, mlp_scale, alphas = params
    count, width = hidden_b.shape
    heads = width // HEAD
    hidden = hidden_b.astype(jnp.float32)
    mixed = jnp.dot(hidden_b, w_qkv, preferred_element_type=jnp.float32)
    query_raw = mixed[:, :width].reshape(count, heads, HEAD)
    key_raw = mixed[:, width : 2 * width].reshape(count, heads, HEAD)
    head_scale = qk_scale.astype(jnp.float32).reshape(heads, HEAD)
    query_b = (unit(query_raw) * head_scale).astype(jnp.bfloat16)
    key_b = (unit(key_raw) * head_scale).astype(jnp.bfloat16).reshape(count, width)
    value_b = mixed[:, 2 * width :].astype(jnp.bfloat16)
    keys, values = (
        lax.all_gather(key_b, "seq", axis=0, tiled=True),
        lax.all_gather(value_b, "seq", axis=0, tiled=True),
    )
    key_heads = keys.reshape(-1, heads, HEAD)
    value_heads = values.reshape(-1, heads, HEAD)
    scores = masked_scores(query_b, key_heads, allowed)
    highest = jnp.max(scores, axis=-1, keepdims=True)
    weights = jnp.exp(scores - highest)
    denominator = jnp.sum(weights, axis=-1, keepdims=True)
    weights = weights / denominator
    log_total = highest + jnp.log(denominator)
    attended = jnp.einsum(
        "hqk,khd->qhd",
        weights.astype(jnp.bfloat16),
        value_heads,
        preferred_element_type=jnp.float32,
    )
    attended_b = attended.reshape(count, width).astype(jnp.bfloat16)
    branch = jnp.dot(attended_b, w_out, preferred_element_type=jnp.float32)
    statistic = jnp.sum(valid * jnp.sum(branch * branch, axis=-1))
    step_sizes = alphas.astype(jnp.float32)
    first_sum = hidden + step_sizes[:width] * (unit(branch) - hidden)
    middle = unit(first_sum)
    middle_b = middle.astype(jnp.bfloat16)
    lifted = jnp.dot(middle_b, w_in, preferred_element_type=jnp.float32)
    units_count = lifted.shape[1] // 2
    scales = mlp_scale.astype(jnp.float32)
    upward = lifted[:, :units_count] * scales[:units_count]
    gating = lifted[:, units_count:] * scales[units_count:] * math.sqrt(width)
    inner_b = (upward * jax.nn.silu(gating)).astype(jnp.bfloat16)
    output = jnp.dot(inner_b, w_down, preferred_element_type=jnp.float32)
    second_sum = middle + step_sizes[width:] * (unit(output) - middle)
    result = unit(second_sum).astype(jnp.bfloat16)
    kept = (
        hidden_b,
        query_raw,
        key_raw,
        query_b,
        keys,
        values,
        log_total,
        attended_b,
        branch,
        first_sum,
        middle_b,
        lifted,
        inner_b,
        output,
        second_sum,
    )
    return (result, kept, statistic)


def backward_layer(kept, params, grad_out, allowed):
    (
        hidden_b,
        query_raw,
        key_raw,
        query_b,
        keys,
        values,
        log_total,
        attended_b,
        branch,
        first_sum,
        middle_b,
        lifted,
        inner_b,
        output,
        second_sum,
    ) = kept
    w_qkv, w_out, w_in, w_down, qk_scale, mlp_scale, alphas = params
    count, width = hidden_b.shape
    heads = width // HEAD
    hidden = hidden_b.astype(jnp.float32)
    step_sizes = alphas.astype(jnp.float32)
    alpha_attn = step_sizes[:width]
    alpha_mlp = step_sizes[width:]
    middle = unit(first_sum)
    grad_second = unit_back(second_sum, grad_out)
    grad_alpha_mlp = jnp.sum(grad_second * (unit(output) - middle), axis=0)
    grad_output = unit_back(output, alpha_mlp * grad_second).astype(jnp.bfloat16)
    grad_middle = grad_second * (1.0 - alpha_mlp)
    grad_down = contract_rows(inner_b, grad_output)
    grad_inner = contract_cols(grad_output, w_down)
    units_count = lifted.shape[1] // 2
    scales = mlp_scale.astype(jnp.float32)
    root = math.sqrt(width)
    lift_up = lifted[:, :units_count]
    lift_gate = lifted[:, units_count:]
    upward = lift_up * scales[:units_count]
    gating = lift_gate * scales[units_count:] * root
    sigmoid = jax.nn.sigmoid(gating)
    grad_upward = grad_inner * jax.nn.silu(gating)
    grad_gating = grad_inner * upward * sigmoid * (1.0 + gating * (1.0 - sigmoid))
    grad_scale_mlp = jnp.concatenate(
        [jnp.sum(grad_upward * lift_up, axis=0), jnp.sum(grad_gating * root * lift_gate, axis=0)]
    )
    grad_lifted = jnp.concatenate(
        [grad_upward * scales[:units_count], grad_gating * root * scales[units_count:]], axis=1
    ).astype(jnp.bfloat16)
    grad_in_proj = contract_rows(middle_b, grad_lifted)
    grad_middle = grad_middle + contract_cols(grad_lifted, w_in)
    grad_first = unit_back(first_sum, grad_middle)
    grad_alpha_attn = jnp.sum(grad_first * (unit(branch) - hidden), axis=0)
    grad_branch = unit_back(branch, alpha_attn * grad_first).astype(jnp.bfloat16)
    grad_hidden = grad_first * (1.0 - alpha_attn)
    grad_out_proj = contract_rows(attended_b, grad_branch)
    grad_attended = (
        contract_cols(grad_branch, w_out).astype(jnp.bfloat16).reshape(count, heads, HEAD)
    )
    key_heads = keys.reshape(-1, heads, HEAD)
    value_heads = values.reshape(-1, heads, HEAD)
    scores = masked_scores(query_b, key_heads, allowed)
    weights = jnp.exp(scores - log_total)
    grad_weights = jnp.einsum(
        "qhd,khd->hqk", grad_attended, value_heads, preferred_element_type=jnp.float32
    )
    delta = jnp.sum(weights * grad_weights, axis=-1, keepdims=True)
    grad_scores = (weights * (grad_weights - delta)).astype(jnp.bfloat16)
    score_scale = math.sqrt(HEAD)
    grad_query = (
        jnp.einsum("hqk,khd->qhd", grad_scores, key_heads, preferred_element_type=jnp.float32)
        * score_scale
    )
    seq_len = keys.shape[0]
    grad_keys = (
        jnp.einsum("hqk,qhd->khd", grad_scores, query_b, preferred_element_type=jnp.float32)
        * score_scale
    )
    grad_values = jnp.einsum(
        "hqk,qhd->khd",
        weights.astype(jnp.bfloat16),
        grad_attended,
        preferred_element_type=jnp.float32,
    )
    grad_key_own, grad_value_own = (
        lax.psum_scatter(
            grad_keys.reshape(seq_len, width).astype(jnp.bfloat16),
            "seq",
            scatter_dimension=0,
            tiled=True,
        ).astype(jnp.float32),
        lax.psum_scatter(
            grad_values.reshape(seq_len, width).astype(jnp.bfloat16),
            "seq",
            scatter_dimension=0,
            tiled=True,
        ).astype(jnp.float32),
    )
    head_scale = qk_scale.astype(jnp.float32).reshape(heads, HEAD)
    grad_key_heads = grad_key_own.reshape(count, heads, HEAD)
    grad_scale_qk = (
        jnp.sum(grad_query * unit(query_raw), axis=0)
        + jnp.sum(grad_key_heads * unit(key_raw), axis=0)
    ).reshape(width)
    grad_query_raw = unit_back(query_raw, grad_query * head_scale).reshape(count, width)
    grad_key_raw = unit_back(key_raw, grad_key_heads * head_scale).reshape(count, width)
    grad_mixed = jnp.concatenate([grad_query_raw, grad_key_raw, grad_value_own], axis=1).astype(
        jnp.bfloat16
    )
    grad_qkv = contract_rows(hidden_b, grad_mixed)
    grad_hidden = grad_hidden + contract_cols(grad_mixed, w_qkv)
    grad_step_sizes = jnp.concatenate([grad_alpha_attn, grad_alpha_mlp])
    grads = (
        grad_qkv,
        grad_out_proj,
        grad_in_proj,
        grad_down,
        grad_scale_qk,
        grad_scale_mlp,
        grad_step_sizes,
    )
    return (grad_hidden, grads)


def per_device_general(
    tokens, cotangent, lengths, valid_mask, w_qkv, w_out, w_in, w_down, qk_scale, mlp_scale, alphas
):
    shards = (w_qkv, w_out, w_in, w_down, qk_scale, mlp_scale, alphas)
    gathered = (
        lax.all_gather(shards[0], "fsdp", axis=1, tiled=True),
        lax.all_gather(shards[1], "fsdp", axis=1, tiled=True),
        lax.all_gather(shards[2], "fsdp", axis=1, tiled=True),
        lax.all_gather(shards[3], "fsdp", axis=1, tiled=True),
        lax.all_gather(shards[4], "fsdp", axis=1, tiled=True),
        lax.all_gather(shards[5], "fsdp", axis=1, tiled=True),
        lax.all_gather(shards[6], "fsdp", axis=1, tiled=True),
    )
    params = tuple((piece[0] for piece in gathered))
    section = lax.axis_index("section")
    micro = tokens.shape[0]
    group = tokens.shape[2]
    width = tokens.shape[3]
    seq_len = group * lax.axis_size("seq")
    offset = lax.axis_index("seq") * group

    def fetch(array, index):
        return lax.dynamic_index_in_dim(array, index, 0, keepdims=False)[0]

    def forward_step(carry, step):
        incoming, stat_sum = carry
        index = step - section
        active = (index >= 0) & (index < micro)
        chosen = jnp.clip(index, 0, micro - 1)
        hidden_in = jnp.where(section == 0, fetch(tokens, chosen), incoming)
        allowed = allowed_pairs(fetch(lengths, chosen), offset, group, seq_len)
        valid = fetch(valid_mask, chosen).astype(jnp.float32)
        result, kept, statistic = forward_layer(hidden_in, params, allowed, valid)
        outgoing = shifted(result, "section", 1)
        stat_sum = stat_sum + jnp.where(active, statistic, 0.0)
        return ((outgoing, stat_sum), (result, kept))

    step_list = jnp.arange(micro + 1, dtype=jnp.int32)
    start = (jnp.zeros((group, width), jnp.bfloat16), jnp.zeros((), jnp.float32))
    (unused_fwd, stat_sum), (results, kept_all) = lax.scan(forward_step, start, step_list)
    late_shards, stat_sum = lax.optimization_barrier((shards, stat_sum))
    again = (
        lax.all_gather(late_shards[0], "fsdp", axis=1, tiled=True),
        lax.all_gather(late_shards[1], "fsdp", axis=1, tiled=True),
        lax.all_gather(late_shards[2], "fsdp", axis=1, tiled=True),
        lax.all_gather(late_shards[3], "fsdp", axis=1, tiled=True),
        lax.all_gather(late_shards[4], "fsdp", axis=1, tiled=True),
        lax.all_gather(late_shards[5], "fsdp", axis=1, tiled=True),
        lax.all_gather(late_shards[6], "fsdp", axis=1, tiled=True),
    )
    params_back = tuple((piece[0] for piece in again))

    def backward_step(carry, step):
        incoming, sums = carry
        index = step - 1 + section
        active = (index >= 0) & (index < micro)
        chosen = jnp.clip(index, 0, micro - 1)
        position = chosen + section

        def take(array):
            return lax.dynamic_index_in_dim(array, position, 0, keepdims=False)

        kept = jax.tree.map(take, kept_all)
        grad_out = jnp.where(
            section == 1, fetch(cotangent, chosen).astype(jnp.float32), incoming.astype(jnp.float32)
        )
        grad_out = jnp.where(active, grad_out, 0.0)
        row_lengths = fetch(lengths, chosen)
        allowed = allowed_pairs(row_lengths, offset, group, seq_len)
        grad_hidden, grads = backward_layer(kept, params_back, grad_out, allowed)
        outgoing = shifted(grad_hidden.astype(jnp.bfloat16), "section", -1)
        sums = tuple((total + piece for total, piece in zip(sums, grads)))
        return ((outgoing, sums), grad_hidden)

    zeros = tuple((jnp.zeros(piece.shape, jnp.float32) for piece in params_back))
    (unused_back, sums), grad_steps = lax.scan(
        backward_step, (jnp.zeros((group, width), jnp.bfloat16), zeros), step_list
    )
    hidden_out = lax.dynamic_slice_in_dim(results, section, micro, 0).reshape(
        1, micro, 1, group, width
    )
    grad_in = lax.dynamic_slice_in_dim(grad_steps, 1 - section, micro, 0).reshape(
        1, micro, 1, group, width
    )
    shard_sums = jax.tree.map(
        lambda part: part.astype(jnp.float32),
        lax.psum_scatter(for_sending(sums), "fsdp", scatter_dimension=0, tiled=True),
    )
    reduced = jax.tree.map(
        lambda part: part.astype(jnp.float32), lax.psum(for_sending(shard_sums), "seq")
    )
    total_stat = lax.psum(stat_sum, ("seq", "fsdp"))
    token_count = micro * lax.axis_size("fsdp") * seq_len
    rms_stats = jnp.sqrt(total_stat / token_count + epsilon).reshape(1)
    return (
        hidden_out,
        grad_in,
        reduced[0][None],
        reduced[1][None],
        reduced[2][None],
        reduced[3][None],
        reduced[4][None],
        reduced[5][None],
        reduced[6][None],
        rms_stats,
    )


FIRST = (1, 2)
SECOND = (0, 3)
EVERY = (0, 1, 2, 3)
BLOCK = 128
SCORE_SCALE = math.sqrt(HEAD)
MASKED = -1e30


def dot(left, right):
    return jnp.dot(left, right, preferred_element_type=jnp.float32)


def low(x):
    return x.astype(jnp.bfloat16)


def swap(x):
    return lax.ppermute(x, "section", [(0, 1), (1, 0)])


def hop(x, bit, planes):
    route = [(s * 4 + f, s * 4 + (f ^ bit)) for s in planes for f in range(4)]
    return lax.ppermute(x, ("seq", "fsdp"), route)


def along(x, route):
    return lax.ppermute(x, "seq", route)


def pick(x, index, axis):
    return lax.dynamic_index_in_dim(x, index, axis, keepdims=False)


def gather_rows(piece, f):
    half = piece.shape[0] // 2
    from_x = hop(piece, 1, EVERY)
    from_y = hop(piece, 2, EVERY)
    across = jnp.concatenate([hop(from_x[:half], 2, EVERY), hop(from_y[half:], 1, EVERY)])
    rows = jnp.zeros((4,) + piece.shape, piece.dtype)
    for bit, block in enumerate((piece, from_x, from_y, across)):
        rows = lax.dynamic_update_index_in_dim(rows, block, f ^ bit, 0)
    return rows.reshape((-1,) + piece.shape[1:])


def scatter_rows(total, f, planes):
    blocks = total.reshape((4, 2, total.shape[0] // 8) + total.shape[1:])

    def block(bit, part):
        return lax.dynamic_slice(
            blocks, (f ^ bit, part, 0, 0), (1, 1) + blocks.shape[2:]
        ).reshape(blocks.shape[2:])

    done = []
    for part, (near, far) in enumerate(((1, 2), (2, 1))):
        got_own = hop(block(near, part), near, planes)
        got_far = hop(block(3, part), near, planes)
        passed = low(block(far, part).astype(jnp.float32) + got_far.astype(jnp.float32))
        got_last = hop(passed, far, planes)
        done.append(
            block(0, part).astype(jnp.float32)
            + got_own.astype(jnp.float32)
            + got_last.astype(jnp.float32)
        )
    return low(jnp.concatenate(done))


def sums_of_halves(x):
    row = lax.broadcasted_iota(jnp.int32, (2 * HEAD, 2 * HEAD), 0) // HEAD
    col = lax.broadcasted_iota(jnp.int32, (2 * HEAD, 2 * HEAD), 1) // HEAD
    same = (row == col).astype(jnp.bfloat16)
    high = x.astype(jnp.bfloat16)
    rest = (x - high.astype(jnp.float32)).astype(jnp.bfloat16)
    return dot(high, same) + dot(rest, same)


def normal_heads(raw):
    factor = lax.rsqrt(sums_of_halves(raw * raw) + epsilon)
    return raw * factor, factor


def merge(to, own, oth):
    for s in range(4):
        to[s * 256 : s * 256 + BLOCK, : own.shape[1]] = own[s * BLOCK : (s + 1) * BLOCK]
        to[s * 256 + BLOCK : (s + 1) * 256, : own.shape[1]] = oth[s * BLOCK : (s + 1) * BLOCK]


def last_dims(left, right):
    return lax.dot_general(left, right, (((1,), (1,)), ((), ())), preferred_element_type=jnp.float32)


def head_lanes(h, dtype):
    lane = lax.broadcasted_iota(jnp.int32, (1, 2 * HEAD), 1) // HEAD
    return (lane == h).astype(dtype)


def attention_kernel(
    q_own, k_own, v_own, q_oth, k_oth, v_oth, scale, place_col, start_col, place_row,
    out_own, out_oth, bias, raw, queries, keys, values,
):
    @pl.when(pl.program_id(0) == 0)
    def _():
        fits = (place_row[...] >= start_col[...]) & (place_row[...] <= place_col[...])
        bias[...] = jnp.where(fits, 0.0, MASKED)
        values[:, 2 * HEAD :] = jnp.ones_like(values[:, 2 * HEAD :])

    merge(raw, q_own[...], q_oth[...])
    normed, _ = normal_heads(raw[...].astype(jnp.float32))
    queries[...] = low(normed * scale[...]) * SCORE_SCALE
    merge(raw, k_own[...], k_oth[...])
    normed, _ = normal_heads(raw[...].astype(jnp.float32))
    keys[...] = low(normed * scale[...])
    merge(values, v_own[...], v_oth[...])
    for s in range(4):
        upto = (s + 1) * 256
        block = queries[s * 256 : upto]
        parts = []
        for h in range(2):
            scores = last_dims(block * head_lanes(h, jnp.bfloat16), keys[:upto])
            weights = jnp.exp(scores + bias[s * 256 : upto, :upto])
            summed = dot(low(weights), values[:upto])
            parts.append(summed[:, : 2 * HEAD] / summed[:, 2 * HEAD :])
        joined = low(jnp.where(head_lanes(0, jnp.float32) > 0, parts[0], parts[1]))
        out_own[s * BLOCK : (s + 1) * BLOCK] = joined[:BLOCK]
        out_oth[s * BLOCK : (s + 1) * BLOCK] = joined[BLOCK:]


def attention_back_kernel(
    q_own, k_own, v_own, q_oth, k_oth, v_oth, g_own, g_oth, scale,
    place_col, place_row, start_row,
    out_own, out_oth, grad_scale, bias, raw, queries, keys, values, grads, dq, dk, dv,
):
    pair = pl.program_id(0)

    @pl.when(pair == 0)
    def _():
        fits = (place_col[...] >= start_row[...]) & (place_col[...] <= place_row[...])
        bias[...] = jnp.where(fits, 0.0, MASKED)

    merge(raw, q_own[...], q_oth[...])
    normed, _ = normal_heads(raw[...].astype(jnp.float32))
    queries[...] = low(normed * scale[...]) * SCORE_SCALE
    merge(raw, k_own[...], k_oth[...])
    normed, _ = normal_heads(raw[...].astype(jnp.float32))
    keys[...] = low(normed * scale[...])
    merge(values, v_own[...], v_oth[...])
    merge(grads, g_own[...], g_oth[...])
    dk[...] = jnp.zeros_like(dk)
    dv[...] = jnp.zeros_like(dv)
    for s in range(4):
        upto = (s + 1) * 256
        total = 0.0
        for h in range(2):
            lanes = head_lanes(h, jnp.bfloat16)
            query = queries[s * 256 : upto] * lanes
            grad = grads[s * 256 : upto] * lanes
            scores = last_dims(keys[:upto], query)
            weights = jnp.exp(scores + bias[:upto, s * 256 : upto])
            weights = weights * (1.0 / jnp.sum(weights, axis=0, keepdims=True))
            grad_weights = last_dims(values[:upto], grad)
            delta = jnp.sum(weights * grad_weights, axis=0, keepdims=True)
            grad_scores = low(weights * (grad_weights - delta))
            dv[:upto] += dot(low(weights), grad)
            dk[:upto] += dot(grad_scores, query)
            total = total + head_lanes(h, jnp.float32) * contract_rows(grad_scores, keys[:upto])
        dq[s * 256 : upto] = total * SCORE_SCALE

    width = out_own.shape[1] // 3
    scale_sum = 0.0
    for part, (own, oth, grad) in enumerate(((q_own, q_oth, dq), (k_own, k_oth, dk))):
        merge(raw, own[...], oth[...])
        normed, factor = normal_heads(raw[...].astype(jnp.float32))
        scale_sum = scale_sum + jnp.sum(grad[...] * normed, axis=0, keepdims=True)
        step = grad[...] * scale[...]
        grad[...] = factor * (step - normed * sums_of_halves(normed * step))
    grad_scale[...] = scale_sum
    for part, grad in enumerate((dq, dk, dv)):
        lanes = pl.ds(pl.multiple_of(part * width + pair * 2 * HEAD, 2 * HEAD), 2 * HEAD)
        for s in range(4):
            rows = slice(s * BLOCK, (s + 1) * BLOCK)
            out_own[rows, lanes] = low(grad[s * 256 : s * 256 + BLOCK])
            out_oth[rows, lanes] = low(grad[s * 256 + BLOCK : (s + 1) * 256])


def mixed_specs(rows, pairs):
    return [
        pl.BlockSpec((rows, 2 * HEAD), lambda p, part=part: (0, part * pairs + p))
        for part in range(3)
    ]


def whole(shape):
    return pl.BlockSpec(shape, lambda p: (0,) * len(shape))


def attention(mixed_own, mixed_oth, scale, places):
    rows, width = mixed_own.shape
    width //= 3
    pairs = width // (2 * HEAD)
    place, start = places
    total = 2 * rows
    spec = pl.BlockSpec((rows, 2 * HEAD), lambda p: (0, p))
    return pl.pallas_call(
        attention_kernel,
        grid=(pairs,),
        out_shape=[jax.ShapeDtypeStruct((rows, width), jnp.bfloat16)] * 2,
        in_specs=mixed_specs(rows, pairs) * 2
        + [pl.BlockSpec((1, 2 * HEAD), lambda p: (0, p))]
        + [whole((total, 1)), whole((total, 1)), whole((1, total))],
        out_specs=[spec, spec],
        scratch_shapes=[
            pltpu.VMEM((total, total), jnp.float32),
            pltpu.VMEM((total, 2 * HEAD), jnp.bfloat16),
            pltpu.VMEM((total, 2 * HEAD), jnp.bfloat16),
            pltpu.VMEM((total, 2 * HEAD), jnp.bfloat16),
            pltpu.VMEM((total, 4 * HEAD), jnp.bfloat16),
        ],
        compiler_params=pltpu.CompilerParams(vmem_limit_bytes=40 * 2**20),
        cost_estimate=pl.CostEstimate(
            flops=8 * total * total * width, bytes_accessed=8 * total * width,
            transcendentals=total * total * pairs,
        ),
    )(
        *[mixed_own] * 3, *[mixed_oth] * 3, scale,
        place[:, None], start[:, None], place[None, :],
    )


def attention_back(mixed_own, mixed_oth, grad_own, grad_oth, scale, places):
    rows, width = mixed_own.shape
    width //= 3
    pairs = width // (2 * HEAD)
    place, start = places
    total = 2 * rows
    spec = pl.BlockSpec((rows, 2 * HEAD), lambda p: (0, p))
    pair_spec = pl.BlockSpec((1, 2 * HEAD), lambda p: (0, p))
    low_scratch = pltpu.VMEM((total, 2 * HEAD), jnp.bfloat16)
    full_scratch = pltpu.VMEM((total, 2 * HEAD), jnp.float32)
    return pl.pallas_call(
        attention_back_kernel,
        grid=(pairs,),
        out_shape=[jax.ShapeDtypeStruct((rows, 3 * width), jnp.bfloat16)] * 2
        + [jax.ShapeDtypeStruct((1, width), jnp.float32)],
        in_specs=mixed_specs(rows, pairs) * 2
        + [spec, spec, pair_spec]
        + [whole((total, 1)), whole((1, total)), whole((1, total))],
        out_specs=[whole((rows, 3 * width)), whole((rows, 3 * width)), pair_spec],
        scratch_shapes=[pltpu.VMEM((total, total), jnp.float32)]
        + [low_scratch] * 5
        + [full_scratch] * 3,
        compiler_params=pltpu.CompilerParams(vmem_limit_bytes=48 * 2**20),
        cost_estimate=pl.CostEstimate(
            flops=20 * total * total * width, bytes_accessed=16 * total * width,
            transcendentals=total * total * pairs,
        ),
    )(
        *[mixed_own] * 3, *[mixed_oth] * 3, grad_own, grad_oth, scale,
        place[:, None], place[None, :], start[None, :],
    )


def forward_row(hidden_own, weights, scales, places):
    w_qkv, w_out, w_up, w_gate, w_down = weights
    scale_qk, scale_up, scale_gate, alpha_attn, alpha_mlp = scales
    hidden_oth = swap(hidden_own)
    mixed_own = low(dot(hidden_own, w_qkv))
    mixed_oth = low(dot(hidden_oth, w_qkv))
    attended_own, attended_oth = attention(mixed_own, mixed_oth, scale_qk, places)
    branch_got = swap(low(dot(attended_oth, w_out)))
    branch = dot(attended_own, w_out) + branch_got.astype(jnp.float32)
    hidden = hidden_own.astype(jnp.float32)
    first_sum = hidden + alpha_attn * (unit(branch) - hidden)
    middle = unit(first_sum)
    middle_own = low(middle)
    middle_oth = swap(middle_own)

    def lift(rows):
        lift_up = low(dot(rows, w_up))
        lift_gate = dot(rows, w_gate)
        upward = lift_up.astype(jnp.float32) * scale_up
        gating = lift_gate * scale_gate
        return lift_up, low(lift_gate), low(upward * jax.nn.silu(gating))

    lifted_own = lift(middle_own)
    lifted_oth = lift(middle_oth)
    output_got = swap(low(dot(lifted_oth[2], w_down)))
    output = dot(lifted_own[2], w_down) + output_got.astype(jnp.float32)
    second_sum = middle + alpha_mlp * (unit(output) - middle)
    result = low(unit(second_sum))
    kept = (
        (hidden_own, hidden_oth), (mixed_own, mixed_oth), (attended_own, attended_oth),
        (middle_own, middle_oth), (lifted_own, lifted_oth), branch, output,
    )
    return result, kept


def backward_row(grad_out, kept, weights, scales, places):
    w_qkv, w_out, w_up, w_gate, w_down = weights
    scale_qk, scale_up, scale_gate, alpha_attn, alpha_mlp = scales
    hiddens, mixed, attended, middles, lifted, branch, output = kept
    hidden = hiddens[0].astype(jnp.float32)
    unit_branch = unit(branch)
    first_sum = hidden + alpha_attn * (unit_branch - hidden)
    middle = unit(first_sum)
    unit_output = unit(output)
    second_sum = middle + alpha_mlp * (unit_output - middle)
    grad_second = unit_back(second_sum, grad_out)
    grad_alpha_mlp = jnp.sum(grad_second * (unit_output - middle), axis=0)
    grad_output_own = low(unit_back(output, alpha_mlp * grad_second))
    grad_output_oth = swap(grad_output_own)

    def unlift(grad_rows, lifts):
        lift_up, lift_gate, _ = lifts
        lift_up = lift_up.astype(jnp.float32)
        lift_gate = lift_gate.astype(jnp.float32)
        grad_inner = contract_cols(grad_rows, w_down)
        gating = lift_gate * scale_gate
        sigmoid = jax.nn.sigmoid(gating)
        grad_up = grad_inner * (gating * sigmoid)
        grad_gate = grad_inner * (lift_up * scale_up) * sigmoid * (1.0 + gating * (1.0 - sigmoid))
        sums = (jnp.sum(grad_up * lift_up, axis=0), jnp.sum(grad_gate * lift_gate, axis=0))
        return low(grad_up * scale_up), low(grad_gate * scale_gate), sums

    grad_lift_own = unlift(grad_output_own, lifted[0])
    grad_lift_oth = unlift(grad_output_oth, lifted[1])
    middle_got = swap(
        low(contract_cols(grad_lift_oth[0], w_up) + contract_cols(grad_lift_oth[1], w_gate))
    )
    grad_middle = (
        contract_cols(grad_lift_own[0], w_up)
        + contract_cols(grad_lift_own[1], w_gate)
        + middle_got.astype(jnp.float32)
        + grad_second * (1.0 - alpha_mlp)
    )
    grad_first = unit_back(first_sum, grad_middle)
    grad_alpha_attn = jnp.sum(grad_first * (unit_branch - hidden), axis=0)
    grad_branch_own = low(unit_back(branch, alpha_attn * grad_first))
    grad_branch_oth = swap(grad_branch_own)
    grad_attended_own = low(contract_cols(grad_branch_own, w_out))
    grad_attended_oth = low(contract_cols(grad_branch_oth, w_out))
    grad_mixed_own, grad_mixed_oth, grad_scale_qk = attention_back(
        *mixed, grad_attended_own, grad_attended_oth, scale_qk, places
    )
    hidden_got = swap(low(contract_cols(grad_mixed_oth, w_qkv)))
    grad_hidden = (
        contract_cols(grad_mixed_own, w_qkv)
        + hidden_got.astype(jnp.float32)
        + grad_first * (1.0 - alpha_attn)
    )
    operands = (
        (hiddens, (grad_mixed_own, grad_mixed_oth)),
        (attended, (grad_branch_own, grad_branch_oth)),
        (middles, (grad_lift_own[0], grad_lift_oth[0])),
        (middles, (grad_lift_own[1], grad_lift_oth[1])),
        ((lifted[0][2], lifted[1][2]), (grad_output_own, grad_output_oth)),
    )
    small = (
        jnp.concatenate([grad_alpha_attn, grad_alpha_mlp]),
        grad_lift_own[2][0] + grad_lift_oth[2][0],
        (grad_lift_own[2][1] + grad_lift_oth[2][1]) * math.sqrt(hidden.shape[1]),
        grad_scale_qk[0],
    )
    return low(grad_hidden), operands, small


def weight_grads(operands):
    return tuple(
        low(contract_rows(jnp.concatenate(left), jnp.concatenate(right)))
        for left, right in operands
    )


def to_rows_of_planes(sent, s):
    return lax.all_to_all(sent, "seq", 0, 0)


def per_device(
    tokens, cotangent, lengths, valid_mask, w_qkv, w_out, w_in, w_down, qk_scale, mlp_scale, alphas
):
    c = lax.axis_index("section")
    s = lax.axis_index("seq")
    f = lax.axis_index("fsdp")
    second = (s == 0) | (s == 3)
    layer = second.astype(jnp.int32)
    micro = s // 2
    width = tokens.shape[3]
    group = tokens.shape[2]
    units = w_down.shape[1] * 4

    sources = jnp.stack([cotangent[0, 0], tokens[0, 0], tokens[1, 0], cotangent[1, 0]])
    sent = pick(sources.reshape(4, 2, BLOCK, width), c, 1)
    row = to_rows_of_planes(sent, s).reshape(4 * BLOCK, width)

    def mine(shard, axis):
        own = pick(shard, c, axis)
        got = swap(pick(shard, 1 - c, axis))
        return jnp.where(layer == c, own, got)

    half_qkv = mine(w_qkv[0].reshape(-1, 3, 4, 2, 2 * HEAD), 3).reshape(-1, 3 * width // 2)
    half_out = mine(w_out[0].reshape(2, -1, width), 0)
    half_in = mine(w_in[0].reshape(-1, 2, 4, 2, units // 8), 3).reshape(-1, 2, units // 2)
    half_down = mine(w_down[0].reshape(2, -1, width), 0)
    weights = (
        gather_rows(half_qkv, f),
        gather_rows(half_out, f),
        gather_rows(half_in[:, 0], f),
        gather_rows(half_in[:, 1], f),
        gather_rows(half_down, f),
    )

    vectors = jnp.concatenate([qk_scale, mlp_scale, alphas], axis=1)
    vectors = lax.all_gather(vectors, ("section", "fsdp"), axis=0, tiled=True)
    vectors = pick(vectors.reshape(2, 4, -1), layer, 0).astype(jnp.float32)
    cut_qk, cut_mlp = qk_scale.shape[1], qk_scale.shape[1] + mlp_scale.shape[1]
    all_qk = vectors[:, :cut_qk].reshape(4, 2, -1)
    all_mlp = vectors[:, cut_qk:cut_mlp].reshape(2, 4, 2, -1)
    all_alphas = vectors[:, cut_mlp:].reshape(2, 1, -1)
    mlp_half = pick(all_mlp, c, 2).reshape(2, 1, -1)
    scales = (
        pick(all_qk, c, 1).reshape(1, -1),
        mlp_half[0],
        mlp_half[1] * math.sqrt(width),
        all_alphas[0],
        all_alphas[1],
    )

    index = jnp.arange(4 * group, dtype=jnp.int32)
    place = (index // 256) * 256 + (((index // BLOCK) + c) % 2) * BLOCK + index % BLOCK
    ends = jnp.cumsum(pick(lengths, micro, 0)[0])[:-1]
    passed = place[:, None] >= ends[None, :]
    start = jnp.max(jnp.where(passed, ends[None, :], 0), axis=1)
    places = (place, start)

    valid = lax.all_gather(low(valid_mask[:, 0]), "seq", axis=0)
    valid = pick(pick(valid, micro, 1).reshape(4, 2, BLOCK), c, 1).reshape(-1).astype(jnp.float32)

    result, _ = forward_row(row, weights, scales, places)
    arrived = along(result, [(1, 0), (2, 3)])
    hidden_own = jnp.where(second, arrived, row)
    result, kept = forward_row(hidden_own, weights, scales, places)
    branch = kept[5]
    statistic = jnp.sum(valid * jnp.sum(branch * branch, axis=-1))

    grad_row = row.astype(jnp.float32)
    grad_hidden, operands, small_second = backward_row(grad_row, kept, weights, scales, places)
    arrived = along(grad_hidden, [(0, 1), (3, 2)])
    grads_second = weight_grads(operands)
    grad_row = jnp.where(second, grad_row, arrived.astype(jnp.float32))
    grad_hidden, operands, small_first = backward_row(grad_row, kept, weights, scales, places)
    grads_first = weight_grads(operands)

    reduced = []
    for from_second, from_first in zip(grads_second, grads_first):
        part = scatter_rows(from_second, f, SECOND)
        near = along(part, [(0, 1), (3, 2)])
        both = jnp.where(second, part, near)
        across = along(both, [(1, 2), (2, 1)])
        far = along(jnp.where(second, part, across), [(1, 0), (2, 3)])
        layer_1 = jnp.where(second, part, near).astype(jnp.float32) + jnp.where(
            second, far, across
        ).astype(jnp.float32)
        part = scatter_rows(from_first, f, FIRST)
        across = along(part, [(1, 2), (2, 1)])
        total = low(part.astype(jnp.float32) + across.astype(jnp.float32))
        outward = along(total, [(1, 0), (2, 3)])
        layer_0 = jnp.where(second, outward, total)
        layer_1 = low(layer_1)
        own = jnp.where(c == 0, layer_0, layer_1)
        got = swap(jnp.where(c == 0, layer_1, layer_0))
        reduced.append((jnp.where(c == 0, own, got), jnp.where(c == 0, got, own)))

    def columns(halves, groups):
        parts = [half.reshape(half.shape[0], groups, -1) for half in halves]
        return jnp.stack(parts, axis=2).reshape(parts[0].shape[0], -1)

    grad_qkv = columns(reduced[0], 12)
    grad_out = jnp.concatenate(reduced[1])
    grad_in_proj = jnp.concatenate([columns(reduced[2], 4), columns(reduced[3], 4)], axis=1)
    grad_down = jnp.concatenate(reduced[4])

    def to_owners(block):
        got = to_rows_of_planes(block.reshape(4, BLOCK, width), s)
        layers = (jnp.stack([got[1], got[2]]), jnp.stack([got[0], got[3]]))
        own = jnp.where(c == 0, layers[0], layers[1])
        other = swap(jnp.where(c == 0, layers[1], layers[0]))
        halves = (jnp.where(c == 0, own, other), jnp.where(c == 0, other, own))
        return jnp.concatenate(halves, axis=1)[None, :, None]

    hidden_out = to_owners(result)
    grad_in = to_owners(grad_hidden).astype(jnp.float32)

    small = [jnp.where(second, late, early) for late, early in zip(small_second, small_first)]
    up_gate = jnp.stack([small[1], small[2]]).reshape(2, 4, 1, -1)
    at_half = jnp.arange(2).reshape(1, 1, 2, 1) == c
    full = jnp.concatenate(
        [
            small[0],
            jnp.where(at_half, up_gate, 0.0).reshape(-1),
            jnp.where(at_half, small[3].reshape(1, 4, 1, -1), 0.0).reshape(-1),
            statistic[None],
        ]
    )
    full = jnp.where(jnp.arange(2)[:, None] == layer, full[None], 0.0)
    full = pick(lax.psum(full, ("section", "seq", "fsdp")), c, 0)
    ends = (2 * width, 2 * width + 2 * units, 3 * width + 2 * units)
    grad_alphas = pick(full[: ends[0]].reshape(4, -1), f, 0)[None]
    grad_mlp_scale = pick(full[ends[0] : ends[1]].reshape(4, -1), f, 0)[None]
    grad_qk_scale = pick(full[ends[1] : ends[2]].reshape(4, -1), f, 0)[None]
    token_count = tokens.shape[0] * lax.axis_size("fsdp") * 4 * group
    rms_stats = jnp.sqrt(full[ends[2] :] / token_count + epsilon)
    as_float = [
        part.astype(jnp.float32)[None] for part in (grad_qkv, grad_out, grad_in_proj, grad_down)
    ]
    return (
        hidden_out, grad_in, *as_float, grad_qk_scale, grad_mlp_scale, grad_alphas, rms_stats,
    )


def solution(mesh):
    placed = (
        P(None, "fsdp", "seq", None),
        P(None, "fsdp", "seq", None),
        P(None, "fsdp", None),
        P(None, "fsdp", "seq"),
        P("section", "fsdp", None),
        P("section", "fsdp", None),
        P("section", "fsdp", None),
        P("section", "fsdp", None),
        P("section", "fsdp"),
        P("section", "fsdp"),
        P("section", "fsdp"),
    )
    planes = mesh.shape["section"] == 2 and mesh.shape["seq"] == 4 and mesh.shape["fsdp"] == 4
    return jax.shard_map(
        per_device if planes else per_device_general,
        mesh=mesh,
        in_specs=placed,
        out_specs=(
            P("section", None, "fsdp", "seq", None),
            P("section", None, "fsdp", "seq", None),
            P("section", "fsdp", None),
            P("section", "fsdp", None),
            P("section", "fsdp", None),
            P("section", "fsdp", None),
            P("section", "fsdp"),
            P("section", "fsdp"),
            P("section", "fsdp"),
            P("section"),
        ),
        check_vma=False,
    )
```

```python
import math

import jax
import jax.numpy as jnp
from jax import lax
from jax.experimental import pallas as pl
from jax.experimental.pallas import tpu as pltpu
from jax.sharding import PartitionSpec as P

HEAD = 64


epsilon = 1e-06


def shifted(block, axis, distance):
    devices = range(lax.axis_size(axis))
    route = [(i - distance, i) for i in devices if i - distance in devices]
    return lax.ppermute(block, axis, route)


def for_sending(x):
    return jax.tree.map(lambda a: a.astype(jnp.bfloat16) if a.dtype == jnp.float32 else a, x)


def unit(values):
    return values * lax.rsqrt(jnp.sum(values * values, axis=-1, keepdims=True) + epsilon)


def unit_back(values, grad):
    factor = lax.rsqrt(jnp.sum(values * values, axis=-1, keepdims=True) + epsilon)
    normed = values * factor
    return factor * (grad - normed * jnp.sum(normed * grad, axis=-1, keepdims=True))


def contract_rows(left, right):
    return lax.dot_general(
        left, right, (((0,), (0,)), ((), ())), preferred_element_type=jnp.float32
    )


def contract_cols(left, right):
    return lax.dot_general(
        left, right, (((1,), (1,)), ((), ())), preferred_element_type=jnp.float32
    )


def segments_of(row_lengths, seq_len):
    ends = jnp.cumsum(row_lengths)[:-1]
    place = jnp.arange(seq_len, dtype=jnp.int32)
    return (place, jnp.sum((place[:, None] >= ends[None, :]).astype(jnp.int32), axis=1))


def allowed_pairs(row_lengths, offset, group, seq_len):
    key_place, key_segment = segments_of(row_lengths, seq_len)
    query_place = offset + jnp.arange(group, dtype=jnp.int32)
    query_segment = lax.dynamic_slice_in_dim(key_segment, offset, group)
    return (query_segment[:, None] == key_segment[None, :]) & (
        key_place[None, :] <= query_place[:, None]
    )


def masked_scores(queries, key_heads, allowed):
    scores = jnp.einsum(
        "qhd,khd->hqk", queries, key_heads, preferred_element_type=jnp.float32
    ) * math.sqrt(HEAD)
    return jnp.where(allowed[None], scores, -1e30)


def forward_layer(hidden_b, params, allowed, valid):
    w_qkv, w_out, w_in, w_down, qk_scale, mlp_scale, alphas = params
    count, width = hidden_b.shape
    heads = width // HEAD
    hidden = hidden_b.astype(jnp.float32)
    mixed = jnp.dot(hidden_b, w_qkv, preferred_element_type=jnp.float32)
    query_raw = mixed[:, :width].reshape(count, heads, HEAD)
    key_raw = mixed[:, width : 2 * width].reshape(count, heads, HEAD)
    head_scale = qk_scale.astype(jnp.float32).reshape(heads, HEAD)
    query_b = (unit(query_raw) * head_scale).astype(jnp.bfloat16)
    key_b = (unit(key_raw) * head_scale).astype(jnp.bfloat16).reshape(count, width)
    value_b = mixed[:, 2 * width :].astype(jnp.bfloat16)
    keys, values = (
        lax.all_gather(key_b, "seq", axis=0, tiled=True),
        lax.all_gather(value_b, "seq", axis=0, tiled=True),
    )
    key_heads = keys.reshape(-1, heads, HEAD)
    value_heads = values.reshape(-1, heads, HEAD)
    scores = masked_scores(query_b, key_heads, allowed)
    highest = jnp.max(scores, axis=-1, keepdims=True)
    weights = jnp.exp(scores - highest)
    denominator = jnp.sum(weights, axis=-1, keepdims=True)
    weights = weights / denominator
    log_total = highest + jnp.log(denominator)
    attended = jnp.einsum(
        "hqk,khd->qhd",
        weights.astype(jnp.bfloat16),
        value_heads,
        preferred_element_type=jnp.float32,
    )
    attended_b = attended.reshape(count, width).astype(jnp.bfloat16)
    branch = jnp.dot(attended_b, w_out, preferred_element_type=jnp.float32)
    statistic = jnp.sum(valid * jnp.sum(branch * branch, axis=-1))
    step_sizes = alphas.astype(jnp.float32)
    first_sum = hidden + step_sizes[:width] * (unit(branch) - hidden)
    middle = unit(first_sum)
    middle_b = middle.astype(jnp.bfloat16)
    lifted = jnp.dot(middle_b, w_in, preferred_element_type=jnp.float32)
    units_count = lifted.shape[1] // 2
    scales = mlp_scale.astype(jnp.float32)
    upward = lifted[:, :units_count] * scales[:units_count]
    gating = lifted[:, units_count:] * scales[units_count:] * math.sqrt(width)
    inner_b = (upward * jax.nn.silu(gating)).astype(jnp.bfloat16)
    output = jnp.dot(inner_b, w_down, preferred_element_type=jnp.float32)
    second_sum = middle + step_sizes[width:] * (unit(output) - middle)
    result = unit(second_sum).astype(jnp.bfloat16)
    kept = (
        hidden_b,
        query_raw,
        key_raw,
        query_b,
        keys,
        values,
        log_total,
        attended_b,
        branch,
        first_sum,
        middle_b,
        lifted,
        inner_b,
        output,
        second_sum,
    )
    return (result, kept, statistic)


def backward_layer(kept, params, grad_out, allowed):
    (
        hidden_b,
        query_raw,
        key_raw,
        query_b,
        keys,
        values,
        log_total,
        attended_b,
        branch,
        first_sum,
        middle_b,
        lifted,
        inner_b,
        output,
        second_sum,
    ) = kept
    w_qkv, w_out, w_in, w_down, qk_scale, mlp_scale, alphas = params
    count, width = hidden_b.shape
    heads = width // HEAD
    hidden = hidden_b.astype(jnp.float32)
    step_sizes = alphas.astype(jnp.float32)
    alpha_attn = step_sizes[:width]
    alpha_mlp = step_sizes[width:]
    middle = unit(first_sum)
    grad_second = unit_back(second_sum, grad_out)
    grad_alpha_mlp = jnp.sum(grad_second * (unit(output) - middle), axis=0)
    grad_output = unit_back(output, alpha_mlp * grad_second).astype(jnp.bfloat16)
    grad_middle = grad_second * (1.0 - alpha_mlp)
    grad_down = contract_rows(inner_b, grad_output)
    grad_inner = contract_cols(grad_output, w_down)
    units_count = lifted.shape[1] // 2
    scales = mlp_scale.astype(jnp.float32)
    root = math.sqrt(width)
    lift_up = lifted[:, :units_count]
    lift_gate = lifted[:, units_count:]
    upward = lift_up * scales[:units_count]
    gating = lift_gate * scales[units_count:] * root
    sigmoid = jax.nn.sigmoid(gating)
    grad_upward = grad_inner * jax.nn.silu(gating)
    grad_gating = grad_inner * upward * sigmoid * (1.0 + gating * (1.0 - sigmoid))
    grad_scale_mlp = jnp.concatenate(
        [jnp.sum(grad_upward * lift_up, axis=0), jnp.sum(grad_gating * root * lift_gate, axis=0)]
    )
    grad_lifted = jnp.concatenate(
        [grad_upward * scales[:units_count], grad_gating * root * scales[units_count:]], axis=1
    ).astype(jnp.bfloat16)
    grad_in_proj = contract_rows(middle_b, grad_lifted)
    grad_middle = grad_middle + contract_cols(grad_lifted, w_in)
    grad_first = unit_back(first_sum, grad_middle)
    grad_alpha_attn = jnp.sum(grad_first * (unit(branch) - hidden), axis=0)
    grad_branch = unit_back(branch, alpha_attn * grad_first).astype(jnp.bfloat16)
    grad_hidden = grad_first * (1.0 - alpha_attn)
    grad_out_proj = contract_rows(attended_b, grad_branch)
    grad_attended = (
        contract_cols(grad_branch, w_out).astype(jnp.bfloat16).reshape(count, heads, HEAD)
    )
    key_heads = keys.reshape(-1, heads, HEAD)
    value_heads = values.reshape(-1, heads, HEAD)
    scores = masked_scores(query_b, key_heads, allowed)
    weights = jnp.exp(scores - log_total)
    grad_weights = jnp.einsum(
        "qhd,khd->hqk", grad_attended, value_heads, preferred_element_type=jnp.float32
    )
    delta = jnp.sum(weights * grad_weights, axis=-1, keepdims=True)
    grad_scores = (weights * (grad_weights - delta)).astype(jnp.bfloat16)
    score_scale = math.sqrt(HEAD)
    grad_query = (
        jnp.einsum("hqk,khd->qhd", grad_scores, key_heads, preferred_element_type=jnp.float32)
        * score_scale
    )
    seq_len = keys.shape[0]
    grad_keys = (
        jnp.einsum("hqk,qhd->khd", grad_scores, query_b, preferred_element_type=jnp.float32)
        * score_scale
    )
    grad_values = jnp.einsum(
        "hqk,qhd->khd",
        weights.astype(jnp.bfloat16),
        grad_attended,
        preferred_element_type=jnp.float32,
    )
    grad_key_own, grad_value_own = (
        lax.psum_scatter(
            grad_keys.reshape(seq_len, width).astype(jnp.bfloat16),
            "seq",
            scatter_dimension=0,
            tiled=True,
        ).astype(jnp.float32),
        lax.psum_scatter(
            grad_values.reshape(seq_len, width).astype(jnp.bfloat16),
            "seq",
            scatter_dimension=0,
            tiled=True,
        ).astype(jnp.float32),
    )
    head_scale = qk_scale.astype(jnp.float32).reshape(heads, HEAD)
    grad_key_heads = grad_key_own.reshape(count, heads, HEAD)
    grad_scale_qk = (
        jnp.sum(grad_query * unit(query_raw), axis=0)
        + jnp.sum(grad_key_heads * unit(key_raw), axis=0)
    ).reshape(width)
    grad_query_raw = unit_back(query_raw, grad_query * head_scale).reshape(count, width)
    grad_key_raw = unit_back(key_raw, grad_key_heads * head_scale).reshape(count, width)
    grad_mixed = jnp.concatenate([grad_query_raw, grad_key_raw, grad_value_own], axis=1).astype(
        jnp.bfloat16
    )
    grad_qkv = contract_rows(hidden_b, grad_mixed)
    grad_hidden = grad_hidden + contract_cols(grad_mixed, w_qkv)
    grad_step_sizes = jnp.concatenate([grad_alpha_attn, grad_alpha_mlp])
    grads = (
        grad_qkv,
        grad_out_proj,
        grad_in_proj,
        grad_down,
        grad_scale_qk,
        grad_scale_mlp,
        grad_step_sizes,
    )
    return (grad_hidden, grads)


def per_device_general(
    tokens, cotangent, lengths, valid_mask, w_qkv, w_out, w_in, w_down, qk_scale, mlp_scale, alphas
):
    shards = (w_qkv, w_out, w_in, w_down, qk_scale, mlp_scale, alphas)
    gathered = (
        lax.all_gather(shards[0], "fsdp", axis=1, tiled=True),
        lax.all_gather(shards[1], "fsdp", axis=1, tiled=True),
        lax.all_gather(shards[2], "fsdp", axis=1, tiled=True),
        lax.all_gather(shards[3], "fsdp", axis=1, tiled=True),
        lax.all_gather(shards[4], "fsdp", axis=1, tiled=True),
        lax.all_gather(shards[5], "fsdp", axis=1, tiled=True),
        lax.all_gather(shards[6], "fsdp", axis=1, tiled=True),
    )
    params = tuple((piece[0] for piece in gathered))
    section = lax.axis_index("section")
    micro = tokens.shape[0]
    group = tokens.shape[2]
    width = tokens.shape[3]
    seq_len = group * lax.axis_size("seq")
    offset = lax.axis_index("seq") * group

    def fetch(array, index):
        return lax.dynamic_index_in_dim(array, index, 0, keepdims=False)[0]

    def forward_step(carry, step):
        incoming, stat_sum = carry
        index = step - section
        active = (index >= 0) & (index < micro)
        chosen = jnp.clip(index, 0, micro - 1)
        hidden_in = jnp.where(section == 0, fetch(tokens, chosen), incoming)
        allowed = allowed_pairs(fetch(lengths, chosen), offset, group, seq_len)
        valid = fetch(valid_mask, chosen).astype(jnp.float32)
        result, kept, statistic = forward_layer(hidden_in, params, allowed, valid)
        outgoing = shifted(result, "section", 1)
        stat_sum = stat_sum + jnp.where(active, statistic, 0.0)
        return ((outgoing, stat_sum), (result, kept))

    step_list = jnp.arange(micro + 1, dtype=jnp.int32)
    start = (jnp.zeros((group, width), jnp.bfloat16), jnp.zeros((), jnp.float32))
    (unused_fwd, stat_sum), (results, kept_all) = lax.scan(forward_step, start, step_list)
    late_shards, stat_sum = lax.optimization_barrier((shards, stat_sum))
    again = (
        lax.all_gather(late_shards[0], "fsdp", axis=1, tiled=True),
        lax.all_gather(late_shards[1], "fsdp", axis=1, tiled=True),
        lax.all_gather(late_shards[2], "fsdp", axis=1, tiled=True),
        lax.all_gather(late_shards[3], "fsdp", axis=1, tiled=True),
        lax.all_gather(late_shards[4], "fsdp", axis=1, tiled=True),
        lax.all_gather(late_shards[5], "fsdp", axis=1, tiled=True),
        lax.all_gather(late_shards[6], "fsdp", axis=1, tiled=True),
    )
    params_back = tuple((piece[0] for piece in again))

    def backward_step(carry, step):
        incoming, sums = carry
        index = step - 1 + section
        active = (index >= 0) & (index < micro)
        chosen = jnp.clip(index, 0, micro - 1)
        position = chosen + section

        def take(array):
            return lax.dynamic_index_in_dim(array, position, 0, keepdims=False)

        kept = jax.tree.map(take, kept_all)
        grad_out = jnp.where(
            section == 1, fetch(cotangent, chosen).astype(jnp.float32), incoming.astype(jnp.float32)
        )
        grad_out = jnp.where(active, grad_out, 0.0)
        row_lengths = fetch(lengths, chosen)
        allowed = allowed_pairs(row_lengths, offset, group, seq_len)
        grad_hidden, grads = backward_layer(kept, params_back, grad_out, allowed)
        outgoing = shifted(grad_hidden.astype(jnp.bfloat16), "section", -1)
        sums = tuple((total + piece for total, piece in zip(sums, grads)))
        return ((outgoing, sums), grad_hidden)

    zeros = tuple((jnp.zeros(piece.shape, jnp.float32) for piece in params_back))
    (unused_back, sums), grad_steps = lax.scan(
        backward_step, (jnp.zeros((group, width), jnp.bfloat16), zeros), step_list
    )
    hidden_out = lax.dynamic_slice_in_dim(results, section, micro, 0).reshape(
        1, micro, 1, group, width
    )
    grad_in = lax.dynamic_slice_in_dim(grad_steps, 1 - section, micro, 0).reshape(
        1, micro, 1, group, width
    )
    shard_sums = jax.tree.map(
        lambda part: part.astype(jnp.float32),
        lax.psum_scatter(for_sending(sums), "fsdp", scatter_dimension=0, tiled=True),
    )
    reduced = jax.tree.map(
        lambda part: part.astype(jnp.float32), lax.psum(for_sending(shard_sums), "seq")
    )
    total_stat = lax.psum(stat_sum, ("seq", "fsdp"))
    token_count = micro * lax.axis_size("fsdp") * seq_len
    rms_stats = jnp.sqrt(total_stat / token_count + epsilon).reshape(1)
    return (
        hidden_out,
        grad_in,
        reduced[0][None],
        reduced[1][None],
        reduced[2][None],
        reduced[3][None],
        reduced[4][None],
        reduced[5][None],
        reduced[6][None],
        rms_stats,
    )


FIRST = (1, 2)
SECOND = (0, 3)
EVERY = (0, 1, 2, 3)
BLOCK = 128
SCORE_SCALE = math.sqrt(HEAD)
MASKED = -1e30


def dot(left, right):
    return jnp.dot(left, right, preferred_element_type=jnp.float32)


def low(x):
    return x.astype(jnp.bfloat16)


def swap(x):
    return lax.ppermute(x, "section", [(0, 1), (1, 0)])


def along(x, route):
    return lax.ppermute(x, "seq", route)


def pick(x, index, axis):
    return lax.dynamic_index_in_dim(x, index, axis, keepdims=False)


def sums_of_halves(x):
    row = lax.broadcasted_iota(jnp.int32, (2 * HEAD, 2 * HEAD), 0) // HEAD
    col = lax.broadcasted_iota(jnp.int32, (2 * HEAD, 2 * HEAD), 1) // HEAD
    same = (row == col).astype(jnp.bfloat16)
    high = x.astype(jnp.bfloat16)
    rest = (x - high.astype(jnp.float32)).astype(jnp.bfloat16)
    return dot(high, same) + dot(rest, same)


def normal_heads(raw):
    factor = lax.rsqrt(sums_of_halves(raw * raw) + epsilon)
    return raw * factor, factor


def merge(to, own, oth):
    for s in range(4):
        to[s * 256 : s * 256 + BLOCK, : own.shape[1]] = own[s * BLOCK : (s + 1) * BLOCK]
        to[s * 256 + BLOCK : (s + 1) * 256, : own.shape[1]] = oth[s * BLOCK : (s + 1) * BLOCK]


def last_dims(left, right):
    return lax.dot_general(left, right, (((1,), (1,)), ((), ())), preferred_element_type=jnp.float32)


def head_lanes(h, dtype):
    lane = lax.broadcasted_iota(jnp.int32, (1, 2 * HEAD), 1) // HEAD
    return (lane == h).astype(dtype)


def attention_kernel(
    q_own, k_own, v_own, q_oth, k_oth, v_oth, scale, place_col, start_col, place_row,
    out_own, out_oth, bias, raw, queries, keys, values,
):
    @pl.when(pl.program_id(0) == 0)
    def _():
        fits = (place_row[...] >= start_col[...]) & (place_row[...] <= place_col[...])
        bias[...] = jnp.where(fits, 0.0, MASKED)
        values[:, 2 * HEAD :] = jnp.ones_like(values[:, 2 * HEAD :])

    merge(raw, q_own[...], q_oth[...])
    normed, _ = normal_heads(raw[...].astype(jnp.float32))
    queries[...] = low(normed * scale[...]) * SCORE_SCALE
    merge(raw, k_own[...], k_oth[...])
    normed, _ = normal_heads(raw[...].astype(jnp.float32))
    keys[...] = low(normed * scale[...])
    merge(values, v_own[...], v_oth[...])
    for s in range(4):
        upto = (s + 1) * 256
        block = queries[s * 256 : upto]
        parts = []
        for h in range(2):
            scores = last_dims(block * head_lanes(h, jnp.bfloat16), keys[:upto])
            weights = jnp.exp(scores + bias[s * 256 : upto, :upto])
            summed = dot(low(weights), values[:upto])
            parts.append(summed[:, : 2 * HEAD] / summed[:, 2 * HEAD :])
        joined = low(jnp.where(head_lanes(0, jnp.float32) > 0, parts[0], parts[1]))
        out_own[s * BLOCK : (s + 1) * BLOCK] = joined[:BLOCK]
        out_oth[s * BLOCK : (s + 1) * BLOCK] = joined[BLOCK:]


def attention_back_kernel(
    q_own, k_own, v_own, q_oth, k_oth, v_oth, g_own, g_oth, scale,
    place_col, place_row, start_row,
    out_own, out_oth, grad_scale, bias, raw, queries, keys, values, grads, dq, dk, dv,
):
    pair = pl.program_id(0)

    @pl.when(pair == 0)
    def _():
        fits = (place_col[...] >= start_row[...]) & (place_col[...] <= place_row[...])
        bias[...] = jnp.where(fits, 0.0, MASKED)

    merge(raw, q_own[...], q_oth[...])
    normed, _ = normal_heads(raw[...].astype(jnp.float32))
    queries[...] = low(normed * scale[...]) * SCORE_SCALE
    merge(raw, k_own[...], k_oth[...])
    normed, _ = normal_heads(raw[...].astype(jnp.float32))
    keys[...] = low(normed * scale[...])
    merge(values, v_own[...], v_oth[...])
    merge(grads, g_own[...], g_oth[...])
    dk[...] = jnp.zeros_like(dk)
    dv[...] = jnp.zeros_like(dv)
    for s in range(4):
        upto = (s + 1) * 256
        total = 0.0
        for h in range(2):
            lanes = head_lanes(h, jnp.bfloat16)
            query = queries[s * 256 : upto] * lanes
            grad = grads[s * 256 : upto] * lanes
            scores = last_dims(keys[:upto], query)
            weights = jnp.exp(scores + bias[:upto, s * 256 : upto])
            weights = weights * (1.0 / jnp.sum(weights, axis=0, keepdims=True))
            grad_weights = last_dims(values[:upto], grad)
            delta = jnp.sum(weights * grad_weights, axis=0, keepdims=True)
            grad_scores = low(weights * (grad_weights - delta))
            dv[:upto] += dot(low(weights), grad)
            dk[:upto] += dot(grad_scores, query)
            total = total + head_lanes(h, jnp.float32) * contract_rows(grad_scores, keys[:upto])
        dq[s * 256 : upto] = total * SCORE_SCALE

    width = out_own.shape[1] // 3
    scale_sum = 0.0
    for part, (own, oth, grad) in enumerate(((q_own, q_oth, dq), (k_own, k_oth, dk))):
        merge(raw, own[...], oth[...])
        normed, factor = normal_heads(raw[...].astype(jnp.float32))
        scale_sum = scale_sum + jnp.sum(grad[...] * normed, axis=0, keepdims=True)
        step = grad[...] * scale[...]
        grad[...] = factor * (step - normed * sums_of_halves(normed * step))
    grad_scale[...] = scale_sum
    for part, grad in enumerate((dq, dk, dv)):
        lanes = pl.ds(pl.multiple_of(part * width + pair * 2 * HEAD, 2 * HEAD), 2 * HEAD)
        for s in range(4):
            rows = slice(s * BLOCK, (s + 1) * BLOCK)
            out_own[rows, lanes] = low(grad[s * 256 : s * 256 + BLOCK])
            out_oth[rows, lanes] = low(grad[s * 256 + BLOCK : (s + 1) * 256])


def mixed_specs(rows, pairs):
    return [
        pl.BlockSpec((rows, 2 * HEAD), lambda p, part=part: (0, part * pairs + p))
        for part in range(3)
    ]


def whole(shape):
    return pl.BlockSpec(shape, lambda p: (0,) * len(shape))


def attention(mixed_own, mixed_oth, scale, places):
    rows, width = mixed_own.shape
    width //= 3
    pairs = width // (2 * HEAD)
    place, start = places
    total = 2 * rows
    spec = pl.BlockSpec((rows, 2 * HEAD), lambda p: (0, p))
    return pl.pallas_call(
        attention_kernel,
        grid=(pairs,),
        out_shape=[jax.ShapeDtypeStruct((rows, width), jnp.bfloat16)] * 2,
        in_specs=mixed_specs(rows, pairs) * 2
        + [pl.BlockSpec((1, 2 * HEAD), lambda p: (0, p))]
        + [whole((total, 1)), whole((total, 1)), whole((1, total))],
        out_specs=[spec, spec],
        scratch_shapes=[
            pltpu.VMEM((total, total), jnp.float32),
            pltpu.VMEM((total, 2 * HEAD), jnp.bfloat16),
            pltpu.VMEM((total, 2 * HEAD), jnp.bfloat16),
            pltpu.VMEM((total, 2 * HEAD), jnp.bfloat16),
            pltpu.VMEM((total, 4 * HEAD), jnp.bfloat16),
        ],
        compiler_params=pltpu.CompilerParams(vmem_limit_bytes=40 * 2**20),
        cost_estimate=pl.CostEstimate(
            flops=8 * total * total * width, bytes_accessed=8 * total * width,
            transcendentals=total * total * pairs,
        ),
    )(
        *[mixed_own] * 3, *[mixed_oth] * 3, scale,
        place[:, None], start[:, None], place[None, :],
    )


def attention_back(mixed_own, mixed_oth, grad_own, grad_oth, scale, places):
    rows, width = mixed_own.shape
    width //= 3
    pairs = width // (2 * HEAD)
    place, start = places
    total = 2 * rows
    spec = pl.BlockSpec((rows, 2 * HEAD), lambda p: (0, p))
    pair_spec = pl.BlockSpec((1, 2 * HEAD), lambda p: (0, p))
    low_scratch = pltpu.VMEM((total, 2 * HEAD), jnp.bfloat16)
    full_scratch = pltpu.VMEM((total, 2 * HEAD), jnp.float32)
    return pl.pallas_call(
        attention_back_kernel,
        grid=(pairs,),
        out_shape=[jax.ShapeDtypeStruct((rows, 3 * width), jnp.bfloat16)] * 2
        + [jax.ShapeDtypeStruct((1, width), jnp.float32)],
        in_specs=mixed_specs(rows, pairs) * 2
        + [spec, spec, pair_spec]
        + [whole((total, 1)), whole((1, total)), whole((1, total))],
        out_specs=[whole((rows, 3 * width)), whole((rows, 3 * width)), pair_spec],
        scratch_shapes=[pltpu.VMEM((total, total), jnp.float32)]
        + [low_scratch] * 5
        + [full_scratch] * 3,
        compiler_params=pltpu.CompilerParams(vmem_limit_bytes=48 * 2**20),
        cost_estimate=pl.CostEstimate(
            flops=20 * total * total * width, bytes_accessed=16 * total * width,
            transcendentals=total * total * pairs,
        ),
    )(
        *[mixed_own] * 3, *[mixed_oth] * 3, grad_own, grad_oth, scale,
        place[:, None], place[None, :], start[None, :],
    )


def forward_row(hiddens, weights, scales, places):
    w_qkv, w_out, w_up, w_gate, w_down = weights
    scale_qk, scale_up, scale_gate, alpha_attn, alpha_mlp = scales
    hidden_own, hidden_oth = hiddens
    mixed_own = low(dot(hidden_own, w_qkv))
    mixed_oth = low(dot(hidden_oth, w_qkv))
    attended_own, attended_oth = attention(mixed_own, mixed_oth, scale_qk, places)
    branch_got = swap(low(dot(attended_oth, w_out)))
    branch = dot(attended_own, w_out) + branch_got.astype(jnp.float32)
    hidden = hidden_own.astype(jnp.float32)
    first_sum = hidden + alpha_attn * (unit(branch) - hidden)
    middle = unit(first_sum)
    middle_own = low(middle)
    middle_oth = swap(middle_own)

    def lift(rows):
        lift_up = low(dot(rows, w_up))
        lift_gate = dot(rows, w_gate)
        upward = lift_up.astype(jnp.float32) * scale_up
        gating = lift_gate * scale_gate
        return lift_up, low(lift_gate), low(upward * jax.nn.silu(gating))

    lifted_own = lift(middle_own)
    lifted_oth = lift(middle_oth)
    output_got = swap(low(dot(lifted_oth[2], w_down)))
    output = dot(lifted_own[2], w_down) + output_got.astype(jnp.float32)
    second_sum = middle + alpha_mlp * (unit(output) - middle)
    result = low(unit(second_sum))
    kept = (
        hiddens, (mixed_own, mixed_oth), (attended_own, attended_oth),
        (middle_own, middle_oth), (lifted_own, lifted_oth), branch, output,
    )
    return result, kept


def backward_row(grad_out, kept, weights, scales, places):
    w_qkv, w_out, w_up, w_gate, w_down = weights
    scale_qk, scale_up, scale_gate, alpha_attn, alpha_mlp = scales
    hiddens, mixed, attended, middles, lifted, branch, output = kept
    hidden = hiddens[0].astype(jnp.float32)
    unit_branch = unit(branch)
    first_sum = hidden + alpha_attn * (unit_branch - hidden)
    middle = unit(first_sum)
    unit_output = unit(output)
    second_sum = middle + alpha_mlp * (unit_output - middle)
    grad_second = unit_back(second_sum, grad_out)
    grad_alpha_mlp = jnp.sum(grad_second * (unit_output - middle), axis=0)
    grad_output_own = low(unit_back(output, alpha_mlp * grad_second))
    grad_output_oth = swap(grad_output_own)

    def unlift(grad_rows, lifts):
        lift_up, lift_gate, _ = lifts
        lift_up = lift_up.astype(jnp.float32)
        lift_gate = lift_gate.astype(jnp.float32)
        grad_inner = contract_cols(grad_rows, w_down)
        gating = lift_gate * scale_gate
        sigmoid = jax.nn.sigmoid(gating)
        grad_up = grad_inner * (gating * sigmoid)
        grad_gate = grad_inner * (lift_up * scale_up) * sigmoid * (1.0 + gating * (1.0 - sigmoid))
        sums = (jnp.sum(grad_up * lift_up, axis=0), jnp.sum(grad_gate * lift_gate, axis=0))
        return low(grad_up * scale_up), low(grad_gate * scale_gate), sums

    grad_lift_own = unlift(grad_output_own, lifted[0])
    grad_lift_oth = unlift(grad_output_oth, lifted[1])
    middle_got = swap(
        low(contract_cols(grad_lift_oth[0], w_up) + contract_cols(grad_lift_oth[1], w_gate))
    )
    grad_middle = (
        contract_cols(grad_lift_own[0], w_up)
        + contract_cols(grad_lift_own[1], w_gate)
        + middle_got.astype(jnp.float32)
        + grad_second * (1.0 - alpha_mlp)
    )
    grad_first = unit_back(first_sum, grad_middle)
    grad_alpha_attn = jnp.sum(grad_first * (unit_branch - hidden), axis=0)
    grad_branch_own = low(unit_back(branch, alpha_attn * grad_first))
    grad_branch_oth = swap(grad_branch_own)
    grad_attended_own = low(contract_cols(grad_branch_own, w_out))
    grad_attended_oth = low(contract_cols(grad_branch_oth, w_out))
    grad_mixed_own, grad_mixed_oth, grad_scale_qk = attention_back(
        *mixed, grad_attended_own, grad_attended_oth, scale_qk, places
    )
    hidden_got = swap(low(contract_cols(grad_mixed_oth, w_qkv)))
    grad_hidden = (
        contract_cols(grad_mixed_own, w_qkv)
        + hidden_got.astype(jnp.float32)
        + grad_first * (1.0 - alpha_attn)
    )
    operands = (
        (hiddens, (grad_mixed_own, grad_mixed_oth)),
        (attended, (grad_branch_own, grad_branch_oth)),
        (middles, (grad_lift_own[0], grad_lift_oth[0])),
        (middles, (grad_lift_own[1], grad_lift_oth[1])),
        ((lifted[0][2], lifted[1][2]), (grad_output_own, grad_output_oth)),
    )
    small = (
        jnp.concatenate([grad_alpha_attn, grad_alpha_mlp]),
        grad_lift_own[2][0] + grad_lift_oth[2][0],
        (grad_lift_own[2][1] + grad_lift_oth[2][1]) * math.sqrt(hidden.shape[1]),
        grad_scale_qk[0],
    )
    return low(grad_hidden), operands, small


def weight_grads(operands):
    return tuple(
        low(contract_rows(jnp.concatenate(left), jnp.concatenate(right)))
        for left, right in operands
    )


MESH = pl.DeviceIdType.MESH


def position():
    c, s, f = (lax.axis_index(name) for name in ("section", "seq", "fsdp"))
    x, y = f % 2, f // 2
    layer = 1 - ((s + 1) // 2) % 2
    return c, s, f, y * 2 + 1 - x, (1 - y) * 2 + x, layer


def greet(devices):
    barrier = pltpu.get_barrier_semaphore()
    for device in devices:
        pl.semaphore_signal(barrier, inc=1, device_id=device, device_id_type=MESH)
    pl.semaphore_wait(barrier, len(devices))


def remote(src, dst, send, recv, device):
    return pltpu.make_async_remote_copy(
        src_ref=src, dst_ref=dst, send_sem=send, recv_sem=recv, device_id=device, device_id_type=MESH
    )


def arrived(ref, sem):
    pltpu.make_async_copy(ref, ref, sem).wait()


def lane(offset):
    return pl.multiple_of(offset, 128)


def gather_kernel(
    w_qkv, w_out, w_in, w_down, vectors, valid, tokens, cotangent,
    o_qkv, o_out, o_up, o_gate, o_down, o_vectors, o_valid, row_own, row_oth,
    first_send, first_recv, next_send, next_recv, row_send, row_recv, valid_send, valid_recv,
    swap_send, swap_recv,
):
    c, s, f, fx, fy, layer = position()
    greet(
        [(1 - c, s, f), (c, s, fx), (1 - c, s, fx), (c, s, fy), (1 - c, s, fy)]
        + [(c, (s + step) % 4, f) for step in (1, 2, 3)]
    )

    for to, held in enumerate((cotangent.at[0], tokens.at[0], tokens.at[1], cotangent.at[1])):
        src = held.at[pl.ds(c * BLOCK, BLOCK)]
        dst = row_own.at[pl.ds(s * BLOCK, BLOCK)]
        flags, flags_to = valid.at[to // 2], o_valid.at[s]

        @pl.when(s == to)
        def _():
            pltpu.make_async_copy(src, dst, row_recv.at[s]).start()
            pltpu.make_async_copy(flags, flags_to, valid_recv.at[s]).start()

        @pl.when(s != to)
        def _():
            remote(src, dst, row_send.at[to], row_recv.at[s], (c, to, f)).start()
            remote(flags, flags_to, valid_send.at[to], valid_recv.at[s], (c, to, f)).start()

    def pieces(item, h):
        if item == 0:
            return [(vectors, o_vectors.at[f])]
        if item == 1:
            return [
                (
                    w_qkv.at[:, pl.ds(lane(part * 256 + h * 128), 128)],
                    o_qkv.at[pl.ds(f * 256, 256), pl.ds(part * 128, 128)],
                )
                for part in range(12)
            ]
        if item == 2:
            return [(w_out.at[pl.ds(h * 128, 128)], o_out.at[pl.ds(f * 128, 128)])]
        if item in (3, 4):
            to = (o_up, o_gate)[item - 3]
            return [
                (
                    w_in.at[:, pl.ds(lane((item - 3) * 4096 + part * 1024 + h * 512), 512)],
                    to.at[pl.ds(f * 256, 256), pl.ds(part * 512, 512)],
                )
                for part in range(4)
            ]
        return [(w_down.at[pl.ds(h * 512, 512)], o_down.at[pl.ds(f * 512, 512)])]

    outputs = (o_vectors, o_qkv, o_out, o_up, o_gate, o_down)

    def block(item, of):
        if item == 0:
            return o_vectors.at[of]
        rows = outputs[item].shape[0] // 4
        return outputs[item].at[pl.ds(of * rows, rows)]

    def part_of(item, of, part):
        if item == 0:
            return o_vectors.at[of, pl.ds(part * 16, 16)]
        rows = outputs[item].shape[0] // 8
        return outputs[item].at[pl.ds(of * 2 * rows + part * rows, rows)]

    targets = (
        ((c, s, fx), c, 1), ((c, s, fy), c, 2), ((1 - c, s, fx), 1 - c, 1),
        ((1 - c, s, fy), 1 - c, 2), ((1 - c, s, f), 1 - c, 0),
    )

    @pl.when(c == layer)
    def _():
        for item in range(6):
            for index, (device, h, came) in enumerate(targets):
                for src, dst in pieces(item, h):
                    remote(
                        src, dst, first_send.at[item, index], first_recv.at[item, came], device
                    ).start()
            for src, dst in pieces(item, c):
                pltpu.make_async_copy(src, dst, first_recv.at[item, 0]).start()

    for came in range(4):
        arrived(row_own.at[pl.ds(came * BLOCK, BLOCK)], row_recv.at[came])
    swapped = remote(row_own, row_oth, swap_send, swap_recv, (1 - c, s, f))
    swapped.start()

    forwards = []
    for item in range(6):
        for part, (came, of, to) in enumerate(((1, fx, fy), (2, fy, fx))):
            arrived(block(item, of), first_recv.at[item, came])
            forward = remote(
                part_of(item, of, part), part_of(item, of, part),
                next_send.at[item, part], next_recv.at[item, part], (c, s, to),
            )
            forward.start()
            forwards.append(forward)

    across = 3 - f
    for item in range(6):
        arrived(block(item, f), first_recv.at[item, 0])
        for part in range(2):
            arrived(part_of(item, across, part), next_recv.at[item, part])
    for forward in forwards:
        forward.wait_send()
    swapped.wait()
    for came in range(4):
        arrived(o_valid.at[came], valid_recv.at[came])

        @pl.when(s != came)
        def _():
            arrived(row_own.at[pl.ds(came * BLOCK, BLOCK)], row_send.at[came])
            arrived(o_valid.at[came], valid_send.at[came])

    @pl.when(c == layer)
    def _():
        for item in range(6):
            for index in range(len(targets)):
                arrived(block(item, f), first_send.at[item, index])


def gather(w_qkv, w_out, w_in, w_down, vectors, valid, tokens, cotangent):
    width = w_out.shape[1]
    units = w_down.shape[0] * 4
    low_shape = lambda *shape: jax.ShapeDtypeStruct(shape, jnp.bfloat16)
    sems = pltpu.SemaphoreType.DMA
    return pl.pallas_call(
        gather_kernel,
        out_shape=[
            low_shape(width, 3 * width // 2),
            low_shape(width // 2, width),
            low_shape(width, units // 2),
            low_shape(width, units // 2),
            low_shape(units // 2, width),
            low_shape(4, *vectors.shape),
            low_shape(4, *valid.shape[1:]),
            low_shape(4 * BLOCK, width),
            low_shape(4 * BLOCK, width),
        ],
        in_specs=[pl.BlockSpec(memory_space=pl.ANY)] * 8,
        out_specs=[pl.BlockSpec(memory_space=pl.ANY)] * 9,
        scratch_shapes=[
            sems((6, 5)), sems((6, 3)), sems((6, 2)), sems((6, 2)), sems((4,)), sems((4,)),
            sems((4,)), sems((4,)), sems, sems,
        ],
        compiler_params=pltpu.CompilerParams(collective_id=0, has_side_effects=True),
    )(w_qkv, w_out, w_in, w_down, vectors, valid, tokens, cotangent)


CHUNKS = 16


BUFFERS, SEMAPHORES = 8, 18


class Flow:
    def __init__(self, buffers, semaphores):
        (
            self.near_own, self.near_far, self.far_in, self.own, self.passing,
            self.from_left, self.from_right, self.pair_sum,
        ) = buffers
        (
            self.load_own, self.load_pass, self.send_own, self.recv_own, self.send_far,
            self.recv_far, self.send_next, self.recv_next, self.send_z, self.recv_left,
            self.recv_right, self.recv_pair, self.send_on, self.send_back, self.send_out,
            self.keep, self.give, self.given,
        ) = semaphores
        self.place_of = position()

    def neighbours(self, k):
        c, s, f, fx, fy, _ = self.place_of
        return fx + (fy - fx) * (k % 2), fy + (fx - fy) * (k % 2)

    def begin(self, k, source):
        c, s, f, _, _, _ = self.place_of
        near, far = self.neighbours(k)
        to = (c, s, near)
        remote(source(near), self.near_own.at[k], self.send_own.at[k], self.recv_own.at[k], to).start()
        remote(
            source(3 - f), self.near_far.at[k], self.send_far.at[k], self.recv_far.at[k], to
        ).start()
        pltpu.make_async_copy(source(far), self.passing.at[k], self.load_pass.at[k]).start()
        pltpu.make_async_copy(source(f), self.own.at[k], self.load_own.at[k]).start()

    def add(self, to, *refs):
        total = refs[0][...].astype(jnp.float32)
        for ref in refs[1:]:
            total = total + ref[...].astype(jnp.float32)
        to[...] = total.astype(to.dtype)

    def pass_on(self, k):
        c, s, f, _, _, _ = self.place_of
        _, far = self.neighbours(k)
        arrived(self.passing.at[k], self.load_pass.at[k])
        arrived(self.near_far.at[k], self.recv_far.at[k])
        self.add(self.passing.at[k], self.passing.at[k], self.near_far.at[k])
        remote(
            self.passing.at[k], self.far_in.at[k], self.send_next.at[k], self.recv_next.at[k],
            (c, s, far),
        ).start()

    def finish_plane(self, k):
        c, s, f, _, _, _ = self.place_of
        own = self.own.at[k]
        arrived(own, self.load_own.at[k])
        arrived(self.near_own.at[k], self.recv_own.at[k])
        arrived(self.far_in.at[k], self.recv_next.at[k])
        self.add(own, own, self.near_own.at[k], self.far_in.at[k])
        send = self.send_z.at[k]

        @pl.when(s == 0)
        def _():
            remote(own, self.from_left.at[k], send, self.recv_left.at[k], (c, 1, f)).start()

        @pl.when(s == 3)
        def _():
            remote(own, self.from_right.at[k], send, self.recv_right.at[k], (c, 2, f)).start()

        @pl.when((s == 1) | (s == 2))
        def _():
            remote(own, self.pair_sum.at[k], send, self.recv_pair.at[k], (c, 3 - s, f)).start()

    def middle_planes(self, k):
        c, s, f, _, _, _ = self.place_of
        left, right, pair = self.from_left.at[k], self.from_right.at[k], self.pair_sum.at[k]

        @pl.when(s == 1)
        def _():
            arrived(left, self.recv_left.at[k])
            remote(left, left, self.send_on.at[k], self.recv_left.at[k], (c, 2, f)).start()

        @pl.when(s == 2)
        def _():
            arrived(right, self.recv_right.at[k])
            remote(right, right, self.send_on.at[k], self.recv_right.at[k], (c, 1, f)).start()

        @pl.when((s == 1) | (s == 2))
        def _():
            arrived(pair, self.recv_pair.at[k])
            arrived(pair, self.send_z.at[k])
            self.add(pair, pair, self.own.at[k])
            to = (c, (s - 1) * 3, f)
            remote(pair, pair, self.send_out.at[k], self.recv_pair.at[k], to).start()

    def all_planes(self, k):
        c, s, f, _, _, _ = self.place_of
        left, right, pair = self.from_left.at[k], self.from_right.at[k], self.pair_sum.at[k]
        own, total = self.own.at[k], self.near_own.at[k]

        @pl.when(s == 1)
        def _():
            arrived(right, self.recv_right.at[k])
            remote(right, right, self.send_back.at[k], self.recv_right.at[k], (c, 0, f)).start()

        @pl.when(s == 2)
        def _():
            arrived(left, self.recv_left.at[k])
            remote(left, left, self.send_back.at[k], self.recv_left.at[k], (c, 3, f)).start()

        @pl.when((s == 1) | (s == 2))
        def _():
            self.add(total, left, right)

        @pl.when(s == 0)
        def _():
            arrived(pair, self.recv_pair.at[k])
            arrived(right, self.recv_right.at[k])
            self.add(total, own, right)

        @pl.when(s == 3)
        def _():
            arrived(pair, self.recv_pair.at[k])
            arrived(left, self.recv_left.at[k])
            self.add(total, own, left)

    def place(self, k, pieces):
        c, s, f, _, _, _ = self.place_of
        for owner, chunk in ((0, self.pair_sum.at[k]), (1, self.near_own.at[k])):
            for src, dst in pieces:

                @pl.when(c == owner)
                def _():
                    pltpu.make_async_copy(src(chunk), dst, self.keep.at[k]).start()

                @pl.when(c != owner)
                def _():
                    remote(
                        src(chunk), dst, self.give.at[k], self.given.at[k], (1 - c, s, f)
                    ).start()

    def settle(self, k):
        c, s, f, _, _, _ = self.place_of
        chunk = self.own.at[k]
        for sem in (
            self.send_own, self.send_far, self.send_next, self.keep, self.give, self.given
        ):
            arrived(chunk, sem.at[k])

        @pl.when((s == 1) | (s == 2))
        def _():
            for sem in (self.send_on, self.send_back, self.send_out):
                arrived(chunk, sem.at[k])

        @pl.when((s == 0) | (s == 3))
        def _():
            arrived(chunk, self.send_z.at[k])


def reduce_kernel(
    g_down, g_up, g_gate, g_out, g_qkv, g_vectors, hidden, grad,
    o_down, o_in, o_out, o_qkv, o_vectors, o_hidden, o_grad,
    *scratch,
):
    c, s, f, fx, fy, layer = position()
    greet(
        [(c, s, fx), (c, s, fy), (1 - c, s, f)]
        + [(core, (s + step) % 4, f) for core in (0, 1) for step in (1, 2, 3)]
    )
    rows_send, rows_recv = scratch[-2:]

    for array, (held, to_ref) in enumerate(((hidden, o_hidden), (grad, o_grad))):
        for to in range(4):
            src = held.at[pl.ds(to * BLOCK, BLOCK)]
            dst = to_ref.at[s // 2, pl.ds(c * BLOCK, BLOCK)]
            recv = rows_recv.at[array, s // 2, c]
            here = (s == to) & (c == layer)

            @pl.when(here)
            def _():
                pltpu.make_async_copy(src, dst, recv).start()

            @pl.when(jnp.logical_not(here))
            def _():
                remote(src, dst, rows_send.at[array, to], recv, (layer, to, f)).start()

    matrices = Flow(scratch[:BUFFERS], scratch[BUFFERS : BUFFERS + SEMAPHORES])
    rest = scratch[BUFFERS + SEMAPHORES : -2]
    vectors = Flow(rest[:BUFFERS], rest[BUFFERS:])

    def start_first(k):
        @pl.when(k < 4)
        def _():
            matrices.begin(
                k,
                lambda to: g_down.at[
                    pl.ds(to * 512 + (k // 2) * 256, 256), pl.ds(lane((k % 2) * 512), 512)
                ],
            )

        for first, ref in ((4, g_up), (8, g_gate), (12, g_out), (13, g_qkv)):
            count = ref.shape[1] // 512

            @pl.when((k >= first) & (k < first + count))
            def _():
                matrices.begin(
                    k,
                    lambda to: ref.at[pl.ds(to * 256, 256), pl.ds(lane((k - first) * 512), 512)],
                )

    def everything(chunk):
        return chunk

    def place(k):
        @pl.when(k < 4)
        def _():
            rows = pl.ds(c * 512 + (k // 2) * 256, 256)
            matrices.place(k, [(everything, o_down.at[rows, pl.ds(lane((k % 2) * 512), 512)])])

        @pl.when((k >= 4) & (k < 12))
        def _():
            lanes = pl.ds(lane((k - 4) * 1024 + c * 512), 512)
            matrices.place(k, [(everything, o_in.at[:, lanes])])

        @pl.when(k == 12)
        def _():
            matrices.place(
                k,
                [
                    (
                        lambda chunk, part=part: chunk.at[pl.ds(part * 128, 128)],
                        o_out.at[pl.ds(c * 128, 128), pl.ds(part * 512, 512)],
                    )
                    for part in range(2)
                ],
            )

        @pl.when(k > 12)
        def _():
            matrices.place(
                k,
                [
                    (
                        lambda chunk, part=part: chunk.at[:, pl.ds(part * 128, 128)],
                        o_qkv.at[:, pl.ds(lane((k - 13) * 1024 + part * 256 + c * 128), 128)],
                    )
                    for part in range(4)
                ],
            )

    vectors.begin(0, lambda to: g_vectors.at[to])
    ahead, lag_plane, lag_middle, lag_all = 3, 2, 4, 7
    for k in range(ahead):
        start_first(k)

    def last(k):
        matrices.all_planes(k)
        place(k)

    def last_vectors(k):
        vectors.all_planes(k)
        vectors.place(k, [(everything, o_vectors.at[c])])

    def step(t, carry):
        @pl.when(t + ahead < CHUNKS)
        def _():
            start_first(t + ahead)

        for lag, work, work_vectors in (
            (0, matrices.pass_on, vectors.pass_on),
            (lag_plane, matrices.finish_plane, vectors.finish_plane),
            (lag_middle, matrices.middle_planes, vectors.middle_planes),
            (lag_all, last, last_vectors),
        ):
            @pl.when(t == lag)
            def _():
                work_vectors(0)

            @pl.when((t >= lag) & (t < CHUNKS + lag))
            def _():
                work(t - lag)

        return carry

    lax.fori_loop(0, CHUNKS + lag_all, step, 0)

    def settle(k, carry):
        matrices.settle(k)
        return carry

    lax.fori_loop(0, CHUNKS, settle, 0)
    vectors.settle(0)
    for array, (held, to_ref) in enumerate(((hidden, o_hidden), (grad, o_grad))):
        for to in range(4):
            @pl.when(jnp.logical_not((s == to) & (c == layer)))
            def _():
                arrived(held.at[pl.ds(to * BLOCK, BLOCK)], rows_send.at[array, to])

        for micro in range(2):
            for core in range(2):
                arrived(
                    to_ref.at[micro, pl.ds(core * BLOCK, BLOCK)], rows_recv.at[array, micro, core]
                )


def reduce_all(g_down, g_up, g_gate, g_out, g_qkv, g_vectors, hidden, grad):
    width = g_down.shape[1]
    low_shape = lambda *shape: jax.ShapeDtypeStruct(shape, jnp.bfloat16)
    sems = pltpu.SemaphoreType.DMA
    small = g_vectors.shape[1:]
    return pl.pallas_call(
        reduce_kernel,
        out_shape=[
            low_shape(g_down.shape[0] // 2, width),
            low_shape(g_up.shape[0] // 4, 4 * g_up.shape[1]),
            low_shape(width // 4, width),
            low_shape(width // 4, 2 * g_qkv.shape[1]),
            jax.ShapeDtypeStruct((2, *small), jnp.float32),
            low_shape(2, 2 * BLOCK, width),
            low_shape(2, 2 * BLOCK, width),
        ],
        in_specs=[pl.BlockSpec(memory_space=pl.ANY)] * 8,
        out_specs=[pl.BlockSpec(memory_space=pl.ANY)] * 7,
        scratch_shapes=[pltpu.VMEM((CHUNKS, 256, 512), jnp.bfloat16)] * BUFFERS
        + [sems((CHUNKS,))] * SEMAPHORES
        + [pltpu.VMEM((1, *small), jnp.float32)] * BUFFERS
        + [sems((1,))] * SEMAPHORES
        + [sems((2, 4)), sems((2, 2, 2))],
        compiler_params=pltpu.CompilerParams(
            collective_id=1, has_side_effects=True, vmem_limit_bytes=48 * 2**20
        ),
    )(g_down, g_up, g_gate, g_out, g_qkv, g_vectors, hidden, grad)


def per_device(
    tokens, cotangent, lengths, valid_mask, w_qkv, w_out, w_in, w_down, qk_scale, mlp_scale, alphas
):
    c, s, f, _, _, layer = position()
    second = layer == 1
    micro = s // 2
    width = tokens.shape[3]
    group = tokens.shape[2]
    units = w_down.shape[1] * 4

    vectors = jnp.concatenate([qk_scale[0], mlp_scale[0], alphas[0]])
    vectors = jnp.pad(vectors, (0, 32 * 128 - vectors.shape[0])).reshape(32, 128)
    valid = low(jnp.pad(valid_mask[:, 0], ((0, 0), (0, 16 * 128 - group)))).reshape(2, 16, 128)
    *weights, vectors, valid, row, row_oth = gather(
        w_qkv[0], w_out[0], w_in[0], w_down[0], vectors, valid, tokens[:, 0], cotangent[:, 0]
    )
    vectors = vectors.reshape(4, -1).astype(jnp.float32)
    cut_qk, cut_mlp = qk_scale.shape[1], qk_scale.shape[1] + mlp_scale.shape[1]
    all_qk = vectors[:, :cut_qk].reshape(4, 2, -1)
    all_mlp = vectors[:, cut_qk:cut_mlp].reshape(2, 4, 2, -1)
    all_alphas = vectors[:, cut_mlp : cut_mlp + alphas.shape[1]].reshape(2, 1, -1)
    mlp_half = pick(all_mlp, c, 2).reshape(2, 1, -1)
    scales = (
        pick(all_qk, c, 1).reshape(1, -1),
        mlp_half[0],
        mlp_half[1] * math.sqrt(width),
        all_alphas[0],
        all_alphas[1],
    )

    index = jnp.arange(4 * group, dtype=jnp.int32)
    place = (index // 256) * 256 + (((index // BLOCK) + c) % 2) * BLOCK + index % BLOCK
    ends = jnp.cumsum(pick(lengths, micro, 0)[0])[:-1]
    passed = place[:, None] >= ends[None, :]
    start = jnp.max(jnp.where(passed, ends[None, :], 0), axis=1)
    places = (place, start)
    valid = pick(valid[:, :2], c, 1).reshape(-1).astype(jnp.float32)

    result, _ = forward_row((row, row_oth), weights, scales, places)
    arrived_row = along(result, [(1, 0), (2, 3)])
    hidden_own = jnp.where(second, arrived_row, row)
    result, kept = forward_row((hidden_own, swap(hidden_own)), weights, scales, places)
    branch = kept[5]
    statistic = jnp.sum(valid * jnp.sum(branch * branch, axis=-1))

    grad_row = row.astype(jnp.float32)
    grad_hidden, _, _ = backward_row(grad_row, kept, weights, scales, places)
    arrived_row = along(grad_hidden, [(0, 1), (3, 2)])
    grad_row = jnp.where(second, grad_row, arrived_row.astype(jnp.float32))
    grad_hidden, operands, small = backward_row(grad_row, kept, weights, scales, places)
    g_qkv, g_out, g_up, g_gate, g_down = weight_grads(operands)
    g_out = g_out.reshape(4, BLOCK, 2, -1).transpose(0, 2, 1, 3).reshape(4 * 2 * BLOCK, -1)

    at_half = jnp.arange(2).reshape(1, 1, 2, 1) == c
    up_gate = jnp.stack([small[1], small[2]]).reshape(2, 4, 1, -1)
    g_vectors = jnp.concatenate(
        [
            jnp.where(at_half[0], small[3].reshape(4, 1, -1), 0.0).reshape(4, -1),
            jnp.where(at_half, up_gate, 0.0).reshape(4, -1),
            small[0].reshape(4, -1),
            jnp.full((4, 1), statistic),
        ],
        axis=1,
    )
    g_vectors = jnp.pad(g_vectors, ((0, 0), (0, 24 * 128 - g_vectors.shape[1]))).reshape(4, 24, 128)
    grad_down, grad_in_proj, grad_out, grad_qkv, vectors, hidden_out, grad_in = reduce_all(
        g_down, g_up, g_gate, g_out, g_qkv, g_vectors, result, grad_hidden
    )
    full = jnp.sum(vectors, axis=0).reshape(-1)
    cuts = (cut_qk, cut_mlp, cut_mlp + alphas.shape[1])
    grad_qk_scale = full[: cuts[0]][None]
    grad_mlp_scale = full[cuts[0] : cuts[1]][None]
    grad_alphas = full[cuts[1] : cuts[2]][None]
    token_count = tokens.shape[0] * lax.axis_size("fsdp") * 4 * group
    rms_stats = jnp.sqrt(full[cuts[2] : cuts[2] + 1] / token_count + epsilon)
    as_float = [
        part.astype(jnp.float32)[None] for part in (grad_qkv, grad_out, grad_in_proj, grad_down)
    ]
    return (
        hidden_out[None, :, None], grad_in.astype(jnp.float32)[None, :, None], *as_float,
        grad_qk_scale, grad_mlp_scale, grad_alphas, rms_stats,
    )


def solution(mesh):
    placed = (
        P(None, "fsdp", "seq", None),
        P(None, "fsdp", "seq", None),
        P(None, "fsdp", None),
        P(None, "fsdp", "seq"),
        P("section", "fsdp", None),
        P("section", "fsdp", None),
        P("section", "fsdp", None),
        P("section", "fsdp", None),
        P("section", "fsdp"),
        P("section", "fsdp"),
        P("section", "fsdp"),
    )
    planes = mesh.shape["section"] == 2 and mesh.shape["seq"] == 4 and mesh.shape["fsdp"] == 4
    return jax.shard_map(
        per_device if planes else per_device_general,
        mesh=mesh,
        in_specs=placed,
        out_specs=(
            P("section", None, "fsdp", "seq", None),
            P("section", None, "fsdp", "seq", None),
            P("section", "fsdp", None),
            P("section", "fsdp", None),
            P("section", "fsdp", None),
            P("section", "fsdp", None),
            P("section", "fsdp"),
            P("section", "fsdp"),
            P("section", "fsdp"),
            P("section"),
        ),
        check_vma=False,
    )
```

```python
import math

import jax
import jax.numpy as jnp
from jax import lax
from jax.experimental import pallas as pl
from jax.experimental.pallas import tpu as pltpu
from jax.sharding import PartitionSpec as P

HEAD = 64


epsilon = 1e-06


def shifted(block, axis, distance):
    devices = range(lax.axis_size(axis))
    route = [(i - distance, i) for i in devices if i - distance in devices]
    return lax.ppermute(block, axis, route)


def for_sending(x):
    return jax.tree.map(lambda a: a.astype(jnp.bfloat16) if a.dtype == jnp.float32 else a, x)


def unit(values):
    return values * lax.rsqrt(jnp.sum(values * values, axis=-1, keepdims=True) + epsilon)


def unit_back(values, grad):
    factor = lax.rsqrt(jnp.sum(values * values, axis=-1, keepdims=True) + epsilon)
    normed = values * factor
    return factor * (grad - normed * jnp.sum(normed * grad, axis=-1, keepdims=True))


def contract_rows(left, right):
    return lax.dot_general(
        left, right, (((0,), (0,)), ((), ())), preferred_element_type=jnp.float32
    )


def contract_cols(left, right):
    return lax.dot_general(
        left, right, (((1,), (1,)), ((), ())), preferred_element_type=jnp.float32
    )


def segments_of(row_lengths, seq_len):
    ends = jnp.cumsum(row_lengths)[:-1]
    place = jnp.arange(seq_len, dtype=jnp.int32)
    return (place, jnp.sum((place[:, None] >= ends[None, :]).astype(jnp.int32), axis=1))


def allowed_pairs(row_lengths, offset, group, seq_len):
    key_place, key_segment = segments_of(row_lengths, seq_len)
    query_place = offset + jnp.arange(group, dtype=jnp.int32)
    query_segment = lax.dynamic_slice_in_dim(key_segment, offset, group)
    return (query_segment[:, None] == key_segment[None, :]) & (
        key_place[None, :] <= query_place[:, None]
    )


def masked_scores(queries, key_heads, allowed):
    scores = jnp.einsum(
        "qhd,khd->hqk", queries, key_heads, preferred_element_type=jnp.float32
    ) * math.sqrt(HEAD)
    return jnp.where(allowed[None], scores, -1e30)


def forward_layer(hidden_b, params, allowed, valid):
    w_qkv, w_out, w_in, w_down, qk_scale, mlp_scale, alphas = params
    count, width = hidden_b.shape
    heads = width // HEAD
    hidden = hidden_b.astype(jnp.float32)
    mixed = jnp.dot(hidden_b, w_qkv, preferred_element_type=jnp.float32)
    query_raw = mixed[:, :width].reshape(count, heads, HEAD)
    key_raw = mixed[:, width : 2 * width].reshape(count, heads, HEAD)
    head_scale = qk_scale.astype(jnp.float32).reshape(heads, HEAD)
    query_b = (unit(query_raw) * head_scale).astype(jnp.bfloat16)
    key_b = (unit(key_raw) * head_scale).astype(jnp.bfloat16).reshape(count, width)
    value_b = mixed[:, 2 * width :].astype(jnp.bfloat16)
    keys, values = (
        lax.all_gather(key_b, "seq", axis=0, tiled=True),
        lax.all_gather(value_b, "seq", axis=0, tiled=True),
    )
    key_heads = keys.reshape(-1, heads, HEAD)
    value_heads = values.reshape(-1, heads, HEAD)
    scores = masked_scores(query_b, key_heads, allowed)
    highest = jnp.max(scores, axis=-1, keepdims=True)
    weights = jnp.exp(scores - highest)
    denominator = jnp.sum(weights, axis=-1, keepdims=True)
    weights = weights / denominator
    log_total = highest + jnp.log(denominator)
    attended = jnp.einsum(
        "hqk,khd->qhd",
        weights.astype(jnp.bfloat16),
        value_heads,
        preferred_element_type=jnp.float32,
    )
    attended_b = attended.reshape(count, width).astype(jnp.bfloat16)
    branch = jnp.dot(attended_b, w_out, preferred_element_type=jnp.float32)
    statistic = jnp.sum(valid * jnp.sum(branch * branch, axis=-1))
    step_sizes = alphas.astype(jnp.float32)
    first_sum = hidden + step_sizes[:width] * (unit(branch) - hidden)
    middle = unit(first_sum)
    middle_b = middle.astype(jnp.bfloat16)
    lifted = jnp.dot(middle_b, w_in, preferred_element_type=jnp.float32)
    units_count = lifted.shape[1] // 2
    scales = mlp_scale.astype(jnp.float32)
    upward = lifted[:, :units_count] * scales[:units_count]
    gating = lifted[:, units_count:] * scales[units_count:] * math.sqrt(width)
    inner_b = (upward * jax.nn.silu(gating)).astype(jnp.bfloat16)
    output = jnp.dot(inner_b, w_down, preferred_element_type=jnp.float32)
    second_sum = middle + step_sizes[width:] * (unit(output) - middle)
    result = unit(second_sum).astype(jnp.bfloat16)
    kept = (
        hidden_b,
        query_raw,
        key_raw,
        query_b,
        keys,
        values,
        log_total,
        attended_b,
        branch,
        first_sum,
        middle_b,
        lifted,
        inner_b,
        output,
        second_sum,
    )
    return (result, kept, statistic)


def backward_layer(kept, params, grad_out, allowed):
    (
        hidden_b,
        query_raw,
        key_raw,
        query_b,
        keys,
        values,
        log_total,
        attended_b,
        branch,
        first_sum,
        middle_b,
        lifted,
        inner_b,
        output,
        second_sum,
    ) = kept
    w_qkv, w_out, w_in, w_down, qk_scale, mlp_scale, alphas = params
    count, width = hidden_b.shape
    heads = width // HEAD
    hidden = hidden_b.astype(jnp.float32)
    step_sizes = alphas.astype(jnp.float32)
    alpha_attn = step_sizes[:width]
    alpha_mlp = step_sizes[width:]
    middle = unit(first_sum)
    grad_second = unit_back(second_sum, grad_out)
    grad_alpha_mlp = jnp.sum(grad_second * (unit(output) - middle), axis=0)
    grad_output = unit_back(output, alpha_mlp * grad_second).astype(jnp.bfloat16)
    grad_middle = grad_second * (1.0 - alpha_mlp)
    grad_down = contract_rows(inner_b, grad_output)
    grad_inner = contract_cols(grad_output, w_down)
    units_count = lifted.shape[1] // 2
    scales = mlp_scale.astype(jnp.float32)
    root = math.sqrt(width)
    lift_up = lifted[:, :units_count]
    lift_gate = lifted[:, units_count:]
    upward = lift_up * scales[:units_count]
    gating = lift_gate * scales[units_count:] * root
    sigmoid = jax.nn.sigmoid(gating)
    grad_upward = grad_inner * jax.nn.silu(gating)
    grad_gating = grad_inner * upward * sigmoid * (1.0 + gating * (1.0 - sigmoid))
    grad_scale_mlp = jnp.concatenate(
        [jnp.sum(grad_upward * lift_up, axis=0), jnp.sum(grad_gating * root * lift_gate, axis=0)]
    )
    grad_lifted = jnp.concatenate(
        [grad_upward * scales[:units_count], grad_gating * root * scales[units_count:]], axis=1
    ).astype(jnp.bfloat16)
    grad_in_proj = contract_rows(middle_b, grad_lifted)
    grad_middle = grad_middle + contract_cols(grad_lifted, w_in)
    grad_first = unit_back(first_sum, grad_middle)
    grad_alpha_attn = jnp.sum(grad_first * (unit(branch) - hidden), axis=0)
    grad_branch = unit_back(branch, alpha_attn * grad_first).astype(jnp.bfloat16)
    grad_hidden = grad_first * (1.0 - alpha_attn)
    grad_out_proj = contract_rows(attended_b, grad_branch)
    grad_attended = (
        contract_cols(grad_branch, w_out).astype(jnp.bfloat16).reshape(count, heads, HEAD)
    )
    key_heads = keys.reshape(-1, heads, HEAD)
    value_heads = values.reshape(-1, heads, HEAD)
    scores = masked_scores(query_b, key_heads, allowed)
    weights = jnp.exp(scores - log_total)
    grad_weights = jnp.einsum(
        "qhd,khd->hqk", grad_attended, value_heads, preferred_element_type=jnp.float32
    )
    delta = jnp.sum(weights * grad_weights, axis=-1, keepdims=True)
    grad_scores = (weights * (grad_weights - delta)).astype(jnp.bfloat16)
    score_scale = math.sqrt(HEAD)
    grad_query = (
        jnp.einsum("hqk,khd->qhd", grad_scores, key_heads, preferred_element_type=jnp.float32)
        * score_scale
    )
    seq_len = keys.shape[0]
    grad_keys = (
        jnp.einsum("hqk,qhd->khd", grad_scores, query_b, preferred_element_type=jnp.float32)
        * score_scale
    )
    grad_values = jnp.einsum(
        "hqk,qhd->khd",
        weights.astype(jnp.bfloat16),
        grad_attended,
        preferred_element_type=jnp.float32,
    )
    grad_key_own, grad_value_own = (
        lax.psum_scatter(
            grad_keys.reshape(seq_len, width).astype(jnp.bfloat16),
            "seq",
            scatter_dimension=0,
            tiled=True,
        ).astype(jnp.float32),
        lax.psum_scatter(
            grad_values.reshape(seq_len, width).astype(jnp.bfloat16),
            "seq",
            scatter_dimension=0,
            tiled=True,
        ).astype(jnp.float32),
    )
    head_scale = qk_scale.astype(jnp.float32).reshape(heads, HEAD)
    grad_key_heads = grad_key_own.reshape(count, heads, HEAD)
    grad_scale_qk = (
        jnp.sum(grad_query * unit(query_raw), axis=0)
        + jnp.sum(grad_key_heads * unit(key_raw), axis=0)
    ).reshape(width)
    grad_query_raw = unit_back(query_raw, grad_query * head_scale).reshape(count, width)
    grad_key_raw = unit_back(key_raw, grad_key_heads * head_scale).reshape(count, width)
    grad_mixed = jnp.concatenate([grad_query_raw, grad_key_raw, grad_value_own], axis=1).astype(
        jnp.bfloat16
    )
    grad_qkv = contract_rows(hidden_b, grad_mixed)
    grad_hidden = grad_hidden + contract_cols(grad_mixed, w_qkv)
    grad_step_sizes = jnp.concatenate([grad_alpha_attn, grad_alpha_mlp])
    grads = (
        grad_qkv,
        grad_out_proj,
        grad_in_proj,
        grad_down,
        grad_scale_qk,
        grad_scale_mlp,
        grad_step_sizes,
    )
    return (grad_hidden, grads)


def per_device_general(
    tokens, cotangent, lengths, valid_mask, w_qkv, w_out, w_in, w_down, qk_scale, mlp_scale, alphas
):
    shards = (w_qkv, w_out, w_in, w_down, qk_scale, mlp_scale, alphas)
    gathered = (
        lax.all_gather(shards[0], "fsdp", axis=1, tiled=True),
        lax.all_gather(shards[1], "fsdp", axis=1, tiled=True),
        lax.all_gather(shards[2], "fsdp", axis=1, tiled=True),
        lax.all_gather(shards[3], "fsdp", axis=1, tiled=True),
        lax.all_gather(shards[4], "fsdp", axis=1, tiled=True),
        lax.all_gather(shards[5], "fsdp", axis=1, tiled=True),
        lax.all_gather(shards[6], "fsdp", axis=1, tiled=True),
    )
    params = tuple((piece[0] for piece in gathered))
    section = lax.axis_index("section")
    micro = tokens.shape[0]
    group = tokens.shape[2]
    width = tokens.shape[3]
    seq_len = group * lax.axis_size("seq")
    offset = lax.axis_index("seq") * group

    def fetch(array, index):
        return lax.dynamic_index_in_dim(array, index, 0, keepdims=False)[0]

    def forward_step(carry, step):
        incoming, stat_sum = carry
        index = step - section
        active = (index >= 0) & (index < micro)
        chosen = jnp.clip(index, 0, micro - 1)
        hidden_in = jnp.where(section == 0, fetch(tokens, chosen), incoming)
        allowed = allowed_pairs(fetch(lengths, chosen), offset, group, seq_len)
        valid = fetch(valid_mask, chosen).astype(jnp.float32)
        result, kept, statistic = forward_layer(hidden_in, params, allowed, valid)
        outgoing = shifted(result, "section", 1)
        stat_sum = stat_sum + jnp.where(active, statistic, 0.0)
        return ((outgoing, stat_sum), (result, kept))

    step_list = jnp.arange(micro + 1, dtype=jnp.int32)
    start = (jnp.zeros((group, width), jnp.bfloat16), jnp.zeros((), jnp.float32))
    (unused_fwd, stat_sum), (results, kept_all) = lax.scan(forward_step, start, step_list)
    late_shards, stat_sum = lax.optimization_barrier((shards, stat_sum))
    again = (
        lax.all_gather(late_shards[0], "fsdp", axis=1, tiled=True),
        lax.all_gather(late_shards[1], "fsdp", axis=1, tiled=True),
        lax.all_gather(late_shards[2], "fsdp", axis=1, tiled=True),
        lax.all_gather(late_shards[3], "fsdp", axis=1, tiled=True),
        lax.all_gather(late_shards[4], "fsdp", axis=1, tiled=True),
        lax.all_gather(late_shards[5], "fsdp", axis=1, tiled=True),
        lax.all_gather(late_shards[6], "fsdp", axis=1, tiled=True),
    )
    params_back = tuple((piece[0] for piece in again))

    def backward_step(carry, step):
        incoming, sums = carry
        index = step - 1 + section
        active = (index >= 0) & (index < micro)
        chosen = jnp.clip(index, 0, micro - 1)
        position = chosen + section

        def take(array):
            return lax.dynamic_index_in_dim(array, position, 0, keepdims=False)

        kept = jax.tree.map(take, kept_all)
        grad_out = jnp.where(
            section == 1, fetch(cotangent, chosen).astype(jnp.float32), incoming.astype(jnp.float32)
        )
        grad_out = jnp.where(active, grad_out, 0.0)
        row_lengths = fetch(lengths, chosen)
        allowed = allowed_pairs(row_lengths, offset, group, seq_len)
        grad_hidden, grads = backward_layer(kept, params_back, grad_out, allowed)
        outgoing = shifted(grad_hidden.astype(jnp.bfloat16), "section", -1)
        sums = tuple((total + piece for total, piece in zip(sums, grads)))
        return ((outgoing, sums), grad_hidden)

    zeros = tuple((jnp.zeros(piece.shape, jnp.float32) for piece in params_back))
    (unused_back, sums), grad_steps = lax.scan(
        backward_step, (jnp.zeros((group, width), jnp.bfloat16), zeros), step_list
    )
    hidden_out = lax.dynamic_slice_in_dim(results, section, micro, 0).reshape(
        1, micro, 1, group, width
    )
    grad_in = lax.dynamic_slice_in_dim(grad_steps, 1 - section, micro, 0).reshape(
        1, micro, 1, group, width
    )
    shard_sums = jax.tree.map(
        lambda part: part.astype(jnp.float32),
        lax.psum_scatter(for_sending(sums), "fsdp", scatter_dimension=0, tiled=True),
    )
    reduced = jax.tree.map(
        lambda part: part.astype(jnp.float32), lax.psum(for_sending(shard_sums), "seq")
    )
    total_stat = lax.psum(stat_sum, ("seq", "fsdp"))
    token_count = micro * lax.axis_size("fsdp") * seq_len
    rms_stats = jnp.sqrt(total_stat / token_count + epsilon).reshape(1)
    return (
        hidden_out,
        grad_in,
        reduced[0][None],
        reduced[1][None],
        reduced[2][None],
        reduced[3][None],
        reduced[4][None],
        reduced[5][None],
        reduced[6][None],
        rms_stats,
    )


FIRST = (1, 2)
SECOND = (0, 3)
EVERY = (0, 1, 2, 3)
BLOCK = 128
SCORE_SCALE = math.sqrt(HEAD)
MASKED = -1e30


def dot(left, right):
    return jnp.dot(left, right, preferred_element_type=jnp.float32)


def low(x):
    return x.astype(jnp.bfloat16)


def pick(x, index, axis):
    return lax.dynamic_index_in_dim(x, index, axis, keepdims=False)


def sums_of_halves(x):
    row = lax.broadcasted_iota(jnp.int32, (2 * HEAD, 2 * HEAD), 0) // HEAD
    col = lax.broadcasted_iota(jnp.int32, (2 * HEAD, 2 * HEAD), 1) // HEAD
    same = (row == col).astype(jnp.bfloat16)
    high = x.astype(jnp.bfloat16)
    rest = (x - high.astype(jnp.float32)).astype(jnp.bfloat16)
    return dot(high, same) + dot(rest, same)


def normal_heads(raw):
    factor = lax.rsqrt(sums_of_halves(raw * raw) + epsilon)
    return raw * factor, factor


def merge(to, own, oth):
    for s in range(4):
        to[s * 256 : s * 256 + BLOCK, : own.shape[1]] = own[s * BLOCK : (s + 1) * BLOCK]
        to[s * 256 + BLOCK : (s + 1) * 256, : own.shape[1]] = oth[s * BLOCK : (s + 1) * BLOCK]


def last_dims(left, right):
    return lax.dot_general(left, right, (((1,), (1,)), ((), ())), preferred_element_type=jnp.float32)


def head_lanes(h, dtype):
    lane = lax.broadcasted_iota(jnp.int32, (1, 2 * HEAD), 1) // HEAD
    return (lane == h).astype(dtype)


MESH = pl.DeviceIdType.MESH


def position():
    c, s, f = (lax.axis_index(name) for name in ("section", "seq", "fsdp"))
    x, y = f % 2, f // 2
    layer = 1 - ((s + 1) // 2) % 2
    return c, s, f, y * 2 + 1 - x, (1 - y) * 2 + x, layer


def greet(devices):
    barrier = pltpu.get_barrier_semaphore()
    for device in devices:
        pl.semaphore_signal(barrier, inc=1, device_id=device, device_id_type=MESH)
    pl.semaphore_wait(barrier, len(devices))


def remote(src, dst, send, recv, device):
    return pltpu.make_async_remote_copy(
        src_ref=src, dst_ref=dst, send_sem=send, recv_sem=recv, device_id=device, device_id_type=MESH
    )


def arrived(ref, sem):
    pltpu.make_async_copy(ref, ref, sem).wait()


def lane(offset):
    return pl.multiple_of(offset, 128)


def every(count, work):
    def step(n, carry):
        work(n)
        return carry

    lax.fori_loop(0, count, step, 0)


def silu(x):
    return x * jax.nn.sigmoid(x)


def forward_kernel(
    w_qkv, w_out, w_in, w_down, vectors, valid, tokens, cotangent, place_col, start_col, place_row,
    o_qkv, o_out, o_up, o_gate, o_down, o_vectors, o_valid, o_row,
    o_hidden, o_mixed, o_attended, o_middle, o_lift_up, o_lift_gate, o_inner, o_branch, o_output,
    o_result, o_log_sums,
    wq, wo, wu, wg, wd, vec, flat, scale_up, scale_gate, alpha_attn, alpha_mlp,
    hid, mixed, att, mid, lift_up, lift_gate, inner, branch, middle, output, result,
    part_one, got_one, part_two, got_two, bias, raw, queries, keys, values, log_sums,
    first_send, first_recv, next_send, next_recv, row_send, row_recv, valid_send, valid_recv,
    own_recv, oth_send, oth_recv, one_send, one_recv, mid_send, mid_recv, two_send, two_recv,
    result_send, kept,
):
    c, s, f, fx, fy, layer = position()
    sibling = (1 - c, s, f)
    early = layer == 0
    late = layer == 1
    next_plane = (c, (s - 1) * 3, f)
    half = 4 * BLOCK
    width = w_out.shape[1]
    greet(
        [sibling, (c, s, fx), (1 - c, s, fx), (c, s, fy), (1 - c, s, fy)]
        + [(c, (s + step) % 4, f) for step in (1, 2, 3)]
    )

    for to, held in enumerate((cotangent.at[0], tokens.at[0], tokens.at[1], cotangent.at[1])):
        src = held.at[pl.ds(c * BLOCK, BLOCK)]
        dst = o_row.at[pl.ds(s * BLOCK, BLOCK)]
        flags, flags_to = valid.at[to // 2], o_valid.at[s]

        @pl.when(s == to)
        def _():
            pltpu.make_async_copy(src, dst, row_recv.at[s]).start()
            pltpu.make_async_copy(flags, flags_to, valid_recv.at[s]).start()

        @pl.when(s != to)
        def _():
            remote(src, dst, row_send.at[to], row_recv.at[s], (c, to, f)).start()
            remote(flags, flags_to, valid_send.at[to], valid_recv.at[s], (c, to, f)).start()

    def pieces(item, h):
        if item == 0:
            return [(vectors, vec.at[f])]
        if item == 1:
            return [
                (
                    w_qkv.at[:, pl.ds(lane(part * 256 + h * 128), 128)],
                    wq.at[pl.ds(f * 256, 256), pl.ds(part * 128, 128)],
                )
                for part in range(12)
            ]
        if item == 2:
            return [(w_out.at[pl.ds(h * 128, 128)], wo.at[pl.ds(f * 128, 128)])]
        if item in (3, 4):
            to = (wu, wg)[item - 3]
            return [
                (
                    w_in.at[:, pl.ds(lane((item - 3) * 4096 + part * 1024 + h * 512), 512)],
                    to.at[pl.ds(f * 256, 256), pl.ds(part * 512, 512)],
                )
                for part in range(4)
            ]
        return [(w_down.at[pl.ds(h * 512, 512)], wd.at[pl.ds(f * 512, 512)])]

    weights = (vec, wq, wo, wu, wg, wd)

    def block(item, of):
        if item == 0:
            return vec.at[of]
        rows = weights[item].shape[0] // 4
        return weights[item].at[pl.ds(of * rows, rows)]

    def part_of(item, of, part):
        if item == 0:
            return vec.at[of, pl.ds(part * 16, 16)]
        rows = weights[item].shape[0] // 8
        return weights[item].at[pl.ds(of * 2 * rows + part * rows, rows)]

    targets = (
        ((c, s, fx), c, 1), ((c, s, fy), c, 2), ((1 - c, s, fx), 1 - c, 1),
        ((1 - c, s, fy), 1 - c, 2), (sibling, 1 - c, 0),
    )

    def spread(*items):
        @pl.when(c == layer)
        def _():
            for item in items:
                for index, (device, h, came) in enumerate(targets):
                    for src, dst in pieces(item, h):
                        remote(
                            src, dst, first_send.at[item, index], first_recv.at[item, came], device
                        ).start()
                for src, dst in pieces(item, c):
                    pltpu.make_async_copy(src, dst, first_recv.at[item, 0]).start()

    spread(0, 1, 2, 3)

    def relay(item):
        for part, (came, of, to) in enumerate(((1, fx, fy), (2, fy, fx))):
            arrived(block(item, of), first_recv.at[item, came])
            moved = part_of(item, of, part)
            remote(
                moved, moved, next_send.at[item, part], next_recv.at[item, part], (c, s, to)
            ).start()

    copies = []

    def keep(src, dst):
        copy = pltpu.make_async_copy(src, dst, kept.at[len(copies)])
        copy.start()
        copies.append(copy)

    kept_weights = (None, o_qkv, o_out, o_up, o_gate, o_down)

    def complete(item):
        arrived(block(item, f), first_recv.at[item, 0])
        for part in range(2):
            arrived(part_of(item, 3 - f, part), next_recv.at[item, part])
        if item:
            keep(weights[item], kept_weights[item])

    fits = (place_row[...] >= start_col[...]) & (place_row[...] <= place_col[...])
    bias[...] = jnp.where(fits, 0.0, MASKED)
    values[:, 2 * HEAD :] = jnp.ones_like(values[:, 2 * HEAD :])

    relay(0)
    relay(1)
    spread(4)
    relay(2)

    def rows_of(b):
        return pl.ds(b * BLOCK, BLOCK)

    def to_sibling(b, src):
        remote(src, hid.at[1, rows_of(b)], oth_send.at[b], oth_recv.at[b], sibling).start()

    @pl.when(early)
    def _():
        for b in range(4):
            held = o_row.at[rows_of(b)]
            arrived(held, row_recv.at[b])
            pltpu.make_async_copy(held, hid.at[0, rows_of(b)], own_recv.at[b]).start()
            to_sibling(b, held)
        for b in range(4):
            arrived(hid.at[0, rows_of(b)], own_recv.at[b])

    @pl.when(late)
    def _():
        relay(3)
        spread(5)
        relay(4)
        relay(5)
        for b in range(4):
            arrived(o_row.at[rows_of(b)], row_recv.at[b])
        for b in range(4):
            arrived(hid.at[0, rows_of(b)], own_recv.at[b])
            to_sibling(b, hid.at[0, rows_of(b)])

    complete(0)
    keep(vec, o_vectors)
    flat[...] = vec[...].astype(jnp.float32)
    for n in range(4):
        for j in range(4):
            at = slice(n * 512 + j * 128, n * 512 + (j + 1) * 128)
            row = 2 + (n % 2) * 8 + j
            scale_up[:, at] = flat[n // 2, pl.ds(row + c * 4, 1), :]
            scale_gate[:, at] = flat[2 + n // 2, pl.ds(row + c * 4, 1), :] * math.sqrt(width)
    for n in range(2):
        for j in range(4):
            at = slice(n * 512 + j * 128, n * 512 + (j + 1) * 128)
            alpha_attn[:, at] = flat[n, 18 + j : 19 + j, :]
            alpha_mlp[:, at] = flat[2 + n, 18 + j : 19 + j, :]

    complete(1)
    for side in range(2):
        if side:
            for b in range(4):
                arrived(hid.at[1, rows_of(b)], oth_recv.at[b])
            keep(hid, o_hidden)

        def mix(n, side=side):
            at = pl.ds(lane(n * 512), 512)
            mixed[side, :, at] = low(dot(hid[side], wq[:, at]))

        every(3, mix)
    keep(mixed, o_mixed)

    first = (lax.broadcasted_iota(jnp.int32, (8, 2 * HEAD), 1) == 0).astype(jnp.bfloat16)

    def attend(pair):
        def normal(to, part):
            at = pl.ds(lane(part * (width // 2) + pair * 2 * HEAD), 2 * HEAD)
            merge(raw, mixed[0, :, at], mixed[1, :, at])
            normed, _ = normal_heads(raw[...].astype(jnp.float32))
            to[...] = low(normed * flat[pair, pl.ds(c, 1), :])

        normal(queries, 0)
        normal(keys, 1)
        at = pl.ds(lane(width + pair * 2 * HEAD), 2 * HEAD)
        merge(values, mixed[0, :, at], mixed[1, :, at])
        at = pl.ds(lane(pair * 2 * HEAD), 2 * HEAD)
        for q in range(4):
            upto = (q + 1) * 256
            query = queries[q * 256 : upto] * SCORE_SCALE
            query = jnp.concatenate([query * head_lanes(h, jnp.bfloat16) for h in range(2)])
            summed = 0.0
            for k in range(q + 1):
                at_keys = slice(k * 256, (k + 1) * 256)
                mask = jnp.concatenate([bias[q * 256 : upto, at_keys]] * 2)
                weighted = jnp.exp(last_dims(query, keys[at_keys]) + mask)
                summed = summed + dot(low(weighted), values[at_keys])
            total = summed[:, 2 * HEAD :]
            parts = summed[:, : 2 * HEAD] / total
            parts = parts[:256], parts[256:]
            log_sum = jnp.log(row_sums(total, first)[:1])
            for h in range(2):
                log_sums[pair, h : h + 1, q * 256 : upto] = log_sum[:, h * 256 : (h + 1) * 256]
            joined = low(jnp.where(head_lanes(0, jnp.float32) > 0, parts[0], parts[1]))
            att[0, q * BLOCK : (q + 1) * BLOCK, at] = joined[:BLOCK]
            att[1, q * BLOCK : (q + 1) * BLOCK, at] = joined[BLOCK:]

    every(4, attend)
    keep(att, o_attended)
    keep(log_sums, o_log_sums)

    complete(2)

    def branch_sent(n):
        at = pl.ds(lane(n * 256), 256)
        part_one[:, at] = low(dot(att[1], wo[:, at]))
        remote(
            part_one.at[:, at], got_one.at[:, at], one_send.at[n], one_recv.at[n], sibling
        ).start()

    def branch_own(n):
        at = pl.ds(lane(n * 256), 256)
        branch[:, at] = dot(att[0], wo[:, at])

    every(4, branch_sent)
    every(4, branch_own)
    for n in range(4):
        arrived(got_one.at[:, pl.ds(n * 256, 256)], one_recv.at[n])

    def first_step(b):
        rows = pl.ds(b * 64, 64)
        total = branch[rows] + got_one[rows].astype(jnp.float32)
        branch[rows] = total
        hidden = hid[0, rows].astype(jnp.float32)
        stepped = unit(hidden + alpha_attn[...] * (unit(total) - hidden))
        middle[rows] = stepped
        mid[0, rows] = low(stepped)

        @pl.when(b % 2 == 1)
        def _():
            sent = rows_of(b // 2)
            remote(
                mid.at[0, sent], mid.at[1, sent], mid_send.at[b // 2], mid_recv.at[b // 2], sibling
            ).start()

    every(8, first_step)
    keep(branch, o_branch)

    @pl.when(early)
    def _():
        relay(3)
        spread(5)

    complete(3)
    for side in range(2):
        if side:
            for b in range(4):
                arrived(mid.at[1, rows_of(b)], mid_recv.at[b])
            keep(mid, o_middle)

        def lift(n, side=side):
            at = pl.ds(lane(n * 512), 512)
            lift_up[side, :, at] = low(dot(mid[side], wu[:, at]))

        every(4, lift)
    keep(lift_up, o_lift_up)

    @pl.when(early)
    def _():
        relay(4)

    complete(4)
    for side in (1, 0):

        def open_gate(n, side=side):
            at = pl.ds(lane(n * 512), 512)
            gate = dot(mid[side], wg[:, at])
            lift_gate[side, :, at] = low(gate)
            upward = lift_up[side, :, at].astype(jnp.float32) * scale_up[:, at]
            inner[side, :, at] = low(upward * silu(gate * scale_gate[:, at]))

        every(4, open_gate)
    keep(lift_gate, o_lift_gate)
    keep(inner, o_inner)

    @pl.when(early)
    def _():
        relay(5)

    complete(5)

    def output_sent(n):
        at = pl.ds(lane(n * 256), 256)
        part_two[:, at] = low(dot(inner[1], wd[:, at]))
        remote(
            part_two.at[:, at], got_two.at[:, at], two_send.at[n], two_recv.at[n], sibling
        ).start()

    def output_own(n):
        at = pl.ds(lane(n * 256), 256)
        output[:, at] = dot(inner[0], wd[:, at])

    every(4, output_sent)
    every(4, output_own)
    for n in range(4):
        arrived(got_two.at[:, pl.ds(n * 256, 256)], two_recv.at[n])

    def second_step(b):
        rows = pl.ds(b * 64, 64)
        total = output[rows] + got_two[rows].astype(jnp.float32)
        output[rows] = total
        start = middle[rows]
        result[rows] = low(unit(start + alpha_mlp[...] * (unit(total) - start)))

        @pl.when(early & (b % 2 == 1))
        def _():
            sent = rows_of(b // 2)
            remote(
                result.at[sent], hid.at[0, sent], result_send.at[b // 2], own_recv.at[b // 2],
                next_plane,
            ).start()

    every(8, second_step)
    keep(output, o_output)
    keep(result, o_result)

    for copy in copies:
        copy.wait()
    for item in range(6):
        for part in range(2):
            arrived(part_of(item, f, part), next_send.at[item, part])
    for b in range(4):
        rows = rows_of(b)
        arrived(hid.at[1, rows], oth_send.at[b])
        arrived(part_one.at[:, pl.ds(b * 256, 256)], one_send.at[b])
        arrived(part_two.at[:, pl.ds(b * 256, 256)], two_send.at[b])
        arrived(mid.at[0, rows], mid_send.at[b])
        arrived(o_valid.at[b], valid_recv.at[b])

        @pl.when(early)
        def _():
            arrived(result.at[rows], result_send.at[b])

        @pl.when(s != b)
        def _():
            arrived(o_row.at[rows], row_send.at[b])
            arrived(o_valid.at[b], valid_send.at[b])

    @pl.when(c == layer)
    def _():
        for item in range(6):
            for index in range(len(targets)):
                arrived(block(item, f), first_send.at[item, index])


def forward_all(w_qkv, w_out, w_in, w_down, vectors, valid, tokens, cotangent, places):
    width = w_out.shape[1]
    units = w_down.shape[0] * 4
    rows = 4 * BLOCK
    place, start = places
    sems = pltpu.SemaphoreType.DMA

    def low_shape(*shape):
        return jax.ShapeDtypeStruct(shape, jnp.bfloat16)

    def low_vmem(*shape):
        return pltpu.VMEM(shape, jnp.bfloat16)

    def full_vmem(*shape):
        return pltpu.VMEM(shape, jnp.float32)

    weights = [
        (width, 3 * width // 2), (width // 2, width), (width, units // 2), (width, units // 2),
        (units // 2, width),
    ]
    sides = [
        (2, rows, width), (2, rows, 3 * width // 2), (2, rows, width // 2), (2, rows, width),
        (2, rows, units // 2), (2, rows, units // 2), (2, rows, units // 2),
    ]
    anywhere = pl.BlockSpec(memory_space=pl.ANY)
    near = pl.BlockSpec(memory_space=pltpu.VMEM)
    return pl.pallas_call(
        forward_kernel,
        out_shape=[low_shape(*shape) for shape in weights]
        + [low_shape(4, *vectors.shape), low_shape(4, *valid.shape[1:]), low_shape(rows, width)]
        + [low_shape(*shape) for shape in sides]
        + [jax.ShapeDtypeStruct((rows, width), jnp.float32)] * 2
        + [low_shape(rows, width)]
        + [jax.ShapeDtypeStruct((4, 2, 2 * rows), jnp.float32)],
        in_specs=[anywhere] * 8 + [near] * 3,
        out_specs=[anywhere] * 19,
        scratch_shapes=[low_vmem(*shape) for shape in weights]
        + [
            low_vmem(4, *vectors.shape), full_vmem(4, *vectors.shape),
            full_vmem(1, units // 2), full_vmem(1, units // 2),
            full_vmem(1, width), full_vmem(1, width),
        ]
        + [low_vmem(*shape) for shape in sides]
        + [full_vmem(rows, width)] * 3
        + [low_vmem(rows, width)] * 5
        + [full_vmem(2 * rows, 2 * rows)]
        + [low_vmem(2 * rows, 2 * HEAD)] * 3
        + [low_vmem(2 * rows, 4 * HEAD)]
        + [full_vmem(4, 2, 2 * rows)]
        + [sems((6, 5)), sems((6, 3)), sems((6, 2)), sems((6, 2))]
        + [sems((4,))] * 14
        + [sems((20,))],
        compiler_params=pltpu.CompilerParams(
            collective_id=0, has_side_effects=True, vmem_limit_bytes=60 * 2**20
        ),
    )(
        w_qkv, w_out, w_in, w_down, vectors, valid, tokens, cotangent,
        place[:, None], start[:, None], place[None, :],
    )


def row_sums(x, lanes):
    high = low(x)
    rest = low(x - high.astype(jnp.float32))
    return last_dims(lanes, high) + last_dims(lanes, rest)


def backward_kernel(
    w_qkv, w_out, w_up, w_gate, w_down, hidden, mixed_in, attended, up_in, gate_in, branch_in,
    output_in, row, log_sums, scale_qk, scale_up, scale_gate, alpha_attn, alpha_mlp,
    place_col, place_row, start_row,
    o_output, o_up, o_gate, o_branch, o_mixed, o_grad, sum_alphas, sum_scales, sum_qk,
    wq, wo, wu, wg, wd, hid, mixed, att, up, gate, branch, output, grad_in,
    grad_output, grad_middle, part_one, got_one, grad_branch, grad_att, part_two, got_two, result,
    bias, raw, queries, keys, values, grads, dq, dk, dv,
    load, grad_recv, out_send, out_recv, one_send, one_recv, branch_send, branch_recv,
    two_send, two_recv, result_send, kept,
):
    c, s, f, _, _, layer = position()
    sibling = (1 - c, s, f)
    early = layer == 0
    late = layer == 1
    partner = (c, (1 - layer) * (s - 1) * 3 + layer * (s // 3 + 1), f)
    width = w_out.shape[1]
    greet([sibling, partner])

    loads = (
        (output_in, output), (hidden.at[0], hid), (branch_in, branch), (w_down, wd), (gate_in, gate),
        (up_in, up), (w_up, wu), (w_gate, wg), (w_out, wo), (mixed_in, mixed), (attended, att),
        (w_qkv, wq),
    )
    for index, (src, dst) in enumerate(loads):
        pltpu.make_async_copy(src, dst, load.at[index]).start()

    def loaded(*names):
        for index in names:
            arrived(loads[index][1], load.at[index])

    copies = []

    def keep(src, dst):
        copy = pltpu.make_async_copy(src, dst, kept.at[len(copies)])
        copy.start()
        copies.append(copy)

    def rows_of(b):
        return pl.ds(b * BLOCK, BLOCK)

    @pl.when(late)
    def _():
        for b in range(4):
            pltpu.make_async_copy(
                row.at[rows_of(b)], grad_in.at[rows_of(b)], grad_recv.at[b]
            ).start()

    fits = (place_col[...] >= start_row[...]) & (place_col[...] <= place_row[...])
    bias[...] = jnp.where(fits, 0.0, MASKED)
    sum_alphas[...] = jnp.zeros_like(sum_alphas)
    sum_scales[...] = jnp.zeros_like(sum_scales)
    loaded(0, 1, 2)

    def both(n):
        return pl.ds(lane(n * 256), 256)

    def second_step(b):
        rows = pl.ds(b * 64, 64)

        @pl.when(b % 2 == 0)
        def _():
            arrived(grad_in.at[rows_of(b // 2)], grad_recv.at[b // 2])

        start = hid[rows].astype(jnp.float32)
        middle = unit(start + alpha_attn[...] * (unit(branch[rows]) - start))
        total = output[rows]
        change = unit(total) - middle
        grad = unit_back(middle + alpha_mlp[...] * change, grad_in[rows].astype(jnp.float32))
        sum_alphas[1:2] += jnp.sum(grad * change, axis=0, keepdims=True)
        grad_output[0, rows] = low(unit_back(total, alpha_mlp[...] * grad))
        grad_middle[rows] = grad * (1.0 - alpha_mlp[...])

        @pl.when(b % 2 == 1)
        def _():
            sent = rows_of(b // 2)
            remote(
                grad_output.at[0, sent], grad_output.at[1, sent], out_send.at[b // 2],
                out_recv.at[b // 2], sibling,
            ).start()

    every(8, second_step)

    loaded(3, 4, 5)
    for side in range(2):
        if side:
            for b in range(4):
                arrived(grad_output.at[1, rows_of(b)], out_recv.at[b])
            keep(grad_output, o_output)

        def close_gate(n, side=side):
            at = pl.ds(lane(n * 512), 512)
            grad = last_dims(grad_output[side], wd[pl.ds(n * 512, 512)])
            lift_up = up[side, :, at].astype(jnp.float32)
            lift_gate = gate[side, :, at].astype(jnp.float32)
            gating = lift_gate * scale_gate[:, at]
            sigmoid = jax.nn.sigmoid(gating)
            grad_up = grad * (gating * sigmoid)
            grad_gate = (
                grad * (lift_up * scale_up[:, at]) * sigmoid * (1.0 + gating * (1.0 - sigmoid))
            )
            sum_scales[0:1, at] += jnp.sum(grad_up * lift_up, axis=0, keepdims=True)
            sum_scales[1:2, at] += jnp.sum(grad_gate * lift_gate, axis=0, keepdims=True)
            up[side, :, at] = low(grad_up * scale_up[:, at])
            gate[side, :, at] = low(grad_gate * scale_gate[:, at])

        every(4, close_gate)
    keep(up, o_up)
    keep(gate, o_gate)
    loaded(6, 7)

    def lifted(side, n):
        rows = pl.ds(n * 256, 256)
        return last_dims(up[side], wu[rows]) + last_dims(gate[side], wg[rows])

    def middle_sent(n):
        at = both(n)
        part_one[:, at] = low(lifted(1, n))
        remote(
            part_one.at[:, at], got_one.at[:, at], one_send.at[n], one_recv.at[n], sibling
        ).start()

    def middle_own(n):
        at = both(n)
        grad_middle[:, at] = grad_middle[:, at] + lifted(0, n)

    every(4, middle_sent)
    every(4, middle_own)
    for n in range(4):
        arrived(got_one.at[:, pl.ds(n * 256, 256)], one_recv.at[n])

    def first_step(b):
        rows = pl.ds(b * 64, 64)
        start = hid[rows].astype(jnp.float32)
        total = branch[rows]
        change = unit(total) - start
        grad = grad_middle[rows] + got_one[rows].astype(jnp.float32)
        grad = unit_back(start + alpha_attn[...] * change, grad)
        sum_alphas[0:1] += jnp.sum(grad * change, axis=0, keepdims=True)
        grad_branch[0, rows] = low(unit_back(total, alpha_attn[...] * grad))
        grad_middle[rows] = grad * (1.0 - alpha_attn[...])

        @pl.when(b % 2 == 1)
        def _():
            sent = rows_of(b // 2)
            remote(
                grad_branch.at[0, sent], grad_branch.at[1, sent], branch_send.at[b // 2],
                branch_recv.at[b // 2], sibling,
            ).start()

    every(8, first_step)
    loaded(8, 9, 10)
    for side in range(2):
        if side:
            for b in range(4):
                arrived(grad_branch.at[1, rows_of(b)], branch_recv.at[b])
            keep(grad_branch, o_branch)

        def attended_grad(n, side=side):
            grad_att[side, :, both(n)] = low(
                last_dims(grad_branch[side], wo[pl.ds(n * 256, 256)])
            )

        every(2, attended_grad)

    def attend_back(pair):
        def lanes(part):
            return pl.ds(lane(part * (width // 2) + pair * 2 * HEAD), 2 * HEAD)

        scale = scale_qk[pl.ds(pair, 1)]

        def normal(part):
            merge(raw, mixed[0, :, lanes(part)], mixed[1, :, lanes(part)])
            return normal_heads(raw[...].astype(jnp.float32))

        queries[...] = low(normal(0)[0] * scale) * SCORE_SCALE
        keys[...] = low(normal(1)[0] * scale)
        merge(values, mixed[0, :, lanes(2)], mixed[1, :, lanes(2)])
        merge(grads, grad_att[0, :, lanes(0)], grad_att[1, :, lanes(0)])
        merge(raw, att[0, :, lanes(0)], att[1, :, lanes(0)])
        dk[...] = jnp.zeros_like(dk)
        dv[...] = jnp.zeros_like(dv)
        head = lax.broadcasted_iota(jnp.int32, (8, 2 * HEAD), 0)
        marks = (lax.broadcasted_iota(jnp.int32, (8, 2 * HEAD), 1) // HEAD == head).astype(
            jnp.bfloat16
        )
        for q in range(4):
            at = slice(q * 256, (q + 1) * 256)
            upto = slice(0, (q + 1) * 256)
            deltas = row_sums(grads[at].astype(jnp.float32) * raw[at].astype(jnp.float32), marks)
            delta = jnp.concatenate([deltas[h : h + 1] for h in range(2)], axis=1)
            log_sum = jnp.concatenate([log_sums[pair, h : h + 1, at] for h in range(2)], axis=1)
            query = jnp.concatenate([queries[at] * head_lanes(h, jnp.bfloat16) for h in range(2)])
            grad = jnp.concatenate([grads[at] * head_lanes(h, jnp.bfloat16) for h in range(2)])
            key = keys[upto]
            mask = jnp.concatenate([bias[upto, at]] * 2, axis=1)
            weights = jnp.exp(last_dims(key, query) + (mask - log_sum))
            grad_scores = low(weights * (last_dims(values[upto], grad) - delta))
            dv[upto] += dot(low(weights), grad)
            dk[upto] += dot(grad_scores, query)
            to_queries = contract_rows(grad_scores, key)
            dq[at] = (
                head_lanes(0, jnp.float32) * to_queries[:256]
                + head_lanes(1, jnp.float32) * to_queries[256:]
            )

        scale_sum = 0.0
        for part, grad in enumerate((dq, dk)):
            normed, factor = normal(part)
            found = grad[...] * SCORE_SCALE if part == 0 else grad[...]
            scale_sum = scale_sum + jnp.sum(found * normed, axis=0, keepdims=True)
            step = found * scale
            grad[...] = factor * (step - normed * sums_of_halves(normed * step))
        sum_qk[pl.ds(pair, 1)] = scale_sum
        for part, grad in enumerate((dq, dk, dv)):
            for q in range(4):
                rows = slice(q * BLOCK, (q + 1) * BLOCK)
                mixed[0, rows, lanes(part)] = low(grad[q * 256 : q * 256 + BLOCK])
                mixed[1, rows, lanes(part)] = low(grad[q * 256 + BLOCK : (q + 1) * 256])

    every(4, attend_back)
    keep(mixed, o_mixed)
    loaded(11)

    def hidden_sent(n):
        at = both(n)
        part_two[:, at] = low(last_dims(mixed[1], wq[pl.ds(n * 256, 256)]))
        remote(
            part_two.at[:, at], got_two.at[:, at], two_send.at[n], two_recv.at[n], sibling
        ).start()

    def hidden_own(n):
        at = both(n)
        grad_middle[:, at] = grad_middle[:, at] + last_dims(mixed[0], wq[pl.ds(n * 256, 256)])

    every(4, hidden_sent)
    every(4, hidden_own)
    for n in range(4):
        arrived(got_two.at[:, pl.ds(n * 256, 256)], two_recv.at[n])

    def finish(b):
        rows = rows_of(b)
        result[rows] = low(grad_middle[rows] + got_two[rows].astype(jnp.float32))

        @pl.when(late)
        def _():
            remote(
                result.at[rows], grad_in.at[rows], result_send.at[b], grad_recv.at[b], partner
            ).start()

    every(4, finish)
    keep(result, o_grad)

    for copy in copies:
        copy.wait()
    for b in range(4):
        rows, at = rows_of(b), pl.ds(b * 256, 256)
        arrived(grad_output.at[0, rows], out_send.at[b])
        arrived(part_one.at[:, at], one_send.at[b])
        arrived(grad_branch.at[0, rows], branch_send.at[b])
        arrived(part_two.at[:, at], two_send.at[b])

        @pl.when(late)
        def _():
            arrived(result.at[rows], result_send.at[b])


def backward_all(weights, kept, row, log_sums, scales, places):
    hidden, mixed, attended, _, (up, gate, _), branch, output = kept
    rows, width = row.shape
    units = up.shape[2]
    place, start = places
    sems = pltpu.SemaphoreType.DMA

    def low_shape(*shape):
        return jax.ShapeDtypeStruct(shape, jnp.bfloat16)

    def full_shape(*shape):
        return jax.ShapeDtypeStruct(shape, jnp.float32)

    def low_vmem(*shape):
        return pltpu.VMEM(shape, jnp.bfloat16)

    def full_vmem(*shape):
        return pltpu.VMEM(shape, jnp.float32)

    anywhere = pl.BlockSpec(memory_space=pl.ANY)
    near = pl.BlockSpec(memory_space=pltpu.VMEM)
    one_side, two_sides = low_vmem(rows, width), low_vmem(2, rows, width)
    return pl.pallas_call(
        backward_kernel,
        out_shape=[
            low_shape(2, rows, width), low_shape(2, rows, units), low_shape(2, rows, units),
            low_shape(2, rows, width), low_shape(2, rows, 3 * width // 2), low_shape(rows, width),
            full_shape(2, width), full_shape(2, units), full_shape(4, 2 * HEAD),
        ],
        in_specs=[anywhere] * 13 + [near] * 9,
        out_specs=[anywhere] * 6 + [near] * 3,
        scratch_shapes=[low_vmem(*weight.shape) for weight in weights]
        + [one_side]
        + [low_vmem(*part.shape) for part in (mixed, attended, up, gate)]
        + [full_vmem(rows, width)] * 2
        + [one_side, two_sides, full_vmem(rows, width), one_side, one_side, two_sides]
        + [low_vmem(2, rows, width // 2), one_side, one_side, one_side]
        + [full_vmem(2 * rows, 2 * rows)]
        + [low_vmem(2 * rows, 2 * HEAD)] * 5
        + [full_vmem(2 * rows, 2 * HEAD)] * 3
        + [sems((12,))]
        + [sems((4,))] * 10
        + [sems((8,))],
        compiler_params=pltpu.CompilerParams(
            collective_id=2, has_side_effects=True, vmem_limit_bytes=60 * 2**20
        ),
    )(
        *weights, hidden, mixed, attended, up, gate, branch, output, row, log_sums, *scales,
        place[:, None], place[None, :], start[None, :],
    )


CHUNKS = 16
BUFFERS, SEMAPHORES = 8, 18


class Flow:
    def __init__(self, buffers, semaphores):
        (
            self.near_own, self.near_far, self.far_in, self.own, self.passing,
            self.from_left, self.from_right, self.pair_sum,
        ) = buffers
        (
            self.load_own, self.load_pass, self.send_own, self.recv_own, self.send_far,
            self.recv_far, self.send_next, self.recv_next, self.send_z, self.recv_left,
            self.recv_right, self.recv_pair, self.send_on, self.send_back, self.send_out,
            self.keep, self.give, self.given,
        ) = semaphores
        self.place_of = position()

    def neighbours(self, k):
        c, s, f, fx, fy, _ = self.place_of
        return fx + (fy - fx) * (k % 2), fy + (fx - fy) * (k % 2)

    def begin(self, k, source):
        c, s, f, _, _, _ = self.place_of
        near, far = self.neighbours(k)
        to = (c, s, near)
        remote(source(near), self.near_own.at[k], self.send_own.at[k], self.recv_own.at[k], to).start()
        remote(
            source(3 - f), self.near_far.at[k], self.send_far.at[k], self.recv_far.at[k], to
        ).start()
        pltpu.make_async_copy(source(far), self.passing.at[k], self.load_pass.at[k]).start()
        pltpu.make_async_copy(source(f), self.own.at[k], self.load_own.at[k]).start()

    def add(self, to, *refs):
        total = refs[0][...].astype(jnp.float32)
        for ref in refs[1:]:
            total = total + ref[...].astype(jnp.float32)
        to[...] = total.astype(to.dtype)

    def pass_on(self, k):
        c, s, f, _, _, _ = self.place_of
        _, far = self.neighbours(k)
        arrived(self.passing.at[k], self.load_pass.at[k])
        arrived(self.near_far.at[k], self.recv_far.at[k])
        self.add(self.passing.at[k], self.passing.at[k], self.near_far.at[k])
        remote(
            self.passing.at[k], self.far_in.at[k], self.send_next.at[k], self.recv_next.at[k],
            (c, s, far),
        ).start()

    def finish_plane(self, k):
        c, s, f, _, _, _ = self.place_of
        own = self.own.at[k]
        arrived(own, self.load_own.at[k])
        arrived(self.near_own.at[k], self.recv_own.at[k])
        arrived(self.far_in.at[k], self.recv_next.at[k])
        self.add(own, own, self.near_own.at[k], self.far_in.at[k])
        send = self.send_z.at[k]

        @pl.when(s == 0)
        def _():
            remote(own, self.from_left.at[k], send, self.recv_left.at[k], (c, 1, f)).start()

        @pl.when(s == 3)
        def _():
            remote(own, self.from_right.at[k], send, self.recv_right.at[k], (c, 2, f)).start()

        @pl.when((s == 1) | (s == 2))
        def _():
            remote(own, self.pair_sum.at[k], send, self.recv_pair.at[k], (c, 3 - s, f)).start()

    def middle_planes(self, k):
        c, s, f, _, _, _ = self.place_of
        left, right, pair = self.from_left.at[k], self.from_right.at[k], self.pair_sum.at[k]

        @pl.when(s == 1)
        def _():
            arrived(left, self.recv_left.at[k])
            remote(left, left, self.send_on.at[k], self.recv_left.at[k], (c, 2, f)).start()

        @pl.when(s == 2)
        def _():
            arrived(right, self.recv_right.at[k])
            remote(right, right, self.send_on.at[k], self.recv_right.at[k], (c, 1, f)).start()

        @pl.when((s == 1) | (s == 2))
        def _():
            arrived(pair, self.recv_pair.at[k])
            arrived(pair, self.send_z.at[k])
            self.add(pair, pair, self.own.at[k])
            to = (c, (s - 1) * 3, f)
            remote(pair, pair, self.send_out.at[k], self.recv_pair.at[k], to).start()

    def all_planes(self, k):
        c, s, f, _, _, _ = self.place_of
        left, right, pair = self.from_left.at[k], self.from_right.at[k], self.pair_sum.at[k]
        own, total = self.own.at[k], self.near_own.at[k]

        @pl.when(s == 1)
        def _():
            arrived(right, self.recv_right.at[k])
            remote(right, right, self.send_back.at[k], self.recv_right.at[k], (c, 0, f)).start()

        @pl.when(s == 2)
        def _():
            arrived(left, self.recv_left.at[k])
            remote(left, left, self.send_back.at[k], self.recv_left.at[k], (c, 3, f)).start()

        @pl.when((s == 1) | (s == 2))
        def _():
            self.add(total, left, right)

        @pl.when(s == 0)
        def _():
            arrived(pair, self.recv_pair.at[k])
            arrived(right, self.recv_right.at[k])
            self.add(total, own, right)

        @pl.when(s == 3)
        def _():
            arrived(pair, self.recv_pair.at[k])
            arrived(left, self.recv_left.at[k])
            self.add(total, own, left)

    def place(self, k, pieces):
        c, s, f, _, _, _ = self.place_of
        for owner, chunk in ((0, self.pair_sum.at[k]), (1, self.near_own.at[k])):
            for src, dst in pieces:

                @pl.when(c == owner)
                def _():
                    pltpu.make_async_copy(src(chunk), dst, self.keep.at[k]).start()

                @pl.when(c != owner)
                def _():
                    remote(
                        src(chunk), dst, self.give.at[k], self.given.at[k], (1 - c, s, f)
                    ).start()

    def settle(self, k):
        c, s, f, _, _, _ = self.place_of
        chunk = self.own.at[k]
        for sem in (
            self.send_own, self.send_far, self.send_next, self.keep, self.give, self.given
        ):
            arrived(chunk, sem.at[k])

        @pl.when((s == 1) | (s == 2))
        def _():
            for sem in (self.send_on, self.send_back, self.send_out):
                arrived(chunk, sem.at[k])

        @pl.when((s == 0) | (s == 3))
        def _():
            arrived(chunk, self.send_z.at[k])


def reduce_kernel(
    g_down, g_up, g_gate, g_out, g_qkv, g_vectors, hidden, grad,
    o_down, o_in, o_out, o_qkv, o_vectors, o_hidden, o_grad,
    *scratch,
):
    c, s, f, fx, fy, layer = position()
    greet(
        [(c, s, fx), (c, s, fy), (1 - c, s, f)]
        + [(core, (s + step) % 4, f) for core in (0, 1) for step in (1, 2, 3)]
    )
    rows_send, rows_recv = scratch[-2:]

    for array, (held, to_ref) in enumerate(((hidden, o_hidden), (grad, o_grad))):
        for to in range(4):
            src = held.at[pl.ds(to * BLOCK, BLOCK)]
            dst = to_ref.at[s // 2, pl.ds(c * BLOCK, BLOCK)]
            recv = rows_recv.at[array, s // 2, c]
            here = (s == to) & (c == layer)

            @pl.when(here)
            def _():
                pltpu.make_async_copy(src, dst, recv).start()

            @pl.when(jnp.logical_not(here))
            def _():
                remote(src, dst, rows_send.at[array, to], recv, (layer, to, f)).start()

    matrices = Flow(scratch[:BUFFERS], scratch[BUFFERS : BUFFERS + SEMAPHORES])
    rest = scratch[BUFFERS + SEMAPHORES : -2]
    vectors = Flow(rest[:BUFFERS], rest[BUFFERS:])

    def start_first(k):
        @pl.when(k < 4)
        def _():
            matrices.begin(
                k,
                lambda to: g_down.at[
                    pl.ds(to * 512 + (k // 2) * 256, 256), pl.ds(lane((k % 2) * 512), 512)
                ],
            )

        for first, ref in ((4, g_up), (8, g_gate), (12, g_out), (13, g_qkv)):
            count = ref.shape[1] // 512

            @pl.when((k >= first) & (k < first + count))
            def _():
                matrices.begin(
                    k,
                    lambda to: ref.at[pl.ds(to * 256, 256), pl.ds(lane((k - first) * 512), 512)],
                )

    def everything(chunk):
        return chunk

    def place(k):
        @pl.when(k < 4)
        def _():
            rows = pl.ds(c * 512 + (k // 2) * 256, 256)
            matrices.place(k, [(everything, o_down.at[rows, pl.ds(lane((k % 2) * 512), 512)])])

        @pl.when((k >= 4) & (k < 12))
        def _():
            lanes = pl.ds(lane((k - 4) * 1024 + c * 512), 512)
            matrices.place(k, [(everything, o_in.at[:, lanes])])

        @pl.when(k == 12)
        def _():
            matrices.place(
                k,
                [
                    (
                        lambda chunk, part=part: chunk.at[pl.ds(part * 128, 128)],
                        o_out.at[pl.ds(c * 128, 128), pl.ds(part * 512, 512)],
                    )
                    for part in range(2)
                ],
            )

        @pl.when(k > 12)
        def _():
            matrices.place(
                k,
                [
                    (
                        lambda chunk, part=part: chunk.at[:, pl.ds(part * 128, 128)],
                        o_qkv.at[:, pl.ds(lane((k - 13) * 1024 + part * 256 + c * 128), 128)],
                    )
                    for part in range(4)
                ],
            )

    vectors.begin(0, lambda to: g_vectors.at[to])
    ahead, lag_plane, lag_middle, lag_all = 3, 2, 4, 7
    for k in range(ahead):
        start_first(k)

    def last(k):
        matrices.all_planes(k)
        place(k)

    def last_vectors(k):
        vectors.all_planes(k)
        vectors.place(k, [(everything, o_vectors.at[c])])

    def step(t, carry):
        @pl.when(t + ahead < CHUNKS)
        def _():
            start_first(t + ahead)

        for lag, work, work_vectors in (
            (0, matrices.pass_on, vectors.pass_on),
            (lag_plane, matrices.finish_plane, vectors.finish_plane),
            (lag_middle, matrices.middle_planes, vectors.middle_planes),
            (lag_all, last, last_vectors),
        ):
            @pl.when(t == lag)
            def _():
                work_vectors(0)

            @pl.when((t >= lag) & (t < CHUNKS + lag))
            def _():
                work(t - lag)

        return carry

    lax.fori_loop(0, CHUNKS + lag_all, step, 0)

    def settle(k, carry):
        matrices.settle(k)
        return carry

    lax.fori_loop(0, CHUNKS, settle, 0)
    vectors.settle(0)
    for array, (held, to_ref) in enumerate(((hidden, o_hidden), (grad, o_grad))):
        for to in range(4):
            @pl.when(jnp.logical_not((s == to) & (c == layer)))
            def _():
                arrived(held.at[pl.ds(to * BLOCK, BLOCK)], rows_send.at[array, to])

        for micro in range(2):
            for core in range(2):
                arrived(
                    to_ref.at[micro, pl.ds(core * BLOCK, BLOCK)], rows_recv.at[array, micro, core]
                )


def reduce_all(g_down, g_up, g_gate, g_out, g_qkv, g_vectors, hidden, grad):
    width = g_down.shape[1]
    low_shape = lambda *shape: jax.ShapeDtypeStruct(shape, jnp.bfloat16)
    sems = pltpu.SemaphoreType.DMA
    small = g_vectors.shape[1:]
    return pl.pallas_call(
        reduce_kernel,
        out_shape=[
            low_shape(g_down.shape[0] // 2, width),
            low_shape(g_up.shape[0] // 4, 4 * g_up.shape[1]),
            low_shape(width // 4, width),
            low_shape(width // 4, 2 * g_qkv.shape[1]),
            jax.ShapeDtypeStruct((2, *small), jnp.float32),
            low_shape(2, 2 * BLOCK, width),
            low_shape(2, 2 * BLOCK, width),
        ],
        in_specs=[pl.BlockSpec(memory_space=pl.ANY)] * 8,
        out_specs=[pl.BlockSpec(memory_space=pl.ANY)] * 7,
        scratch_shapes=[pltpu.VMEM((CHUNKS, 256, 512), jnp.bfloat16)] * BUFFERS
        + [sems((CHUNKS,))] * SEMAPHORES
        + [pltpu.VMEM((1, *small), jnp.float32)] * BUFFERS
        + [sems((1,))] * SEMAPHORES
        + [sems((2, 4)), sems((2, 2, 2))],
        compiler_params=pltpu.CompilerParams(
            collective_id=1, has_side_effects=True, vmem_limit_bytes=48 * 2**20
        ),
    )(g_down, g_up, g_gate, g_out, g_qkv, g_vectors, hidden, grad)


def per_device(
    tokens, cotangent, lengths, valid_mask, w_qkv, w_out, w_in, w_down, qk_scale, mlp_scale, alphas
):
    c, s, f, _, _, layer = position()
    second = layer == 1
    micro = s // 2
    width = tokens.shape[3]
    group = tokens.shape[2]
    units = w_down.shape[1] * 4

    vectors = jnp.concatenate([qk_scale[0], mlp_scale[0], alphas[0]])
    vectors = jnp.pad(vectors, (0, 32 * 128 - vectors.shape[0])).reshape(32, 128)
    valid = low(jnp.pad(valid_mask[:, 0], ((0, 0), (0, 16 * 128 - group)))).reshape(2, 16, 128)
    index = jnp.arange(4 * group, dtype=jnp.int32)
    place = (index // 256) * 256 + (((index // BLOCK) + c) % 2) * BLOCK + index % BLOCK
    ends = jnp.cumsum(pick(lengths, micro, 0)[0])[:-1]
    passed = place[:, None] >= ends[None, :]
    start = jnp.max(jnp.where(passed, ends[None, :], 0), axis=1)
    places = (place, start)
    (
        *weights, vectors, valid, row,
        hidden, mixed, attended, middle, up, gate, inner, branch, output, result, log_sums,
    ) = forward_all(
        w_qkv[0], w_out[0], w_in[0], w_down[0], vectors, valid, tokens[:, 0], cotangent[:, 0], places
    )
    kept = (hidden, mixed, attended, middle, (up, gate, inner), branch, output)
    vectors = vectors.reshape(4, -1).astype(jnp.float32)
    cut_qk, cut_mlp = qk_scale.shape[1], qk_scale.shape[1] + mlp_scale.shape[1]
    all_qk = vectors[:, :cut_qk].reshape(4, 2, -1)
    all_mlp = vectors[:, cut_qk:cut_mlp].reshape(2, 4, 2, -1)
    all_alphas = vectors[:, cut_mlp : cut_mlp + alphas.shape[1]].reshape(2, 1, -1)
    mlp_half = pick(all_mlp, c, 2).reshape(2, 1, -1)
    scales = (
        pick(all_qk, c, 1),
        mlp_half[0],
        mlp_half[1] * math.sqrt(width),
        all_alphas[0],
        all_alphas[1],
    )

    valid = pick(valid[:, :2], c, 1).reshape(-1).astype(jnp.float32)

    statistic = jnp.sum(valid * jnp.sum(branch * branch, axis=-1))

    (
        grad_output, grad_up, grad_gate, grad_branch, grad_mixed, grad_hidden,
        sum_alphas, sum_scales, sum_qk,
    ) = backward_all(weights, kept, row, log_sums, scales, places)
    small = (sum_alphas.reshape(-1), sum_scales[0], sum_scales[1] * math.sqrt(width), sum_qk)

    def weight_grad(left, right):
        flat = [part.reshape(-1, part.shape[2]) for part in (left, right)]
        return low(contract_rows(*flat))

    g_down = weight_grad(inner, grad_output)
    g_up = weight_grad(middle, grad_up)
    g_gate = weight_grad(middle, grad_gate)
    g_out = weight_grad(attended, grad_branch)
    g_qkv = weight_grad(hidden, grad_mixed)
    g_out = g_out.reshape(4, BLOCK, 2, -1).transpose(0, 2, 1, 3).reshape(4 * 2 * BLOCK, -1)

    at_half = jnp.arange(2).reshape(1, 1, 2, 1) == c
    up_gate = jnp.stack([small[1], small[2]]).reshape(2, 4, 1, -1)
    g_vectors = jnp.concatenate(
        [
            jnp.where(at_half[0], small[3].reshape(4, 1, -1), 0.0).reshape(4, -1),
            jnp.where(at_half, up_gate, 0.0).reshape(4, -1),
            small[0].reshape(4, -1),
            jnp.full((4, 1), statistic),
        ],
        axis=1,
    )
    g_vectors = jnp.pad(g_vectors, ((0, 0), (0, 24 * 128 - g_vectors.shape[1]))).reshape(4, 24, 128)
    grad_down, grad_in_proj, grad_out, grad_qkv, vectors, hidden_out, grad_in = reduce_all(
        g_down, g_up, g_gate, g_out, g_qkv, g_vectors, result, grad_hidden
    )
    full = jnp.sum(vectors, axis=0).reshape(-1)
    cuts = (cut_qk, cut_mlp, cut_mlp + alphas.shape[1])
    grad_qk_scale = full[: cuts[0]][None]
    grad_mlp_scale = full[cuts[0] : cuts[1]][None]
    grad_alphas = full[cuts[1] : cuts[2]][None]
    token_count = tokens.shape[0] * lax.axis_size("fsdp") * 4 * group
    rms_stats = jnp.sqrt(full[cuts[2] : cuts[2] + 1] / token_count + epsilon)
    as_float = [
        part.astype(jnp.float32)[None] for part in (grad_qkv, grad_out, grad_in_proj, grad_down)
    ]
    return (
        hidden_out[None, :, None], grad_in.astype(jnp.float32)[None, :, None], *as_float,
        grad_qk_scale, grad_mlp_scale, grad_alphas, rms_stats,
    )


def solution(mesh):
    placed = (
        P(None, "fsdp", "seq", None),
        P(None, "fsdp", "seq", None),
        P(None, "fsdp", None),
        P(None, "fsdp", "seq"),
        P("section", "fsdp", None),
        P("section", "fsdp", None),
        P("section", "fsdp", None),
        P("section", "fsdp", None),
        P("section", "fsdp"),
        P("section", "fsdp"),
        P("section", "fsdp"),
    )
    planes = mesh.shape["section"] == 2 and mesh.shape["seq"] == 4 and mesh.shape["fsdp"] == 4
    return jax.shard_map(
        per_device if planes else per_device_general,
        mesh=mesh,
        in_specs=placed,
        out_specs=(
            P("section", None, "fsdp", "seq", None),
            P("section", None, "fsdp", "seq", None),
            P("section", "fsdp", None),
            P("section", "fsdp", None),
            P("section", "fsdp", None),
            P("section", "fsdp", None),
            P("section", "fsdp"),
            P("section", "fsdp"),
            P("section", "fsdp"),
            P("section"),
        ),
        check_vma=False,
    )
```

```python
import functools
import math
import types

import jax
import jax.numpy as jnp
from jax import lax
from jax.experimental import pallas as pl
from jax.experimental.pallas import tpu as pltpu
from jax.sharding import PartitionSpec as P

HEAD = 64


epsilon = 1e-06


def shifted(block, axis, distance):
    devices = range(lax.axis_size(axis))
    route = [(i - distance, i) for i in devices if i - distance in devices]
    return lax.ppermute(block, axis, route)


def for_sending(x):
    return jax.tree.map(lambda a: a.astype(jnp.bfloat16) if a.dtype == jnp.float32 else a, x)


def unit(values):
    return values * lax.rsqrt(jnp.sum(values * values, axis=-1, keepdims=True) + epsilon)


def unit_back(values, grad):
    factor = lax.rsqrt(jnp.sum(values * values, axis=-1, keepdims=True) + epsilon)
    normed = values * factor
    return factor * (grad - normed * jnp.sum(normed * grad, axis=-1, keepdims=True))


def contract_rows(left, right):
    return lax.dot_general(
        left, right, (((0,), (0,)), ((), ())), preferred_element_type=jnp.float32
    )


def contract_cols(left, right):
    return lax.dot_general(
        left, right, (((1,), (1,)), ((), ())), preferred_element_type=jnp.float32
    )


def segments_of(row_lengths, seq_len):
    ends = jnp.cumsum(row_lengths)[:-1]
    place = jnp.arange(seq_len, dtype=jnp.int32)
    return (place, jnp.sum((place[:, None] >= ends[None, :]).astype(jnp.int32), axis=1))


def allowed_pairs(row_lengths, offset, group, seq_len):
    key_place, key_segment = segments_of(row_lengths, seq_len)
    query_place = offset + jnp.arange(group, dtype=jnp.int32)
    query_segment = lax.dynamic_slice_in_dim(key_segment, offset, group)
    return (query_segment[:, None] == key_segment[None, :]) & (
        key_place[None, :] <= query_place[:, None]
    )


def masked_scores(queries, key_heads, allowed):
    scores = jnp.einsum(
        "qhd,khd->hqk", queries, key_heads, preferred_element_type=jnp.float32
    ) * math.sqrt(HEAD)
    return jnp.where(allowed[None], scores, -1e30)


def forward_layer(hidden_b, params, allowed, valid):
    w_qkv, w_out, w_in, w_down, qk_scale, mlp_scale, alphas = params
    count, width = hidden_b.shape
    heads = width // HEAD
    hidden = hidden_b.astype(jnp.float32)
    mixed = jnp.dot(hidden_b, w_qkv, preferred_element_type=jnp.float32)
    query_raw = mixed[:, :width].reshape(count, heads, HEAD)
    key_raw = mixed[:, width : 2 * width].reshape(count, heads, HEAD)
    head_scale = qk_scale.astype(jnp.float32).reshape(heads, HEAD)
    query_b = (unit(query_raw) * head_scale).astype(jnp.bfloat16)
    key_b = (unit(key_raw) * head_scale).astype(jnp.bfloat16).reshape(count, width)
    value_b = mixed[:, 2 * width :].astype(jnp.bfloat16)
    keys, values = (
        lax.all_gather(key_b, "seq", axis=0, tiled=True),
        lax.all_gather(value_b, "seq", axis=0, tiled=True),
    )
    key_heads = keys.reshape(-1, heads, HEAD)
    value_heads = values.reshape(-1, heads, HEAD)
    scores = masked_scores(query_b, key_heads, allowed)
    highest = jnp.max(scores, axis=-1, keepdims=True)
    weights = jnp.exp(scores - highest)
    denominator = jnp.sum(weights, axis=-1, keepdims=True)
    weights = weights / denominator
    log_total = highest + jnp.log(denominator)
    attended = jnp.einsum(
        "hqk,khd->qhd",
        weights.astype(jnp.bfloat16),
        value_heads,
        preferred_element_type=jnp.float32,
    )
    attended_b = attended.reshape(count, width).astype(jnp.bfloat16)
    branch = jnp.dot(attended_b, w_out, preferred_element_type=jnp.float32)
    statistic = jnp.sum(valid * jnp.sum(branch * branch, axis=-1))
    step_sizes = alphas.astype(jnp.float32)
    first_sum = hidden + step_sizes[:width] * (unit(branch) - hidden)
    middle = unit(first_sum)
    middle_b = middle.astype(jnp.bfloat16)
    lifted = jnp.dot(middle_b, w_in, preferred_element_type=jnp.float32)
    units_count = lifted.shape[1] // 2
    scales = mlp_scale.astype(jnp.float32)
    upward = lifted[:, :units_count] * scales[:units_count]
    gating = lifted[:, units_count:] * scales[units_count:] * math.sqrt(width)
    inner_b = (upward * jax.nn.silu(gating)).astype(jnp.bfloat16)
    output = jnp.dot(inner_b, w_down, preferred_element_type=jnp.float32)
    second_sum = middle + step_sizes[width:] * (unit(output) - middle)
    result = unit(second_sum).astype(jnp.bfloat16)
    kept = (
        hidden_b,
        query_raw,
        key_raw,
        query_b,
        keys,
        values,
        log_total,
        attended_b,
        branch,
        first_sum,
        middle_b,
        lifted,
        inner_b,
        output,
        second_sum,
    )
    return (result, kept, statistic)


def backward_layer(kept, params, grad_out, allowed):
    (
        hidden_b,
        query_raw,
        key_raw,
        query_b,
        keys,
        values,
        log_total,
        attended_b,
        branch,
        first_sum,
        middle_b,
        lifted,
        inner_b,
        output,
        second_sum,
    ) = kept
    w_qkv, w_out, w_in, w_down, qk_scale, mlp_scale, alphas = params
    count, width = hidden_b.shape
    heads = width // HEAD
    hidden = hidden_b.astype(jnp.float32)
    step_sizes = alphas.astype(jnp.float32)
    alpha_attn = step_sizes[:width]
    alpha_mlp = step_sizes[width:]
    middle = unit(first_sum)
    grad_second = unit_back(second_sum, grad_out)
    grad_alpha_mlp = jnp.sum(grad_second * (unit(output) - middle), axis=0)
    grad_output = unit_back(output, alpha_mlp * grad_second).astype(jnp.bfloat16)
    grad_middle = grad_second * (1.0 - alpha_mlp)
    grad_down = contract_rows(inner_b, grad_output)
    grad_inner = contract_cols(grad_output, w_down)
    units_count = lifted.shape[1] // 2
    scales = mlp_scale.astype(jnp.float32)
    root = math.sqrt(width)
    lift_up = lifted[:, :units_count]
    lift_gate = lifted[:, units_count:]
    upward = lift_up * scales[:units_count]
    gating = lift_gate * scales[units_count:] * root
    sigmoid = jax.nn.sigmoid(gating)
    grad_upward = grad_inner * jax.nn.silu(gating)
    grad_gating = grad_inner * upward * sigmoid * (1.0 + gating * (1.0 - sigmoid))
    grad_scale_mlp = jnp.concatenate(
        [jnp.sum(grad_upward * lift_up, axis=0), jnp.sum(grad_gating * root * lift_gate, axis=0)]
    )
    grad_lifted = jnp.concatenate(
        [grad_upward * scales[:units_count], grad_gating * root * scales[units_count:]], axis=1
    ).astype(jnp.bfloat16)
    grad_in_proj = contract_rows(middle_b, grad_lifted)
    grad_middle = grad_middle + contract_cols(grad_lifted, w_in)
    grad_first = unit_back(first_sum, grad_middle)
    grad_alpha_attn = jnp.sum(grad_first * (unit(branch) - hidden), axis=0)
    grad_branch = unit_back(branch, alpha_attn * grad_first).astype(jnp.bfloat16)
    grad_hidden = grad_first * (1.0 - alpha_attn)
    grad_out_proj = contract_rows(attended_b, grad_branch)
    grad_attended = (
        contract_cols(grad_branch, w_out).astype(jnp.bfloat16).reshape(count, heads, HEAD)
    )
    key_heads = keys.reshape(-1, heads, HEAD)
    value_heads = values.reshape(-1, heads, HEAD)
    scores = masked_scores(query_b, key_heads, allowed)
    weights = jnp.exp(scores - log_total)
    grad_weights = jnp.einsum(
        "qhd,khd->hqk", grad_attended, value_heads, preferred_element_type=jnp.float32
    )
    delta = jnp.sum(weights * grad_weights, axis=-1, keepdims=True)
    grad_scores = (weights * (grad_weights - delta)).astype(jnp.bfloat16)
    score_scale = math.sqrt(HEAD)
    grad_query = (
        jnp.einsum("hqk,khd->qhd", grad_scores, key_heads, preferred_element_type=jnp.float32)
        * score_scale
    )
    seq_len = keys.shape[0]
    grad_keys = (
        jnp.einsum("hqk,qhd->khd", grad_scores, query_b, preferred_element_type=jnp.float32)
        * score_scale
    )
    grad_values = jnp.einsum(
        "hqk,qhd->khd",
        weights.astype(jnp.bfloat16),
        grad_attended,
        preferred_element_type=jnp.float32,
    )
    grad_key_own, grad_value_own = (
        lax.psum_scatter(
            grad_keys.reshape(seq_len, width).astype(jnp.bfloat16),
            "seq",
            scatter_dimension=0,
            tiled=True,
        ).astype(jnp.float32),
        lax.psum_scatter(
            grad_values.reshape(seq_len, width).astype(jnp.bfloat16),
            "seq",
            scatter_dimension=0,
            tiled=True,
        ).astype(jnp.float32),
    )
    head_scale = qk_scale.astype(jnp.float32).reshape(heads, HEAD)
    grad_key_heads = grad_key_own.reshape(count, heads, HEAD)
    grad_scale_qk = (
        jnp.sum(grad_query * unit(query_raw), axis=0)
        + jnp.sum(grad_key_heads * unit(key_raw), axis=0)
    ).reshape(width)
    grad_query_raw = unit_back(query_raw, grad_query * head_scale).reshape(count, width)
    grad_key_raw = unit_back(key_raw, grad_key_heads * head_scale).reshape(count, width)
    grad_mixed = jnp.concatenate([grad_query_raw, grad_key_raw, grad_value_own], axis=1).astype(
        jnp.bfloat16
    )
    grad_qkv = contract_rows(hidden_b, grad_mixed)
    grad_hidden = grad_hidden + contract_cols(grad_mixed, w_qkv)
    grad_step_sizes = jnp.concatenate([grad_alpha_attn, grad_alpha_mlp])
    grads = (
        grad_qkv,
        grad_out_proj,
        grad_in_proj,
        grad_down,
        grad_scale_qk,
        grad_scale_mlp,
        grad_step_sizes,
    )
    return (grad_hidden, grads)


def per_device_general(
    tokens, cotangent, lengths, valid_mask, w_qkv, w_out, w_in, w_down, qk_scale, mlp_scale, alphas
):
    shards = (w_qkv, w_out, w_in, w_down, qk_scale, mlp_scale, alphas)
    gathered = (
        lax.all_gather(shards[0], "fsdp", axis=1, tiled=True),
        lax.all_gather(shards[1], "fsdp", axis=1, tiled=True),
        lax.all_gather(shards[2], "fsdp", axis=1, tiled=True),
        lax.all_gather(shards[3], "fsdp", axis=1, tiled=True),
        lax.all_gather(shards[4], "fsdp", axis=1, tiled=True),
        lax.all_gather(shards[5], "fsdp", axis=1, tiled=True),
        lax.all_gather(shards[6], "fsdp", axis=1, tiled=True),
    )
    params = tuple((piece[0] for piece in gathered))
    section = lax.axis_index("section")
    micro = tokens.shape[0]
    group = tokens.shape[2]
    width = tokens.shape[3]
    seq_len = group * lax.axis_size("seq")
    offset = lax.axis_index("seq") * group

    def fetch(array, index):
        return lax.dynamic_index_in_dim(array, index, 0, keepdims=False)[0]

    def forward_step(carry, step):
        incoming, stat_sum = carry
        index = step - section
        active = (index >= 0) & (index < micro)
        chosen = jnp.clip(index, 0, micro - 1)
        hidden_in = jnp.where(section == 0, fetch(tokens, chosen), incoming)
        allowed = allowed_pairs(fetch(lengths, chosen), offset, group, seq_len)
        valid = fetch(valid_mask, chosen).astype(jnp.float32)
        result, kept, statistic = forward_layer(hidden_in, params, allowed, valid)
        outgoing = shifted(result, "section", 1)
        stat_sum = stat_sum + jnp.where(active, statistic, 0.0)
        return ((outgoing, stat_sum), (result, kept))

    step_list = jnp.arange(micro + 1, dtype=jnp.int32)
    start = (jnp.zeros((group, width), jnp.bfloat16), jnp.zeros((), jnp.float32))
    (unused_fwd, stat_sum), (results, kept_all) = lax.scan(forward_step, start, step_list)
    late_shards, stat_sum = lax.optimization_barrier((shards, stat_sum))
    again = (
        lax.all_gather(late_shards[0], "fsdp", axis=1, tiled=True),
        lax.all_gather(late_shards[1], "fsdp", axis=1, tiled=True),
        lax.all_gather(late_shards[2], "fsdp", axis=1, tiled=True),
        lax.all_gather(late_shards[3], "fsdp", axis=1, tiled=True),
        lax.all_gather(late_shards[4], "fsdp", axis=1, tiled=True),
        lax.all_gather(late_shards[5], "fsdp", axis=1, tiled=True),
        lax.all_gather(late_shards[6], "fsdp", axis=1, tiled=True),
    )
    params_back = tuple((piece[0] for piece in again))

    def backward_step(carry, step):
        incoming, sums = carry
        index = step - 1 + section
        active = (index >= 0) & (index < micro)
        chosen = jnp.clip(index, 0, micro - 1)
        position = chosen + section

        def take(array):
            return lax.dynamic_index_in_dim(array, position, 0, keepdims=False)

        kept = jax.tree.map(take, kept_all)
        grad_out = jnp.where(
            section == 1, fetch(cotangent, chosen).astype(jnp.float32), incoming.astype(jnp.float32)
        )
        grad_out = jnp.where(active, grad_out, 0.0)
        row_lengths = fetch(lengths, chosen)
        allowed = allowed_pairs(row_lengths, offset, group, seq_len)
        grad_hidden, grads = backward_layer(kept, params_back, grad_out, allowed)
        outgoing = shifted(grad_hidden.astype(jnp.bfloat16), "section", -1)
        sums = tuple((total + piece for total, piece in zip(sums, grads)))
        return ((outgoing, sums), grad_hidden)

    zeros = tuple((jnp.zeros(piece.shape, jnp.float32) for piece in params_back))
    (unused_back, sums), grad_steps = lax.scan(
        backward_step, (jnp.zeros((group, width), jnp.bfloat16), zeros), step_list
    )
    hidden_out = lax.dynamic_slice_in_dim(results, section, micro, 0).reshape(
        1, micro, 1, group, width
    )
    grad_in = lax.dynamic_slice_in_dim(grad_steps, 1 - section, micro, 0).reshape(
        1, micro, 1, group, width
    )
    shard_sums = jax.tree.map(
        lambda part: part.astype(jnp.float32),
        lax.psum_scatter(for_sending(sums), "fsdp", scatter_dimension=0, tiled=True),
    )
    reduced = jax.tree.map(
        lambda part: part.astype(jnp.float32), lax.psum(for_sending(shard_sums), "seq")
    )
    total_stat = lax.psum(stat_sum, ("seq", "fsdp"))
    token_count = micro * lax.axis_size("fsdp") * seq_len
    rms_stats = jnp.sqrt(total_stat / token_count + epsilon).reshape(1)
    return (
        hidden_out,
        grad_in,
        reduced[0][None],
        reduced[1][None],
        reduced[2][None],
        reduced[3][None],
        reduced[4][None],
        reduced[5][None],
        reduced[6][None],
        rms_stats,
    )


BLOCK = 128
SCORE_SCALE = math.sqrt(HEAD)
MASKED = -1e30


def dot(left, right):
    return jnp.dot(left, right, preferred_element_type=jnp.float32)


def low(x):
    return x.astype(jnp.bfloat16)


def pick(x, index, axis):
    return lax.dynamic_index_in_dim(x, index, axis, keepdims=False)


def sums_of_halves(x):
    row = lax.broadcasted_iota(jnp.int32, (2 * HEAD, 2 * HEAD), 0) // HEAD
    col = lax.broadcasted_iota(jnp.int32, (2 * HEAD, 2 * HEAD), 1) // HEAD
    same = (row == col).astype(jnp.bfloat16)
    high = x.astype(jnp.bfloat16)
    rest = (x - high.astype(jnp.float32)).astype(jnp.bfloat16)
    return dot(high, same) + dot(rest, same)


def normal_heads(raw):
    factor = lax.rsqrt(sums_of_halves(raw * raw) + epsilon)
    return raw * factor, factor


def merge(to, own, oth):
    for s in range(4):
        to[s * 256 : s * 256 + BLOCK, : own.shape[1]] = own[s * BLOCK : (s + 1) * BLOCK]
        to[s * 256 + BLOCK : (s + 1) * 256, : own.shape[1]] = oth[s * BLOCK : (s + 1) * BLOCK]


def last_dims(left, right):
    return lax.dot_general(left, right, (((1,), (1,)), ((), ())), preferred_element_type=jnp.float32)


def head_lanes(h, dtype):
    lane = lax.broadcasted_iota(jnp.int32, (1, 2 * HEAD), 1) // HEAD
    return (lane == h).astype(dtype)


MESH = pl.DeviceIdType.MESH


def position():
    c, s, f = (lax.axis_index(name) for name in ("section", "seq", "fsdp"))
    x, y = f % 2, f // 2
    layer = 1 - ((s + 1) // 2) % 2
    return c, s, f, y * 2 + 1 - x, (1 - y) * 2 + x, layer


def greet(devices):
    barrier = pltpu.get_barrier_semaphore()
    for device in devices:
        pl.semaphore_signal(barrier, inc=1, device_id=device, device_id_type=MESH)
    pl.semaphore_wait(barrier, len(devices))


def remote(src, dst, send, recv, device):
    return pltpu.make_async_remote_copy(
        src_ref=src, dst_ref=dst, send_sem=send, recv_sem=recv, device_id=device, device_id_type=MESH
    )


def arrived(ref, sem):
    pltpu.make_async_copy(ref, ref, sem).wait()


def lane(offset):
    return pl.multiple_of(offset, 128)


def every(count, work):
    def step(n, carry):
        work(n)
        return carry

    lax.fori_loop(0, count, step, 0)


def silu(x):
    return x * jax.nn.sigmoid(x)


def row_sums(x, lanes):
    high = low(x)
    rest = low(x - high.astype(jnp.float32))
    return last_dims(lanes, high) + last_dims(lanes, rest)


class Flow:
    def __init__(self, buffers, semaphores):
        (
            self.near_own, self.near_far, self.far_in, self.own, self.passing,
            self.from_left, self.from_right, self.pair_sum,
        ) = buffers
        (
            self.load_own, self.load_pass, self.send_own, self.recv_own, self.send_far,
            self.recv_far, self.send_next, self.recv_next, self.send_z, self.recv_left,
            self.recv_right, self.recv_pair, self.send_on, self.send_back, self.send_out,
            self.keep, self.give, self.given,
        ) = [semaphores.at[n] for n in range(VECTOR_SEMAPHORES)]
        self.place_of = position()

    def begin(self, source):
        c, s, f, fx, fy, _ = self.place_of
        to = (c, s, fx)
        remote(source(fx), self.near_own, self.send_own, self.recv_own, to).start()
        remote(source(3 - f), self.near_far, self.send_far, self.recv_far, to).start()
        pltpu.make_async_copy(source(fy), self.passing, self.load_pass).start()
        pltpu.make_async_copy(source(f), self.own, self.load_own).start()

    def pass_on(self):
        c, s, _, _, fy, _ = self.place_of
        arrived(self.passing, self.load_pass)
        arrived(self.near_far, self.recv_far)
        add(self.passing, self.passing, self.near_far)
        remote(self.passing, self.far_in, self.send_next, self.recv_next, (c, s, fy)).start()

    def finish_plane(self):
        c, s, f, _, _, _ = self.place_of
        own, send = self.own, self.send_z
        arrived(own, self.load_own)
        arrived(self.near_own, self.recv_own)
        arrived(self.far_in, self.recv_next)
        add(own, own, self.near_own, self.far_in)

        @pl.when(s == 0)
        def _():
            remote(own, self.from_left, send, self.recv_left, (c, 1, f)).start()

        @pl.when(s == 3)
        def _():
            remote(own, self.from_right, send, self.recv_right, (c, 2, f)).start()

        @pl.when((s == 1) | (s == 2))
        def _():
            remote(own, self.pair_sum, send, self.recv_pair, (c, 3 - s, f)).start()

    def middle_planes(self):
        c, s, f, _, _, _ = self.place_of
        left, right, pair = self.from_left, self.from_right, self.pair_sum

        @pl.when(s == 1)
        def _():
            arrived(left, self.recv_left)
            remote(left, left, self.send_on, self.recv_left, (c, 2, f)).start()

        @pl.when(s == 2)
        def _():
            arrived(right, self.recv_right)
            remote(right, right, self.send_on, self.recv_right, (c, 1, f)).start()

        @pl.when((s == 1) | (s == 2))
        def _():
            arrived(pair, self.recv_pair)
            arrived(pair, self.send_z)
            add(pair, pair, self.own)
            remote(pair, pair, self.send_out, self.recv_pair, (c, (s - 1) * 3, f)).start()

    def all_planes(self, dst):
        c, s, f, _, _, _ = self.place_of
        left, right, pair = self.from_left, self.from_right, self.pair_sum
        own, total = self.own, self.near_own

        @pl.when(s == 1)
        def _():
            arrived(right, self.recv_right)
            remote(right, right, self.send_back, self.recv_right, (c, 0, f)).start()

        @pl.when(s == 2)
        def _():
            arrived(left, self.recv_left)
            remote(left, left, self.send_back, self.recv_left, (c, 3, f)).start()

        @pl.when((s == 1) | (s == 2))
        def _():
            add(total, left, right)

        @pl.when(s == 0)
        def _():
            arrived(pair, self.recv_pair)
            arrived(right, self.recv_right)
            add(total, own, right)

        @pl.when(s == 3)
        def _():
            arrived(pair, self.recv_pair)
            arrived(left, self.recv_left)
            add(total, own, left)

        for owner, chunk in ((0, pair), (1, total)):

            @pl.when(c == owner)
            def _():
                pltpu.make_async_copy(chunk, dst, self.keep).start()

            @pl.when(c != owner)
            def _():
                remote(chunk, dst, self.give, self.given, (1 - c, s, f)).start()

    def settle(self):
        _, s, _, _, _, _ = self.place_of
        for sem in (
            self.send_own, self.send_far, self.send_next, self.keep, self.give, self.given
        ):
            arrived(self.own, sem)

        @pl.when((s == 1) | (s == 2))
        def _():
            for sem in (self.send_on, self.send_back, self.send_out):
                arrived(self.own, sem)

        @pl.when((s == 0) | (s == 3))
        def _():
            arrived(self.own, self.send_z)


def add(to, *refs):
    total = refs[0][...].astype(jnp.float32)
    for ref in refs[1:]:
        total = total + ref[...].astype(jnp.float32)
    to[...] = total.astype(to.dtype)


VECTOR_SEMAPHORES = 18
CHUNKS = 16
READY = 4
AHEAD = 3
INPUTS = 11
OUTPUTS = 19


def scratch_of(width, units, vector_rows, flag_rows):
    rows = 4 * BLOCK
    half = units // 2

    def low_vmem(*shape):
        return pltpu.VMEM(shape, jnp.bfloat16)

    def full_vmem(*shape):
        return pltpu.VMEM(shape, jnp.float32)

    def sems(*shape):
        return pltpu.SemaphoreType.DMA(shape)

    low_row, full_row, low_rows = low_vmem(rows, width), full_vmem(rows, width), low_vmem(2, rows, width)
    pair, pair_full = low_vmem(2 * rows, 2 * HEAD), full_vmem(2 * rows, 2 * HEAD)
    return dict(
        wq=low_vmem(width, 3 * width // 2), wo=low_vmem(width // 2, width),
        wu=low_vmem(width, half), wg=low_vmem(width, half), wd=low_vmem(half, width),
        vec=low_vmem(4, vector_rows, 128), flat=full_vmem(4, vector_rows, 128),
        flags=low_vmem(4, flag_rows, 128), flags_full=full_vmem(4, flag_rows, 128),
        scale_up=full_vmem(1, half), scale_gate=full_vmem(1, half),
        alpha_attn=full_vmem(1, width), alpha_mlp=full_vmem(1, width),
        hid=low_rows, mixed=low_vmem(2, rows, 3 * width // 2), att=low_vmem(2, rows, width // 2),
        mid=low_rows, up=low_vmem(2, rows, half), gate=low_vmem(2, rows, half),
        inner=low_vmem(2, rows, half), branch=full_row, middle=full_row, output=full_row,
        result=low_row, part=low_row, got=low_row,
        bias=full_vmem(2 * rows, 2 * rows), raw=pair, queries=pair, keys=pair,
        values=low_vmem(2 * rows, 4 * HEAD), grads=pair, dq=pair_full, dk=pair_full, dv=pair_full,
        log_sums=full_vmem(4, 2, 2 * rows),
        grad_in=low_row, grad_rows=low_rows,
        sum_alphas=full_vmem(2, width), sum_scales=full_vmem(2, half), sum_qk=full_vmem(4, 2 * HEAD),
        sum_valid=full_vmem(1, 128), terms=full_vmem(4, 24, 128),
        v0=full_vmem(24, 128), v1=full_vmem(24, 128), v2=full_vmem(24, 128), v3=full_vmem(24, 128),
        v4=full_vmem(24, 128), v5=full_vmem(24, 128), v6=full_vmem(24, 128), v7=full_vmem(24, 128),
        first_send=sems(6, 5), first_recv=sems(6, 3), next_send=sems(6, 2), next_recv=sems(6, 2),
        row_send=sems(4), row_recv=sems(4), flag_send=sems(4), flag_recv=sems(4),
        own_recv=sems(4), oth_send=sems(4), oth_recv=sems(4),
        part_send=sems(4, 4), part_recv=sems(4, 4),
        mid_send=sems(3, 4), mid_recv=sems(3, 4), result_send=sems(4), grad_recv=sems(4),
        owner_send=sems(2, 4), owner_recv=sems(2, 2, 2),
        vector=sems(VECTOR_SEMAPHORES), staged=sems(2), load=sems(9, 4),
        send_own=sems(CHUNKS), recv_own=sems(CHUNKS), send_far=sems(CHUNKS), recv_far=sems(CHUNKS),
        send_next=sems(CHUNKS), recv_next=sems(CHUNKS), send_z=sems(CHUNKS), stored=sems(CHUNKS),
        recv_left=sems(CHUNKS), recv_right=sems(CHUNKS), recv_pair=sems(CHUNKS),
        send_on=sems(CHUNKS), send_back=sems(CHUNKS), send_out=sems(CHUNKS),
        keep=sems(CHUNKS), give=sems(CHUNKS), given=sems(CHUNKS),
    )


def relay_kernel(names, *refs):
    (
        w_qkv, w_out, w_in, w_down, vectors, valid, tokens, cotangent,
        start_col, place_row, start_row,
    ) = refs[:INPUTS]
    (
        o_down, o_in, o_out, o_qkv, o_vectors, o_hidden, o_grad, o_row,
        g_down, g_up, g_gate, g_out, g_qkv,
        near_own, near_far, far_in, from_left, from_right, pair_sum,
    ) = refs[INPUTS : INPUTS + OUTPUTS]
    plane_sum, *refs = refs[INPUTS + OUTPUTS :]
    r = types.SimpleNamespace(**dict(zip(names, refs)))
    c, s, f, fx, fy, layer = position()
    sibling = (1 - c, s, f)
    early, late = layer == 0, layer == 1
    late_plane = (c, (s - 1) * 3, f)
    early_plane = (c, s // 3 + 1, f)
    width = w_out.shape[1]
    full = jnp.float32
    greet(
        [sibling, (c, s, fx), (1 - c, s, fx), (c, s, fy), (1 - c, s, fy)]
        + [(core, (s + step) % 4, f) for core in (0, 1) for step in (1, 2, 3)]
    )

    def rows_of(b):
        return pl.ds(b * BLOCK, BLOCK)

    def columns(n):
        return pl.ds(lane(n * 256), 256)

    for to, held in enumerate((cotangent.at[0], tokens.at[0], tokens.at[1], cotangent.at[1])):
        src = held.at[pl.ds(c * BLOCK, BLOCK)]
        dst = o_row.at[rows_of(s)]
        flags, flags_to = valid.at[to // 2], r.flags.at[s]

        @pl.when(s == to)
        def _():
            pltpu.make_async_copy(src, dst, r.row_recv.at[s]).start()
            pltpu.make_async_copy(flags, flags_to, r.flag_recv.at[s]).start()

        @pl.when(s != to)
        def _():
            remote(src, dst, r.row_send.at[to], r.row_recv.at[s], (c, to, f)).start()
            remote(flags, flags_to, r.flag_send.at[to], r.flag_recv.at[s], (c, to, f)).start()

    def pieces(item, h):
        if item == 0:
            return [(vectors, r.vec.at[f])]
        if item == 1:
            return [
                (
                    w_qkv.at[:, pl.ds(lane(part * 256 + h * 128), 128)],
                    r.wq.at[pl.ds(f * 256, 256), pl.ds(part * 128, 128)],
                )
                for part in range(12)
            ]
        if item == 2:
            return [(w_out.at[pl.ds(h * 128, 128)], r.wo.at[pl.ds(f * 128, 128)])]
        if item in (3, 4):
            to = (r.wu, r.wg)[item - 3]
            return [
                (
                    w_in.at[:, pl.ds(lane((item - 3) * 4096 + part * 1024 + h * 512), 512)],
                    to.at[pl.ds(f * 256, 256), pl.ds(part * 512, 512)],
                )
                for part in range(4)
            ]
        return [(w_down.at[pl.ds(h * 512, 512)], r.wd.at[pl.ds(f * 512, 512)])]

    weights = (r.vec, r.wq, r.wo, r.wu, r.wg, r.wd)

    def block(item, of):
        if item == 0:
            return r.vec.at[of]
        rows = weights[item].shape[0] // 4
        return weights[item].at[pl.ds(of * rows, rows)]

    def part_of(item, of, part):
        if item == 0:
            return r.vec.at[of, pl.ds(part * 16, 16)]
        rows = weights[item].shape[0] // 8
        return weights[item].at[pl.ds(of * 2 * rows + part * rows, rows)]

    targets = (
        ((c, s, fx), c, 1), ((c, s, fy), c, 2), ((1 - c, s, fx), 1 - c, 1),
        ((1 - c, s, fy), 1 - c, 2), (sibling, 1 - c, 0),
    )

    def spread(*items):
        @pl.when(c == layer)
        def _():
            for item in items:
                for index, (device, h, came) in enumerate(targets):
                    for src, dst in pieces(item, h):
                        remote(
                            src, dst, r.first_send.at[item, index], r.first_recv.at[item, came],
                            device,
                        ).start()
                for src, dst in pieces(item, c):
                    pltpu.make_async_copy(src, dst, r.first_recv.at[item, 0]).start()

    def relay(item):
        for part, (came, of, to) in enumerate(((1, fx, fy), (2, fy, fx))):
            arrived(block(item, of), r.first_recv.at[item, came])
            moved = part_of(item, of, part)
            remote(
                moved, moved, r.next_send.at[item, part], r.next_recv.at[item, part], (c, s, to)
            ).start()

    def complete(item):
        arrived(block(item, f), r.first_recv.at[item, 0])
        for part in range(2):
            arrived(part_of(item, 3 - f, part), r.next_recv.at[item, part])

    spread(0, 1, 2, 3)
    index = lax.broadcasted_iota(jnp.int32, (8 * BLOCK, 1), 0)
    place_col = (index // 256) * 256 + (index // BLOCK + c) % 2 * BLOCK + index % BLOCK
    fits = (place_row[...] >= start_col[...]) & (place_row[...] <= place_col)
    r.bias[...] = jnp.where(fits, 0.0, MASKED)
    r.values[:, 2 * HEAD :] = jnp.ones_like(r.values[:, 2 * HEAD :])
    for sums in (r.sum_alphas, r.sum_scales, r.sum_valid, r.terms):
        sums[...] = jnp.zeros_like(sums)
    relay(0)
    relay(1)
    spread(4)
    relay(2)

    def to_sibling(b, src):
        remote(src, r.hid.at[1, rows_of(b)], r.oth_send.at[b], r.oth_recv.at[b], sibling).start()

    @pl.when(early)
    def _():
        for b in range(4):
            held = o_row.at[rows_of(b)]
            arrived(held, r.row_recv.at[b])
            pltpu.make_async_copy(held, r.hid.at[0, rows_of(b)], r.own_recv.at[b]).start()
            to_sibling(b, held)
        for b in range(4):
            arrived(r.hid.at[0, rows_of(b)], r.own_recv.at[b])

    @pl.when(late)
    def _():
        relay(3)
        spread(5)
        relay(4)
        relay(5)
        for b in range(4):
            held = o_row.at[rows_of(b)]
            arrived(held, r.row_recv.at[b])
            pltpu.make_async_copy(held, r.grad_in.at[rows_of(b)], r.grad_recv.at[b]).start()
        for b in range(4):
            arrived(r.hid.at[0, rows_of(b)], r.own_recv.at[b])
            to_sibling(b, r.hid.at[0, rows_of(b)])

    complete(0)
    r.flat[...] = r.vec[...].astype(full)
    for n in range(4):
        for j in range(4):
            at = slice(n * 512 + j * 128, n * 512 + (j + 1) * 128)
            row = pl.ds(2 + (n % 2) * 8 + j + c * 4, 1)
            r.scale_up[:, at] = r.flat[n // 2, row, :]
            r.scale_gate[:, at] = r.flat[2 + n // 2, row, :] * math.sqrt(width)
    for n in range(2):
        for j in range(4):
            at = slice(n * 512 + j * 128, n * 512 + (j + 1) * 128)
            r.alpha_attn[:, at] = r.flat[n, 18 + j : 19 + j, :]
            r.alpha_mlp[:, at] = r.flat[2 + n, 18 + j : 19 + j, :]

    complete(1)
    for side in range(2):
        if side:
            for b in range(4):
                arrived(r.hid.at[1, rows_of(b)], r.oth_recv.at[b])

        def mix(n, side=side):
            at = pl.ds(lane(n * 512), 512)
            r.mixed[side, :, at] = low(dot(r.hid[side], r.wq[:, at]))

        every(3, mix)

    first = (lax.broadcasted_iota(jnp.int32, (8, 2 * HEAD), 1) == 0).astype(jnp.bfloat16)

    def lanes_of(pair, part):
        return pl.ds(lane(part * (width // 2) + pair * 2 * HEAD), 2 * HEAD)

    def normal(pair, part):
        at = lanes_of(pair, part)
        merge(r.raw, r.mixed[0, :, at], r.mixed[1, :, at])
        return normal_heads(r.raw[...].astype(full))

    def prepare(pair):
        scale = r.flat[pair, pl.ds(c, 1), :]
        r.queries[...] = low(normal(pair, 0)[0] * scale) * SCORE_SCALE
        r.keys[...] = low(normal(pair, 1)[0] * scale)
        at = lanes_of(pair, 2)
        merge(r.values, r.mixed[0, :, at], r.mixed[1, :, at])

    def of_heads(block):
        return jnp.concatenate([block * head_lanes(h, jnp.bfloat16) for h in range(2)])

    def attend(pair):
        @pl.when(early & (pair == 2))
        def _():
            relay(3)
            spread(5)

        prepare(pair)
        at = lanes_of(pair, 0)
        for q in range(4):
            upto = (q + 1) * 256
            query = of_heads(r.queries[q * 256 : upto])
            summed = 0.0
            for k in range(q + 1):
                at_keys = slice(k * 256, (k + 1) * 256)
                mask = jnp.concatenate([r.bias[q * 256 : upto, at_keys]] * 2)
                weighted = jnp.exp(last_dims(query, r.keys[at_keys]) + mask)
                summed = summed + dot(low(weighted), r.values[at_keys])
            total = summed[:, 2 * HEAD :]
            parts = summed[:, : 2 * HEAD] / total
            log_sum = jnp.log(row_sums(total, first)[:1])
            for h in range(2):
                r.log_sums[pair, h : h + 1, q * 256 : upto] = log_sum[:, h * 256 : (h + 1) * 256]
            joined = low(jnp.where(head_lanes(0, full) > 0, parts[:256], parts[256:]))
            r.att[0, q * BLOCK : (q + 1) * BLOCK, at] = joined[:BLOCK]
            r.att[1, q * BLOCK : (q + 1) * BLOCK, at] = joined[BLOCK:]

    every(4, attend)

    def exchange(index, product, to):
        send, recv = r.part_send.at[index], r.part_recv.at[index]

        def sent(n):
            at = columns(n)
            r.part[:, at] = low(product(1, n))
            remote(r.part.at[:, at], r.got.at[:, at], send.at[n], recv.at[n], sibling).start()

        def own(n):
            at = columns(n)
            to[:, at] = product(0, n) if to is not r.middle else to[:, at] + product(0, n)

        every(4, sent)
        every(4, own)
        for n in range(4):
            arrived(r.got.at[:, columns(n)], recv.at[n])

    def settle_sent(index):
        for n in range(4):
            arrived(r.part.at[:, columns(n)], r.part_send.at[index, n])

    def share_rows(array, index, b):
        @pl.when(b % 2 == 1)
        def _():
            rows = rows_of(b // 2)
            remote(
                array.at[0, rows], array.at[1, rows], r.mid_send.at[index, b // 2],
                r.mid_recv.at[index, b // 2], sibling,
            ).start()

    def shared(array, index):
        for b in range(4):
            arrived(array.at[1, rows_of(b)], r.mid_recv.at[index, b])

    def settle_shared(array, index):
        for b in range(4):
            arrived(array.at[0, rows_of(b)], r.mid_send.at[index, b])

    complete(2)
    exchange(
        0, lambda side, n: dot(r.att[side], r.wo[:, columns(n)]), r.branch,
    )

    def first_step(b):
        rows = pl.ds(b * 64, 64)
        total = r.branch[rows] + r.got[rows].astype(full)
        r.branch[rows] = total
        hidden = r.hid[0, rows].astype(full)
        stepped = unit(hidden + r.alpha_attn[...] * (unit(total) - hidden))
        r.middle[rows] = stepped
        r.mid[0, rows] = low(stepped)
        share_rows(r.mid, 0, b)

    every(8, first_step)

    @pl.when(early)
    def _():
        relay(4)

    complete(3)
    for side in range(2):
        if side:
            shared(r.mid, 0)

        def lift(n, side=side):
            at = pl.ds(lane(n * 512), 512)
            r.up[side, :, at] = low(dot(r.mid[side], r.wu[:, at]))

        every(4, lift)

    @pl.when(early)
    def _():
        relay(5)

    complete(4)
    for side in (1, 0):

        def open_gate(n, side=side):
            at = pl.ds(lane(n * 512), 512)
            gate = dot(r.mid[side], r.wg[:, at])
            r.gate[side, :, at] = low(gate)
            upward = r.up[side, :, at].astype(full) * r.scale_up[:, at]
            r.inner[side, :, at] = low(upward * silu(gate * r.scale_gate[:, at]))

        every(4, open_gate)

    complete(5)
    settle_sent(0)
    exchange(
        1, lambda side, n: dot(r.inner[side], r.wd[:, columns(n)]), r.output,
    )

    def second_step(b):
        rows = pl.ds(b * 64, 64)
        total = r.output[rows] + r.got[rows].astype(full)
        r.output[rows] = total
        start = r.middle[rows]
        r.result[rows] = low(unit(start + r.alpha_mlp[...] * (unit(total) - start)))

        @pl.when(early & (b % 2 == 1))
        def _():
            sent = rows_of(b // 2)
            remote(
                r.result.at[sent], r.hid.at[0, sent], r.result_send.at[b // 2],
                r.own_recv.at[b // 2], late_plane,
            ).start()

    every(8, second_step)

    def to_owners(array, held, to_ref):
        for to in range(4):
            src = held.at[rows_of(to)]
            dst = to_ref.at[s // 2, pl.ds(c * BLOCK, BLOCK)]
            recv = r.owner_recv.at[array, s // 2, c]
            here = (s == to) & (c == layer)

            @pl.when(here)
            def _():
                pltpu.make_async_copy(src, dst, r.owner_send.at[array, to]).start()

            @pl.when(jnp.logical_not(here))
            def _():
                remote(src, dst, r.owner_send.at[array, to], recv, (layer, to, f)).start()

    to_owners(0, r.result, o_hidden)

    for b in range(4):
        arrived(r.flags.at[b], r.flag_recv.at[b])
    r.flags_full[...] = r.flags[...].astype(full)
    ones = jnp.ones((8, width), jnp.bfloat16)
    for b in range(4):
        squares = row_sums(r.branch[rows_of(b)] * r.branch[rows_of(b)], ones)[:1]
        r.sum_valid[...] += squares * r.flags_full[b, pl.ds(c, 1), :]

    def near_of(k):
        return fx + (fy - fx) * (k % 2)

    def far_of(k):
        return fy + (fx - fy) * (k % 2)

    def with_source(k, work):
        @pl.when(k < 4)
        def _():
            at = pl.ds(lane((k % 2) * 512), 512)
            work(lambda to: g_down.at[pl.ds(to * 512 + (k // 2) * 256, 256), at])

        for begins, ref in ((4, g_up), (8, g_gate), (12, g_out), (13, g_qkv)):

            @pl.when((k >= begins) & (k < begins + ref.shape[1] // 512))
            def _():
                at = pl.ds(lane((k - begins) * 512), 512)
                work(lambda to: ref.at[pl.ds(to * 256, 256), at])

    def begin(k):
        def start(source):
            to = (c, s, near_of(k))
            remote(
                source(near_of(k)), near_own.at[k], r.send_own.at[k], r.recv_own.at[k], to
            ).start()
            remote(source(3 - f), near_far.at[k], r.send_far.at[k], r.recv_far.at[k], to).start()

        with_source(k, start)

    places = {
        "pass": (r.wu, 0, 4), "own": (r.wu, 4, 4), "pair": (r.wu, 8, 4), "far": (r.wu, 12, 2),
        "other": (r.wu, 14, 2), "late": (r.wg, 0, 4), "near": (r.wg, 4, 2), "last": (r.wg, 6, 2),
        "side": (r.wg, 8, 2),
    }
    order = list(places)

    def slot(name, k):
        ref, base, count = places[name]
        n = base + k % count
        return ref.at[pl.ds(n // 4 * 256, 256), pl.ds(lane(n % 4 * 512), 512)]

    def load_sem(name, k):
        return r.load.at[order.index(name), k % places[name][2]]

    def fetch(src, name, k):
        pltpu.make_async_copy(src, slot(name, k), load_sem(name, k)).start()

    def fetched(name, k):
        arrived(slot(name, k), load_sem(name, k))

    def again(k, work):
        pl.when(k >= 4)(work)

    def pass_load(k):
        arrived(near_far.at[k], r.recv_far.at[k])

        again(k, lambda: arrived(slot("pass", k), r.send_next.at[k - 4]))
        with_source(k, lambda source: fetch(source(far_of(k)), "pass", k))
        fetch(near_far.at[k], "far", k)

    def pass_send(k):
        fetched("pass", k)
        fetched("far", k)
        total = slot("pass", k)
        add(total, total, slot("far", k))
        remote(
            total, far_in.at[k], r.send_next.at[k], r.recv_next.at[k], (c, s, far_of(k))
        ).start()

    def plane_load(k):
        arrived(near_own.at[k], r.recv_own.at[k])
        arrived(far_in.at[k], r.recv_next.at[k])

        again(k, lambda: arrived(slot("own", k), r.send_z.at[k - 4]))
        with_source(k, lambda source: fetch(source(f), "own", k))
        fetch(near_own.at[k], "near", k)
        fetch(far_in.at[k], "last", k)

    def plane_send(k):
        for name in ("own", "near", "last"):
            fetched(name, k)
        own, send = slot("own", k), r.send_z.at[k]
        add(own, own, slot("near", k), slot("last", k))
        pltpu.make_async_copy(own, plane_sum.at[k], r.stored.at[k]).start()

        @pl.when(s == 0)
        def _():
            remote(own, from_left.at[k], send, r.recv_left.at[k], (c, 1, f)).start()

        @pl.when(s == 3)
        def _():
            remote(own, from_right.at[k], send, r.recv_right.at[k], (c, 2, f)).start()

        @pl.when(early)
        def _():
            remote(own, pair_sum.at[k], send, r.recv_pair.at[k], (c, 3 - s, f)).start()

    def plane_done(k):
        arrived(plane_sum.at[k], r.stored.at[k])

    def in_plane(t, least, most, slack):
        for lag, work in (
            (0, pass_load), (1, pass_send), (5 + slack, plane_done), (3 + slack, plane_load),
            (4 + slack, plane_send),
        ):
            @pl.when((t >= lag + least) & (t < lag + most))
            def _():
                work(t - lag)

    def relay_on(k):
        @pl.when(s == 1)
        def _():
            arrived(from_left.at[k], r.recv_left.at[k])
            remote(
                from_left.at[k], from_left.at[k], r.send_on.at[k], r.recv_left.at[k], (c, 2, f)
            ).start()

        @pl.when(s == 2)
        def _():
            arrived(from_right.at[k], r.recv_right.at[k])
            remote(
                from_right.at[k], from_right.at[k], r.send_on.at[k], r.recv_right.at[k], (c, 1, f)
            ).start()

    def relay_out(k):
        @pl.when(s == 1)
        def _():
            arrived(from_right.at[k], r.recv_right.at[k])
            remote(
                from_right.at[k], from_right.at[k], r.send_back.at[k], r.recv_right.at[k], (c, 0, f)
            ).start()

        @pl.when(s == 2)
        def _():
            arrived(from_left.at[k], r.recv_left.at[k])
            remote(
                from_left.at[k], from_left.at[k], r.send_back.at[k], r.recv_left.at[k], (c, 3, f)
            ).start()

    def everything(chunk):
        return chunk

    def place(k, owner, chunk):
        def put(pieces):
            for src, dst in pieces:

                @pl.when(c == owner)
                def _():
                    pltpu.make_async_copy(src(chunk), dst, r.keep.at[k]).start()

                @pl.when(c != owner)
                def _():
                    remote(src(chunk), dst, r.give.at[k], r.given.at[k], sibling).start()

        @pl.when(k < 4)
        def _():
            rows = pl.ds(c * 512 + (k // 2) * 256, 256)
            put([(everything, o_down.at[rows, pl.ds(lane((k % 2) * 512), 512)])])

        @pl.when((k >= 4) & (k < 12))
        def _():
            put([(everything, o_in.at[:, pl.ds(lane((k - 4) * 1024 + c * 512), 512)])])

        @pl.when(k == 12)
        def _():
            put([
                (
                    lambda chunk, part=part: chunk.at[pl.ds(part * 128, 128)],
                    o_out.at[pl.ds(c * 128, 128), pl.ds(part * 512, 512)],
                )
                for part in range(2)
            ])

        @pl.when(k > 12)
        def _():
            put([
                (
                    lambda chunk, part=part: chunk.at[:, pl.ds(part * 128, 128)],
                    o_qkv.at[:, pl.ds(lane((k - 13) * 1024 + part * 256 + c * 128), 128)],
                )
                for part in range(4)
            ])

    def placed(k, owner):
        @pl.when(c == owner)
        def _():
            arrived(plane_sum.at[k], r.keep.at[k])

        @pl.when(c != owner)
        def _():
            arrived(plane_sum.at[k], r.give.at[k])

    def pair_load(k):
        @pl.when(early)
        def _():
            arrived(pair_sum.at[k], r.recv_pair.at[k])

            @pl.when(k >= 4)
            def _():
                arrived(slot("pair", k), r.send_out.at[k - 4])
                placed(k - 4, 0)

            fetch(plane_sum.at[k], "pair", k)
            fetch(pair_sum.at[k], "other", k)

    def pair_send(k):
        @pl.when(early)
        def _():
            fetched("pair", k)
            fetched("other", k)
            total = slot("pair", k)
            add(total, total, slot("other", k))
            remote(total, pair_sum.at[k], r.send_out.at[k], r.recv_pair.at[k], late_plane).start()
            place(k, 0, total)

    def pair_take(k):
        @pl.when(late)
        def _():
            arrived(pair_sum.at[k], r.recv_pair.at[k])
            place(k, 0, pair_sum.at[k])

    def late_load(k):
        again(k, lambda: placed(k - 4, 1))

        @pl.when(early)
        def _():
            fetch(from_left.at[k], "late", k)
            fetch(from_right.at[k], "side", k)

        @pl.when(s == 0)
        def _():
            arrived(from_right.at[k], r.recv_right.at[k])
            fetch(from_right.at[k], "side", k)

        @pl.when(s == 3)
        def _():
            arrived(from_left.at[k], r.recv_left.at[k])
            fetch(from_left.at[k], "side", k)

        @pl.when(late)
        def _():
            fetch(plane_sum.at[k], "late", k)

    def late_place(k):
        fetched("late", k)
        fetched("side", k)
        total = slot("late", k)
        add(total, total, slot("side", k))
        place(k, 1, total)

    def between_planes(t):
        @pl.when(early)
        def _():
            for lag, work in ((1, relay_on), (3, relay_out)):
                @pl.when((t >= lag + READY) & (t < lag + CHUNKS))
                def _():
                    work(t - lag)

        for lag, work, least, most in (
            (4, pair_load, 0, READY), (5, pair_send, 0, READY), (8, pair_load, READY, CHUNKS),
            (9, pair_send, READY, CHUNKS), (18, pair_take, 0, CHUNKS),
            (6 + 8 * layer, late_load, 0, CHUNKS), (7 + 8 * layer, late_place, 0, CHUNKS),
        ):
            @pl.when((t >= lag + least) & (t < lag + most))
            def _():
                work(t - lag)

    def weight_grad(count, tile, width_of, pieces):
        def stage(n):
            return r.wd.at[pl.ds((n % 2) * 256, 256), pl.ds(0, width_of)]

        def work(n):
            @pl.when(n >= 2)
            def _():
                arrived(stage(n), r.staged.at[n % 2])

            left, right = tile(n)
            total = contract_rows(left(0), right(0)) + contract_rows(left(1), right(1))
            stage(n)[...] = low(total)
            for src, dst in pieces(n, stage(n)):
                pltpu.make_async_copy(src, dst, r.staged.at[n % 2]).start()

        every(count, work)
        for n in range(count - 2, count):
            arrived(stage(n), r.staged.at[n % 2])

    def grad_of_down():
        weight_grad(
            8,
            lambda n: (lambda side: r.inner[side, :, columns(n)], lambda side: r.grad_rows[side]),
            width,
            lambda n, src: [(src, g_down.at[pl.ds(n * 256, 256)])],
        )

    def grad_of_lift(ref, to):
        weight_grad(
            8,
            lambda n: (
                lambda side: r.mid[side, :, columns(n // 2)],
                lambda side: ref[side, :, pl.ds(lane((n % 2) * 1024), 1024)],
            ),
            1024,
            lambda n, src: [
                (src, to.at[pl.ds((n // 2) * 256, 256), pl.ds(lane((n % 2) * 1024), 1024)])
            ],
        )

    def grad_of_out():
        weight_grad(
            2,
            lambda n: (lambda side: r.att[side, :, columns(n)], lambda side: r.grad_rows[side]),
            width,
            lambda n, src: [
                (
                    src.at[pl.ds(owner * 128, 128), pl.ds(part * 512, 512)],
                    g_out.at[pl.ds(n * 512 + owner * 256 + part * 128, 128)],
                )
                for owner in range(2)
                for part in range(2)
            ],
        )

    def grad_of_qkv():
        weight_grad(
            12,
            lambda n: (
                lambda side: r.hid[side, :, columns(n // 3)],
                lambda side: r.mixed[side, :, pl.ds(lane((n % 3) * 512), 512)],
            ),
            512,
            lambda n, src: [
                (src, g_qkv.at[pl.ds((n // 3) * 256, 256), pl.ds(lane((n % 3) * 512), 512)])
            ],
        )

    fits = (place_col >= start_row[...]) & (place_col <= place_row[...])
    r.bias[...] = jnp.where(fits, 0.0, MASKED)
    for item in range(6):
        for part in range(2):
            arrived(part_of(item, f, part), r.next_send.at[item, part])

    @pl.when(early)
    def _():
        for k in range(2):
            relay_on(k)

    def second_back(b):
        rows = pl.ds(b * 64, 64)

        @pl.when(b % 2 == 0)
        def _():
            arrived(r.grad_in.at[rows_of(b // 2)], r.grad_recv.at[b // 2])

        start = r.hid[0, rows].astype(full)
        middle = unit(start + r.alpha_attn[...] * (unit(r.branch[rows]) - start))
        total = r.output[rows]
        change = unit(total) - middle
        grad = unit_back(middle + r.alpha_mlp[...] * change, r.grad_in[rows].astype(full))
        r.sum_alphas[1:2] += jnp.sum(grad * change, axis=0, keepdims=True)
        r.grad_rows[0, rows] = low(unit_back(total, r.alpha_mlp[...] * grad))
        r.middle[rows] = grad * (1.0 - r.alpha_mlp[...])
        share_rows(r.grad_rows, 1, b)

    every(8, second_back)

    for side in range(2):
        if side:
            shared(r.grad_rows, 1)

        def close_gate(n, side=side):
            at = pl.ds(lane(n * 512), 512)
            grad = last_dims(r.grad_rows[side], r.wd[pl.ds(n * 512, 512)])
            lift_up = r.up[side, :, at].astype(full)
            lift_gate = r.gate[side, :, at].astype(full)
            gating = lift_gate * r.scale_gate[:, at]
            sigmoid = jax.nn.sigmoid(gating)
            grad_up = grad * (gating * sigmoid)
            grad_gate = (
                grad * (lift_up * r.scale_up[:, at]) * sigmoid * (1.0 + gating * (1.0 - sigmoid))
            )
            r.sum_scales[0:1, at] += jnp.sum(grad_up * lift_up, axis=0, keepdims=True)
            r.sum_scales[1:2, at] += jnp.sum(grad_gate * lift_gate, axis=0, keepdims=True)
            r.up[side, :, at] = low(grad_up * r.scale_up[:, at])
            r.gate[side, :, at] = low(grad_gate * r.scale_gate[:, at])

        every(4, close_gate)
    grad_of_down()
    for k in range(READY):
        begin(k)

    def lifted(side, n):
        rows = pl.ds(n * 256, 256)
        return last_dims(r.up[side], r.wu[rows]) + last_dims(r.gate[side], r.wg[rows])

    settle_sent(1)
    exchange(2, lifted, r.middle)
    in_plane(0, 0, READY, 0)
    settle_shared(r.grad_rows, 1)

    def first_back(b):
        rows = pl.ds(b * 64, 64)
        start = r.hid[0, rows].astype(full)
        total = r.branch[rows]
        change = unit(total) - start
        grad = r.middle[rows] + r.got[rows].astype(full)
        grad = unit_back(start + r.alpha_attn[...] * change, grad)
        r.sum_alphas[0:1] += jnp.sum(grad * change, axis=0, keepdims=True)
        r.grad_rows[0, rows] = low(unit_back(total, r.alpha_attn[...] * grad))
        r.middle[rows] = grad * (1.0 - r.alpha_attn[...])
        share_rows(r.grad_rows, 2, b)

    every(8, first_back)

    @pl.when(early)
    def _():
        for k in range(2, READY):
            relay_on(k)

    shared(r.grad_rows, 2)
    in_plane(1, 0, READY, 0)

    marks = (
        lax.broadcasted_iota(jnp.int32, (8, 2 * HEAD), 1) // HEAD
        == lax.broadcasted_iota(jnp.int32, (8, 2 * HEAD), 0)
    ).astype(jnp.bfloat16)

    def attend_back(pair):
        in_plane(2 + pair, 0, READY, 0)

        @pl.when(early)
        def _():
            relay_out(pair)

        prepare(pair)
        at = lanes_of(pair, 0)
        heads = r.wo[pl.ds(pair * 128, 128)]
        merge(r.grads, *(low(last_dims(r.grad_rows[side], heads)) for side in range(2)))
        merge(r.raw, r.att[0, :, at], r.att[1, :, at])
        r.dk[...] = jnp.zeros_like(r.dk)
        r.dv[...] = jnp.zeros_like(r.dv)
        for q in range(4):
            at = slice(q * 256, (q + 1) * 256)
            upto = slice(0, (q + 1) * 256)
            deltas = row_sums(r.grads[at].astype(full) * r.raw[at].astype(full), marks)
            delta = jnp.concatenate([deltas[h : h + 1] for h in range(2)], axis=1)
            log_sum = jnp.concatenate([r.log_sums[pair, h : h + 1, at] for h in range(2)], axis=1)
            query, grad, key = of_heads(r.queries[at]), of_heads(r.grads[at]), r.keys[upto]
            mask = jnp.concatenate([r.bias[upto, at]] * 2, axis=1)
            weighted = jnp.exp(last_dims(key, query) + (mask - log_sum))
            grad_scores = low(
                weighted * (last_dims(r.values[upto, : 2 * HEAD], grad) - delta)
            )
            r.dv[upto] += dot(low(weighted), grad)
            r.dk[upto] += dot(grad_scores, query)
            to_queries = contract_rows(grad_scores, key)
            r.dq[at] = (
                head_lanes(0, full) * to_queries[:256] + head_lanes(1, full) * to_queries[256:]
            )

        scale = r.flat[pair, pl.ds(c, 1), :]
        scale_sum = 0.0
        for part, grad in enumerate((r.dq, r.dk)):
            normed, factor = normal(pair, part)
            found = grad[...] * SCORE_SCALE if part == 0 else grad[...]
            scale_sum = scale_sum + jnp.sum(found * normed, axis=0, keepdims=True)
            step = found * scale
            grad[...] = factor * (step - normed * sums_of_halves(normed * step))
        r.sum_qk[pl.ds(pair, 1)] = scale_sum
        for part, grad in enumerate((r.dq, r.dk, r.dv)):
            at = lanes_of(pair, part)
            for q in range(4):
                rows = slice(q * BLOCK, (q + 1) * BLOCK)
                r.mixed[0, rows, at] = low(grad[q * 256 : q * 256 + BLOCK])
                r.mixed[1, rows, at] = low(grad[q * 256 + BLOCK : (q + 1) * 256])

    every(4, attend_back)

    settle_sent(2)
    exchange(
        3, lambda side, n: last_dims(r.mixed[side], r.wq[pl.ds(n * 256, 256)]), r.middle,
    )

    for b in range(4):
        rows = rows_of(b)

        @pl.when(early)
        def _():
            arrived(r.result.at[rows], r.result_send.at[b])

        arrived(r.result.at[rows], r.owner_send.at[0, b])

    def finish(b):
        rows = rows_of(b)
        r.result[rows] = low(r.middle[rows] + r.got[rows].astype(full))

        @pl.when(late)
        def _():
            remote(
                r.result.at[rows], r.grad_in.at[rows], r.result_send.at[b], r.grad_recv.at[b],
                early_plane,
            ).start()

    every(4, finish)
    to_owners(1, r.result, o_grad)

    for owner in range(4):
        r.terms[owner, pl.ds(c, 1), :] = r.sum_qk[owner : owner + 1]
        for n in range(2):
            for j in range(4):
                at = slice((owner % 2 * 2 + n) * 512 + j * 128, (owner % 2 * 2 + n) * 512 + (j + 1) * 128)
                scale = math.sqrt(width) if owner // 2 else 1.0
                r.terms[owner, pl.ds(2 + n * 8 + j + c * 4, 1), :] = (
                    r.sum_scales[owner // 2 : owner // 2 + 1, at] * scale
                )
        for j in range(4):
            at = slice(owner % 2 * 512 + j * 128, owner % 2 * 512 + (j + 1) * 128)
            r.terms[owner, 18 + j : 19 + j, :] = r.sum_alphas[owner // 2 : owner // 2 + 1, at]
        r.terms[owner, 22:23, :] = r.sum_valid[...]
    flow = Flow((r.v0, r.v1, r.v2, r.v3, r.v4, r.v5, r.v6, r.v7), r.vector)
    flow.begin(lambda to: r.terms.at[to])

    every(3, lambda n: in_plane(6 + n, 0, READY, 0))
    grad_of_lift(r.up, g_up)
    for k in range(READY, READY + AHEAD):
        begin(k)

    def step(t):
        @pl.when(t == READY + 1)
        def _():
            grad_of_lift(r.gate, g_gate)

        @pl.when(t == READY + 5)
        def _():
            grad_of_out()
            grad_of_qkv()

        @pl.when(t + AHEAD < CHUNKS)
        def _():
            begin(t + AHEAD)

        in_plane(t, READY, CHUNKS, 2)
        between_planes(t)
        for at, work in (
            (READY + 2, flow.pass_on), (READY + 4, flow.finish_plane), (READY + 10, flow.middle_planes),
        ):
            pl.when(t == at)(work)

        @pl.when(t == READY + 14 + 14 * layer)
        def _():
            flow.all_planes(o_vectors.at[c])

    every(CHUNKS + 18 - READY, lambda n: step(n + READY))

    def settle(k):
        chunk = plane_sum.at[k]
        for sem in (r.send_own, r.send_far, r.given):
            arrived(chunk, sem.at[k])

        @pl.when(early)
        def _():
            arrived(chunk, r.send_on.at[k])
            arrived(chunk, r.send_back.at[k])

        @pl.when(k >= CHUNKS - 4)
        def _():
            arrived(chunk, r.send_next.at[k])
            arrived(chunk, r.send_z.at[k])
            placed(k, 1)

        @pl.when(early & (k >= CHUNKS - 4))
        def _():
            arrived(chunk, r.send_out.at[k])
            placed(k, 0)

        @pl.when(late)
        def _():
            placed(k, 0)

    every(CHUNKS, settle)
    flow.settle()
    settle_shared(r.mid, 0)
    settle_shared(r.grad_rows, 2)
    settle_sent(3)
    for b in range(4):
        rows = rows_of(b)
        arrived(r.hid.at[1, rows], r.oth_send.at[b])

        @pl.when(late)
        def _():
            arrived(r.result.at[rows], r.result_send.at[b])

        @pl.when(s != b)
        def _():
            arrived(o_row.at[rows], r.row_send.at[b])
            arrived(r.flags.at[b], r.flag_send.at[b])

        arrived(r.result.at[rows], r.owner_send.at[1, b])

    for array, to_ref in enumerate((o_hidden, o_grad)):
        for micro in range(2):
            for core in range(2):

                @pl.when(jnp.logical_not((c == layer) & (c == core) & (s // 2 == micro)))
                def _():
                    arrived(
                        to_ref.at[micro, pl.ds(core * BLOCK, BLOCK)],
                        r.owner_recv.at[array, micro, core],
                    )

    @pl.when(c == layer)
    def _():
        for item in range(6):
            for index in range(len(targets)):
                arrived(block(item, f), r.first_send.at[item, index])


def relay_all(w_qkv, w_out, w_in, w_down, vectors, valid, tokens, cotangent, places):
    width = w_out.shape[1]
    units = w_down.shape[0] * 4
    half = units // 2
    place, start = places

    def low_shape(*shape):
        return jax.ShapeDtypeStruct(shape, jnp.bfloat16)

    chunks = low_shape(CHUNKS, 256, 512)
    rows = low_shape(2, 2 * BLOCK, width)
    anywhere = pl.BlockSpec(memory_space=pl.ANY)
    near = pl.BlockSpec(memory_space=pltpu.VMEM)
    scratch = scratch_of(width, units, vectors.shape[0], valid.shape[1])
    out_shape = [
        low_shape(half // 2, width), low_shape(width // 4, 2 * units), low_shape(width // 4, width),
        low_shape(width // 4, 3 * width), jax.ShapeDtypeStruct((2, 24, 128), jnp.float32),
        rows, rows, low_shape(4 * BLOCK, width),
        low_shape(half, width), low_shape(width, half), low_shape(width, half),
        low_shape(width, width // 2), low_shape(width, 3 * width // 2),
    ] + [chunks] * 7
    return pl.pallas_call(
        functools.partial(relay_kernel, tuple(scratch)),
        out_shape=out_shape,
        in_specs=[anywhere] * 8 + [near] * 3,
        out_specs=[anywhere] * len(out_shape),
        scratch_shapes=list(scratch.values()),
        compiler_params=pltpu.CompilerParams(
            collective_id=0, has_side_effects=True, vmem_limit_bytes=62 * 2**20
        ),
    )(
        w_qkv, w_out, w_in, w_down, vectors, valid, tokens, cotangent,
        start[:, None], place[None, :], start[None, :],
    )[:7]


def per_device(
    tokens, cotangent, lengths, valid_mask, w_qkv, w_out, w_in, w_down, qk_scale, mlp_scale, alphas
):
    c, s, f, _, _, layer = position()
    second = layer == 1
    micro = s // 2
    width = tokens.shape[3]
    group = tokens.shape[2]
    units = w_down.shape[1] * 4

    vectors = jnp.concatenate([qk_scale[0], mlp_scale[0], alphas[0]])
    vectors = jnp.pad(vectors, (0, 32 * 128 - vectors.shape[0])).reshape(32, 128)
    valid = low(jnp.pad(valid_mask[:, 0], ((0, 0), (0, 16 * 128 - group)))).reshape(2, 16, 128)
    index = jnp.arange(4 * group, dtype=jnp.int32)
    place = (index // 256) * 256 + (((index // BLOCK) + c) % 2) * BLOCK + index % BLOCK
    ends = jnp.cumsum(pick(lengths, micro, 0)[0])[:-1]
    passed = place[:, None] >= ends[None, :]
    start = jnp.max(jnp.where(passed, ends[None, :], 0), axis=1)
    places = (place, start)
    grad_down, grad_in_proj, grad_out, grad_qkv, vectors, hidden_out, grad_in = relay_all(
        w_qkv[0], w_out[0], w_in[0], w_down[0], vectors, valid, tokens[:, 0], cotangent[:, 0], places
    )
    cut_qk, cut_mlp = qk_scale.shape[1], qk_scale.shape[1] + mlp_scale.shape[1]
    full = jnp.sum(vectors, axis=0).reshape(-1)
    cuts = (cut_qk, cut_mlp, cut_mlp + alphas.shape[1])
    grad_qk_scale = full[: cuts[0]][None]
    grad_mlp_scale = full[cuts[0] : cuts[1]][None]
    grad_alphas = full[cuts[1] : cuts[2]][None]
    token_count = tokens.shape[0] * lax.axis_size("fsdp") * 4 * group
    total = jnp.sum(full[cuts[2] : cuts[2] + 128], keepdims=True)
    rms_stats = jnp.sqrt(total / token_count + epsilon)
    as_float = [
        part.astype(jnp.float32)[None] for part in (grad_qkv, grad_out, grad_in_proj, grad_down)
    ]
    return (
        hidden_out[None, :, None], grad_in.astype(jnp.float32)[None, :, None], *as_float,
        grad_qk_scale, grad_mlp_scale, grad_alphas, rms_stats,
    )


def solution(mesh):
    placed = (
        P(None, "fsdp", "seq", None),
        P(None, "fsdp", "seq", None),
        P(None, "fsdp", None),
        P(None, "fsdp", "seq"),
        P("section", "fsdp", None),
        P("section", "fsdp", None),
        P("section", "fsdp", None),
        P("section", "fsdp", None),
        P("section", "fsdp"),
        P("section", "fsdp"),
        P("section", "fsdp"),
    )
    planes = mesh.shape["section"] == 2 and mesh.shape["seq"] == 4 and mesh.shape["fsdp"] == 4
    return jax.shard_map(
        per_device if planes else per_device_general,
        mesh=mesh,
        in_specs=placed,
        out_specs=(
            P("section", None, "fsdp", "seq", None),
            P("section", None, "fsdp", "seq", None),
            P("section", "fsdp", None),
            P("section", "fsdp", None),
            P("section", "fsdp", None),
            P("section", "fsdp", None),
            P("section", "fsdp"),
            P("section", "fsdp"),
            P("section", "fsdp"),
            P("section"),
        ),
        check_vma=False,
    )
```

```python
import functools
import math
import types

import jax
import jax.numpy as jnp
from jax import lax
from jax.experimental import pallas as pl
from jax.experimental.pallas import tpu as pltpu
from jax.sharding import PartitionSpec as P

HEAD = 64


epsilon = 1e-06


def shifted(block, axis, distance):
    devices = range(lax.axis_size(axis))
    route = [(i - distance, i) for i in devices if i - distance in devices]
    return lax.ppermute(block, axis, route)


def for_sending(x):
    return jax.tree.map(lambda a: a.astype(jnp.bfloat16) if a.dtype == jnp.float32 else a, x)


def unit(values):
    return values * lax.rsqrt(jnp.sum(values * values, axis=-1, keepdims=True) + epsilon)


def unit_back(values, grad):
    factor = lax.rsqrt(jnp.sum(values * values, axis=-1, keepdims=True) + epsilon)
    normed = values * factor
    return factor * (grad - normed * jnp.sum(normed * grad, axis=-1, keepdims=True))


def contract_rows(left, right):
    return lax.dot_general(
        left, right, (((0,), (0,)), ((), ())), preferred_element_type=jnp.float32
    )


def contract_cols(left, right):
    return lax.dot_general(
        left, right, (((1,), (1,)), ((), ())), preferred_element_type=jnp.float32
    )


def segments_of(row_lengths, seq_len):
    ends = jnp.cumsum(row_lengths)[:-1]
    place = jnp.arange(seq_len, dtype=jnp.int32)
    return (place, jnp.sum((place[:, None] >= ends[None, :]).astype(jnp.int32), axis=1))


def allowed_pairs(row_lengths, offset, group, seq_len):
    key_place, key_segment = segments_of(row_lengths, seq_len)
    query_place = offset + jnp.arange(group, dtype=jnp.int32)
    query_segment = lax.dynamic_slice_in_dim(key_segment, offset, group)
    return (query_segment[:, None] == key_segment[None, :]) & (
        key_place[None, :] <= query_place[:, None]
    )


def masked_scores(queries, key_heads, allowed):
    scores = jnp.einsum(
        "qhd,khd->hqk", queries, key_heads, preferred_element_type=jnp.float32
    ) * math.sqrt(HEAD)
    return jnp.where(allowed[None], scores, -1e30)


def forward_layer(hidden_b, params, allowed, valid):
    w_qkv, w_out, w_in, w_down, qk_scale, mlp_scale, alphas = params
    count, width = hidden_b.shape
    heads = width // HEAD
    hidden = hidden_b.astype(jnp.float32)
    mixed = jnp.dot(hidden_b, w_qkv, preferred_element_type=jnp.float32)
    query_raw = mixed[:, :width].reshape(count, heads, HEAD)
    key_raw = mixed[:, width : 2 * width].reshape(count, heads, HEAD)
    head_scale = qk_scale.astype(jnp.float32).reshape(heads, HEAD)
    query_b = (unit(query_raw) * head_scale).astype(jnp.bfloat16)
    key_b = (unit(key_raw) * head_scale).astype(jnp.bfloat16).reshape(count, width)
    value_b = mixed[:, 2 * width :].astype(jnp.bfloat16)
    keys, values = (
        lax.all_gather(key_b, "seq", axis=0, tiled=True),
        lax.all_gather(value_b, "seq", axis=0, tiled=True),
    )
    key_heads = keys.reshape(-1, heads, HEAD)
    value_heads = values.reshape(-1, heads, HEAD)
    scores = masked_scores(query_b, key_heads, allowed)
    highest = jnp.max(scores, axis=-1, keepdims=True)
    weights = jnp.exp(scores - highest)
    denominator = jnp.sum(weights, axis=-1, keepdims=True)
    weights = weights / denominator
    log_total = highest + jnp.log(denominator)
    attended = jnp.einsum(
        "hqk,khd->qhd",
        weights.astype(jnp.bfloat16),
        value_heads,
        preferred_element_type=jnp.float32,
    )
    attended_b = attended.reshape(count, width).astype(jnp.bfloat16)
    branch = jnp.dot(attended_b, w_out, preferred_element_type=jnp.float32)
    statistic = jnp.sum(valid * jnp.sum(branch * branch, axis=-1))
    step_sizes = alphas.astype(jnp.float32)
    first_sum = hidden + step_sizes[:width] * (unit(branch) - hidden)
    middle = unit(first_sum)
    middle_b = middle.astype(jnp.bfloat16)
    lifted = jnp.dot(middle_b, w_in, preferred_element_type=jnp.float32)
    units_count = lifted.shape[1] // 2
    scales = mlp_scale.astype(jnp.float32)
    upward = lifted[:, :units_count] * scales[:units_count]
    gating = lifted[:, units_count:] * scales[units_count:] * math.sqrt(width)
    inner_b = (upward * jax.nn.silu(gating)).astype(jnp.bfloat16)
    output = jnp.dot(inner_b, w_down, preferred_element_type=jnp.float32)
    second_sum = middle + step_sizes[width:] * (unit(output) - middle)
    result = unit(second_sum).astype(jnp.bfloat16)
    kept = (
        hidden_b,
        query_raw,
        key_raw,
        query_b,
        keys,
        values,
        log_total,
        attended_b,
        branch,
        first_sum,
        middle_b,
        lifted,
        inner_b,
        output,
        second_sum,
    )
    return (result, kept, statistic)


def backward_layer(kept, params, grad_out, allowed):
    (
        hidden_b,
        query_raw,
        key_raw,
        query_b,
        keys,
        values,
        log_total,
        attended_b,
        branch,
        first_sum,
        middle_b,
        lifted,
        inner_b,
        output,
        second_sum,
    ) = kept
    w_qkv, w_out, w_in, w_down, qk_scale, mlp_scale, alphas = params
    count, width = hidden_b.shape
    heads = width // HEAD
    hidden = hidden_b.astype(jnp.float32)
    step_sizes = alphas.astype(jnp.float32)
    alpha_attn = step_sizes[:width]
    alpha_mlp = step_sizes[width:]
    middle = unit(first_sum)
    grad_second = unit_back(second_sum, grad_out)
    grad_alpha_mlp = jnp.sum(grad_second * (unit(output) - middle), axis=0)
    grad_output = unit_back(output, alpha_mlp * grad_second).astype(jnp.bfloat16)
    grad_middle = grad_second * (1.0 - alpha_mlp)
    grad_down = contract_rows(inner_b, grad_output)
    grad_inner = contract_cols(grad_output, w_down)
    units_count = lifted.shape[1] // 2
    scales = mlp_scale.astype(jnp.float32)
    root = math.sqrt(width)
    lift_up = lifted[:, :units_count]
    lift_gate = lifted[:, units_count:]
    upward = lift_up * scales[:units_count]
    gating = lift_gate * scales[units_count:] * root
    sigmoid = jax.nn.sigmoid(gating)
    grad_upward = grad_inner * jax.nn.silu(gating)
    grad_gating = grad_inner * upward * sigmoid * (1.0 + gating * (1.0 - sigmoid))
    grad_scale_mlp = jnp.concatenate(
        [jnp.sum(grad_upward * lift_up, axis=0), jnp.sum(grad_gating * root * lift_gate, axis=0)]
    )
    grad_lifted = jnp.concatenate(
        [grad_upward * scales[:units_count], grad_gating * root * scales[units_count:]], axis=1
    ).astype(jnp.bfloat16)
    grad_in_proj = contract_rows(middle_b, grad_lifted)
    grad_middle = grad_middle + contract_cols(grad_lifted, w_in)
    grad_first = unit_back(first_sum, grad_middle)
    grad_alpha_attn = jnp.sum(grad_first * (unit(branch) - hidden), axis=0)
    grad_branch = unit_back(branch, alpha_attn * grad_first).astype(jnp.bfloat16)
    grad_hidden = grad_first * (1.0 - alpha_attn)
    grad_out_proj = contract_rows(attended_b, grad_branch)
    grad_attended = (
        contract_cols(grad_branch, w_out).astype(jnp.bfloat16).reshape(count, heads, HEAD)
    )
    key_heads = keys.reshape(-1, heads, HEAD)
    value_heads = values.reshape(-1, heads, HEAD)
    scores = masked_scores(query_b, key_heads, allowed)
    weights = jnp.exp(scores - log_total)
    grad_weights = jnp.einsum(
        "qhd,khd->hqk", grad_attended, value_heads, preferred_element_type=jnp.float32
    )
    delta = jnp.sum(weights * grad_weights, axis=-1, keepdims=True)
    grad_scores = (weights * (grad_weights - delta)).astype(jnp.bfloat16)
    score_scale = math.sqrt(HEAD)
    grad_query = (
        jnp.einsum("hqk,khd->qhd", grad_scores, key_heads, preferred_element_type=jnp.float32)
        * score_scale
    )
    seq_len = keys.shape[0]
    grad_keys = (
        jnp.einsum("hqk,qhd->khd", grad_scores, query_b, preferred_element_type=jnp.float32)
        * score_scale
    )
    grad_values = jnp.einsum(
        "hqk,qhd->khd",
        weights.astype(jnp.bfloat16),
        grad_attended,
        preferred_element_type=jnp.float32,
    )
    grad_key_own, grad_value_own = (
        lax.psum_scatter(
            grad_keys.reshape(seq_len, width).astype(jnp.bfloat16),
            "seq",
            scatter_dimension=0,
            tiled=True,
        ).astype(jnp.float32),
        lax.psum_scatter(
            grad_values.reshape(seq_len, width).astype(jnp.bfloat16),
            "seq",
            scatter_dimension=0,
            tiled=True,
        ).astype(jnp.float32),
    )
    head_scale = qk_scale.astype(jnp.float32).reshape(heads, HEAD)
    grad_key_heads = grad_key_own.reshape(count, heads, HEAD)
    grad_scale_qk = (
        jnp.sum(grad_query * unit(query_raw), axis=0)
        + jnp.sum(grad_key_heads * unit(key_raw), axis=0)
    ).reshape(width)
    grad_query_raw = unit_back(query_raw, grad_query * head_scale).reshape(count, width)
    grad_key_raw = unit_back(key_raw, grad_key_heads * head_scale).reshape(count, width)
    grad_mixed = jnp.concatenate([grad_query_raw, grad_key_raw, grad_value_own], axis=1).astype(
        jnp.bfloat16
    )
    grad_qkv = contract_rows(hidden_b, grad_mixed)
    grad_hidden = grad_hidden + contract_cols(grad_mixed, w_qkv)
    grad_step_sizes = jnp.concatenate([grad_alpha_attn, grad_alpha_mlp])
    grads = (
        grad_qkv,
        grad_out_proj,
        grad_in_proj,
        grad_down,
        grad_scale_qk,
        grad_scale_mlp,
        grad_step_sizes,
    )
    return (grad_hidden, grads)


def per_device_general(
    tokens, cotangent, lengths, valid_mask, w_qkv, w_out, w_in, w_down, qk_scale, mlp_scale, alphas
):
    shards = (w_qkv, w_out, w_in, w_down, qk_scale, mlp_scale, alphas)
    gathered = (
        lax.all_gather(shards[0], "fsdp", axis=1, tiled=True),
        lax.all_gather(shards[1], "fsdp", axis=1, tiled=True),
        lax.all_gather(shards[2], "fsdp", axis=1, tiled=True),
        lax.all_gather(shards[3], "fsdp", axis=1, tiled=True),
        lax.all_gather(shards[4], "fsdp", axis=1, tiled=True),
        lax.all_gather(shards[5], "fsdp", axis=1, tiled=True),
        lax.all_gather(shards[6], "fsdp", axis=1, tiled=True),
    )
    params = tuple((piece[0] for piece in gathered))
    section = lax.axis_index("section")
    micro = tokens.shape[0]
    group = tokens.shape[2]
    width = tokens.shape[3]
    seq_len = group * lax.axis_size("seq")
    offset = lax.axis_index("seq") * group

    def fetch(array, index):
        return lax.dynamic_index_in_dim(array, index, 0, keepdims=False)[0]

    def forward_step(carry, step):
        incoming, stat_sum = carry
        index = step - section
        active = (index >= 0) & (index < micro)
        chosen = jnp.clip(index, 0, micro - 1)
        hidden_in = jnp.where(section == 0, fetch(tokens, chosen), incoming)
        allowed = allowed_pairs(fetch(lengths, chosen), offset, group, seq_len)
        valid = fetch(valid_mask, chosen).astype(jnp.float32)
        result, kept, statistic = forward_layer(hidden_in, params, allowed, valid)
        outgoing = shifted(result, "section", 1)
        stat_sum = stat_sum + jnp.where(active, statistic, 0.0)
        return ((outgoing, stat_sum), (result, kept))

    step_list = jnp.arange(micro + 1, dtype=jnp.int32)
    start = (jnp.zeros((group, width), jnp.bfloat16), jnp.zeros((), jnp.float32))
    (unused_fwd, stat_sum), (results, kept_all) = lax.scan(forward_step, start, step_list)
    late_shards, stat_sum = lax.optimization_barrier((shards, stat_sum))
    again = (
        lax.all_gather(late_shards[0], "fsdp", axis=1, tiled=True),
        lax.all_gather(late_shards[1], "fsdp", axis=1, tiled=True),
        lax.all_gather(late_shards[2], "fsdp", axis=1, tiled=True),
        lax.all_gather(late_shards[3], "fsdp", axis=1, tiled=True),
        lax.all_gather(late_shards[4], "fsdp", axis=1, tiled=True),
        lax.all_gather(late_shards[5], "fsdp", axis=1, tiled=True),
        lax.all_gather(late_shards[6], "fsdp", axis=1, tiled=True),
    )
    params_back = tuple((piece[0] for piece in again))

    def backward_step(carry, step):
        incoming, sums = carry
        index = step - 1 + section
        active = (index >= 0) & (index < micro)
        chosen = jnp.clip(index, 0, micro - 1)
        position = chosen + section

        def take(array):
            return lax.dynamic_index_in_dim(array, position, 0, keepdims=False)

        kept = jax.tree.map(take, kept_all)
        grad_out = jnp.where(
            section == 1, fetch(cotangent, chosen).astype(jnp.float32), incoming.astype(jnp.float32)
        )
        grad_out = jnp.where(active, grad_out, 0.0)
        row_lengths = fetch(lengths, chosen)
        allowed = allowed_pairs(row_lengths, offset, group, seq_len)
        grad_hidden, grads = backward_layer(kept, params_back, grad_out, allowed)
        outgoing = shifted(grad_hidden.astype(jnp.bfloat16), "section", -1)
        sums = tuple((total + piece for total, piece in zip(sums, grads)))
        return ((outgoing, sums), grad_hidden)

    zeros = tuple((jnp.zeros(piece.shape, jnp.float32) for piece in params_back))
    (unused_back, sums), grad_steps = lax.scan(
        backward_step, (jnp.zeros((group, width), jnp.bfloat16), zeros), step_list
    )
    hidden_out = lax.dynamic_slice_in_dim(results, section, micro, 0).reshape(
        1, micro, 1, group, width
    )
    grad_in = lax.dynamic_slice_in_dim(grad_steps, 1 - section, micro, 0).reshape(
        1, micro, 1, group, width
    )
    shard_sums = jax.tree.map(
        lambda part: part.astype(jnp.float32),
        lax.psum_scatter(for_sending(sums), "fsdp", scatter_dimension=0, tiled=True),
    )
    reduced = jax.tree.map(
        lambda part: part.astype(jnp.float32), lax.psum(for_sending(shard_sums), "seq")
    )
    total_stat = lax.psum(stat_sum, ("seq", "fsdp"))
    token_count = micro * lax.axis_size("fsdp") * seq_len
    rms_stats = jnp.sqrt(total_stat / token_count + epsilon).reshape(1)
    return (
        hidden_out,
        grad_in,
        reduced[0][None],
        reduced[1][None],
        reduced[2][None],
        reduced[3][None],
        reduced[4][None],
        reduced[5][None],
        reduced[6][None],
        rms_stats,
    )


BLOCK = 128
SCORE_SCALE = math.sqrt(HEAD)
MASKED = -1e30


def dot(left, right):
    return jnp.dot(left, right, preferred_element_type=jnp.float32)


def low(x):
    return x.astype(jnp.bfloat16)


def pick(x, index, axis):
    return lax.dynamic_index_in_dim(x, index, axis, keepdims=False)


def sums_of_halves(x):
    row = lax.broadcasted_iota(jnp.int32, (2 * HEAD, 2 * HEAD), 0) // HEAD
    col = lax.broadcasted_iota(jnp.int32, (2 * HEAD, 2 * HEAD), 1) // HEAD
    same = (row == col).astype(jnp.bfloat16)
    high = x.astype(jnp.bfloat16)
    rest = (x - high.astype(jnp.float32)).astype(jnp.bfloat16)
    return dot(high, same) + dot(rest, same)


def normal_heads(raw):
    factor = lax.rsqrt(sums_of_halves(raw * raw) + epsilon)
    return raw * factor, factor


def merge(to, own, oth):
    for s in range(4):
        to[s * 256 : s * 256 + BLOCK, : own.shape[1]] = own[s * BLOCK : (s + 1) * BLOCK]
        to[s * 256 + BLOCK : (s + 1) * 256, : own.shape[1]] = oth[s * BLOCK : (s + 1) * BLOCK]


def last_dims(left, right):
    return lax.dot_general(left, right, (((1,), (1,)), ((), ())), preferred_element_type=jnp.float32)


def head_lanes(h, dtype):
    lane = lax.broadcasted_iota(jnp.int32, (1, 2 * HEAD), 1) // HEAD
    return (lane == h).astype(dtype)


MESH = pl.DeviceIdType.MESH


def position():
    c, s, f = (lax.axis_index(name) for name in ("section", "seq", "fsdp"))
    x, y = f % 2, f // 2
    layer = 1 - ((s + 1) // 2) % 2
    return c, s, f, y * 2 + 1 - x, (1 - y) * 2 + x, layer


def greet(devices):
    barrier = pltpu.get_barrier_semaphore()
    for device in devices:
        pl.semaphore_signal(barrier, inc=1, device_id=device, device_id_type=MESH)
    pl.semaphore_wait(barrier, len(devices))


def remote(src, dst, send, recv, device):
    return pltpu.make_async_remote_copy(
        src_ref=src, dst_ref=dst, send_sem=send, recv_sem=recv, device_id=device, device_id_type=MESH
    )


def arrived(ref, sem):
    pltpu.make_async_copy(ref, ref, sem).wait()


def lane(offset):
    return pl.multiple_of(offset, 128)


def every(count, work):
    def step(n, carry):
        work(n)
        return carry

    lax.fori_loop(0, count, step, 0)


def silu(x):
    return x * jax.nn.sigmoid(x)


def row_sums(x, lanes):
    high = low(x)
    rest = low(x - high.astype(jnp.float32))
    return last_dims(lanes, high) + last_dims(lanes, rest)


class Flow:
    def __init__(self, buffers, semaphores):
        (
            self.near_own, self.near_far, self.far_in, self.own, self.passing,
            self.from_left, self.from_right, self.pair_sum,
        ) = buffers
        (
            self.load_own, self.load_pass, self.send_own, self.recv_own, self.send_far,
            self.recv_far, self.send_next, self.recv_next, self.send_z, self.recv_left,
            self.recv_right, self.recv_pair, self.send_on, self.send_back, self.send_out,
            self.keep, self.give, self.given,
        ) = [semaphores.at[n] for n in range(VECTOR_SEMAPHORES)]
        self.place_of = position()

    def begin(self, source):
        c, s, f, fx, fy, _ = self.place_of
        to = (c, s, fx)
        remote(source(fx), self.near_own, self.send_own, self.recv_own, to).start()
        remote(source(3 - f), self.near_far, self.send_far, self.recv_far, to).start()
        pltpu.make_async_copy(source(fy), self.passing, self.load_pass).start()
        pltpu.make_async_copy(source(f), self.own, self.load_own).start()

    def pass_on(self):
        c, s, _, _, fy, _ = self.place_of
        arrived(self.passing, self.load_pass)
        arrived(self.near_far, self.recv_far)
        add(self.passing, self.passing, self.near_far)
        remote(self.passing, self.far_in, self.send_next, self.recv_next, (c, s, fy)).start()

    def finish_plane(self):
        c, s, f, _, _, _ = self.place_of
        own, send = self.own, self.send_z
        arrived(own, self.load_own)
        arrived(self.near_own, self.recv_own)
        arrived(self.far_in, self.recv_next)
        add(own, own, self.near_own, self.far_in)

        @pl.when(s == 0)
        def _():
            remote(own, self.from_left, send, self.recv_left, (c, 1, f)).start()

        @pl.when(s == 3)
        def _():
            remote(own, self.from_right, send, self.recv_right, (c, 2, f)).start()

        @pl.when((s == 1) | (s == 2))
        def _():
            remote(own, self.pair_sum, send, self.recv_pair, (c, 3 - s, f)).start()

    def middle_planes(self):
        c, s, f, _, _, _ = self.place_of
        left, right, pair = self.from_left, self.from_right, self.pair_sum

        @pl.when(s == 1)
        def _():
            arrived(left, self.recv_left)
            remote(left, left, self.send_on, self.recv_left, (c, 2, f)).start()

        @pl.when(s == 2)
        def _():
            arrived(right, self.recv_right)
            remote(right, right, self.send_on, self.recv_right, (c, 1, f)).start()

        @pl.when((s == 1) | (s == 2))
        def _():
            arrived(pair, self.recv_pair)
            arrived(pair, self.send_z)
            add(pair, pair, self.own)
            remote(pair, pair, self.send_out, self.recv_pair, (c, (s - 1) * 3, f)).start()

    def all_planes(self, dst):
        c, s, f, _, _, _ = self.place_of
        left, right, pair = self.from_left, self.from_right, self.pair_sum
        own, total = self.own, self.near_own

        @pl.when(s == 1)
        def _():
            arrived(right, self.recv_right)
            remote(right, right, self.send_back, self.recv_right, (c, 0, f)).start()

        @pl.when(s == 2)
        def _():
            arrived(left, self.recv_left)
            remote(left, left, self.send_back, self.recv_left, (c, 3, f)).start()

        @pl.when((s == 1) | (s == 2))
        def _():
            add(total, left, right)

        @pl.when(s == 0)
        def _():
            arrived(pair, self.recv_pair)
            arrived(right, self.recv_right)
            add(total, own, right)

        @pl.when(s == 3)
        def _():
            arrived(pair, self.recv_pair)
            arrived(left, self.recv_left)
            add(total, own, left)

        for owner, chunk in ((0, pair), (1, total)):

            @pl.when(c == owner)
            def _():
                pltpu.make_async_copy(chunk, dst, self.keep).start()

            @pl.when(c != owner)
            def _():
                remote(chunk, dst, self.give, self.given, (1 - c, s, f)).start()

    def settle(self):
        _, s, _, _, _, _ = self.place_of
        for sem in (
            self.send_own, self.send_far, self.send_next, self.keep, self.give, self.given
        ):
            arrived(self.own, sem)

        @pl.when((s == 1) | (s == 2))
        def _():
            for sem in (self.send_on, self.send_back, self.send_out):
                arrived(self.own, sem)

        @pl.when((s == 0) | (s == 3))
        def _():
            arrived(self.own, self.send_z)


def add(to, *refs):
    total = refs[0][...].astype(jnp.float32)
    for ref in refs[1:]:
        total = total + ref[...].astype(jnp.float32)
    to[...] = total.astype(to.dtype)


VECTOR_SEMAPHORES = 18
CHUNKS = 16
SHARED = (1, 2, 3, 4)
READY = 4
AHEAD = 3
INPUTS = 11
OUTPUTS = 19


def scratch_of(width, units, vector_rows, flag_rows):
    rows = 4 * BLOCK
    half = units // 2

    def low_vmem(*shape):
        return pltpu.VMEM(shape, jnp.bfloat16)

    def full_vmem(*shape):
        return pltpu.VMEM(shape, jnp.float32)

    def sems(*shape):
        return pltpu.SemaphoreType.DMA(shape)

    low_row, full_row, low_rows = low_vmem(rows, width), full_vmem(rows, width), low_vmem(2, rows, width)
    pair, pair_full = low_vmem(2 * rows, 2 * HEAD), full_vmem(2 * rows, 2 * HEAD)
    return dict(
        wq=low_vmem(width, 3 * width // 2), wo=low_vmem(width // 2, width),
        wu=low_vmem(width, half), wg=low_vmem(width, half), wd=low_vmem(half, width),
        vec=low_vmem(4, vector_rows, 128), flat=full_vmem(4, vector_rows, 128),
        flags=low_vmem(4, flag_rows, 128), flags_full=full_vmem(4, flag_rows, 128),
        scale_up=full_vmem(1, half), scale_gate=full_vmem(1, half),
        alpha_attn=full_vmem(1, width), alpha_mlp=full_vmem(1, width),
        hid=low_rows, mixed=low_vmem(2, rows, 3 * width // 2), att=low_vmem(2, rows, width // 2),
        mid=low_rows, up=low_vmem(2, rows, half), gate=low_vmem(2, rows, half),
        inner=low_vmem(2, rows, half), branch=full_row, middle=full_row, output=full_row,
        result=low_row, part=low_row, got=low_row,
        bias=full_vmem(2 * rows, 2 * rows), raw=pair, queries=pair, keys=pair,
        values=low_vmem(2 * rows, 4 * HEAD), grads=pair, dq=pair_full, dk=pair_full, dv=pair_full,
        log_sums=full_vmem(4, 2, 2 * rows),
        grad_in=low_row, grad_rows=low_rows,
        sum_alphas=full_vmem(2, width), sum_scales=full_vmem(2, half), sum_qk=full_vmem(4, 2 * HEAD),
        sum_valid=full_vmem(1, 128), terms=full_vmem(4, 24, 128),
        v0=full_vmem(24, 128), v1=full_vmem(24, 128), v2=full_vmem(24, 128), v3=full_vmem(24, 128),
        v4=full_vmem(24, 128), v5=full_vmem(24, 128), v6=full_vmem(24, 128), v7=full_vmem(24, 128),
        first_send=sems(6, 3), first_recv=sems(6, 3), next_send=sems(6, 2), next_recv=sems(6, 2),
        plane_send=sems(6, 3), plane_recv=sems(6, 3),
        row_send=sems(4), row_recv=sems(4), flag_send=sems(4), flag_recv=sems(4),
        own_recv=sems(4), oth_send=sems(4), oth_recv=sems(4),
        part_send=sems(4, 4), part_recv=sems(4, 4),
        mid_send=sems(3, 4), mid_recv=sems(3, 4), result_send=sems(4), grad_recv=sems(4),
        owner_send=sems(2, 4), owner_recv=sems(2, 2, 2),
        vector=sems(VECTOR_SEMAPHORES), staged=sems(2), load=sems(9, 4),
        send_own=sems(CHUNKS), recv_own=sems(CHUNKS), send_far=sems(CHUNKS), recv_far=sems(CHUNKS),
        send_next=sems(CHUNKS), recv_next=sems(CHUNKS), send_z=sems(CHUNKS), stored=sems(CHUNKS),
        recv_left=sems(CHUNKS), recv_right=sems(CHUNKS), recv_pair=sems(CHUNKS),
        send_on=sems(CHUNKS), send_back=sems(CHUNKS), send_out=sems(CHUNKS),
        keep=sems(CHUNKS), give=sems(CHUNKS), given=sems(CHUNKS),
    )


def relay_kernel(names, *refs):
    (
        w_qkv, w_out, w_in, w_down, vectors, valid, tokens, cotangent,
        start_col, place_row, start_row,
    ) = refs[:INPUTS]
    (
        o_down, o_in, o_out, o_qkv, o_vectors, o_hidden, o_grad, o_row,
        g_down, g_up, g_gate, g_out, g_qkv,
        near_own, near_far, far_in, from_left, from_right, pair_sum,
    ) = refs[INPUTS : INPUTS + OUTPUTS]
    plane_sum, *refs = refs[INPUTS + OUTPUTS :]
    r = types.SimpleNamespace(**dict(zip(names, refs)))
    c, s, f, fx, fy, layer = position()
    sibling = (1 - c, s, f)
    early, late = layer == 0, layer == 1
    late_plane = (c, (s - 1) * 3, f)
    early_plane = (c, s // 3 + 1, f)
    width = w_out.shape[1]
    full = jnp.float32
    greet(
        [sibling, (c, s, fx), (c, s, fy)]
        + [(core, (s + step) % 4, f) for core in (0, 1) for step in (1, 2, 3)]
    )

    def rows_of(b):
        return pl.ds(b * BLOCK, BLOCK)

    def columns(n):
        return pl.ds(lane(n * 256), 256)

    def send_row(to, held):
        src, dst = held.at[pl.ds(c * BLOCK, BLOCK)], o_row.at[rows_of(s)]
        flags, flags_to = valid.at[to // 2], r.flags.at[s]

        @pl.when(s == to)
        def _():
            pltpu.make_async_copy(src, dst, r.row_recv.at[s]).start()
            pltpu.make_async_copy(flags, flags_to, r.flag_recv.at[s]).start()

        @pl.when(s != to)
        def _():
            remote(src, dst, r.row_send.at[to], r.row_recv.at[s], (c, to, f)).start()
            remote(flags, flags_to, r.flag_send.at[to], r.flag_recv.at[s], (c, to, f)).start()

    send_row(1, tokens.at[0])
    send_row(2, tokens.at[1])

    def pieces(item, h):
        if item == 0:
            return [(vectors, r.vec.at[f])]
        if item == 1:
            return [
                (
                    w_qkv.at[:, pl.ds(lane(part * 256 + h * 128), 128)],
                    r.wq.at[pl.ds(f * 256, 256), pl.ds(part * 128, 128)],
                )
                for part in range(12)
            ]
        if item == 2:
            return [(w_out.at[pl.ds(h * 128, 128)], r.wo.at[pl.ds(f * 128, 128)])]
        if item in (3, 4):
            to = (r.wu, r.wg)[item - 3]
            return [
                (
                    w_in.at[:, pl.ds(lane((item - 3) * 4096 + part * 1024 + h * 512), 512)],
                    to.at[pl.ds(f * 256, 256), pl.ds(part * 512, 512)],
                )
                for part in range(4)
            ]
        return [(w_down.at[pl.ds(h * 512, 512)], r.wd.at[pl.ds(f * 512, 512)])]

    weights = (r.vec, r.wq, r.wo, r.wu, r.wg, r.wd)
    other_plane = (c, 3 - s, f)

    def quarter(item):
        return 0 if item == 0 else weights[item].shape[0] // 16

    def block(item, of):
        if item == 0:
            return r.vec.at[of]
        rows = weights[item].shape[0] // 4
        return weights[item].at[pl.ds(of * rows, rows)]

    def part_of(item, of, part):
        if item == 0:
            return r.vec.at[of, pl.ds(part * 16, 16)]
        rows = weights[item].shape[0] // 8
        return weights[item].at[pl.ds(of * 2 * rows + part * rows, rows)]

    def quarters(item, of, least, count):
        size = quarter(item)
        return weights[item].at[pl.ds(of * 4 * size + least * size, count * size)]

    @pl.when(c == layer)
    def _():
        for item in range(6):
            for src, dst in pieces(item, 1 - c):
                remote(
                    src, dst, r.first_send.at[item, 2], r.first_recv.at[item, 0], sibling
                ).start()
            for src, dst in pieces(item, c):
                pltpu.make_async_copy(src, dst, r.first_recv.at[item, 0]).start()

    ways = ((1, fx, fy), (2, fy, fx))

    def spread(*items):
        for item in items:
            arrived(block(item, f), r.first_recv.at[item, 0])

            def send(moved, item=item):
                for part, (came, to, _) in enumerate(ways):
                    remote(
                        moved, moved, r.first_send.at[item, part], r.first_recv.at[item, came],
                        (c, s, to),
                    ).start()

            if item in SHARED:

                @pl.when(early)
                def _():
                    send(quarters(item, f, s - 1, 3))

                @pl.when(late)
                def _():
                    send(block(item, f))
            else:
                send(block(item, f))

    def forward(moved, item, part, to):
        remote(moved, moved, r.next_send.at[item, part], r.next_recv.at[item, part], to).start()

    def share(moved, item, part):
        remote(
            moved, moved, r.plane_send.at[item, part], r.plane_recv.at[item, part], other_plane
        ).start()

    def relay(item):
        def halves():
            for part, (came, of, to) in enumerate(ways):
                arrived(block(item, of), r.first_recv.at[item, came])
                forward(part_of(item, of, part), item, part, (c, s, to))

        if item not in SHARED:
            halves()
        else:
            pl.when(late)(halves)

            @pl.when(early)
            def _():
                for part, (came, of, to) in enumerate(ways):
                    arrived(quarters(item, of, 0, 3), r.first_recv.at[item, came])
                    forward(quarters(item, of, (s - 1) * 2 + part, 1), item, part, (c, s, to))
                for part, (came, of, to) in enumerate(ways):
                    share(quarters(item, of, (s - 1) * 3, 1), item, part)

    def relay_across(item):
        @pl.when(early)
        def _():
            for part in range(2):
                arrived(quarters(item, 3 - f, (s - 1) * 2 + part, 1), r.next_recv.at[item, part])
            share(quarters(item, 3 - f, (s - 1) * 2, 2), item, 2)

    def complete(item):
        def halves():
            for part in range(2):
                arrived(part_of(item, 3 - f, part), r.next_recv.at[item, part])

        if item not in SHARED:
            halves()
        else:
            pl.when(late)(halves)

            @pl.when(early)
            def _():
                for part, of in ((0, fx), (1, fy)):
                    arrived(quarters(item, of, (2 - s) * 3, 1), r.plane_recv.at[item, part])
                arrived(quarters(item, 3 - f, (2 - s) * 2, 2), r.plane_recv.at[item, 2])

    def settle_relays():
        for item in range(6):

            def halves():
                for part in range(2):
                    arrived(part_of(item, f, part), r.next_send.at[item, part])

            if item not in SHARED:
                halves()
            else:
                pl.when(late)(halves)

                @pl.when(early)
                def _():
                    for part in range(2):
                        arrived(quarters(item, f, 0, 1), r.next_send.at[item, part])
                        arrived(quarters(item, f, 0, 1), r.plane_send.at[item, part])
                    arrived(quarters(item, f, 0, 2), r.plane_send.at[item, 2])

    def settle_spread():
        for item in range(6):

            def sent(moved, item=item):
                for part in range(2):
                    arrived(moved, r.first_send.at[item, part])

            if item in SHARED:
                pl.when(early)(lambda: sent(quarters(item, f, 0, 3)))
                pl.when(late)(lambda: sent(block(item, f)))
            else:
                sent(block(item, f))

        @pl.when(c == layer)
        def _():
            for item in range(6):
                arrived(block(item, f), r.first_send.at[item, 2])

    spread(0, 1, 2)
    index = lax.broadcasted_iota(jnp.int32, (8 * BLOCK, 1), 0)
    place_col = (index // 256) * 256 + (index // BLOCK + c) % 2 * BLOCK + index % BLOCK
    fits = (place_row[...] >= start_col[...]) & (place_row[...] <= place_col)
    r.bias[...] = jnp.where(fits, 0.0, MASKED)
    r.values[:, 2 * HEAD :] = jnp.ones_like(r.values[:, 2 * HEAD :])
    for sums in (r.sum_alphas, r.sum_scales, r.sum_valid, r.terms):
        sums[...] = jnp.zeros_like(sums)
    relay(0)
    relay(1)
    spread(3)
    relay(2)
    relay_across(1)

    def to_sibling(b, src):
        remote(src, r.hid.at[1, rows_of(b)], r.oth_send.at[b], r.oth_recv.at[b], sibling).start()

    @pl.when(early)
    def _():
        for b in range(4):
            held = o_row.at[rows_of(b)]
            arrived(held, r.row_recv.at[b])
            pltpu.make_async_copy(held, r.hid.at[0, rows_of(b)], r.own_recv.at[b]).start()
            to_sibling(b, held)
        for b in range(4):
            arrived(r.hid.at[0, rows_of(b)], r.own_recv.at[b])

    @pl.when(late)
    def _():
        spread(4)
        relay(3)
        spread(5)
        relay(4)
        relay(5)
        for b in range(4):
            arrived(r.hid.at[0, rows_of(b)], r.own_recv.at[b])
            to_sibling(b, r.hid.at[0, rows_of(b)])

    complete(0)
    r.flat[...] = r.vec[...].astype(full)
    for n in range(4):
        for j in range(4):
            at = slice(n * 512 + j * 128, n * 512 + (j + 1) * 128)
            row = pl.ds(2 + (n % 2) * 8 + j + c * 4, 1)
            r.scale_up[:, at] = r.flat[n // 2, row, :]
            r.scale_gate[:, at] = r.flat[2 + n // 2, row, :] * math.sqrt(width)
    for n in range(2):
        for j in range(4):
            at = slice(n * 512 + j * 128, n * 512 + (j + 1) * 128)
            r.alpha_attn[:, at] = r.flat[n, 18 + j : 19 + j, :]
            r.alpha_mlp[:, at] = r.flat[2 + n, 18 + j : 19 + j, :]

    complete(1)
    for side in range(2):
        if side:
            for b in range(4):
                arrived(r.hid.at[1, rows_of(b)], r.oth_recv.at[b])

        def mix(n, side=side):
            at = pl.ds(lane(n * 512), 512)
            r.mixed[side, :, at] = low(dot(r.hid[side], r.wq[:, at]))

        every(3, mix)

    first = (lax.broadcasted_iota(jnp.int32, (8, 2 * HEAD), 1) == 0).astype(jnp.bfloat16)

    def lanes_of(pair, part):
        return pl.ds(lane(part * (width // 2) + pair * 2 * HEAD), 2 * HEAD)

    def normal(pair, part):
        at = lanes_of(pair, part)
        merge(r.raw, r.mixed[0, :, at], r.mixed[1, :, at])
        return normal_heads(r.raw[...].astype(full))

    def prepare(pair):
        scale = r.flat[pair, pl.ds(c, 1), :]
        r.queries[...] = low(normal(pair, 0)[0] * scale) * SCORE_SCALE
        r.keys[...] = low(normal(pair, 1)[0] * scale)
        at = lanes_of(pair, 2)
        merge(r.values, r.mixed[0, :, at], r.mixed[1, :, at])

    def of_heads(block):
        return jnp.concatenate([block * head_lanes(h, jnp.bfloat16) for h in range(2)])

    def attend(pair):
        @pl.when(early & (pair == 0))
        def _():
            relay_across(2)
            spread(4)

        @pl.when(early & (pair == 2))
        def _():
            relay(3)

        @pl.when(early & (pair == 3))
        def _():
            spread(5)

        prepare(pair)
        at = lanes_of(pair, 0)
        for q in range(4):
            upto = (q + 1) * 256
            query = of_heads(r.queries[q * 256 : upto])
            summed = 0.0
            for k in range(q + 1):
                at_keys = slice(k * 256, (k + 1) * 256)
                mask = jnp.concatenate([r.bias[q * 256 : upto, at_keys]] * 2)
                weighted = jnp.exp(last_dims(query, r.keys[at_keys]) + mask)
                summed = summed + dot(low(weighted), r.values[at_keys])
            total = summed[:, 2 * HEAD :]
            parts = summed[:, : 2 * HEAD] / total
            log_sum = jnp.log(row_sums(total, first)[:1])
            for h in range(2):
                r.log_sums[pair, h : h + 1, q * 256 : upto] = log_sum[:, h * 256 : (h + 1) * 256]
            joined = low(jnp.where(head_lanes(0, full) > 0, parts[:256], parts[256:]))
            r.att[0, q * BLOCK : (q + 1) * BLOCK, at] = joined[:BLOCK]
            r.att[1, q * BLOCK : (q + 1) * BLOCK, at] = joined[BLOCK:]

    every(4, attend)

    def exchange(index, product, to):
        send, recv = r.part_send.at[index], r.part_recv.at[index]

        def sent(n):
            at = columns(n)
            r.part[:, at] = low(product(1, n))
            remote(r.part.at[:, at], r.got.at[:, at], send.at[n], recv.at[n], sibling).start()

        def own(n):
            at = columns(n)
            to[:, at] = product(0, n) if to is not r.middle else to[:, at] + product(0, n)

        every(4, sent)
        every(4, own)
        for n in range(4):
            arrived(r.got.at[:, columns(n)], recv.at[n])

    def settle_sent(index):
        for n in range(4):
            arrived(r.part.at[:, columns(n)], r.part_send.at[index, n])

    def share_rows(array, index, b):
        @pl.when(b % 2 == 1)
        def _():
            rows = rows_of(b // 2)
            remote(
                array.at[0, rows], array.at[1, rows], r.mid_send.at[index, b // 2],
                r.mid_recv.at[index, b // 2], sibling,
            ).start()

    def shared(array, index):
        for b in range(4):
            arrived(array.at[1, rows_of(b)], r.mid_recv.at[index, b])

    def settle_shared(array, index):
        for b in range(4):
            arrived(array.at[0, rows_of(b)], r.mid_send.at[index, b])

    complete(2)
    exchange(
        0, lambda side, n: dot(r.att[side], r.wo[:, columns(n)]), r.branch,
    )

    def first_step(b):
        rows = pl.ds(b * 64, 64)
        total = r.branch[rows] + r.got[rows].astype(full)
        r.branch[rows] = total
        hidden = r.hid[0, rows].astype(full)
        stepped = unit(hidden + r.alpha_attn[...] * (unit(total) - hidden))
        r.middle[rows] = stepped
        r.mid[0, rows] = low(stepped)
        share_rows(r.mid, 0, b)

    relay_across(3)
    send_row(0, cotangent.at[0])
    send_row(3, cotangent.at[1])
    every(8, first_step)

    @pl.when(early)
    def _():
        relay(4)

    complete(3)
    for side in range(2):
        if side:
            shared(r.mid, 0)

        def lift(n, side=side):
            at = pl.ds(lane(n * 512), 512)
            r.up[side, :, at] = low(dot(r.mid[side], r.wu[:, at]))

        every(4, lift)

    relay_across(4)

    @pl.when(early)
    def _():
        relay(5)

    complete(4)
    for side in (1, 0):

        def open_gate(n, side=side):
            at = pl.ds(lane(n * 512), 512)
            gate = dot(r.mid[side], r.wg[:, at])
            r.gate[side, :, at] = low(gate)
            upward = r.up[side, :, at].astype(full) * r.scale_up[:, at]
            r.inner[side, :, at] = low(upward * silu(gate * r.scale_gate[:, at]))

        every(4, open_gate)

    complete(5)
    settle_sent(0)
    exchange(
        1, lambda side, n: dot(r.inner[side], r.wd[:, columns(n)]), r.output,
    )

    def second_step(b):
        rows = pl.ds(b * 64, 64)
        total = r.output[rows] + r.got[rows].astype(full)
        r.output[rows] = total
        start = r.middle[rows]
        r.result[rows] = low(unit(start + r.alpha_mlp[...] * (unit(total) - start)))

        @pl.when(early & (b % 2 == 1))
        def _():
            sent = rows_of(b // 2)
            remote(
                r.result.at[sent], r.hid.at[0, sent], r.result_send.at[b // 2],
                r.own_recv.at[b // 2], late_plane,
            ).start()

    every(8, second_step)

    def to_owners(array, held, to_ref):
        for to in range(4):
            src = held.at[rows_of(to)]
            dst = to_ref.at[s // 2, pl.ds(c * BLOCK, BLOCK)]
            recv = r.owner_recv.at[array, s // 2, c]
            here = (s == to) & (c == layer)

            @pl.when(here)
            def _():
                pltpu.make_async_copy(src, dst, r.owner_send.at[array, to]).start()

            @pl.when(jnp.logical_not(here))
            def _():
                remote(src, dst, r.owner_send.at[array, to], recv, (layer, to, f)).start()

    to_owners(0, r.result, o_hidden)

    @pl.when(late)
    def _():
        for b in range(4):
            held = o_row.at[rows_of(b)]
            arrived(held, r.row_recv.at[b])
            pltpu.make_async_copy(held, r.grad_in.at[rows_of(b)], r.grad_recv.at[b]).start()

    for b in range(4):
        arrived(r.flags.at[b], r.flag_recv.at[b])
    r.flags_full[...] = r.flags[...].astype(full)
    ones = jnp.ones((8, width), jnp.bfloat16)
    for b in range(4):
        squares = row_sums(r.branch[rows_of(b)] * r.branch[rows_of(b)], ones)[:1]
        r.sum_valid[...] += squares * r.flags_full[b, pl.ds(c, 1), :]

    def near_of(k):
        return fx + (fy - fx) * (k % 2)

    def far_of(k):
        return fy + (fx - fy) * (k % 2)

    def with_source(k, work):
        @pl.when(k < 4)
        def _():
            at = pl.ds(lane((k % 2) * 512), 512)
            work(lambda to: g_down.at[pl.ds(to * 512 + (k // 2) * 256, 256), at])

        for begins, ref in ((4, g_up), (8, g_gate), (12, g_out), (13, g_qkv)):

            @pl.when((k >= begins) & (k < begins + ref.shape[1] // 512))
            def _():
                at = pl.ds(lane((k - begins) * 512), 512)
                work(lambda to: ref.at[pl.ds(to * 256, 256), at])

    def begin(k):
        def start(source):
            to = (c, s, near_of(k))
            remote(source(3 - f), near_far.at[k], r.send_far.at[k], r.recv_far.at[k], to).start()
            remote(
                source(near_of(k)), near_own.at[k], r.send_own.at[k], r.recv_own.at[k], to
            ).start()

        with_source(k, start)

    places = {
        "pass": (r.wu, 0, 4), "own": (r.wu, 4, 4), "pair": (r.wu, 8, 4), "far": (r.wu, 12, 2),
        "other": (r.wu, 14, 2), "late": (r.wg, 0, 4), "near": (r.wg, 4, 2), "last": (r.wg, 6, 2),
        "side": (r.wg, 8, 2),
    }
    order = list(places)

    def slot(name, k):
        ref, base, count = places[name]
        n = base + k % count
        return ref.at[pl.ds(n // 4 * 256, 256), pl.ds(lane(n % 4 * 512), 512)]

    def load_sem(name, k):
        return r.load.at[order.index(name), k % places[name][2]]

    def fetch(src, name, k):
        pltpu.make_async_copy(src, slot(name, k), load_sem(name, k)).start()

    def fetched(name, k):
        arrived(slot(name, k), load_sem(name, k))

    def again(k, work):
        pl.when(k >= 4)(work)

    def pass_load(k):
        arrived(near_far.at[k], r.recv_far.at[k])

        again(k, lambda: arrived(slot("pass", k), r.send_next.at[k - 4]))
        with_source(k, lambda source: fetch(source(far_of(k)), "pass", k))
        fetch(near_far.at[k], "far", k)

    def pass_send(k):
        fetched("pass", k)
        fetched("far", k)
        total = slot("pass", k)
        add(total, total, slot("far", k))
        remote(
            total, far_in.at[k], r.send_next.at[k], r.recv_next.at[k], (c, s, far_of(k))
        ).start()

    def plane_load(k):
        arrived(near_own.at[k], r.recv_own.at[k])
        arrived(far_in.at[k], r.recv_next.at[k])

        again(k, lambda: arrived(slot("own", k), r.send_z.at[k - 4]))
        with_source(k, lambda source: fetch(source(f), "own", k))
        fetch(near_own.at[k], "near", k)
        fetch(far_in.at[k], "last", k)

    def plane_send(k):
        for name in ("own", "near", "last"):
            fetched(name, k)
        own, send = slot("own", k), r.send_z.at[k]
        add(own, own, slot("near", k), slot("last", k))
        pltpu.make_async_copy(own, plane_sum.at[k], r.stored.at[k]).start()

        @pl.when(s == 0)
        def _():
            remote(own, from_left.at[k], send, r.recv_left.at[k], (c, 1, f)).start()

        @pl.when(s == 3)
        def _():
            remote(own, from_right.at[k], send, r.recv_right.at[k], (c, 2, f)).start()

        @pl.when(early)
        def _():
            remote(own, pair_sum.at[k], send, r.recv_pair.at[k], (c, 3 - s, f)).start()

    def plane_done(k):
        arrived(plane_sum.at[k], r.stored.at[k])

    def in_plane(t, least, most, slack):
        for lag, work in (
            (5 + slack, plane_done), (4 + slack, plane_send), (3 + slack, plane_load),
            (1, pass_send), (0, pass_load),
        ):
            @pl.when((t >= lag + least) & (t < lag + most))
            def _():
                work(t - lag)

    def relay_on(k):
        @pl.when(s == 1)
        def _():
            arrived(from_left.at[k], r.recv_left.at[k])
            remote(
                from_left.at[k], from_left.at[k], r.send_on.at[k], r.recv_left.at[k], (c, 2, f)
            ).start()

        @pl.when(s == 2)
        def _():
            arrived(from_right.at[k], r.recv_right.at[k])
            remote(
                from_right.at[k], from_right.at[k], r.send_on.at[k], r.recv_right.at[k], (c, 1, f)
            ).start()

    def relay_out(k):
        @pl.when(s == 1)
        def _():
            arrived(from_right.at[k], r.recv_right.at[k])
            remote(
                from_right.at[k], from_right.at[k], r.send_back.at[k], r.recv_right.at[k], (c, 0, f)
            ).start()

        @pl.when(s == 2)
        def _():
            arrived(from_left.at[k], r.recv_left.at[k])
            remote(
                from_left.at[k], from_left.at[k], r.send_back.at[k], r.recv_left.at[k], (c, 3, f)
            ).start()

    def everything(chunk):
        return chunk

    def place(k, owner, chunk):
        def put(pieces):
            for src, dst in pieces:

                @pl.when(c == owner)
                def _():
                    pltpu.make_async_copy(src(chunk), dst, r.keep.at[k]).start()

                @pl.when(c != owner)
                def _():
                    remote(src(chunk), dst, r.give.at[k], r.given.at[k], sibling).start()

        @pl.when(k < 4)
        def _():
            rows = pl.ds(c * 512 + (k // 2) * 256, 256)
            put([(everything, o_down.at[rows, pl.ds(lane((k % 2) * 512), 512)])])

        @pl.when((k >= 4) & (k < 12))
        def _():
            put([(everything, o_in.at[:, pl.ds(lane((k - 4) * 1024 + c * 512), 512)])])

        @pl.when(k == 12)
        def _():
            put([
                (
                    lambda chunk, part=part: chunk.at[pl.ds(part * 128, 128)],
                    o_out.at[pl.ds(c * 128, 128), pl.ds(part * 512, 512)],
                )
                for part in range(2)
            ])

        @pl.when(k > 12)
        def _():
            put([
                (
                    lambda chunk, part=part: chunk.at[:, pl.ds(part * 128, 128)],
                    o_qkv.at[:, pl.ds(lane((k - 13) * 1024 + part * 256 + c * 128), 128)],
                )
                for part in range(4)
            ])

    def placed(k, owner):
        @pl.when(c == owner)
        def _():
            arrived(plane_sum.at[k], r.keep.at[k])

        @pl.when(c != owner)
        def _():
            arrived(plane_sum.at[k], r.give.at[k])

    def pair_load(k):
        @pl.when(early)
        def _():
            arrived(pair_sum.at[k], r.recv_pair.at[k])

            @pl.when(k >= 4)
            def _():
                arrived(slot("pair", k), r.send_out.at[k - 4])
                placed(k - 4, 0)

            fetch(plane_sum.at[k], "pair", k)
            fetch(pair_sum.at[k], "other", k)

    def pair_send(k):
        @pl.when(early)
        def _():
            fetched("pair", k)
            fetched("other", k)
            total = slot("pair", k)
            add(total, total, slot("other", k))
            remote(total, pair_sum.at[k], r.send_out.at[k], r.recv_pair.at[k], late_plane).start()
            place(k, 0, total)

    def pair_take(k):
        @pl.when(late)
        def _():
            arrived(pair_sum.at[k], r.recv_pair.at[k])
            place(k, 0, pair_sum.at[k])

    def late_load(k):
        again(k, lambda: placed(k - 4, 1))

        @pl.when(early)
        def _():
            fetch(from_left.at[k], "late", k)
            fetch(from_right.at[k], "side", k)

        @pl.when(s == 0)
        def _():
            arrived(from_right.at[k], r.recv_right.at[k])
            fetch(from_right.at[k], "side", k)

        @pl.when(s == 3)
        def _():
            arrived(from_left.at[k], r.recv_left.at[k])
            fetch(from_left.at[k], "side", k)

        @pl.when(late)
        def _():
            fetch(plane_sum.at[k], "late", k)

    def late_place(k):
        fetched("late", k)
        fetched("side", k)
        total = slot("late", k)
        add(total, total, slot("side", k))
        place(k, 1, total)

    def between_planes(t):
        @pl.when(early)
        def _():
            for lag, work, least in ((-2, relay_on, READY + 2), (0, relay_out, READY)):
                @pl.when((t >= lag + least) & (t < lag + CHUNKS))
                def _():
                    work(t - lag)

        for lag, work, least, most in (
            (7, pair_load, READY, CHUNKS), (8, pair_send, READY, CHUNKS), (18, pair_take, 0, CHUNKS),
            (6 + 8 * layer, late_load, 0, CHUNKS), (7 + 8 * layer, late_place, 0, CHUNKS),
        ):
            @pl.when((t >= lag + least) & (t < lag + most))
            def _():
                work(t - lag)

    def weight_grad(count, tile, width_of, pieces):
        def stage(n):
            return r.wd.at[pl.ds((n % 2) * 256, 256), pl.ds(0, width_of)]

        def work(n):
            @pl.when(n >= 2)
            def _():
                arrived(stage(n), r.staged.at[n % 2])

            left, right = tile(n)
            total = contract_rows(left(0), right(0)) + contract_rows(left(1), right(1))
            stage(n)[...] = low(total)
            for src, dst in pieces(n, stage(n)):
                pltpu.make_async_copy(src, dst, r.staged.at[n % 2]).start()

        every(count, work)
        for n in range(count - 2, count):
            arrived(stage(n), r.staged.at[n % 2])

    def grad_of_down():
        weight_grad(
            8,
            lambda n: (lambda side: r.inner[side, :, columns(n)], lambda side: r.grad_rows[side]),
            width,
            lambda n, src: [(src, g_down.at[pl.ds(n * 256, 256)])],
        )

    def grad_of_lift(ref, to):
        weight_grad(
            8,
            lambda n: (
                lambda side: r.mid[side, :, columns(n // 2)],
                lambda side: ref[side, :, pl.ds(lane((n % 2) * 1024), 1024)],
            ),
            1024,
            lambda n, src: [
                (src, to.at[pl.ds((n // 2) * 256, 256), pl.ds(lane((n % 2) * 1024), 1024)])
            ],
        )

    def grad_of_out():
        weight_grad(
            2,
            lambda n: (lambda side: r.att[side, :, columns(n)], lambda side: r.grad_rows[side]),
            width,
            lambda n, src: [
                (
                    src.at[pl.ds(owner * 128, 128), pl.ds(part * 512, 512)],
                    g_out.at[pl.ds(n * 512 + owner * 256 + part * 128, 128)],
                )
                for owner in range(2)
                for part in range(2)
            ],
        )

    def grad_of_qkv():
        weight_grad(
            12,
            lambda n: (
                lambda side: r.hid[side, :, columns(n // 3)],
                lambda side: r.mixed[side, :, pl.ds(lane((n % 3) * 512), 512)],
            ),
            512,
            lambda n, src: [
                (src, g_qkv.at[pl.ds((n // 3) * 256, 256), pl.ds(lane((n % 3) * 512), 512)])
            ],
        )

    fits = (place_col >= start_row[...]) & (place_col <= place_row[...])
    r.bias[...] = jnp.where(fits, 0.0, MASKED)
    settle_relays()
    settle_spread()

    @pl.when(early)
    def _():
        for k in range(2):
            relay_on(k)

    def second_back(b):
        rows = pl.ds(b * 64, 64)

        @pl.when(b % 2 == 0)
        def _():
            arrived(r.grad_in.at[rows_of(b // 2)], r.grad_recv.at[b // 2])

        start = r.hid[0, rows].astype(full)
        middle = unit(start + r.alpha_attn[...] * (unit(r.branch[rows]) - start))
        total = r.output[rows]
        change = unit(total) - middle
        grad = unit_back(middle + r.alpha_mlp[...] * change, r.grad_in[rows].astype(full))
        r.sum_alphas[1:2] += jnp.sum(grad * change, axis=0, keepdims=True)
        r.grad_rows[0, rows] = low(unit_back(total, r.alpha_mlp[...] * grad))
        r.middle[rows] = grad * (1.0 - r.alpha_mlp[...])
        share_rows(r.grad_rows, 1, b)

    every(8, second_back)

    for side in range(2):
        if side:
            shared(r.grad_rows, 1)

        def close_gate(n, side=side):
            at = pl.ds(lane(n * 512), 512)
            grad = last_dims(r.grad_rows[side], r.wd[pl.ds(n * 512, 512)])
            lift_up = r.up[side, :, at].astype(full)
            lift_gate = r.gate[side, :, at].astype(full)
            gating = lift_gate * r.scale_gate[:, at]
            sigmoid = jax.nn.sigmoid(gating)
            grad_up = grad * (gating * sigmoid)
            grad_gate = (
                grad * (lift_up * r.scale_up[:, at]) * sigmoid * (1.0 + gating * (1.0 - sigmoid))
            )
            r.sum_scales[0:1, at] += jnp.sum(grad_up * lift_up, axis=0, keepdims=True)
            r.sum_scales[1:2, at] += jnp.sum(grad_gate * lift_gate, axis=0, keepdims=True)
            r.up[side, :, at] = low(grad_up * r.scale_up[:, at])
            r.gate[side, :, at] = low(grad_gate * r.scale_gate[:, at])

        every(4, close_gate)
    grad_of_down()
    for k in range(READY):
        begin(k)

    @pl.when(early)
    def _():
        for k in range(2, READY):
            relay_on(k)
        for k in range(2):
            relay_out(k)

    def lifted(side, n):
        rows = pl.ds(n * 256, 256)
        return last_dims(r.up[side], r.wu[rows]) + last_dims(r.gate[side], r.wg[rows])

    settle_sent(1)
    exchange(2, lifted, r.middle)
    in_plane(0, 0, READY, 0)
    settle_shared(r.grad_rows, 1)

    def first_back(b):
        rows = pl.ds(b * 64, 64)
        start = r.hid[0, rows].astype(full)
        total = r.branch[rows]
        change = unit(total) - start
        grad = r.middle[rows] + r.got[rows].astype(full)
        grad = unit_back(start + r.alpha_attn[...] * change, grad)
        r.sum_alphas[0:1] += jnp.sum(grad * change, axis=0, keepdims=True)
        r.grad_rows[0, rows] = low(unit_back(total, r.alpha_attn[...] * grad))
        r.middle[rows] = grad * (1.0 - r.alpha_attn[...])
        share_rows(r.grad_rows, 2, b)

    every(8, first_back)

    @pl.when(early)
    def _():
        for k in range(2, READY):
            relay_out(k)

    shared(r.grad_rows, 2)
    in_plane(1, 0, READY, 0)

    marks = (
        lax.broadcasted_iota(jnp.int32, (8, 2 * HEAD), 1) // HEAD
        == lax.broadcasted_iota(jnp.int32, (8, 2 * HEAD), 0)
    ).astype(jnp.bfloat16)

    def attend_back(pair):
        in_plane(2 + pair, 0, READY, 0)

        @pl.when(early & (pair % 2 == 1))
        def _():
            relay_on(READY + pair // 2)

        prepare(pair)
        at = lanes_of(pair, 0)
        heads = r.wo[pl.ds(pair * 128, 128)]
        merge(r.grads, *(low(last_dims(r.grad_rows[side], heads)) for side in range(2)))
        merge(r.raw, r.att[0, :, at], r.att[1, :, at])
        r.dk[...] = jnp.zeros_like(r.dk)
        r.dv[...] = jnp.zeros_like(r.dv)
        for q in range(4):
            at = slice(q * 256, (q + 1) * 256)
            upto = slice(0, (q + 1) * 256)
            deltas = row_sums(r.grads[at].astype(full) * r.raw[at].astype(full), marks)
            delta = jnp.concatenate([deltas[h : h + 1] for h in range(2)], axis=1)
            log_sum = jnp.concatenate([r.log_sums[pair, h : h + 1, at] for h in range(2)], axis=1)
            query, grad, key = of_heads(r.queries[at]), of_heads(r.grads[at]), r.keys[upto]
            mask = jnp.concatenate([r.bias[upto, at]] * 2, axis=1)
            weighted = jnp.exp(last_dims(key, query) + (mask - log_sum))
            grad_scores = low(
                weighted * (last_dims(r.values[upto, : 2 * HEAD], grad) - delta)
            )
            r.dv[upto] += dot(low(weighted), grad)
            r.dk[upto] += dot(grad_scores, query)
            to_queries = contract_rows(grad_scores, key)
            r.dq[at] = (
                head_lanes(0, full) * to_queries[:256] + head_lanes(1, full) * to_queries[256:]
            )

        scale = r.flat[pair, pl.ds(c, 1), :]
        scale_sum = 0.0
        for part, grad in enumerate((r.dq, r.dk)):
            normed, factor = normal(pair, part)
            found = grad[...] * SCORE_SCALE if part == 0 else grad[...]
            scale_sum = scale_sum + jnp.sum(found * normed, axis=0, keepdims=True)
            step = found * scale
            grad[...] = factor * (step - normed * sums_of_halves(normed * step))
        r.sum_qk[pl.ds(pair, 1)] = scale_sum
        for part, grad in enumerate((r.dq, r.dk, r.dv)):
            at = lanes_of(pair, part)
            for q in range(4):
                rows = slice(q * BLOCK, (q + 1) * BLOCK)
                r.mixed[0, rows, at] = low(grad[q * 256 : q * 256 + BLOCK])
                r.mixed[1, rows, at] = low(grad[q * 256 + BLOCK : (q + 1) * 256])

    every(4, attend_back)

    settle_sent(2)
    exchange(
        3, lambda side, n: last_dims(r.mixed[side], r.wq[pl.ds(n * 256, 256)]), r.middle,
    )

    for b in range(4):
        rows = rows_of(b)

        @pl.when(early)
        def _():
            arrived(r.result.at[rows], r.result_send.at[b])

        arrived(r.result.at[rows], r.owner_send.at[0, b])

    def finish(b):
        rows = rows_of(b)
        r.result[rows] = low(r.middle[rows] + r.got[rows].astype(full))

        @pl.when(late)
        def _():
            remote(
                r.result.at[rows], r.grad_in.at[rows], r.result_send.at[b], r.grad_recv.at[b],
                early_plane,
            ).start()

    every(4, finish)
    to_owners(1, r.result, o_grad)

    for owner in range(4):
        r.terms[owner, pl.ds(c, 1), :] = r.sum_qk[owner : owner + 1]
        for n in range(2):
            for j in range(4):
                at = slice((owner % 2 * 2 + n) * 512 + j * 128, (owner % 2 * 2 + n) * 512 + (j + 1) * 128)
                scale = math.sqrt(width) if owner // 2 else 1.0
                r.terms[owner, pl.ds(2 + n * 8 + j + c * 4, 1), :] = (
                    r.sum_scales[owner // 2 : owner // 2 + 1, at] * scale
                )
        for j in range(4):
            at = slice(owner % 2 * 512 + j * 128, owner % 2 * 512 + (j + 1) * 128)
            r.terms[owner, 18 + j : 19 + j, :] = r.sum_alphas[owner // 2 : owner // 2 + 1, at]
        r.terms[owner, 22:23, :] = r.sum_valid[...]
    flow = Flow((r.v0, r.v1, r.v2, r.v3, r.v4, r.v5, r.v6, r.v7), r.vector)
    flow.begin(lambda to: r.terms.at[to])

    every(3, lambda n: in_plane(6 + n, 0, READY, 0))
    grad_of_lift(r.up, g_up)
    for k in range(READY, READY + AHEAD):
        begin(k)
    for k in range(READY + 1):
        if k < READY:
            pair_load(k)
        if k:
            pair_send(k - 1)

    def step(t):
        @pl.when(t == READY + 1)
        def _():
            grad_of_lift(r.gate, g_gate)

        @pl.when(t == READY + 5)
        def _():
            grad_of_out()
            grad_of_qkv()

        @pl.when(t + AHEAD < CHUNKS)
        def _():
            begin(t + AHEAD)

        between_planes(t)
        in_plane(t, READY, CHUNKS, 1)
        for at, work in (
            (READY + 2, flow.pass_on), (READY + 4, flow.finish_plane), (READY + 10, flow.middle_planes),
        ):
            pl.when(t == at)(work)

        @pl.when(t == READY + 14 + 14 * layer)
        def _():
            flow.all_planes(o_vectors.at[c])

    every(CHUNKS + 18 - READY, lambda n: step(n + READY))

    def settle(k):
        chunk = plane_sum.at[k]
        for sem in (r.send_own, r.send_far, r.given):
            arrived(chunk, sem.at[k])

        @pl.when(early)
        def _():
            arrived(chunk, r.send_on.at[k])
            arrived(chunk, r.send_back.at[k])

        @pl.when(k >= CHUNKS - 4)
        def _():
            arrived(chunk, r.send_next.at[k])
            arrived(chunk, r.send_z.at[k])
            placed(k, 1)

        @pl.when(early & (k >= CHUNKS - 4))
        def _():
            arrived(chunk, r.send_out.at[k])
            placed(k, 0)

        @pl.when(late)
        def _():
            placed(k, 0)

    every(CHUNKS, settle)
    flow.settle()
    settle_shared(r.mid, 0)
    settle_shared(r.grad_rows, 2)
    settle_sent(3)
    for b in range(4):
        rows = rows_of(b)
        arrived(r.hid.at[1, rows], r.oth_send.at[b])

        @pl.when(late)
        def _():
            arrived(r.result.at[rows], r.result_send.at[b])

        @pl.when(s != b)
        def _():
            arrived(o_row.at[rows], r.row_send.at[b])
            arrived(r.flags.at[b], r.flag_send.at[b])

        arrived(r.result.at[rows], r.owner_send.at[1, b])

    for array, to_ref in enumerate((o_hidden, o_grad)):
        for micro in range(2):
            for core in range(2):

                @pl.when(jnp.logical_not((c == layer) & (c == core) & (s // 2 == micro)))
                def _():
                    arrived(
                        to_ref.at[micro, pl.ds(core * BLOCK, BLOCK)],
                        r.owner_recv.at[array, micro, core],
                    )


def relay_all(w_qkv, w_out, w_in, w_down, vectors, valid, tokens, cotangent, places):
    width = w_out.shape[1]
    units = w_down.shape[0] * 4
    half = units // 2
    place, start = places

    def low_shape(*shape):
        return jax.ShapeDtypeStruct(shape, jnp.bfloat16)

    chunks = low_shape(CHUNKS, 256, 512)
    rows = low_shape(2, 2 * BLOCK, width)
    anywhere = pl.BlockSpec(memory_space=pl.ANY)
    near = pl.BlockSpec(memory_space=pltpu.VMEM)
    scratch = scratch_of(width, units, vectors.shape[0], valid.shape[1])
    out_shape = [
        low_shape(half // 2, width), low_shape(width // 4, 2 * units), low_shape(width // 4, width),
        low_shape(width // 4, 3 * width), jax.ShapeDtypeStruct((2, 24, 128), jnp.float32),
        rows, rows, low_shape(4 * BLOCK, width),
        low_shape(half, width), low_shape(width, half), low_shape(width, half),
        low_shape(width, width // 2), low_shape(width, 3 * width // 2),
    ] + [chunks] * 7
    return pl.pallas_call(
        functools.partial(relay_kernel, tuple(scratch)),
        out_shape=out_shape,
        in_specs=[anywhere] * 8 + [near] * 3,
        out_specs=[anywhere] * len(out_shape),
        scratch_shapes=list(scratch.values()),
        compiler_params=pltpu.CompilerParams(
            collective_id=0, has_side_effects=True, vmem_limit_bytes=62 * 2**20
        ),
    )(
        w_qkv, w_out, w_in, w_down, vectors, valid, tokens, cotangent,
        start[:, None], place[None, :], start[None, :],
    )[:7]


def per_device(
    tokens, cotangent, lengths, valid_mask, w_qkv, w_out, w_in, w_down, qk_scale, mlp_scale, alphas
):
    c, s, f, _, _, layer = position()
    second = layer == 1
    micro = s // 2
    width = tokens.shape[3]
    group = tokens.shape[2]
    units = w_down.shape[1] * 4

    vectors = jnp.concatenate([qk_scale[0], mlp_scale[0], alphas[0]])
    vectors = jnp.pad(vectors, (0, 32 * 128 - vectors.shape[0])).reshape(32, 128)
    valid = low(jnp.pad(valid_mask[:, 0], ((0, 0), (0, 16 * 128 - group)))).reshape(2, 16, 128)
    index = jnp.arange(4 * group, dtype=jnp.int32)
    place = (index // 256) * 256 + (((index // BLOCK) + c) % 2) * BLOCK + index % BLOCK
    ends = jnp.cumsum(pick(lengths, micro, 0)[0])[:-1]
    passed = place[:, None] >= ends[None, :]
    start = jnp.max(jnp.where(passed, ends[None, :], 0), axis=1)
    places = (place, start)
    grad_down, grad_in_proj, grad_out, grad_qkv, vectors, hidden_out, grad_in = relay_all(
        w_qkv[0], w_out[0], w_in[0], w_down[0], vectors, valid, tokens[:, 0], cotangent[:, 0], places
    )
    cut_qk, cut_mlp = qk_scale.shape[1], qk_scale.shape[1] + mlp_scale.shape[1]
    full = jnp.sum(vectors, axis=0).reshape(-1)
    cuts = (cut_qk, cut_mlp, cut_mlp + alphas.shape[1])
    grad_qk_scale = full[: cuts[0]][None]
    grad_mlp_scale = full[cuts[0] : cuts[1]][None]
    grad_alphas = full[cuts[1] : cuts[2]][None]
    token_count = tokens.shape[0] * lax.axis_size("fsdp") * 4 * group
    total = jnp.sum(full[cuts[2] : cuts[2] + 128], keepdims=True)
    rms_stats = jnp.sqrt(total / token_count + epsilon)
    as_float = [
        part.astype(jnp.float32)[None] for part in (grad_qkv, grad_out, grad_in_proj, grad_down)
    ]
    return (
        hidden_out[None, :, None], grad_in.astype(jnp.float32)[None, :, None], *as_float,
        grad_qk_scale, grad_mlp_scale, grad_alphas, rms_stats,
    )


def solution(mesh):
    placed = (
        P(None, "fsdp", "seq", None),
        P(None, "fsdp", "seq", None),
        P(None, "fsdp", None),
        P(None, "fsdp", "seq"),
        P("section", "fsdp", None),
        P("section", "fsdp", None),
        P("section", "fsdp", None),
        P("section", "fsdp", None),
        P("section", "fsdp"),
        P("section", "fsdp"),
        P("section", "fsdp"),
    )
    planes = mesh.shape["section"] == 2 and mesh.shape["seq"] == 4 and mesh.shape["fsdp"] == 4
    return jax.shard_map(
        per_device if planes else per_device_general,
        mesh=mesh,
        in_specs=placed,
        out_specs=(
            P("section", None, "fsdp", "seq", None),
            P("section", None, "fsdp", "seq", None),
            P("section", "fsdp", None),
            P("section", "fsdp", None),
            P("section", "fsdp", None),
            P("section", "fsdp", None),
            P("section", "fsdp"),
            P("section", "fsdp"),
            P("section", "fsdp"),
            P("section"),
        ),
        check_vma=False,
    )
```

```python
import functools
import math
import types

import jax
import jax.numpy as jnp
from jax import lax
from jax.experimental import pallas as pl
from jax.experimental.pallas import tpu as pltpu
from jax.sharding import PartitionSpec as P

HEAD = 64


epsilon = 1e-06


def shifted(block, axis, distance):
    devices = range(lax.axis_size(axis))
    route = [(i - distance, i) for i in devices if i - distance in devices]
    return lax.ppermute(block, axis, route)


def for_sending(x):
    return jax.tree.map(lambda a: a.astype(jnp.bfloat16) if a.dtype == jnp.float32 else a, x)


def unit(values):
    return values * lax.rsqrt(jnp.sum(values * values, axis=-1, keepdims=True) + epsilon)


def unit_back(values, grad):
    factor = lax.rsqrt(jnp.sum(values * values, axis=-1, keepdims=True) + epsilon)
    normed = values * factor
    return factor * (grad - normed * jnp.sum(normed * grad, axis=-1, keepdims=True))


def contract_rows(left, right):
    return lax.dot_general(
        left, right, (((0,), (0,)), ((), ())), preferred_element_type=jnp.float32
    )


def contract_cols(left, right):
    return lax.dot_general(
        left, right, (((1,), (1,)), ((), ())), preferred_element_type=jnp.float32
    )


def segments_of(row_lengths, seq_len):
    ends = jnp.cumsum(row_lengths)[:-1]
    place = jnp.arange(seq_len, dtype=jnp.int32)
    return (place, jnp.sum((place[:, None] >= ends[None, :]).astype(jnp.int32), axis=1))


def allowed_pairs(row_lengths, offset, group, seq_len):
    key_place, key_segment = segments_of(row_lengths, seq_len)
    query_place = offset + jnp.arange(group, dtype=jnp.int32)
    query_segment = lax.dynamic_slice_in_dim(key_segment, offset, group)
    return (query_segment[:, None] == key_segment[None, :]) & (
        key_place[None, :] <= query_place[:, None]
    )


def masked_scores(queries, key_heads, allowed):
    scores = jnp.einsum(
        "qhd,khd->hqk", queries, key_heads, preferred_element_type=jnp.float32
    ) * math.sqrt(HEAD)
    return jnp.where(allowed[None], scores, -1e30)


def forward_layer(hidden_b, params, allowed, valid):
    w_qkv, w_out, w_in, w_down, qk_scale, mlp_scale, alphas = params
    count, width = hidden_b.shape
    heads = width // HEAD
    hidden = hidden_b.astype(jnp.float32)
    mixed = jnp.dot(hidden_b, w_qkv, preferred_element_type=jnp.float32)
    query_raw = mixed[:, :width].reshape(count, heads, HEAD)
    key_raw = mixed[:, width : 2 * width].reshape(count, heads, HEAD)
    head_scale = qk_scale.astype(jnp.float32).reshape(heads, HEAD)
    query_b = (unit(query_raw) * head_scale).astype(jnp.bfloat16)
    key_b = (unit(key_raw) * head_scale).astype(jnp.bfloat16).reshape(count, width)
    value_b = mixed[:, 2 * width :].astype(jnp.bfloat16)
    keys, values = (
        lax.all_gather(key_b, "seq", axis=0, tiled=True),
        lax.all_gather(value_b, "seq", axis=0, tiled=True),
    )
    key_heads = keys.reshape(-1, heads, HEAD)
    value_heads = values.reshape(-1, heads, HEAD)
    scores = masked_scores(query_b, key_heads, allowed)
    highest = jnp.max(scores, axis=-1, keepdims=True)
    weights = jnp.exp(scores - highest)
    denominator = jnp.sum(weights, axis=-1, keepdims=True)
    weights = weights / denominator
    log_total = highest + jnp.log(denominator)
    attended = jnp.einsum(
        "hqk,khd->qhd",
        weights.astype(jnp.bfloat16),
        value_heads,
        preferred_element_type=jnp.float32,
    )
    attended_b = attended.reshape(count, width).astype(jnp.bfloat16)
    branch = jnp.dot(attended_b, w_out, preferred_element_type=jnp.float32)
    statistic = jnp.sum(valid * jnp.sum(branch * branch, axis=-1))
    step_sizes = alphas.astype(jnp.float32)
    first_sum = hidden + step_sizes[:width] * (unit(branch) - hidden)
    middle = unit(first_sum)
    middle_b = middle.astype(jnp.bfloat16)
    lifted = jnp.dot(middle_b, w_in, preferred_element_type=jnp.float32)
    units_count = lifted.shape[1] // 2
    scales = mlp_scale.astype(jnp.float32)
    upward = lifted[:, :units_count] * scales[:units_count]
    gating = lifted[:, units_count:] * scales[units_count:] * math.sqrt(width)
    inner_b = (upward * jax.nn.silu(gating)).astype(jnp.bfloat16)
    output = jnp.dot(inner_b, w_down, preferred_element_type=jnp.float32)
    second_sum = middle + step_sizes[width:] * (unit(output) - middle)
    result = unit(second_sum).astype(jnp.bfloat16)
    kept = (
        hidden_b,
        query_raw,
        key_raw,
        query_b,
        keys,
        values,
        log_total,
        attended_b,
        branch,
        first_sum,
        middle_b,
        lifted,
        inner_b,
        output,
        second_sum,
    )
    return (result, kept, statistic)


def backward_layer(kept, params, grad_out, allowed):
    (
        hidden_b,
        query_raw,
        key_raw,
        query_b,
        keys,
        values,
        log_total,
        attended_b,
        branch,
        first_sum,
        middle_b,
        lifted,
        inner_b,
        output,
        second_sum,
    ) = kept
    w_qkv, w_out, w_in, w_down, qk_scale, mlp_scale, alphas = params
    count, width = hidden_b.shape
    heads = width // HEAD
    hidden = hidden_b.astype(jnp.float32)
    step_sizes = alphas.astype(jnp.float32)
    alpha_attn = step_sizes[:width]
    alpha_mlp = step_sizes[width:]
    middle = unit(first_sum)
    grad_second = unit_back(second_sum, grad_out)
    grad_alpha_mlp = jnp.sum(grad_second * (unit(output) - middle), axis=0)
    grad_output = unit_back(output, alpha_mlp * grad_second).astype(jnp.bfloat16)
    grad_middle = grad_second * (1.0 - alpha_mlp)
    grad_down = contract_rows(inner_b, grad_output)
    grad_inner = contract_cols(grad_output, w_down)
    units_count = lifted.shape[1] // 2
    scales = mlp_scale.astype(jnp.float32)
    root = math.sqrt(width)
    lift_up = lifted[:, :units_count]
    lift_gate = lifted[:, units_count:]
    upward = lift_up * scales[:units_count]
    gating = lift_gate * scales[units_count:] * root
    sigmoid = jax.nn.sigmoid(gating)
    grad_upward = grad_inner * jax.nn.silu(gating)
    grad_gating = grad_inner * upward * sigmoid * (1.0 + gating * (1.0 - sigmoid))
    grad_scale_mlp = jnp.concatenate(
        [jnp.sum(grad_upward * lift_up, axis=0), jnp.sum(grad_gating * root * lift_gate, axis=0)]
    )
    grad_lifted = jnp.concatenate(
        [grad_upward * scales[:units_count], grad_gating * root * scales[units_count:]], axis=1
    ).astype(jnp.bfloat16)
    grad_in_proj = contract_rows(middle_b, grad_lifted)
    grad_middle = grad_middle + contract_cols(grad_lifted, w_in)
    grad_first = unit_back(first_sum, grad_middle)
    grad_alpha_attn = jnp.sum(grad_first * (unit(branch) - hidden), axis=0)
    grad_branch = unit_back(branch, alpha_attn * grad_first).astype(jnp.bfloat16)
    grad_hidden = grad_first * (1.0 - alpha_attn)
    grad_out_proj = contract_rows(attended_b, grad_branch)
    grad_attended = (
        contract_cols(grad_branch, w_out).astype(jnp.bfloat16).reshape(count, heads, HEAD)
    )
    key_heads = keys.reshape(-1, heads, HEAD)
    value_heads = values.reshape(-1, heads, HEAD)
    scores = masked_scores(query_b, key_heads, allowed)
    weights = jnp.exp(scores - log_total)
    grad_weights = jnp.einsum(
        "qhd,khd->hqk", grad_attended, value_heads, preferred_element_type=jnp.float32
    )
    delta = jnp.sum(weights * grad_weights, axis=-1, keepdims=True)
    grad_scores = (weights * (grad_weights - delta)).astype(jnp.bfloat16)
    score_scale = math.sqrt(HEAD)
    grad_query = (
        jnp.einsum("hqk,khd->qhd", grad_scores, key_heads, preferred_element_type=jnp.float32)
        * score_scale
    )
    seq_len = keys.shape[0]
    grad_keys = (
        jnp.einsum("hqk,qhd->khd", grad_scores, query_b, preferred_element_type=jnp.float32)
        * score_scale
    )
    grad_values = jnp.einsum(
        "hqk,qhd->khd",
        weights.astype(jnp.bfloat16),
        grad_attended,
        preferred_element_type=jnp.float32,
    )
    grad_key_own, grad_value_own = (
        lax.psum_scatter(
            grad_keys.reshape(seq_len, width).astype(jnp.bfloat16),
            "seq",
            scatter_dimension=0,
            tiled=True,
        ).astype(jnp.float32),
        lax.psum_scatter(
            grad_values.reshape(seq_len, width).astype(jnp.bfloat16),
            "seq",
            scatter_dimension=0,
            tiled=True,
        ).astype(jnp.float32),
    )
    head_scale = qk_scale.astype(jnp.float32).reshape(heads, HEAD)
    grad_key_heads = grad_key_own.reshape(count, heads, HEAD)
    grad_scale_qk = (
        jnp.sum(grad_query * unit(query_raw), axis=0)
        + jnp.sum(grad_key_heads * unit(key_raw), axis=0)
    ).reshape(width)
    grad_query_raw = unit_back(query_raw, grad_query * head_scale).reshape(count, width)
    grad_key_raw = unit_back(key_raw, grad_key_heads * head_scale).reshape(count, width)
    grad_mixed = jnp.concatenate([grad_query_raw, grad_key_raw, grad_value_own], axis=1).astype(
        jnp.bfloat16
    )
    grad_qkv = contract_rows(hidden_b, grad_mixed)
    grad_hidden = grad_hidden + contract_cols(grad_mixed, w_qkv)
    grad_step_sizes = jnp.concatenate([grad_alpha_attn, grad_alpha_mlp])
    grads = (
        grad_qkv,
        grad_out_proj,
        grad_in_proj,
        grad_down,
        grad_scale_qk,
        grad_scale_mlp,
        grad_step_sizes,
    )
    return (grad_hidden, grads)


def per_device_general(
    tokens, cotangent, lengths, valid_mask, w_qkv, w_out, w_in, w_down, qk_scale, mlp_scale, alphas
):
    shards = (w_qkv, w_out, w_in, w_down, qk_scale, mlp_scale, alphas)
    gathered = (
        lax.all_gather(shards[0], "fsdp", axis=1, tiled=True),
        lax.all_gather(shards[1], "fsdp", axis=1, tiled=True),
        lax.all_gather(shards[2], "fsdp", axis=1, tiled=True),
        lax.all_gather(shards[3], "fsdp", axis=1, tiled=True),
        lax.all_gather(shards[4], "fsdp", axis=1, tiled=True),
        lax.all_gather(shards[5], "fsdp", axis=1, tiled=True),
        lax.all_gather(shards[6], "fsdp", axis=1, tiled=True),
    )
    params = tuple((piece[0] for piece in gathered))
    section = lax.axis_index("section")
    micro = tokens.shape[0]
    group = tokens.shape[2]
    width = tokens.shape[3]
    seq_len = group * lax.axis_size("seq")
    offset = lax.axis_index("seq") * group

    def fetch(array, index):
        return lax.dynamic_index_in_dim(array, index, 0, keepdims=False)[0]

    def forward_step(carry, step):
        incoming, stat_sum = carry
        index = step - section
        active = (index >= 0) & (index < micro)
        chosen = jnp.clip(index, 0, micro - 1)
        hidden_in = jnp.where(section == 0, fetch(tokens, chosen), incoming)
        allowed = allowed_pairs(fetch(lengths, chosen), offset, group, seq_len)
        valid = fetch(valid_mask, chosen).astype(jnp.float32)
        result, kept, statistic = forward_layer(hidden_in, params, allowed, valid)
        outgoing = shifted(result, "section", 1)
        stat_sum = stat_sum + jnp.where(active, statistic, 0.0)
        return ((outgoing, stat_sum), (result, kept))

    step_list = jnp.arange(micro + 1, dtype=jnp.int32)
    start = (jnp.zeros((group, width), jnp.bfloat16), jnp.zeros((), jnp.float32))
    (unused_fwd, stat_sum), (results, kept_all) = lax.scan(forward_step, start, step_list)
    late_shards, stat_sum = lax.optimization_barrier((shards, stat_sum))
    again = (
        lax.all_gather(late_shards[0], "fsdp", axis=1, tiled=True),
        lax.all_gather(late_shards[1], "fsdp", axis=1, tiled=True),
        lax.all_gather(late_shards[2], "fsdp", axis=1, tiled=True),
        lax.all_gather(late_shards[3], "fsdp", axis=1, tiled=True),
        lax.all_gather(late_shards[4], "fsdp", axis=1, tiled=True),
        lax.all_gather(late_shards[5], "fsdp", axis=1, tiled=True),
        lax.all_gather(late_shards[6], "fsdp", axis=1, tiled=True),
    )
    params_back = tuple((piece[0] for piece in again))

    def backward_step(carry, step):
        incoming, sums = carry
        index = step - 1 + section
        active = (index >= 0) & (index < micro)
        chosen = jnp.clip(index, 0, micro - 1)
        position = chosen + section

        def take(array):
            return lax.dynamic_index_in_dim(array, position, 0, keepdims=False)

        kept = jax.tree.map(take, kept_all)
        grad_out = jnp.where(
            section == 1, fetch(cotangent, chosen).astype(jnp.float32), incoming.astype(jnp.float32)
        )
        grad_out = jnp.where(active, grad_out, 0.0)
        row_lengths = fetch(lengths, chosen)
        allowed = allowed_pairs(row_lengths, offset, group, seq_len)
        grad_hidden, grads = backward_layer(kept, params_back, grad_out, allowed)
        outgoing = shifted(grad_hidden.astype(jnp.bfloat16), "section", -1)
        sums = tuple((total + piece for total, piece in zip(sums, grads)))
        return ((outgoing, sums), grad_hidden)

    zeros = tuple((jnp.zeros(piece.shape, jnp.float32) for piece in params_back))
    (unused_back, sums), grad_steps = lax.scan(
        backward_step, (jnp.zeros((group, width), jnp.bfloat16), zeros), step_list
    )
    hidden_out = lax.dynamic_slice_in_dim(results, section, micro, 0).reshape(
        1, micro, 1, group, width
    )
    grad_in = lax.dynamic_slice_in_dim(grad_steps, 1 - section, micro, 0).reshape(
        1, micro, 1, group, width
    )
    shard_sums = jax.tree.map(
        lambda part: part.astype(jnp.float32),
        lax.psum_scatter(for_sending(sums), "fsdp", scatter_dimension=0, tiled=True),
    )
    reduced = jax.tree.map(
        lambda part: part.astype(jnp.float32), lax.psum(for_sending(shard_sums), "seq")
    )
    total_stat = lax.psum(stat_sum, ("seq", "fsdp"))
    token_count = micro * lax.axis_size("fsdp") * seq_len
    rms_stats = jnp.sqrt(total_stat / token_count + epsilon).reshape(1)
    return (
        hidden_out,
        grad_in,
        reduced[0][None],
        reduced[1][None],
        reduced[2][None],
        reduced[3][None],
        reduced[4][None],
        reduced[5][None],
        reduced[6][None],
        rms_stats,
    )


BLOCK = 128
SCORE_SCALE = math.sqrt(HEAD)
MASKED = -1e30


def dot(left, right):
    return jnp.dot(left, right, preferred_element_type=jnp.float32)


def low(x):
    return x.astype(jnp.bfloat16)


def pick(x, index, axis):
    return lax.dynamic_index_in_dim(x, index, axis, keepdims=False)


def sums_of_halves(x):
    row = lax.broadcasted_iota(jnp.int32, (2 * HEAD, 2 * HEAD), 0) // HEAD
    col = lax.broadcasted_iota(jnp.int32, (2 * HEAD, 2 * HEAD), 1) // HEAD
    same = (row == col).astype(jnp.bfloat16)
    high = x.astype(jnp.bfloat16)
    rest = (x - high.astype(jnp.float32)).astype(jnp.bfloat16)
    return dot(high, same) + dot(rest, same)


def normal_heads(raw):
    factor = lax.rsqrt(sums_of_halves(raw * raw) + epsilon)
    return raw * factor, factor


def merge(to, own, oth):
    for s in range(4):
        to[s * 256 : s * 256 + BLOCK, : own.shape[1]] = own[s * BLOCK : (s + 1) * BLOCK]
        to[s * 256 + BLOCK : (s + 1) * 256, : own.shape[1]] = oth[s * BLOCK : (s + 1) * BLOCK]


def last_dims(left, right):
    return lax.dot_general(left, right, (((1,), (1,)), ((), ())), preferred_element_type=jnp.float32)


def head_lanes(h, dtype):
    lane = lax.broadcasted_iota(jnp.int32, (1, 2 * HEAD), 1) // HEAD
    return (lane == h).astype(dtype)


MESH = pl.DeviceIdType.MESH


def position():
    c, s, f = (lax.axis_index(name) for name in ("section", "seq", "fsdp"))
    x, y = f % 2, f // 2
    layer = 1 - ((s + 1) // 2) % 2
    return c, s, f, y * 2 + 1 - x, (1 - y) * 2 + x, layer


def greet(devices):
    barrier = pltpu.get_barrier_semaphore()
    for device in devices:
        pl.semaphore_signal(barrier, inc=1, device_id=device, device_id_type=MESH)
    pl.semaphore_wait(barrier, len(devices))


def remote(src, dst, send, recv, device):
    return pltpu.make_async_remote_copy(
        src_ref=src, dst_ref=dst, send_sem=send, recv_sem=recv, device_id=device, device_id_type=MESH
    )


def arrived(ref, sem):
    pltpu.make_async_copy(ref, ref, sem).wait()


def lane(offset):
    return pl.multiple_of(offset, 128)


def every(count, work):
    def step(n, carry):
        work(n)
        return carry

    lax.fori_loop(0, count, step, 0)


def silu(x):
    return x * jax.nn.sigmoid(x)


def row_sums(x, lanes):
    high = low(x)
    rest = low(x - high.astype(jnp.float32))
    return last_dims(lanes, high) + last_dims(lanes, rest)


class Flow:
    def __init__(self, buffers, semaphores):
        (
            self.near_own, self.near_far, self.far_in, self.own, self.passing,
            self.from_left, self.from_right, self.pair_sum,
        ) = buffers
        (
            self.load_own, self.load_pass, self.send_own, self.recv_own, self.send_far,
            self.recv_far, self.send_next, self.recv_next, self.send_z, self.recv_left,
            self.recv_right, self.recv_pair, self.send_on, self.send_back, self.send_out,
            self.keep, self.give, self.given,
        ) = [semaphores.at[n] for n in range(VECTOR_SEMAPHORES)]
        self.place_of = position()

    def begin(self, source):
        c, s, f, fx, fy, _ = self.place_of
        to = (c, s, fx)
        remote(source(fx), self.near_own, self.send_own, self.recv_own, to).start()
        remote(source(3 - f), self.near_far, self.send_far, self.recv_far, to).start()
        pltpu.make_async_copy(source(fy), self.passing, self.load_pass).start()
        pltpu.make_async_copy(source(f), self.own, self.load_own).start()

    def pass_on(self):
        c, s, _, _, fy, _ = self.place_of
        arrived(self.passing, self.load_pass)
        arrived(self.near_far, self.recv_far)
        add(self.passing, self.passing, self.near_far)
        remote(self.passing, self.far_in, self.send_next, self.recv_next, (c, s, fy)).start()

    def finish_plane(self):
        c, s, f, _, _, _ = self.place_of
        own, send = self.own, self.send_z
        arrived(own, self.load_own)
        arrived(self.near_own, self.recv_own)
        arrived(self.far_in, self.recv_next)
        add(own, own, self.near_own, self.far_in)

        @pl.when(s == 0)
        def _():
            remote(own, self.from_left, send, self.recv_left, (c, 1, f)).start()

        @pl.when(s == 3)
        def _():
            remote(own, self.from_right, send, self.recv_right, (c, 2, f)).start()

        @pl.when((s == 1) | (s == 2))
        def _():
            remote(own, self.pair_sum, send, self.recv_pair, (c, 3 - s, f)).start()

    def middle_planes(self):
        c, s, f, _, _, _ = self.place_of
        left, right, pair = self.from_left, self.from_right, self.pair_sum

        @pl.when(s == 1)
        def _():
            arrived(left, self.recv_left)
            remote(left, left, self.send_on, self.recv_left, (c, 2, f)).start()

        @pl.when(s == 2)
        def _():
            arrived(right, self.recv_right)
            remote(right, right, self.send_on, self.recv_right, (c, 1, f)).start()

        @pl.when((s == 1) | (s == 2))
        def _():
            arrived(pair, self.recv_pair)
            arrived(pair, self.send_z)
            add(pair, pair, self.own)
            remote(pair, pair, self.send_out, self.recv_pair, (c, (s - 1) * 3, f)).start()

    def all_planes(self, dst):
        c, s, f, _, _, _ = self.place_of
        left, right, pair = self.from_left, self.from_right, self.pair_sum
        own, total = self.own, self.near_own

        @pl.when(s == 1)
        def _():
            arrived(right, self.recv_right)
            remote(right, right, self.send_back, self.recv_right, (c, 0, f)).start()

        @pl.when(s == 2)
        def _():
            arrived(left, self.recv_left)
            remote(left, left, self.send_back, self.recv_left, (c, 3, f)).start()

        @pl.when((s == 1) | (s == 2))
        def _():
            add(total, left, right)

        @pl.when(s == 0)
        def _():
            arrived(pair, self.recv_pair)
            arrived(right, self.recv_right)
            add(total, own, right)

        @pl.when(s == 3)
        def _():
            arrived(pair, self.recv_pair)
            arrived(left, self.recv_left)
            add(total, own, left)

        for owner, chunk in ((0, pair), (1, total)):

            @pl.when(c == owner)
            def _():
                pltpu.make_async_copy(chunk, dst, self.keep).start()

            @pl.when(c != owner)
            def _():
                remote(chunk, dst, self.give, self.given, (1 - c, s, f)).start()

    def settle(self):
        _, s, _, _, _, _ = self.place_of
        for sem in (
            self.send_own, self.send_far, self.send_next, self.keep, self.give, self.given
        ):
            arrived(self.own, sem)

        @pl.when((s == 1) | (s == 2))
        def _():
            for sem in (self.send_on, self.send_back, self.send_out):
                arrived(self.own, sem)

        @pl.when((s == 0) | (s == 3))
        def _():
            arrived(self.own, self.send_z)


def add(to, *refs):
    total = refs[0][...].astype(jnp.float32)
    for ref in refs[1:]:
        total = total + ref[...].astype(jnp.float32)
    to[...] = total.astype(to.dtype)


VECTOR_SEMAPHORES = 18
CHUNKS = 16
SHARED = (1, 2, 3, 4)
AHEAD = 3
INPUTS = 11
OUTPUTS = 19


def scratch_of(width, units, vector_rows, flag_rows):
    rows = 4 * BLOCK
    half = units // 2

    def low_vmem(*shape):
        return pltpu.VMEM(shape, jnp.bfloat16)

    def full_vmem(*shape):
        return pltpu.VMEM(shape, jnp.float32)

    def sems(*shape):
        return pltpu.SemaphoreType.DMA(shape)

    low_row, full_row, low_rows = low_vmem(rows, width), full_vmem(rows, width), low_vmem(2, rows, width)
    pair, pair_full = low_vmem(2 * rows, 2 * HEAD), full_vmem(2 * rows, 2 * HEAD)
    return dict(
        wq=low_vmem(width, 3 * width // 2), wo=low_vmem(width // 2, width),
        wu=low_vmem(width, half), wg=low_vmem(width, half), wd=low_vmem(half, width),
        vec=low_vmem(4, vector_rows, 128), flat=full_vmem(4, vector_rows, 128),
        flags=low_vmem(4, flag_rows, 128), flags_full=full_vmem(4, flag_rows, 128),
        scale_up=full_vmem(1, half), scale_gate=full_vmem(1, half),
        alpha_attn=full_vmem(1, width), alpha_mlp=full_vmem(1, width),
        hid=low_rows, mixed=low_vmem(2, rows, 3 * width // 2), att=low_vmem(2, rows, width // 2),
        mid=low_rows, up=low_vmem(2, rows, half), gate=low_vmem(2, rows, half),
        inner=low_vmem(2, rows, half), branch=full_row, middle=full_row, output=full_row,
        result=low_row, part=low_row, got=low_row,
        bias=full_vmem(2 * rows, 2 * rows), raw=pair, queries=pair, keys=pair,
        values=low_vmem(2 * rows, 4 * HEAD), grads=pair, dq=pair_full, dk=pair_full, dv=pair_full,
        log_sums=full_vmem(4, 2, 2 * rows),
        grad_in=low_row, grad_rows=low_rows,
        sum_alphas=full_vmem(2, width), sum_scales=full_vmem(2, half), sum_qk=full_vmem(4, 2 * HEAD),
        sum_valid=full_vmem(1, 128), terms=full_vmem(4, 24, 128),
        v0=full_vmem(24, 128), v1=full_vmem(24, 128), v2=full_vmem(24, 128), v3=full_vmem(24, 128),
        v4=full_vmem(24, 128), v5=full_vmem(24, 128), v6=full_vmem(24, 128), v7=full_vmem(24, 128),
        first_send=sems(6, 3), first_recv=sems(6, 3), next_send=sems(6, 2), next_recv=sems(6, 2),
        plane_send=sems(6, 3), plane_recv=sems(6, 3),
        row_send=sems(4), row_recv=sems(4), flag_send=sems(4), flag_recv=sems(4),
        own_recv=sems(4), oth_send=sems(4), oth_recv=sems(4),
        part_send=sems(4, 4), part_recv=sems(4, 4),
        mid_send=sems(3, 4), mid_recv=sems(3, 4), result_send=sems(4), grad_recv=sems(4),
        owner_send=sems(2, 4), owner_recv=sems(2, 2, 2),
        vector=sems(VECTOR_SEMAPHORES), staged=sems(2), load=sems(9, 4),
        send_own=sems(CHUNKS), recv_own=sems(CHUNKS), send_far=sems(CHUNKS), recv_far=sems(CHUNKS),
        send_next=sems(CHUNKS), recv_next=sems(CHUNKS), send_z=sems(CHUNKS), stored=sems(CHUNKS),
        recv_left=sems(CHUNKS), recv_right=sems(CHUNKS), recv_pair=sems(CHUNKS),
        send_on=sems(CHUNKS), send_back=sems(CHUNKS), send_out=sems(CHUNKS),
        keep=sems(CHUNKS), give=sems(CHUNKS), given=sems(CHUNKS),
    )


def relay_kernel(names, *refs):
    (
        w_qkv, w_out, w_in, w_down, vectors, valid, tokens, cotangent,
        start_col, place_row, start_row,
    ) = refs[:INPUTS]
    (
        o_down, o_in, o_out, o_qkv, o_vectors, o_hidden, o_grad, o_row,
        g_down, g_up, g_gate, g_out, g_qkv,
        near_own, near_far, far_in, from_left, from_right, pair_sum,
    ) = refs[INPUTS : INPUTS + OUTPUTS]
    plane_sum, *refs = refs[INPUTS + OUTPUTS :]
    r = types.SimpleNamespace(**dict(zip(names, refs)))
    c, s, f, fx, fy, layer = position()
    sibling = (1 - c, s, f)
    early, late = layer == 0, layer == 1
    late_plane = (c, (s - 1) * 3, f)
    early_plane = (c, s // 3 + 1, f)
    width = w_out.shape[1]
    full = jnp.float32
    greet(
        [sibling, (c, s, fx), (c, s, fy)]
        + [(core, (s + step) % 4, f) for core in (0, 1) for step in (1, 2, 3)]
    )

    def rows_of(b):
        return pl.ds(b * BLOCK, BLOCK)

    def columns(n):
        return pl.ds(lane(n * 256), 256)

    def send_row(to, held):
        src, dst = held.at[pl.ds(c * BLOCK, BLOCK)], o_row.at[rows_of(s)]
        flags, flags_to = valid.at[to // 2], r.flags.at[s]

        @pl.when(s == to)
        def _():
            pltpu.make_async_copy(src, dst, r.row_recv.at[s]).start()
            pltpu.make_async_copy(flags, flags_to, r.flag_recv.at[s]).start()

        @pl.when(s != to)
        def _():
            remote(src, dst, r.row_send.at[to], r.row_recv.at[s], (c, to, f)).start()
            remote(flags, flags_to, r.flag_send.at[to], r.flag_recv.at[s], (c, to, f)).start()

    send_row(1, tokens.at[0])
    send_row(2, tokens.at[1])

    def pieces(item, h):
        if item == 0:
            return [(vectors, r.vec.at[f])]
        if item == 1:
            return [
                (
                    w_qkv.at[:, pl.ds(lane(part * 256 + h * 128), 128)],
                    r.wq.at[pl.ds(f * 256, 256), pl.ds(part * 128, 128)],
                )
                for part in range(12)
            ]
        if item == 2:
            return [(w_out.at[pl.ds(h * 128, 128)], r.wo.at[pl.ds(f * 128, 128)])]
        if item in (3, 4):
            to = (r.wu, r.wg)[item - 3]
            return [
                (
                    w_in.at[:, pl.ds(lane((item - 3) * 4096 + part * 1024 + h * 512), 512)],
                    to.at[pl.ds(f * 256, 256), pl.ds(part * 512, 512)],
                )
                for part in range(4)
            ]
        return [(w_down.at[pl.ds(h * 512, 512)], r.wd.at[pl.ds(f * 512, 512)])]

    weights = (r.vec, r.wq, r.wo, r.wu, r.wg, r.wd)
    other_plane = (c, 3 - s, f)

    def quarter(item):
        return 0 if item == 0 else weights[item].shape[0] // 16

    def block(item, of):
        if item == 0:
            return r.vec.at[of]
        rows = weights[item].shape[0] // 4
        return weights[item].at[pl.ds(of * rows, rows)]

    def part_of(item, of, part):
        if item == 0:
            return r.vec.at[of, pl.ds(part * 16, 16)]
        rows = weights[item].shape[0] // 8
        return weights[item].at[pl.ds(of * 2 * rows + part * rows, rows)]

    def quarters(item, of, least, count):
        size = quarter(item)
        return weights[item].at[pl.ds(of * 4 * size + least * size, count * size)]

    @pl.when(c == layer)
    def _():
        for item in range(6):
            for src, dst in pieces(item, 1 - c):
                remote(
                    src, dst, r.first_send.at[item, 2], r.first_recv.at[item, 0], sibling
                ).start()
            for src, dst in pieces(item, c):
                pltpu.make_async_copy(src, dst, r.first_recv.at[item, 0]).start()

    ways = ((1, fx, fy), (2, fy, fx))

    def spread(*items):
        for item in items:
            arrived(block(item, f), r.first_recv.at[item, 0])

            def send(moved, item=item):
                for part, (came, to, _) in enumerate(ways):
                    remote(
                        moved, moved, r.first_send.at[item, part], r.first_recv.at[item, came],
                        (c, s, to),
                    ).start()

            if item in SHARED:

                @pl.when(early)
                def _():
                    send(quarters(item, f, s - 1, 3))

                @pl.when(late)
                def _():
                    send(block(item, f))
            else:
                send(block(item, f))

    def forward(moved, item, part, to):
        remote(moved, moved, r.next_send.at[item, part], r.next_recv.at[item, part], to).start()

    def share(moved, item, part):
        remote(
            moved, moved, r.plane_send.at[item, part], r.plane_recv.at[item, part], other_plane
        ).start()

    def relay(item):
        def halves():
            for part, (came, of, to) in enumerate(ways):
                arrived(block(item, of), r.first_recv.at[item, came])
                forward(part_of(item, of, part), item, part, (c, s, to))

        if item not in SHARED:
            halves()
        else:
            pl.when(late)(halves)

            @pl.when(early)
            def _():
                for part, (came, of, to) in enumerate(ways):
                    arrived(quarters(item, of, 0, 3), r.first_recv.at[item, came])
                    forward(quarters(item, of, (s - 1) * 2 + part, 1), item, part, (c, s, to))
                for part, (came, of, to) in enumerate(ways):
                    share(quarters(item, of, (s - 1) * 3, 1), item, part)

    def relay_across(item):
        @pl.when(early)
        def _():
            for part in range(2):
                arrived(quarters(item, 3 - f, (s - 1) * 2 + part, 1), r.next_recv.at[item, part])
            share(quarters(item, 3 - f, (s - 1) * 2, 2), item, 2)

    def complete(item):
        def halves():
            for part in range(2):
                arrived(part_of(item, 3 - f, part), r.next_recv.at[item, part])

        if item not in SHARED:
            halves()
        else:
            pl.when(late)(halves)

            @pl.when(early)
            def _():
                for part, of in ((0, fx), (1, fy)):
                    arrived(quarters(item, of, (2 - s) * 3, 1), r.plane_recv.at[item, part])
                arrived(quarters(item, 3 - f, (2 - s) * 2, 2), r.plane_recv.at[item, 2])

    def settle_relays():
        for item in range(6):

            def halves():
                for part in range(2):
                    arrived(part_of(item, f, part), r.next_send.at[item, part])

            if item not in SHARED:
                halves()
            else:
                pl.when(late)(halves)

                @pl.when(early)
                def _():
                    for part in range(2):
                        arrived(quarters(item, f, 0, 1), r.next_send.at[item, part])
                        arrived(quarters(item, f, 0, 1), r.plane_send.at[item, part])
                    arrived(quarters(item, f, 0, 2), r.plane_send.at[item, 2])

    def settle_spread():
        for item in range(6):

            def sent(moved, item=item):
                for part in range(2):
                    arrived(moved, r.first_send.at[item, part])

            if item in SHARED:
                pl.when(early)(lambda: sent(quarters(item, f, 0, 3)))
                pl.when(late)(lambda: sent(block(item, f)))
            else:
                sent(block(item, f))

        @pl.when(c == layer)
        def _():
            for item in range(6):
                arrived(block(item, f), r.first_send.at[item, 2])

    spread(0, 1, 2)
    index = lax.broadcasted_iota(jnp.int32, (8 * BLOCK, 1), 0)
    place_col = (index // 256) * 256 + (index // BLOCK + c) % 2 * BLOCK + index % BLOCK
    fits = (place_row[...] >= start_col[...]) & (place_row[...] <= place_col)
    r.bias[...] = jnp.where(fits, 0.0, MASKED)
    r.values[:, 2 * HEAD :] = jnp.ones_like(r.values[:, 2 * HEAD :])
    for sums in (r.sum_alphas, r.sum_scales, r.sum_valid, r.terms):
        sums[...] = jnp.zeros_like(sums)
    relay(0)
    relay(1)
    spread(3)
    relay(2)
    relay_across(1)

    def to_sibling(b, src):
        remote(src, r.hid.at[1, rows_of(b)], r.oth_send.at[b], r.oth_recv.at[b], sibling).start()

    @pl.when(early)
    def _():
        for b in range(4):
            held = o_row.at[rows_of(b)]
            arrived(held, r.row_recv.at[b])
            pltpu.make_async_copy(held, r.hid.at[0, rows_of(b)], r.own_recv.at[b]).start()
            to_sibling(b, held)
        for b in range(4):
            arrived(r.hid.at[0, rows_of(b)], r.own_recv.at[b])

    @pl.when(late)
    def _():
        spread(4)
        relay(3)
        spread(5)
        relay(4)
        relay(5)
        for b in range(4):
            arrived(r.hid.at[0, rows_of(b)], r.own_recv.at[b])
            to_sibling(b, r.hid.at[0, rows_of(b)])

    complete(0)
    r.flat[...] = r.vec[...].astype(full)
    for n in range(4):
        for j in range(4):
            at = slice(n * 512 + j * 128, n * 512 + (j + 1) * 128)
            row = pl.ds(2 + (n % 2) * 8 + j + c * 4, 1)
            r.scale_up[:, at] = r.flat[n // 2, row, :]
            r.scale_gate[:, at] = r.flat[2 + n // 2, row, :] * math.sqrt(width)
    for n in range(2):
        for j in range(4):
            at = slice(n * 512 + j * 128, n * 512 + (j + 1) * 128)
            r.alpha_attn[:, at] = r.flat[n, 18 + j : 19 + j, :]
            r.alpha_mlp[:, at] = r.flat[2 + n, 18 + j : 19 + j, :]

    complete(1)
    for side in range(2):
        if side:
            for b in range(4):
                arrived(r.hid.at[1, rows_of(b)], r.oth_recv.at[b])

        def mix(n, side=side):
            at = pl.ds(lane(n * 512), 512)
            r.mixed[side, :, at] = low(dot(r.hid[side], r.wq[:, at]))

        every(3, mix)

    first = (lax.broadcasted_iota(jnp.int32, (8, 2 * HEAD), 1) == 0).astype(jnp.bfloat16)

    def lanes_of(pair, part):
        return pl.ds(lane(part * (width // 2) + pair * 2 * HEAD), 2 * HEAD)

    def normal(pair, part):
        at = lanes_of(pair, part)
        merge(r.raw, r.mixed[0, :, at], r.mixed[1, :, at])
        return normal_heads(r.raw[...].astype(full))

    def prepare(pair):
        scale = r.flat[pair, pl.ds(c, 1), :]
        r.queries[...] = low(normal(pair, 0)[0] * scale) * SCORE_SCALE
        r.keys[...] = low(normal(pair, 1)[0] * scale)
        at = lanes_of(pair, 2)
        merge(r.values, r.mixed[0, :, at], r.mixed[1, :, at])

    def of_heads(block):
        return jnp.concatenate([block * head_lanes(h, jnp.bfloat16) for h in range(2)])

    def attend(pair):
        @pl.when(early & (pair == 0))
        def _():
            relay_across(2)
            spread(4)

        @pl.when(early & (pair == 2))
        def _():
            relay(3)

        @pl.when(early & (pair == 3))
        def _():
            spread(5)

        prepare(pair)
        at = lanes_of(pair, 0)
        for q in range(4):
            upto = (q + 1) * 256
            query = of_heads(r.queries[q * 256 : upto])
            summed = 0.0
            for k in range(q + 1):
                at_keys = slice(k * 256, (k + 1) * 256)
                mask = jnp.concatenate([r.bias[q * 256 : upto, at_keys]] * 2)
                weighted = jnp.exp(last_dims(query, r.keys[at_keys]) + mask)
                summed = summed + dot(low(weighted), r.values[at_keys])
            total = summed[:, 2 * HEAD :]
            parts = summed[:, : 2 * HEAD] / total
            log_sum = jnp.log(row_sums(total, first)[:1])
            for h in range(2):
                r.log_sums[pair, h : h + 1, q * 256 : upto] = log_sum[:, h * 256 : (h + 1) * 256]
            joined = low(jnp.where(head_lanes(0, full) > 0, parts[:256], parts[256:]))
            r.att[0, q * BLOCK : (q + 1) * BLOCK, at] = joined[:BLOCK]
            r.att[1, q * BLOCK : (q + 1) * BLOCK, at] = joined[BLOCK:]

    every(4, attend)

    def exchange(index, product, to):
        send, recv = r.part_send.at[index], r.part_recv.at[index]

        def sent(n):
            at = columns(n)
            r.part[:, at] = low(product(1, n))
            remote(r.part.at[:, at], r.got.at[:, at], send.at[n], recv.at[n], sibling).start()

        def own(n):
            at = columns(n)
            to[:, at] = product(0, n) if to is not r.middle else to[:, at] + product(0, n)

        every(4, sent)
        every(4, own)
        for n in range(4):
            arrived(r.got.at[:, columns(n)], recv.at[n])

    def settle_sent(index):
        for n in range(4):
            arrived(r.part.at[:, columns(n)], r.part_send.at[index, n])

    def share_rows(array, index, b):
        @pl.when(b % 2 == 1)
        def _():
            rows = rows_of(b // 2)
            remote(
                array.at[0, rows], array.at[1, rows], r.mid_send.at[index, b // 2],
                r.mid_recv.at[index, b // 2], sibling,
            ).start()

    def shared(array, index):
        for b in range(4):
            arrived(array.at[1, rows_of(b)], r.mid_recv.at[index, b])

    def settle_shared(array, index):
        for b in range(4):
            arrived(array.at[0, rows_of(b)], r.mid_send.at[index, b])

    complete(2)
    exchange(
        0, lambda side, n: dot(r.att[side], r.wo[:, columns(n)]), r.branch,
    )

    def first_step(b):
        rows = pl.ds(b * 64, 64)
        total = r.branch[rows] + r.got[rows].astype(full)
        r.branch[rows] = total
        hidden = r.hid[0, rows].astype(full)
        stepped = unit(hidden + r.alpha_attn[...] * (unit(total) - hidden))
        r.middle[rows] = stepped
        r.mid[0, rows] = low(stepped)
        share_rows(r.mid, 0, b)

    relay_across(3)
    send_row(0, cotangent.at[0])
    send_row(3, cotangent.at[1])
    every(8, first_step)

    @pl.when(early)
    def _():
        relay(4)

    complete(3)
    for side in range(2):
        if side:
            shared(r.mid, 0)

        def lift(n, side=side):
            at = pl.ds(lane(n * 512), 512)
            r.up[side, :, at] = low(dot(r.mid[side], r.wu[:, at]))

        every(4, lift)

    relay_across(4)

    @pl.when(early)
    def _():
        relay(5)

    complete(4)
    for side in (1, 0):

        def open_gate(n, side=side):
            at = pl.ds(lane(n * 512), 512)
            gate = dot(r.mid[side], r.wg[:, at])
            r.gate[side, :, at] = low(gate)
            upward = r.up[side, :, at].astype(full) * r.scale_up[:, at]
            r.inner[side, :, at] = low(upward * silu(gate * r.scale_gate[:, at]))

        every(4, open_gate)

    complete(5)
    settle_sent(0)
    exchange(
        1, lambda side, n: dot(r.inner[side], r.wd[:, columns(n)]), r.output,
    )

    def second_step(b):
        rows = pl.ds(b * 64, 64)
        total = r.output[rows] + r.got[rows].astype(full)
        r.output[rows] = total
        start = r.middle[rows]
        r.result[rows] = low(unit(start + r.alpha_mlp[...] * (unit(total) - start)))

        @pl.when(early & (b % 2 == 1))
        def _():
            sent = rows_of(b // 2)
            remote(
                r.result.at[sent], r.hid.at[0, sent], r.result_send.at[b // 2],
                r.own_recv.at[b // 2], late_plane,
            ).start()

    every(8, second_step)

    def to_owners(array, held, to_ref):
        for to in range(4):
            src = held.at[rows_of(to)]
            dst = to_ref.at[s // 2, pl.ds(c * BLOCK, BLOCK)]
            recv = r.owner_recv.at[array, s // 2, c]
            here = (s == to) & (c == layer)

            @pl.when(here)
            def _():
                pltpu.make_async_copy(src, dst, r.owner_send.at[array, to]).start()

            @pl.when(jnp.logical_not(here))
            def _():
                remote(src, dst, r.owner_send.at[array, to], recv, (layer, to, f)).start()

    to_owners(0, r.result, o_hidden)

    @pl.when(late)
    def _():
        for b in range(4):
            held = o_row.at[rows_of(b)]
            arrived(held, r.row_recv.at[b])
            pltpu.make_async_copy(held, r.grad_in.at[rows_of(b)], r.grad_recv.at[b]).start()

    def near_of(k):
        return fx + (fy - fx) * (k % 2)

    def far_of(k):
        return fy + (fx - fy) * (k % 2)

    def with_source(k, work):
        @pl.when(k < 4)
        def _():
            at = pl.ds(lane((k % 2) * 512), 512)
            work(lambda to: g_down.at[pl.ds(to * 512 + (k // 2) * 256, 256), at])

        for begins, ref in ((4, g_up), (8, g_gate), (12, g_out), (13, g_qkv)):

            @pl.when((k >= begins) & (k < begins + ref.shape[1] // 512))
            def _():
                at = pl.ds(lane((k - begins) * 512), 512)
                work(lambda to: ref.at[pl.ds(to * 256, 256), at])

    def begin(k):
        def start(source):
            to = (c, s, near_of(k))
            remote(source(3 - f), near_far.at[k], r.send_far.at[k], r.recv_far.at[k], to).start()
            remote(
                source(near_of(k)), near_own.at[k], r.send_own.at[k], r.recv_own.at[k], to
            ).start()

        with_source(k, start)

    places = {
        "pass": (r.wu, 0, 4), "own": (r.wu, 4, 4), "pair": (r.wu, 8, 4), "far": (r.wu, 12, 2),
        "other": (r.wu, 14, 2), "late": (r.wg, 0, 4), "near": (r.wg, 4, 2), "last": (r.wg, 6, 2),
        "side": (r.wg, 8, 2),
    }
    order = list(places)

    def slot(name, k):
        ref, base, count = places[name]
        n = base + k % count
        return ref.at[pl.ds(n // 4 * 256, 256), pl.ds(lane(n % 4 * 512), 512)]

    def load_sem(name, k):
        return r.load.at[order.index(name), k % places[name][2]]

    def fetch(src, name, k):
        pltpu.make_async_copy(src, slot(name, k), load_sem(name, k)).start()

    def fetched(name, k):
        arrived(slot(name, k), load_sem(name, k))

    def again(k, work):
        pl.when(k >= 4)(work)

    def pass_on(k):
        arrived(near_far.at[k], r.recv_far.at[k])

        again(k, lambda: arrived(slot("pass", k), r.send_next.at[k - 4]))
        with_source(k, lambda source: fetch(source(far_of(k)), "pass", k))
        fetch(near_far.at[k], "far", k)
        fetched("pass", k)
        fetched("far", k)
        total = slot("pass", k)
        add(total, total, slot("far", k))
        remote(
            total, far_in.at[k], r.send_next.at[k], r.recv_next.at[k], (c, s, far_of(k))
        ).start()

    def plane_total(k):
        arrived(near_own.at[k], r.recv_own.at[k])
        arrived(far_in.at[k], r.recv_next.at[k])

        again(k, lambda: arrived(slot("own", k), r.send_z.at[k - 4]))
        with_source(k, lambda source: fetch(source(f), "own", k))
        fetch(near_own.at[k], "near", k)
        fetch(far_in.at[k], "last", k)
        for name in ("own", "near", "last"):
            fetched(name, k)
        own, send = slot("own", k), r.send_z.at[k]
        add(own, own, slot("near", k), slot("last", k))
        pltpu.make_async_copy(own, plane_sum.at[k], r.stored.at[k]).start()

        @pl.when(s == 0)
        def _():
            remote(own, from_left.at[k], send, r.recv_left.at[k], (c, 1, f)).start()

        @pl.when(s == 3)
        def _():
            remote(own, from_right.at[k], send, r.recv_right.at[k], (c, 2, f)).start()

        @pl.when(early)
        def _():
            remote(own, pair_sum.at[k], send, r.recv_pair.at[k], (c, 3 - s, f)).start()

    def plane_done(k):
        arrived(plane_sum.at[k], r.stored.at[k])

    def in_plane(t):
        @pl.when((t + AHEAD < CHUNKS) & (early | (t == 0) | (t > 3)))
        def _():
            begin(t + AHEAD)

        @pl.when(late & (t == 3))
        def _():
            for k in range(4, 7):
                begin(k)

        for lag, work in ((3, plane_done), (2, plane_total), (0, pass_on)):
            @pl.when((t >= lag) & (t < lag + CHUNKS))
            def _():
                work(t - lag)

    def relay_on(k):
        @pl.when(s == 1)
        def _():
            arrived(from_left.at[k], r.recv_left.at[k])
            remote(
                from_left.at[k], from_left.at[k], r.send_on.at[k], r.recv_left.at[k], (c, 2, f)
            ).start()

        @pl.when(s == 2)
        def _():
            arrived(from_right.at[k], r.recv_right.at[k])
            remote(
                from_right.at[k], from_right.at[k], r.send_on.at[k], r.recv_right.at[k], (c, 1, f)
            ).start()

    def relay_out(k):
        @pl.when(s == 1)
        def _():
            arrived(from_right.at[k], r.recv_right.at[k])
            remote(
                from_right.at[k], from_right.at[k], r.send_back.at[k], r.recv_right.at[k], (c, 0, f)
            ).start()

        @pl.when(s == 2)
        def _():
            arrived(from_left.at[k], r.recv_left.at[k])
            remote(
                from_left.at[k], from_left.at[k], r.send_back.at[k], r.recv_left.at[k], (c, 3, f)
            ).start()

    def everything(chunk):
        return chunk

    def place(k, owner, chunk):
        def put(pieces):
            for src, dst in pieces:

                @pl.when(c == owner)
                def _():
                    pltpu.make_async_copy(src(chunk), dst, r.keep.at[k]).start()

                @pl.when(c != owner)
                def _():
                    remote(src(chunk), dst, r.give.at[k], r.given.at[k], sibling).start()

        @pl.when(k < 4)
        def _():
            rows = pl.ds(c * 512 + (k // 2) * 256, 256)
            put([(everything, o_down.at[rows, pl.ds(lane((k % 2) * 512), 512)])])

        @pl.when((k >= 4) & (k < 12))
        def _():
            put([(everything, o_in.at[:, pl.ds(lane((k - 4) * 1024 + c * 512), 512)])])

        @pl.when(k == 12)
        def _():
            put([
                (
                    lambda chunk, part=part: chunk.at[pl.ds(part * 128, 128)],
                    o_out.at[pl.ds(c * 128, 128), pl.ds(part * 512, 512)],
                )
                for part in range(2)
            ])

        @pl.when(k > 12)
        def _():
            put([
                (
                    lambda chunk, part=part: chunk.at[:, pl.ds(part * 128, 128)],
                    o_qkv.at[:, pl.ds(lane((k - 13) * 1024 + part * 256 + c * 128), 128)],
                )
                for part in range(4)
            ])

    def placed(k, owner):
        @pl.when(c == owner)
        def _():
            arrived(plane_sum.at[k], r.keep.at[k])

        @pl.when(c != owner)
        def _():
            arrived(plane_sum.at[k], r.give.at[k])

    def pair_load(k):
        @pl.when(early)
        def _():
            arrived(pair_sum.at[k], r.recv_pair.at[k])

            @pl.when(k >= 4)
            def _():
                arrived(slot("pair", k), r.send_out.at[k - 4])
                placed(k - 4, 0)

            fetch(plane_sum.at[k], "pair", k)
            fetch(pair_sum.at[k], "other", k)

    def pair_send(k):
        @pl.when(early)
        def _():
            fetched("pair", k)
            fetched("other", k)
            total = slot("pair", k)
            add(total, total, slot("other", k))
            remote(total, pair_sum.at[k], r.send_out.at[k], r.recv_pair.at[k], late_plane).start()
            place(k, 0, total)

    def pair_take(k):
        @pl.when(late)
        def _():
            arrived(pair_sum.at[k], r.recv_pair.at[k])
            again(k, lambda: placed(k - 4, 0))
            fetch(pair_sum.at[k], "pair", k)
            fetched("pair", k)
            place(k, 0, slot("pair", k))

    def late_load(k):
        again(k, lambda: placed(k - 4, 1))

        @pl.when(early)
        def _():
            fetch(from_left.at[k], "late", k)
            fetch(from_right.at[k], "side", k)

        @pl.when(s == 0)
        def _():
            arrived(from_right.at[k], r.recv_right.at[k])
            fetch(from_right.at[k], "side", k)

        @pl.when(s == 3)
        def _():
            arrived(from_left.at[k], r.recv_left.at[k])
            fetch(from_left.at[k], "side", k)

        @pl.when(late)
        def _():
            fetch(plane_sum.at[k], "late", k)

    def late_place(k):
        fetched("late", k)
        fetched("side", k)
        total = slot("late", k)
        add(total, total, slot("side", k))
        place(k, 1, total)

    def between_planes(t):
        @pl.when(early)
        def _():
            for lag, work in ((-4, relay_on), (-2, relay_out)):
                @pl.when(t < lag + CHUNKS)
                def _():
                    work(t - lag)

        for lag, work in (
            (4, pair_load), (4, pair_send), (19, pair_take), (6 + 10 * layer, late_load),
            (6 + 10 * layer, late_place),
        ):
            @pl.when((t >= lag) & (t < lag + CHUNKS))
            def _():
                work(t - lag)

    def weight_grad(count, tile, width_of, pieces):
        def stage(n):
            return r.wd.at[pl.ds((n % 2) * 256, 256), pl.ds(0, width_of)]

        def work(n):
            @pl.when(n >= 2)
            def _():
                arrived(stage(n), r.staged.at[n % 2])

            left, right = tile(n)
            total = contract_rows(left(0), right(0)) + contract_rows(left(1), right(1))
            stage(n)[...] = low(total)
            for src, dst in pieces(n, stage(n)):
                pltpu.make_async_copy(src, dst, r.staged.at[n % 2]).start()

        every(count, work)
        for n in range(count - 2, count):
            arrived(stage(n), r.staged.at[n % 2])

    def grad_of_down():
        weight_grad(
            8,
            lambda n: (lambda side: r.inner[side, :, columns(n)], lambda side: r.grad_rows[side]),
            width,
            lambda n, src: [(src, g_down.at[pl.ds(n * 256, 256)])],
        )

    def grad_of_lift(ref, to):
        weight_grad(
            8,
            lambda n: (
                lambda side: r.mid[side, :, columns(n // 2)],
                lambda side: ref[side, :, pl.ds(lane((n % 2) * 1024), 1024)],
            ),
            1024,
            lambda n, src: [
                (src, to.at[pl.ds((n // 2) * 256, 256), pl.ds(lane((n % 2) * 1024), 1024)])
            ],
        )

    def grad_of_out():
        weight_grad(
            2,
            lambda n: (lambda side: r.att[side, :, columns(n)], lambda side: r.grad_rows[side]),
            width,
            lambda n, src: [
                (
                    src.at[pl.ds(owner * 128, 128), pl.ds(part * 512, 512)],
                    g_out.at[pl.ds(n * 512 + owner * 256 + part * 128, 128)],
                )
                for owner in range(2)
                for part in range(2)
            ],
        )

    def grad_of_qkv():
        weight_grad(
            12,
            lambda n: (
                lambda side: r.hid[side, :, columns(n // 3)],
                lambda side: r.mixed[side, :, pl.ds(lane((n % 3) * 512), 512)],
            ),
            512,
            lambda n, src: [
                (src, g_qkv.at[pl.ds((n // 3) * 256, 256), pl.ds(lane((n % 3) * 512), 512)])
            ],
        )

    fits = (place_col >= start_row[...]) & (place_col <= place_row[...])
    r.bias[...] = jnp.where(fits, 0.0, MASKED)
    settle_relays()
    settle_spread()

    @pl.when(early)
    def _():
        relay_on(0)

    def second_back(b):
        rows = pl.ds(b * 64, 64)

        @pl.when(b % 2 == 0)
        def _():
            arrived(r.grad_in.at[rows_of(b // 2)], r.grad_recv.at[b // 2])

        start = r.hid[0, rows].astype(full)
        middle = unit(start + r.alpha_attn[...] * (unit(r.branch[rows]) - start))
        total = r.output[rows]
        change = unit(total) - middle
        grad = unit_back(middle + r.alpha_mlp[...] * change, r.grad_in[rows].astype(full))
        r.sum_alphas[1:2] += jnp.sum(grad * change, axis=0, keepdims=True)
        r.grad_rows[0, rows] = low(unit_back(total, r.alpha_mlp[...] * grad))
        r.middle[rows] = grad * (1.0 - r.alpha_mlp[...])
        share_rows(r.grad_rows, 1, b)

    every(8, second_back)

    for side in range(2):
        if side:
            shared(r.grad_rows, 1)

        def close_gate(n, side=side):
            at = pl.ds(lane(n * 512), 512)
            grad = last_dims(r.grad_rows[side], r.wd[pl.ds(n * 512, 512)])
            lift_up = r.up[side, :, at].astype(full)
            lift_gate = r.gate[side, :, at].astype(full)
            gating = lift_gate * r.scale_gate[:, at]
            sigmoid = jax.nn.sigmoid(gating)
            grad_up = grad * (gating * sigmoid)
            grad_gate = (
                grad * (lift_up * r.scale_up[:, at]) * sigmoid * (1.0 + gating * (1.0 - sigmoid))
            )
            r.sum_scales[0:1, at] += jnp.sum(grad_up * lift_up, axis=0, keepdims=True)
            r.sum_scales[1:2, at] += jnp.sum(grad_gate * lift_gate, axis=0, keepdims=True)
            r.up[side, :, at] = low(grad_up * r.scale_up[:, at])
            r.gate[side, :, at] = low(grad_gate * r.scale_gate[:, at])

        every(4, close_gate)
    grad_of_down()
    for k in range(AHEAD):
        begin(k)

    def relays(on, out):
        @pl.when(early)
        def _():
            for k in on:
                relay_on(k)
            for k in out:
                relay_out(k)

    relays((1, 2), (0,))

    @pl.when(early)
    def _():
        grad_of_lift(r.up, g_up)

    relays((3,), (1,))

    def lifted(side, n):
        rows = pl.ds(n * 256, 256)
        return last_dims(r.up[side], r.wu[rows]) + last_dims(r.gate[side], r.wg[rows])

    settle_sent(1)
    exchange(2, lifted, r.middle)
    in_plane(0)
    relays((4,), (2,))
    settle_shared(r.grad_rows, 1)

    def first_back(b):
        rows = pl.ds(b * 64, 64)
        start = r.hid[0, rows].astype(full)
        total = r.branch[rows]
        change = unit(total) - start
        grad = r.middle[rows] + r.got[rows].astype(full)
        grad = unit_back(start + r.alpha_attn[...] * change, grad)
        r.sum_alphas[0:1] += jnp.sum(grad * change, axis=0, keepdims=True)
        r.grad_rows[0, rows] = low(unit_back(total, r.alpha_attn[...] * grad))
        r.middle[rows] = grad * (1.0 - r.alpha_attn[...])
        share_rows(r.grad_rows, 2, b)

    every(8, first_back)

    shared(r.grad_rows, 2)

    marks = (
        lax.broadcasted_iota(jnp.int32, (8, 2 * HEAD), 1) // HEAD
        == lax.broadcasted_iota(jnp.int32, (8, 2 * HEAD), 0)
    ).astype(jnp.bfloat16)

    def attend_back(pair):
        @pl.when(pair % 2 == 0)
        def _():
            in_plane(1 + pair // 2)

        @pl.when(early & (pair % 2 == 0))
        def _():
            relay_on(5 + pair // 2)
            relay_out(3 + pair // 2)

        prepare(pair)
        at = lanes_of(pair, 0)
        heads = r.wo[pl.ds(pair * 128, 128)]
        merge(r.grads, *(low(last_dims(r.grad_rows[side], heads)) for side in range(2)))
        merge(r.raw, r.att[0, :, at], r.att[1, :, at])
        r.dk[...] = jnp.zeros_like(r.dk)
        r.dv[...] = jnp.zeros_like(r.dv)
        for q in range(4):
            at = slice(q * 256, (q + 1) * 256)
            upto = slice(0, (q + 1) * 256)
            deltas = row_sums(r.grads[at].astype(full) * r.raw[at].astype(full), marks)
            delta = jnp.concatenate([deltas[h : h + 1] for h in range(2)], axis=1)
            log_sum = jnp.concatenate([r.log_sums[pair, h : h + 1, at] for h in range(2)], axis=1)
            query, grad, key = of_heads(r.queries[at]), of_heads(r.grads[at]), r.keys[upto]
            mask = jnp.concatenate([r.bias[upto, at]] * 2, axis=1)
            weighted = jnp.exp(last_dims(key, query) + (mask - log_sum))
            grad_scores = low(
                weighted * (last_dims(r.values[upto, : 2 * HEAD], grad) - delta)
            )
            r.dv[upto] += dot(low(weighted), grad)
            r.dk[upto] += dot(grad_scores, query)
            to_queries = contract_rows(grad_scores, key)
            r.dq[at] = (
                head_lanes(0, full) * to_queries[:256] + head_lanes(1, full) * to_queries[256:]
            )

        scale = r.flat[pair, pl.ds(c, 1), :]
        scale_sum = 0.0
        for part, grad in enumerate((r.dq, r.dk)):
            normed, factor = normal(pair, part)
            found = grad[...] * SCORE_SCALE if part == 0 else grad[...]
            scale_sum = scale_sum + jnp.sum(found * normed, axis=0, keepdims=True)
            step = found * scale
            grad[...] = factor * (step - normed * sums_of_halves(normed * step))
        r.sum_qk[pl.ds(pair, 1)] = scale_sum
        for part, grad in enumerate((r.dq, r.dk, r.dv)):
            at = lanes_of(pair, part)
            for q in range(4):
                rows = slice(q * BLOCK, (q + 1) * BLOCK)
                r.mixed[0, rows, at] = low(grad[q * 256 : q * 256 + BLOCK])
                r.mixed[1, rows, at] = low(grad[q * 256 + BLOCK : (q + 1) * 256])

    every(4, attend_back)

    relays((7,), (5,))
    settle_sent(2)
    exchange(
        3, lambda side, n: last_dims(r.mixed[side], r.wq[pl.ds(n * 256, 256)]), r.middle,
    )

    for b in range(4):
        rows = rows_of(b)

        @pl.when(early)
        def _():
            arrived(r.result.at[rows], r.result_send.at[b])

        arrived(r.result.at[rows], r.owner_send.at[0, b])

    def finish(b):
        rows = rows_of(b)
        r.result[rows] = low(r.middle[rows] + r.got[rows].astype(full))

        @pl.when(late)
        def _():
            remote(
                r.result.at[rows], r.grad_in.at[rows], r.result_send.at[b], r.grad_recv.at[b],
                early_plane,
            ).start()

    every(4, finish)
    to_owners(1, r.result, o_grad)

    for b in range(4):
        arrived(r.flags.at[b], r.flag_recv.at[b])
    r.flags_full[...] = r.flags[...].astype(full)
    ones = jnp.ones((8, width), jnp.bfloat16)
    for b in range(4):
        squares = row_sums(r.branch[rows_of(b)] * r.branch[rows_of(b)], ones)[:1]
        r.sum_valid[...] += squares * r.flags_full[b, pl.ds(c, 1), :]

    for owner in range(4):
        r.terms[owner, pl.ds(c, 1), :] = r.sum_qk[owner : owner + 1]
        for n in range(2):
            for j in range(4):
                at = slice((owner % 2 * 2 + n) * 512 + j * 128, (owner % 2 * 2 + n) * 512 + (j + 1) * 128)
                scale = math.sqrt(width) if owner // 2 else 1.0
                r.terms[owner, pl.ds(2 + n * 8 + j + c * 4, 1), :] = (
                    r.sum_scales[owner // 2 : owner // 2 + 1, at] * scale
                )
        for j in range(4):
            at = slice(owner % 2 * 512 + j * 128, owner % 2 * 512 + (j + 1) * 128)
            r.terms[owner, 18 + j : 19 + j, :] = r.sum_alphas[owner // 2 : owner // 2 + 1, at]
        r.terms[owner, 22:23, :] = r.sum_valid[...]
    flow = Flow((r.v0, r.v1, r.v2, r.v3, r.v4, r.v5, r.v6, r.v7), r.vector)
    flow.begin(lambda to: r.terms.at[to])

    @pl.when(late)
    def _():
        grad_of_lift(r.up, g_up)

    in_plane(3)

    def step(t):
        @pl.when(t == 4)
        def _():
            grad_of_lift(r.gate, g_gate)

        @pl.when(t == 8)
        def _():
            grad_of_out()
            grad_of_qkv()

        between_planes(t)
        in_plane(t)
        for at, work in ((6, flow.pass_on), (8, flow.finish_plane), (12, flow.middle_planes)):
            pl.when(t == at)(work)

        @pl.when(t == 16 + 18 * layer)
        def _():
            flow.all_planes(o_vectors.at[c])

    every(CHUNKS + 19 - 4, lambda n: step(n + 4))

    def settle(k):
        chunk = plane_sum.at[k]
        for sem in (r.send_own, r.send_far, r.given):
            arrived(chunk, sem.at[k])

        @pl.when(early)
        def _():
            arrived(chunk, r.send_on.at[k])
            arrived(chunk, r.send_back.at[k])

        @pl.when(k >= CHUNKS - 4)
        def _():
            arrived(chunk, r.send_next.at[k])
            arrived(chunk, r.send_z.at[k])
            placed(k, 1)

        @pl.when(k >= CHUNKS - 4)
        def _():
            placed(k, 0)

        @pl.when(early & (k >= CHUNKS - 4))
        def _():
            arrived(chunk, r.send_out.at[k])

    every(CHUNKS, settle)
    flow.settle()
    settle_shared(r.mid, 0)
    settle_shared(r.grad_rows, 2)
    settle_sent(3)
    for b in range(4):
        rows = rows_of(b)
        arrived(r.hid.at[1, rows], r.oth_send.at[b])

        @pl.when(late)
        def _():
            arrived(r.result.at[rows], r.result_send.at[b])

        @pl.when(s != b)
        def _():
            arrived(o_row.at[rows], r.row_send.at[b])
            arrived(r.flags.at[b], r.flag_send.at[b])

        arrived(r.result.at[rows], r.owner_send.at[1, b])

    for array, to_ref in enumerate((o_hidden, o_grad)):
        for micro in range(2):
            for core in range(2):

                @pl.when(jnp.logical_not((c == layer) & (c == core) & (s // 2 == micro)))
                def _():
                    arrived(
                        to_ref.at[micro, pl.ds(core * BLOCK, BLOCK)],
                        r.owner_recv.at[array, micro, core],
                    )


def relay_all(w_qkv, w_out, w_in, w_down, vectors, valid, tokens, cotangent, places):
    width = w_out.shape[1]
    units = w_down.shape[0] * 4
    half = units // 2
    place, start = places

    def low_shape(*shape):
        return jax.ShapeDtypeStruct(shape, jnp.bfloat16)

    chunks = low_shape(CHUNKS, 256, 512)
    rows = low_shape(2, 2 * BLOCK, width)
    anywhere = pl.BlockSpec(memory_space=pl.ANY)
    near = pl.BlockSpec(memory_space=pltpu.VMEM)
    scratch = scratch_of(width, units, vectors.shape[0], valid.shape[1])
    out_shape = [
        low_shape(half // 2, width), low_shape(width // 4, 2 * units), low_shape(width // 4, width),
        low_shape(width // 4, 3 * width), jax.ShapeDtypeStruct((2, 24, 128), jnp.float32),
        rows, rows, low_shape(4 * BLOCK, width),
        low_shape(half, width), low_shape(width, half), low_shape(width, half),
        low_shape(width, width // 2), low_shape(width, 3 * width // 2),
    ] + [chunks] * 7
    return pl.pallas_call(
        functools.partial(relay_kernel, tuple(scratch)),
        out_shape=out_shape,
        in_specs=[anywhere] * 8 + [near] * 3,
        out_specs=[anywhere] * len(out_shape),
        scratch_shapes=list(scratch.values()),
        compiler_params=pltpu.CompilerParams(
            collective_id=0, has_side_effects=True, vmem_limit_bytes=62 * 2**20
        ),
    )(
        w_qkv, w_out, w_in, w_down, vectors, valid, tokens, cotangent,
        start[:, None], place[None, :], start[None, :],
    )[:7]


def per_device(
    tokens, cotangent, lengths, valid_mask, w_qkv, w_out, w_in, w_down, qk_scale, mlp_scale, alphas
):
    c, s, f, _, _, layer = position()
    second = layer == 1
    micro = s // 2
    width = tokens.shape[3]
    group = tokens.shape[2]
    units = w_down.shape[1] * 4

    vectors = jnp.concatenate([qk_scale[0], mlp_scale[0], alphas[0]])
    vectors = jnp.pad(vectors, (0, 32 * 128 - vectors.shape[0])).reshape(32, 128)
    valid = low(jnp.pad(valid_mask[:, 0], ((0, 0), (0, 16 * 128 - group)))).reshape(2, 16, 128)
    index = jnp.arange(4 * group, dtype=jnp.int32)
    place = (index // 256) * 256 + (((index // BLOCK) + c) % 2) * BLOCK + index % BLOCK
    ends = jnp.cumsum(pick(lengths, micro, 0)[0])[:-1]
    passed = place[:, None] >= ends[None, :]
    start = jnp.max(jnp.where(passed, ends[None, :], 0), axis=1)
    places = (place, start)
    grad_down, grad_in_proj, grad_out, grad_qkv, vectors, hidden_out, grad_in = relay_all(
        w_qkv[0], w_out[0], w_in[0], w_down[0], vectors, valid, tokens[:, 0], cotangent[:, 0], places
    )
    cut_qk, cut_mlp = qk_scale.shape[1], qk_scale.shape[1] + mlp_scale.shape[1]
    full = jnp.sum(vectors, axis=0).reshape(-1)
    cuts = (cut_qk, cut_mlp, cut_mlp + alphas.shape[1])
    grad_qk_scale = full[: cuts[0]][None]
    grad_mlp_scale = full[cuts[0] : cuts[1]][None]
    grad_alphas = full[cuts[1] : cuts[2]][None]
    token_count = tokens.shape[0] * lax.axis_size("fsdp") * 4 * group
    total = jnp.sum(full[cuts[2] : cuts[2] + 128], keepdims=True)
    rms_stats = jnp.sqrt(total / token_count + epsilon)
    as_float = [
        part.astype(jnp.float32)[None] for part in (grad_qkv, grad_out, grad_in_proj, grad_down)
    ]
    return (
        hidden_out[None, :, None], grad_in.astype(jnp.float32)[None, :, None], *as_float,
        grad_qk_scale, grad_mlp_scale, grad_alphas, rms_stats,
    )


def solution(mesh):
    placed = (
        P(None, "fsdp", "seq", None),
        P(None, "fsdp", "seq", None),
        P(None, "fsdp", None),
        P(None, "fsdp", "seq"),
        P("section", "fsdp", None),
        P("section", "fsdp", None),
        P("section", "fsdp", None),
        P("section", "fsdp", None),
        P("section", "fsdp"),
        P("section", "fsdp"),
        P("section", "fsdp"),
    )
    planes = mesh.shape["section"] == 2 and mesh.shape["seq"] == 4 and mesh.shape["fsdp"] == 4
    return jax.shard_map(
        per_device if planes else per_device_general,
        mesh=mesh,
        in_specs=placed,
        out_specs=(
            P("section", None, "fsdp", "seq", None),
            P("section", None, "fsdp", "seq", None),
            P("section", "fsdp", None),
            P("section", "fsdp", None),
            P("section", "fsdp", None),
            P("section", "fsdp", None),
            P("section", "fsdp"),
            P("section", "fsdp"),
            P("section", "fsdp"),
            P("section"),
        ),
        check_vma=False,
    )
```

```python
import functools
import math
import types

import jax
import jax.numpy as jnp
from jax import lax
from jax.experimental import pallas as pl
from jax.experimental.pallas import tpu as pltpu
from jax.sharding import PartitionSpec as P

HEAD = 64


epsilon = 1e-06


def shifted(block, axis, distance):
    devices = range(lax.axis_size(axis))
    route = [(i - distance, i) for i in devices if i - distance in devices]
    return lax.ppermute(block, axis, route)


def for_sending(x):
    return jax.tree.map(lambda a: a.astype(jnp.bfloat16) if a.dtype == jnp.float32 else a, x)


def unit(values):
    return values * lax.rsqrt(jnp.sum(values * values, axis=-1, keepdims=True) + epsilon)


def unit_back(values, grad):
    factor = lax.rsqrt(jnp.sum(values * values, axis=-1, keepdims=True) + epsilon)
    normed = values * factor
    return factor * (grad - normed * jnp.sum(normed * grad, axis=-1, keepdims=True))


def contract_rows(left, right):
    return lax.dot_general(
        left, right, (((0,), (0,)), ((), ())), preferred_element_type=jnp.float32
    )


def contract_cols(left, right):
    return lax.dot_general(
        left, right, (((1,), (1,)), ((), ())), preferred_element_type=jnp.float32
    )


def segments_of(row_lengths, seq_len):
    ends = jnp.cumsum(row_lengths)[:-1]
    place = jnp.arange(seq_len, dtype=jnp.int32)
    return (place, jnp.sum((place[:, None] >= ends[None, :]).astype(jnp.int32), axis=1))


def allowed_pairs(row_lengths, offset, group, seq_len):
    key_place, key_segment = segments_of(row_lengths, seq_len)
    query_place = offset + jnp.arange(group, dtype=jnp.int32)
    query_segment = lax.dynamic_slice_in_dim(key_segment, offset, group)
    return (query_segment[:, None] == key_segment[None, :]) & (
        key_place[None, :] <= query_place[:, None]
    )


def masked_scores(queries, key_heads, allowed):
    scores = jnp.einsum(
        "qhd,khd->hqk", queries, key_heads, preferred_element_type=jnp.float32
    ) * math.sqrt(HEAD)
    return jnp.where(allowed[None], scores, -1e30)


def forward_layer(hidden_b, params, allowed, valid):
    w_qkv, w_out, w_in, w_down, qk_scale, mlp_scale, alphas = params
    count, width = hidden_b.shape
    heads = width // HEAD
    hidden = hidden_b.astype(jnp.float32)
    mixed = jnp.dot(hidden_b, w_qkv, preferred_element_type=jnp.float32)
    query_raw = mixed[:, :width].reshape(count, heads, HEAD)
    key_raw = mixed[:, width : 2 * width].reshape(count, heads, HEAD)
    head_scale = qk_scale.astype(jnp.float32).reshape(heads, HEAD)
    query_b = (unit(query_raw) * head_scale).astype(jnp.bfloat16)
    key_b = (unit(key_raw) * head_scale).astype(jnp.bfloat16).reshape(count, width)
    value_b = mixed[:, 2 * width :].astype(jnp.bfloat16)
    keys, values = (
        lax.all_gather(key_b, "seq", axis=0, tiled=True),
        lax.all_gather(value_b, "seq", axis=0, tiled=True),
    )
    key_heads = keys.reshape(-1, heads, HEAD)
    value_heads = values.reshape(-1, heads, HEAD)
    scores = masked_scores(query_b, key_heads, allowed)
    highest = jnp.max(scores, axis=-1, keepdims=True)
    weights = jnp.exp(scores - highest)
    denominator = jnp.sum(weights, axis=-1, keepdims=True)
    weights = weights / denominator
    log_total = highest + jnp.log(denominator)
    attended = jnp.einsum(
        "hqk,khd->qhd",
        weights.astype(jnp.bfloat16),
        value_heads,
        preferred_element_type=jnp.float32,
    )
    attended_b = attended.reshape(count, width).astype(jnp.bfloat16)
    branch = jnp.dot(attended_b, w_out, preferred_element_type=jnp.float32)
    statistic = jnp.sum(valid * jnp.sum(branch * branch, axis=-1))
    step_sizes = alphas.astype(jnp.float32)
    first_sum = hidden + step_sizes[:width] * (unit(branch) - hidden)
    middle = unit(first_sum)
    middle_b = middle.astype(jnp.bfloat16)
    lifted = jnp.dot(middle_b, w_in, preferred_element_type=jnp.float32)
    units_count = lifted.shape[1] // 2
    scales = mlp_scale.astype(jnp.float32)
    upward = lifted[:, :units_count] * scales[:units_count]
    gating = lifted[:, units_count:] * scales[units_count:] * math.sqrt(width)
    inner_b = (upward * jax.nn.silu(gating)).astype(jnp.bfloat16)
    output = jnp.dot(inner_b, w_down, preferred_element_type=jnp.float32)
    second_sum = middle + step_sizes[width:] * (unit(output) - middle)
    result = unit(second_sum).astype(jnp.bfloat16)
    kept = (
        hidden_b,
        query_raw,
        key_raw,
        query_b,
        keys,
        values,
        log_total,
        attended_b,
        branch,
        first_sum,
        middle_b,
        lifted,
        inner_b,
        output,
        second_sum,
    )
    return (result, kept, statistic)


def backward_layer(kept, params, grad_out, allowed):
    (
        hidden_b,
        query_raw,
        key_raw,
        query_b,
        keys,
        values,
        log_total,
        attended_b,
        branch,
        first_sum,
        middle_b,
        lifted,
        inner_b,
        output,
        second_sum,
    ) = kept
    w_qkv, w_out, w_in, w_down, qk_scale, mlp_scale, alphas = params
    count, width = hidden_b.shape
    heads = width // HEAD
    hidden = hidden_b.astype(jnp.float32)
    step_sizes = alphas.astype(jnp.float32)
    alpha_attn = step_sizes[:width]
    alpha_mlp = step_sizes[width:]
    middle = unit(first_sum)
    grad_second = unit_back(second_sum, grad_out)
    grad_alpha_mlp = jnp.sum(grad_second * (unit(output) - middle), axis=0)
    grad_output = unit_back(output, alpha_mlp * grad_second).astype(jnp.bfloat16)
    grad_middle = grad_second * (1.0 - alpha_mlp)
    grad_down = contract_rows(inner_b, grad_output)
    grad_inner = contract_cols(grad_output, w_down)
    units_count = lifted.shape[1] // 2
    scales = mlp_scale.astype(jnp.float32)
    root = math.sqrt(width)
    lift_up = lifted[:, :units_count]
    lift_gate = lifted[:, units_count:]
    upward = lift_up * scales[:units_count]
    gating = lift_gate * scales[units_count:] * root
    sigmoid = jax.nn.sigmoid(gating)
    grad_upward = grad_inner * jax.nn.silu(gating)
    grad_gating = grad_inner * upward * sigmoid * (1.0 + gating * (1.0 - sigmoid))
    grad_scale_mlp = jnp.concatenate(
        [jnp.sum(grad_upward * lift_up, axis=0), jnp.sum(grad_gating * root * lift_gate, axis=0)]
    )
    grad_lifted = jnp.concatenate(
        [grad_upward * scales[:units_count], grad_gating * root * scales[units_count:]], axis=1
    ).astype(jnp.bfloat16)
    grad_in_proj = contract_rows(middle_b, grad_lifted)
    grad_middle = grad_middle + contract_cols(grad_lifted, w_in)
    grad_first = unit_back(first_sum, grad_middle)
    grad_alpha_attn = jnp.sum(grad_first * (unit(branch) - hidden), axis=0)
    grad_branch = unit_back(branch, alpha_attn * grad_first).astype(jnp.bfloat16)
    grad_hidden = grad_first * (1.0 - alpha_attn)
    grad_out_proj = contract_rows(attended_b, grad_branch)
    grad_attended = (
        contract_cols(grad_branch, w_out).astype(jnp.bfloat16).reshape(count, heads, HEAD)
    )
    key_heads = keys.reshape(-1, heads, HEAD)
    value_heads = values.reshape(-1, heads, HEAD)
    scores = masked_scores(query_b, key_heads, allowed)
    weights = jnp.exp(scores - log_total)
    grad_weights = jnp.einsum(
        "qhd,khd->hqk", grad_attended, value_heads, preferred_element_type=jnp.float32
    )
    delta = jnp.sum(weights * grad_weights, axis=-1, keepdims=True)
    grad_scores = (weights * (grad_weights - delta)).astype(jnp.bfloat16)
    score_scale = math.sqrt(HEAD)
    grad_query = (
        jnp.einsum("hqk,khd->qhd", grad_scores, key_heads, preferred_element_type=jnp.float32)
        * score_scale
    )
    seq_len = keys.shape[0]
    grad_keys = (
        jnp.einsum("hqk,qhd->khd", grad_scores, query_b, preferred_element_type=jnp.float32)
        * score_scale
    )
    grad_values = jnp.einsum(
        "hqk,qhd->khd",
        weights.astype(jnp.bfloat16),
        grad_attended,
        preferred_element_type=jnp.float32,
    )
    grad_key_own, grad_value_own = (
        lax.psum_scatter(
            grad_keys.reshape(seq_len, width).astype(jnp.bfloat16),
            "seq",
            scatter_dimension=0,
            tiled=True,
        ).astype(jnp.float32),
        lax.psum_scatter(
            grad_values.reshape(seq_len, width).astype(jnp.bfloat16),
            "seq",
            scatter_dimension=0,
            tiled=True,
        ).astype(jnp.float32),
    )
    head_scale = qk_scale.astype(jnp.float32).reshape(heads, HEAD)
    grad_key_heads = grad_key_own.reshape(count, heads, HEAD)
    grad_scale_qk = (
        jnp.sum(grad_query * unit(query_raw), axis=0)
        + jnp.sum(grad_key_heads * unit(key_raw), axis=0)
    ).reshape(width)
    grad_query_raw = unit_back(query_raw, grad_query * head_scale).reshape(count, width)
    grad_key_raw = unit_back(key_raw, grad_key_heads * head_scale).reshape(count, width)
    grad_mixed = jnp.concatenate([grad_query_raw, grad_key_raw, grad_value_own], axis=1).astype(
        jnp.bfloat16
    )
    grad_qkv = contract_rows(hidden_b, grad_mixed)
    grad_hidden = grad_hidden + contract_cols(grad_mixed, w_qkv)
    grad_step_sizes = jnp.concatenate([grad_alpha_attn, grad_alpha_mlp])
    grads = (
        grad_qkv,
        grad_out_proj,
        grad_in_proj,
        grad_down,
        grad_scale_qk,
        grad_scale_mlp,
        grad_step_sizes,
    )
    return (grad_hidden, grads)


def per_device_general(
    tokens, cotangent, lengths, valid_mask, w_qkv, w_out, w_in, w_down, qk_scale, mlp_scale, alphas
):
    shards = (w_qkv, w_out, w_in, w_down, qk_scale, mlp_scale, alphas)
    gathered = (
        lax.all_gather(shards[0], "fsdp", axis=1, tiled=True),
        lax.all_gather(shards[1], "fsdp", axis=1, tiled=True),
        lax.all_gather(shards[2], "fsdp", axis=1, tiled=True),
        lax.all_gather(shards[3], "fsdp", axis=1, tiled=True),
        lax.all_gather(shards[4], "fsdp", axis=1, tiled=True),
        lax.all_gather(shards[5], "fsdp", axis=1, tiled=True),
        lax.all_gather(shards[6], "fsdp", axis=1, tiled=True),
    )
    params = tuple((piece[0] for piece in gathered))
    section = lax.axis_index("section")
    micro = tokens.shape[0]
    group = tokens.shape[2]
    width = tokens.shape[3]
    seq_len = group * lax.axis_size("seq")
    offset = lax.axis_index("seq") * group

    def fetch(array, index):
        return lax.dynamic_index_in_dim(array, index, 0, keepdims=False)[0]

    def forward_step(carry, step):
        incoming, stat_sum = carry
        index = step - section
        active = (index >= 0) & (index < micro)
        chosen = jnp.clip(index, 0, micro - 1)
        hidden_in = jnp.where(section == 0, fetch(tokens, chosen), incoming)
        allowed = allowed_pairs(fetch(lengths, chosen), offset, group, seq_len)
        valid = fetch(valid_mask, chosen).astype(jnp.float32)
        result, kept, statistic = forward_layer(hidden_in, params, allowed, valid)
        outgoing = shifted(result, "section", 1)
        stat_sum = stat_sum + jnp.where(active, statistic, 0.0)
        return ((outgoing, stat_sum), (result, kept))

    step_list = jnp.arange(micro + 1, dtype=jnp.int32)
    start = (jnp.zeros((group, width), jnp.bfloat16), jnp.zeros((), jnp.float32))
    (unused_fwd, stat_sum), (results, kept_all) = lax.scan(forward_step, start, step_list)
    late_shards, stat_sum = lax.optimization_barrier((shards, stat_sum))
    again = (
        lax.all_gather(late_shards[0], "fsdp", axis=1, tiled=True),
        lax.all_gather(late_shards[1], "fsdp", axis=1, tiled=True),
        lax.all_gather(late_shards[2], "fsdp", axis=1, tiled=True),
        lax.all_gather(late_shards[3], "fsdp", axis=1, tiled=True),
        lax.all_gather(late_shards[4], "fsdp", axis=1, tiled=True),
        lax.all_gather(late_shards[5], "fsdp", axis=1, tiled=True),
        lax.all_gather(late_shards[6], "fsdp", axis=1, tiled=True),
    )
    params_back = tuple((piece[0] for piece in again))

    def backward_step(carry, step):
        incoming, sums = carry
        index = step - 1 + section
        active = (index >= 0) & (index < micro)
        chosen = jnp.clip(index, 0, micro - 1)
        position = chosen + section

        def take(array):
            return lax.dynamic_index_in_dim(array, position, 0, keepdims=False)

        kept = jax.tree.map(take, kept_all)
        grad_out = jnp.where(
            section == 1, fetch(cotangent, chosen).astype(jnp.float32), incoming.astype(jnp.float32)
        )
        grad_out = jnp.where(active, grad_out, 0.0)
        row_lengths = fetch(lengths, chosen)
        allowed = allowed_pairs(row_lengths, offset, group, seq_len)
        grad_hidden, grads = backward_layer(kept, params_back, grad_out, allowed)
        outgoing = shifted(grad_hidden.astype(jnp.bfloat16), "section", -1)
        sums = tuple((total + piece for total, piece in zip(sums, grads)))
        return ((outgoing, sums), grad_hidden)

    zeros = tuple((jnp.zeros(piece.shape, jnp.float32) for piece in params_back))
    (unused_back, sums), grad_steps = lax.scan(
        backward_step, (jnp.zeros((group, width), jnp.bfloat16), zeros), step_list
    )
    hidden_out = lax.dynamic_slice_in_dim(results, section, micro, 0).reshape(
        1, micro, 1, group, width
    )
    grad_in = lax.dynamic_slice_in_dim(grad_steps, 1 - section, micro, 0).reshape(
        1, micro, 1, group, width
    )
    shard_sums = jax.tree.map(
        lambda part: part.astype(jnp.float32),
        lax.psum_scatter(for_sending(sums), "fsdp", scatter_dimension=0, tiled=True),
    )
    reduced = jax.tree.map(
        lambda part: part.astype(jnp.float32), lax.psum(for_sending(shard_sums), "seq")
    )
    total_stat = lax.psum(stat_sum, ("seq", "fsdp"))
    token_count = micro * lax.axis_size("fsdp") * seq_len
    rms_stats = jnp.sqrt(total_stat / token_count + epsilon).reshape(1)
    return (
        hidden_out,
        grad_in,
        reduced[0][None],
        reduced[1][None],
        reduced[2][None],
        reduced[3][None],
        reduced[4][None],
        reduced[5][None],
        reduced[6][None],
        rms_stats,
    )


BLOCK = 128
SCORE_SCALE = math.sqrt(HEAD)
MASKED = -1e30


def dot(left, right):
    return jnp.dot(left, right, preferred_element_type=jnp.float32)


def low(x):
    return x.astype(jnp.bfloat16)


def pick(x, index, axis):
    return lax.dynamic_index_in_dim(x, index, axis, keepdims=False)


def sums_of_halves(x):
    row = lax.broadcasted_iota(jnp.int32, (2 * HEAD, 2 * HEAD), 0) // HEAD
    col = lax.broadcasted_iota(jnp.int32, (2 * HEAD, 2 * HEAD), 1) // HEAD
    same = (row == col).astype(jnp.bfloat16)
    high = x.astype(jnp.bfloat16)
    rest = (x - high.astype(jnp.float32)).astype(jnp.bfloat16)
    return dot(high, same) + dot(rest, same)


def normal_heads(raw):
    factor = lax.rsqrt(sums_of_halves(raw * raw) + epsilon)
    return raw * factor, factor


def merge(to, own, oth):
    for s in range(4):
        to[s * 256 : s * 256 + BLOCK, : own.shape[1]] = own[s * BLOCK : (s + 1) * BLOCK]
        to[s * 256 + BLOCK : (s + 1) * 256, : own.shape[1]] = oth[s * BLOCK : (s + 1) * BLOCK]


def last_dims(left, right):
    return lax.dot_general(left, right, (((1,), (1,)), ((), ())), preferred_element_type=jnp.float32)


def head_lanes(h, dtype):
    lane = lax.broadcasted_iota(jnp.int32, (1, 2 * HEAD), 1) // HEAD
    return (lane == h).astype(dtype)


MESH = pl.DeviceIdType.MESH


def position():
    c, s, f = (lax.axis_index(name) for name in ("section", "seq", "fsdp"))
    x, y = f % 2, f // 2
    layer = 1 - ((s + 1) // 2) % 2
    return c, s, f, y * 2 + 1 - x, (1 - y) * 2 + x, layer


def greet(devices):
    barrier = pltpu.get_barrier_semaphore()
    for device in devices:
        pl.semaphore_signal(barrier, inc=1, device_id=device, device_id_type=MESH)
    pl.semaphore_wait(barrier, len(devices))


def remote(src, dst, send, recv, device):
    return pltpu.make_async_remote_copy(
        src_ref=src, dst_ref=dst, send_sem=send, recv_sem=recv, device_id=device, device_id_type=MESH
    )


def arrived(ref, sem):
    pltpu.make_async_copy(ref, ref, sem).wait()


def lane(offset):
    return pl.multiple_of(offset, 128)


def every(count, work):
    def step(n, carry):
        work(n)
        return carry

    lax.fori_loop(0, count, step, 0)


def silu(x):
    return x * jax.nn.sigmoid(x)


def row_sums(x, lanes):
    high = low(x)
    rest = low(x - high.astype(jnp.float32))
    return last_dims(lanes, high) + last_dims(lanes, rest)


class Flow:
    def __init__(self, buffers, semaphores):
        (
            self.near_own, self.near_far, self.far_in, self.own, self.passing,
            self.from_left, self.from_right, self.pair_sum,
        ) = buffers
        (
            self.load_own, self.load_pass, self.send_own, self.recv_own, self.send_far,
            self.recv_far, self.send_next, self.recv_next, self.send_z, self.recv_left,
            self.recv_right, self.recv_pair, self.send_on, self.send_back, self.send_out,
            self.keep, self.give, self.given,
        ) = [semaphores.at[n] for n in range(VECTOR_SEMAPHORES)]
        self.place_of = position()

    def begin(self, source):
        c, s, f, fx, fy, _ = self.place_of
        to = (c, s, fx)
        remote(source(fx), self.near_own, self.send_own, self.recv_own, to).start()
        remote(source(3 - f), self.near_far, self.send_far, self.recv_far, to).start()
        pltpu.make_async_copy(source(fy), self.passing, self.load_pass).start()
        pltpu.make_async_copy(source(f), self.own, self.load_own).start()

    def pass_on(self):
        c, s, _, _, fy, _ = self.place_of
        arrived(self.passing, self.load_pass)
        arrived(self.near_far, self.recv_far)
        add(self.passing, self.passing, self.near_far)
        remote(self.passing, self.far_in, self.send_next, self.recv_next, (c, s, fy)).start()

    def finish_plane(self):
        c, s, f, _, _, _ = self.place_of
        own, send = self.own, self.send_z
        arrived(own, self.load_own)
        arrived(self.near_own, self.recv_own)
        arrived(self.far_in, self.recv_next)
        add(own, own, self.near_own, self.far_in)

        @pl.when(s == 0)
        def _():
            remote(own, self.from_left, send, self.recv_left, (c, 1, f)).start()

        @pl.when(s == 3)
        def _():
            remote(own, self.from_right, send, self.recv_right, (c, 2, f)).start()

        @pl.when((s == 1) | (s == 2))
        def _():
            remote(own, self.pair_sum, send, self.recv_pair, (c, 3 - s, f)).start()

    def middle_planes(self):
        c, s, f, _, _, _ = self.place_of
        left, right, pair = self.from_left, self.from_right, self.pair_sum

        @pl.when(s == 1)
        def _():
            arrived(left, self.recv_left)
            remote(left, left, self.send_on, self.recv_left, (c, 2, f)).start()

        @pl.when(s == 2)
        def _():
            arrived(right, self.recv_right)
            remote(right, right, self.send_on, self.recv_right, (c, 1, f)).start()

        @pl.when((s == 1) | (s == 2))
        def _():
            arrived(pair, self.recv_pair)
            arrived(pair, self.send_z)
            add(pair, pair, self.own)
            remote(pair, pair, self.send_out, self.recv_pair, (c, (s - 1) * 3, f)).start()

    def all_planes(self, dst):
        c, s, f, _, _, _ = self.place_of
        left, right, pair = self.from_left, self.from_right, self.pair_sum
        own, total = self.own, self.near_own

        @pl.when(s == 1)
        def _():
            arrived(right, self.recv_right)
            remote(right, right, self.send_back, self.recv_right, (c, 0, f)).start()

        @pl.when(s == 2)
        def _():
            arrived(left, self.recv_left)
            remote(left, left, self.send_back, self.recv_left, (c, 3, f)).start()

        @pl.when((s == 1) | (s == 2))
        def _():
            add(total, left, right)

        @pl.when(s == 0)
        def _():
            arrived(pair, self.recv_pair)
            arrived(right, self.recv_right)
            add(total, own, right)

        @pl.when(s == 3)
        def _():
            arrived(pair, self.recv_pair)
            arrived(left, self.recv_left)
            add(total, own, left)

        for owner, chunk in ((0, pair), (1, total)):

            @pl.when(c == owner)
            def _():
                pltpu.make_async_copy(chunk, dst, self.keep).start()

            @pl.when(c != owner)
            def _():
                remote(chunk, dst, self.give, self.given, (1 - c, s, f)).start()

    def settle(self):
        _, s, _, _, _, _ = self.place_of
        for sem in (
            self.send_own, self.send_far, self.send_next, self.keep, self.give, self.given
        ):
            arrived(self.own, sem)

        @pl.when((s == 1) | (s == 2))
        def _():
            for sem in (self.send_on, self.send_back, self.send_out):
                arrived(self.own, sem)

        @pl.when((s == 0) | (s == 3))
        def _():
            arrived(self.own, self.send_z)


def add(to, *refs):
    total = refs[0][...].astype(jnp.float32)
    for ref in refs[1:]:
        total = total + ref[...].astype(jnp.float32)
    to[...] = total.astype(to.dtype)


VECTOR_SEMAPHORES = 18
CHUNKS = 16
SHARED = (1, 2, 3, 4)
AHEAD = 3
INPUTS = 9
OUTPUTS = 19


def scratch_of(width, units, vector_rows, flag_rows):
    rows = 4 * BLOCK
    half = units // 2

    def low_vmem(*shape):
        return pltpu.VMEM(shape, jnp.bfloat16)

    def full_vmem(*shape):
        return pltpu.VMEM(shape, jnp.float32)

    def sems(*shape):
        return pltpu.SemaphoreType.DMA(shape)

    low_row, full_row, low_rows = low_vmem(rows, width), full_vmem(rows, width), low_vmem(2, rows, width)
    pair, pair_full = low_vmem(2 * rows, 2 * HEAD), full_vmem(2 * rows, 2 * HEAD)
    return dict(
        wq=low_vmem(width, 3 * width // 2), wo=low_vmem(width // 2, width),
        wu=low_vmem(width, half), wg=low_vmem(width, half), wd=low_vmem(half, width),
        vec=low_vmem(4, vector_rows, 128), flat=full_vmem(4, vector_rows, 128),
        flags=low_vmem(4, flag_rows, 128), flags_full=full_vmem(4, flag_rows, 128),
        scale_up=full_vmem(1, half), scale_gate=full_vmem(1, half),
        alpha_attn=full_vmem(1, width), alpha_mlp=full_vmem(1, width),
        hid=low_rows, mixed=low_vmem(2, rows, 3 * width // 2), att=low_vmem(2, rows, width // 2),
        mid=low_rows, up=low_vmem(2, rows, half), gate=low_vmem(2, rows, half),
        inner=low_vmem(2, rows, half), branch=full_row, middle=full_row, output=full_row,
        result=low_row, part=low_row, got=low_row,
        bias=full_vmem(2 * rows, 2 * rows), raw=pair, queries=pair, keys=pair,
        values=low_vmem(2 * rows, 4 * HEAD), grads=pair, dq=pair_full, dk=pair_full, dv=pair_full,
        log_sums=full_vmem(4, 2, 2 * rows),
        grad_in=low_row, grad_rows=low_rows,
        sum_alphas=full_vmem(2, width), sum_scales=full_vmem(2, half), sum_qk=full_vmem(4, 2 * HEAD),
        sum_valid=full_vmem(1, 128), terms=full_vmem(4, 24, 128),
        v0=full_vmem(24, 128), v1=full_vmem(24, 128), v2=full_vmem(24, 128), v3=full_vmem(24, 128),
        v4=full_vmem(24, 128), v5=full_vmem(24, 128), v6=full_vmem(24, 128), v7=full_vmem(24, 128),
        first_send=sems(6, 3), first_recv=sems(6, 3), next_send=sems(6, 2), next_recv=sems(6, 2),
        plane_send=sems(6, 3), plane_recv=sems(6, 3),
        row_send=sems(4), row_recv=sems(4), flag_send=sems(4), flag_recv=sems(4),
        own_recv=sems(4), oth_send=sems(4), oth_recv=sems(4),
        part_send=sems(4, 4), part_recv=sems(4, 4),
        mid_send=sems(3, 4), mid_recv=sems(3, 4), result_send=sems(4), grad_recv=sems(4),
        owner_send=sems(2, 4), owner_recv=sems(2, 2, 2),
        vector=sems(VECTOR_SEMAPHORES), staged=sems(2), load=sems(9, 4),
        send_own=sems(CHUNKS), recv_own=sems(CHUNKS), send_far=sems(CHUNKS), recv_far=sems(CHUNKS),
        send_next=sems(CHUNKS), recv_next=sems(CHUNKS), send_z=sems(CHUNKS), stored=sems(CHUNKS),
        recv_left=sems(CHUNKS), recv_right=sems(CHUNKS), recv_pair=sems(CHUNKS),
        send_on=sems(CHUNKS), send_back=sems(CHUNKS), send_out=sems(CHUNKS),
        keep=sems(CHUNKS), give=sems(CHUNKS), given=sems(CHUNKS),
    )


def relay_kernel(names, *refs):
    (
        w_qkv, w_out, w_in, w_down, vectors, valid, tokens, cotangent,
        ends,
    ) = refs[:INPUTS]
    (
        o_down, o_in, o_out, o_qkv, o_vectors, o_hidden, o_grad, o_row,
        g_down, g_up, g_gate, g_out, g_qkv,
        near_own, near_far, far_in, from_left, from_right, pair_sum,
    ) = refs[INPUTS : INPUTS + OUTPUTS]
    plane_sum, *refs = refs[INPUTS + OUTPUTS :]
    r = types.SimpleNamespace(**dict(zip(names, refs)))
    c, s, f, fx, fy, layer = position()
    sibling = (1 - c, s, f)
    early, late = layer == 0, layer == 1
    late_plane = (c, (s - 1) * 3, f)
    early_plane = (c, s // 3 + 1, f)
    width = w_out.shape[1]
    full = jnp.float32
    greet(
        [sibling, (c, s, fx), (c, s, fy)]
        + [(core, (s + step) % 4, f) for core in (0, 1) for step in (1, 2, 3)]
    )

    def rows_of(b):
        return pl.ds(b * BLOCK, BLOCK)

    def columns(n):
        return pl.ds(lane(n * 256), 256)

    def send_row(to, held):
        src, dst = held.at[pl.ds(c * BLOCK, BLOCK)], o_row.at[rows_of(s)]
        flags, flags_to = valid.at[to // 2], r.flags.at[s]

        @pl.when(s == to)
        def _():
            pltpu.make_async_copy(src, dst, r.row_recv.at[s]).start()
            pltpu.make_async_copy(flags, flags_to, r.flag_recv.at[s]).start()

        @pl.when(s != to)
        def _():
            remote(src, dst, r.row_send.at[to], r.row_recv.at[s], (c, to, f)).start()
            remote(flags, flags_to, r.flag_send.at[to], r.flag_recv.at[s], (c, to, f)).start()

    send_row(1, tokens.at[0])
    send_row(2, tokens.at[1])

    def pieces(item, h):
        if item == 0:
            return [(vectors, r.vec.at[f])]
        if item == 1:
            return [
                (
                    w_qkv.at[:, pl.ds(lane(part * 256 + h * 128), 128)],
                    r.wq.at[pl.ds(f * 256, 256), pl.ds(part * 128, 128)],
                )
                for part in range(12)
            ]
        if item == 2:
            return [(w_out.at[pl.ds(h * 128, 128)], r.wo.at[pl.ds(f * 128, 128)])]
        if item in (3, 4):
            to = (r.wu, r.wg)[item - 3]
            return [
                (
                    w_in.at[:, pl.ds(lane((item - 3) * 4096 + part * 1024 + h * 512), 512)],
                    to.at[pl.ds(f * 256, 256), pl.ds(part * 512, 512)],
                )
                for part in range(4)
            ]
        return [(w_down.at[pl.ds(h * 512, 512)], r.wd.at[pl.ds(f * 512, 512)])]

    weights = (r.vec, r.wq, r.wo, r.wu, r.wg, r.wd)
    other_plane = (c, 3 - s, f)

    def quarter(item):
        return 0 if item == 0 else weights[item].shape[0] // 16

    def block(item, of):
        if item == 0:
            return r.vec.at[of]
        rows = weights[item].shape[0] // 4
        return weights[item].at[pl.ds(of * rows, rows)]

    def part_of(item, of, part):
        if item == 0:
            return r.vec.at[of, pl.ds(part * 16, 16)]
        rows = weights[item].shape[0] // 8
        return weights[item].at[pl.ds(of * 2 * rows + part * rows, rows)]

    def quarters(item, of, least, count):
        size = quarter(item)
        return weights[item].at[pl.ds(of * 4 * size + least * size, count * size)]

    @pl.when(c == layer)
    def _():
        for item in range(6):
            for src, dst in pieces(item, 1 - c):
                remote(
                    src, dst, r.first_send.at[item, 2], r.first_recv.at[item, 0], sibling
                ).start()
            for src, dst in pieces(item, c):
                pltpu.make_async_copy(src, dst, r.first_recv.at[item, 0]).start()

    ways = ((1, fx, fy), (2, fy, fx))

    def spread(*items):
        for item in items:
            arrived(block(item, f), r.first_recv.at[item, 0])

            def send(moved, item=item):
                for part, (came, to, _) in enumerate(ways):
                    remote(
                        moved, moved, r.first_send.at[item, part], r.first_recv.at[item, came],
                        (c, s, to),
                    ).start()

            if item in SHARED:

                @pl.when(early)
                def _():
                    send(quarters(item, f, s - 1, 3))

                @pl.when(late)
                def _():
                    send(block(item, f))
            else:
                send(block(item, f))

    def forward(moved, item, part, to):
        remote(moved, moved, r.next_send.at[item, part], r.next_recv.at[item, part], to).start()

    def share(moved, item, part):
        remote(
            moved, moved, r.plane_send.at[item, part], r.plane_recv.at[item, part], other_plane
        ).start()

    def relay(item):
        def halves():
            for part, (came, of, to) in enumerate(ways):
                arrived(block(item, of), r.first_recv.at[item, came])
                forward(part_of(item, of, part), item, part, (c, s, to))

        if item not in SHARED:
            halves()
        else:
            pl.when(late)(halves)

            @pl.when(early)
            def _():
                for part, (came, of, to) in enumerate(ways):
                    arrived(quarters(item, of, 0, 3), r.first_recv.at[item, came])
                    forward(quarters(item, of, (s - 1) * 2 + part, 1), item, part, (c, s, to))
                for part, (came, of, to) in enumerate(ways):
                    share(quarters(item, of, (s - 1) * 3, 1), item, part)

    def relay_across(item):
        @pl.when(early)
        def _():
            for part in range(2):
                arrived(quarters(item, 3 - f, (s - 1) * 2 + part, 1), r.next_recv.at[item, part])
            share(quarters(item, 3 - f, (s - 1) * 2, 2), item, 2)

    def complete(item):
        def halves():
            for part in range(2):
                arrived(part_of(item, 3 - f, part), r.next_recv.at[item, part])

        if item not in SHARED:
            halves()
        else:
            pl.when(late)(halves)

            @pl.when(early)
            def _():
                for part, of in ((0, fx), (1, fy)):
                    arrived(quarters(item, of, (2 - s) * 3, 1), r.plane_recv.at[item, part])
                arrived(quarters(item, 3 - f, (2 - s) * 2, 2), r.plane_recv.at[item, 2])

    def settle_relays():
        for item in range(6):

            def halves():
                for part in range(2):
                    arrived(part_of(item, f, part), r.next_send.at[item, part])

            if item not in SHARED:
                halves()
            else:
                pl.when(late)(halves)

                @pl.when(early)
                def _():
                    for part in range(2):
                        arrived(quarters(item, f, 0, 1), r.next_send.at[item, part])
                        arrived(quarters(item, f, 0, 1), r.plane_send.at[item, part])
                    arrived(quarters(item, f, 0, 2), r.plane_send.at[item, 2])

    def settle_spread():
        for item in range(6):

            def sent(moved, item=item):
                for part in range(2):
                    arrived(moved, r.first_send.at[item, part])

            if item in SHARED:
                pl.when(early)(lambda: sent(quarters(item, f, 0, 3)))
                pl.when(late)(lambda: sent(block(item, f)))
            else:
                sent(block(item, f))

        @pl.when(c == layer)
        def _():
            for item in range(6):
                arrived(block(item, f), r.first_send.at[item, 2])

    spread(0, 1, 2)

    def placed_at(axis):
        index = lax.broadcasted_iota(jnp.int32, (1, 8 * BLOCK) if axis else (8 * BLOCK, 1), axis)
        place = (index // 256) * 256 + (index // BLOCK + c) % 2 * BLOCK + index % BLOCK
        start = jnp.zeros_like(place)
        for n in range(ends.shape[0]):
            start = jnp.maximum(start, jnp.where(place >= ends[n], ends[n], 0))
        return place, start

    place_col, start_col = placed_at(0)
    place_row, start_row = placed_at(1)
    fits = (place_row >= start_col) & (place_row <= place_col)
    r.bias[...] = jnp.where(fits, 0.0, MASKED)
    r.values[:, 2 * HEAD :] = jnp.ones_like(r.values[:, 2 * HEAD :])
    for sums in (r.sum_alphas, r.sum_scales, r.sum_valid, r.terms):
        sums[...] = jnp.zeros_like(sums)
    relay(0)
    relay(1)
    spread(3)
    relay(2)
    relay_across(1)

    def to_sibling(b, src):
        remote(src, r.hid.at[1, rows_of(b)], r.oth_send.at[b], r.oth_recv.at[b], sibling).start()

    @pl.when(early)
    def _():
        for b in range(4):
            held = o_row.at[rows_of(b)]
            arrived(held, r.row_recv.at[b])
            pltpu.make_async_copy(held, r.hid.at[0, rows_of(b)], r.own_recv.at[b]).start()
            to_sibling(b, held)
        for b in range(4):
            arrived(r.hid.at[0, rows_of(b)], r.own_recv.at[b])

    @pl.when(late)
    def _():
        spread(4)
        relay(3)
        spread(5)
        relay(4)
        relay(5)
        for b in range(4):
            arrived(r.hid.at[0, rows_of(b)], r.own_recv.at[b])
            to_sibling(b, r.hid.at[0, rows_of(b)])

    complete(0)
    r.flat[...] = r.vec[...].astype(full)
    for n in range(4):
        for j in range(4):
            at = slice(n * 512 + j * 128, n * 512 + (j + 1) * 128)
            row = pl.ds(2 + (n % 2) * 8 + j + c * 4, 1)
            r.scale_up[:, at] = r.flat[n // 2, row, :]
            r.scale_gate[:, at] = r.flat[2 + n // 2, row, :] * math.sqrt(width)
    for n in range(2):
        for j in range(4):
            at = slice(n * 512 + j * 128, n * 512 + (j + 1) * 128)
            r.alpha_attn[:, at] = r.flat[n, 18 + j : 19 + j, :]
            r.alpha_mlp[:, at] = r.flat[2 + n, 18 + j : 19 + j, :]

    complete(1)
    for side in range(2):
        if side:
            for b in range(4):
                arrived(r.hid.at[1, rows_of(b)], r.oth_recv.at[b])

        def mix(n, side=side):
            at = pl.ds(lane(n * 512), 512)
            r.mixed[side, :, at] = low(dot(r.hid[side], r.wq[:, at]))

        every(3, mix)

    first = (lax.broadcasted_iota(jnp.int32, (8, 2 * HEAD), 1) == 0).astype(jnp.bfloat16)

    def lanes_of(pair, part):
        return pl.ds(lane(part * (width // 2) + pair * 2 * HEAD), 2 * HEAD)

    def normal(pair, part):
        at = lanes_of(pair, part)
        merge(r.raw, r.mixed[0, :, at], r.mixed[1, :, at])
        return normal_heads(r.raw[...].astype(full))

    def prepare(pair):
        scale = r.flat[pair, pl.ds(c, 1), :]
        r.queries[...] = low(normal(pair, 0)[0] * scale) * SCORE_SCALE
        r.keys[...] = low(normal(pair, 1)[0] * scale)
        at = lanes_of(pair, 2)
        merge(r.values, r.mixed[0, :, at], r.mixed[1, :, at])

    def of_heads(block):
        return jnp.concatenate([block * head_lanes(h, jnp.bfloat16) for h in range(2)])

    def attend(pair):
        @pl.when(early & (pair == 0))
        def _():
            relay_across(2)
            spread(4)

        @pl.when(early & (pair == 2))
        def _():
            relay(3)

        @pl.when(early & (pair == 3))
        def _():
            spread(5)

        prepare(pair)
        at = lanes_of(pair, 0)
        for q in range(4):
            upto = (q + 1) * 256
            query = of_heads(r.queries[q * 256 : upto])
            summed = 0.0
            for k in range(q + 1):
                at_keys = slice(k * 256, (k + 1) * 256)
                mask = jnp.concatenate([r.bias[q * 256 : upto, at_keys]] * 2)
                weighted = jnp.exp(last_dims(query, r.keys[at_keys]) + mask)
                summed = summed + dot(low(weighted), r.values[at_keys])
            total = summed[:, 2 * HEAD :]
            parts = summed[:, : 2 * HEAD] / total
            log_sum = jnp.log(row_sums(total, first)[:1])
            for h in range(2):
                r.log_sums[pair, h : h + 1, q * 256 : upto] = log_sum[:, h * 256 : (h + 1) * 256]
            joined = low(jnp.where(head_lanes(0, full) > 0, parts[:256], parts[256:]))
            r.att[0, q * BLOCK : (q + 1) * BLOCK, at] = joined[:BLOCK]
            r.att[1, q * BLOCK : (q + 1) * BLOCK, at] = joined[BLOCK:]

    every(4, attend)

    def exchange(index, product, to):
        send, recv = r.part_send.at[index], r.part_recv.at[index]

        def sent(n):
            at = columns(n)
            r.part[:, at] = low(product(1, n))
            remote(r.part.at[:, at], r.got.at[:, at], send.at[n], recv.at[n], sibling).start()

        def own(n):
            at = columns(n)
            to[:, at] = product(0, n) if to is not r.middle else to[:, at] + product(0, n)

        every(4, sent)
        every(4, own)
        for n in range(4):
            arrived(r.got.at[:, columns(n)], recv.at[n])

    def settle_sent(index):
        for n in range(4):
            arrived(r.part.at[:, columns(n)], r.part_send.at[index, n])

    def share_rows(array, index, b):
        @pl.when(b % 2 == 1)
        def _():
            rows = rows_of(b // 2)
            remote(
                array.at[0, rows], array.at[1, rows], r.mid_send.at[index, b // 2],
                r.mid_recv.at[index, b // 2], sibling,
            ).start()

    def shared(array, index):
        for b in range(4):
            arrived(array.at[1, rows_of(b)], r.mid_recv.at[index, b])

    def settle_shared(array, index):
        for b in range(4):
            arrived(array.at[0, rows_of(b)], r.mid_send.at[index, b])

    complete(2)
    exchange(
        0, lambda side, n: dot(r.att[side], r.wo[:, columns(n)]), r.branch,
    )

    def first_step(b):
        rows = pl.ds(b * 64, 64)
        total = r.branch[rows] + r.got[rows].astype(full)
        r.branch[rows] = total
        hidden = r.hid[0, rows].astype(full)
        stepped = unit(hidden + r.alpha_attn[...] * (unit(total) - hidden))
        r.middle[rows] = stepped
        r.mid[0, rows] = low(stepped)
        share_rows(r.mid, 0, b)

    relay_across(3)
    send_row(0, cotangent.at[0])
    send_row(3, cotangent.at[1])
    every(8, first_step)

    @pl.when(early)
    def _():
        relay(4)

    complete(3)
    for side in range(2):
        if side:
            shared(r.mid, 0)

        def lift(n, side=side):
            at = pl.ds(lane(n * 512), 512)
            r.up[side, :, at] = low(dot(r.mid[side], r.wu[:, at]))

        every(4, lift)

    relay_across(4)

    @pl.when(early)
    def _():
        relay(5)

    complete(4)
    for side in (1, 0):

        def open_gate(n, side=side):
            at = pl.ds(lane(n * 512), 512)
            gate = dot(r.mid[side], r.wg[:, at])
            r.gate[side, :, at] = low(gate)
            upward = r.up[side, :, at].astype(full) * r.scale_up[:, at]
            r.inner[side, :, at] = low(upward * silu(gate * r.scale_gate[:, at]))

        every(4, open_gate)

    complete(5)
    settle_sent(0)
    exchange(
        1, lambda side, n: dot(r.inner[side], r.wd[:, columns(n)]), r.output,
    )

    def second_step(b):
        rows = pl.ds(b * 64, 64)
        total = r.output[rows] + r.got[rows].astype(full)
        r.output[rows] = total
        start = r.middle[rows]
        r.result[rows] = low(unit(start + r.alpha_mlp[...] * (unit(total) - start)))

        @pl.when(early & (b % 2 == 1))
        def _():
            sent = rows_of(b // 2)
            remote(
                r.result.at[sent], r.hid.at[0, sent], r.result_send.at[b // 2],
                r.own_recv.at[b // 2], late_plane,
            ).start()

    every(8, second_step)

    def to_owners(array, held, to_ref):
        for to in range(4):
            src = held.at[rows_of(to)]
            dst = to_ref.at[s // 2, pl.ds(c * BLOCK, BLOCK)]
            recv = r.owner_recv.at[array, s // 2, c]
            here = (s == to) & (c == layer)

            @pl.when(here)
            def _():
                pltpu.make_async_copy(src, dst, r.owner_send.at[array, to]).start()

            @pl.when(jnp.logical_not(here))
            def _():
                remote(src, dst, r.owner_send.at[array, to], recv, (layer, to, f)).start()

    to_owners(0, r.result, o_hidden)

    @pl.when(late)
    def _():
        for b in range(4):
            held = o_row.at[rows_of(b)]
            arrived(held, r.row_recv.at[b])
            pltpu.make_async_copy(held, r.grad_in.at[rows_of(b)], r.grad_recv.at[b]).start()

    def near_of(k):
        return fx + (fy - fx) * (k % 2)

    def far_of(k):
        return fy + (fx - fy) * (k % 2)

    def with_source(k, work):
        @pl.when(k < 4)
        def _():
            at = pl.ds(lane((k % 2) * 512), 512)
            work(lambda to: g_down.at[pl.ds(to * 512 + (k // 2) * 256, 256), at])

        for begins, ref in ((4, g_up), (8, g_gate), (12, g_out), (13, g_qkv)):

            @pl.when((k >= begins) & (k < begins + ref.shape[1] // 512))
            def _():
                at = pl.ds(lane((k - begins) * 512), 512)
                work(lambda to: ref.at[pl.ds(to * 256, 256), at])

    def begin(k):
        def start(source):
            to = (c, s, near_of(k))
            remote(source(3 - f), near_far.at[k], r.send_far.at[k], r.recv_far.at[k], to).start()
            remote(
                source(near_of(k)), near_own.at[k], r.send_own.at[k], r.recv_own.at[k], to
            ).start()

        with_source(k, start)

    places = {
        "pass": (r.wu, 0, 4), "own": (r.wu, 4, 4), "pair": (r.wu, 8, 4), "far": (r.wu, 12, 2),
        "other": (r.wu, 14, 2), "late": (r.wg, 0, 4), "near": (r.wg, 4, 2), "last": (r.wg, 6, 2),
        "side": (r.wg, 8, 2),
    }
    order = list(places)

    def slot(name, k):
        ref, base, count = places[name]
        n = base + k % count
        return ref.at[pl.ds(n // 4 * 256, 256), pl.ds(lane(n % 4 * 512), 512)]

    def load_sem(name, k):
        return r.load.at[order.index(name), k % places[name][2]]

    def fetch(src, name, k):
        pltpu.make_async_copy(src, slot(name, k), load_sem(name, k)).start()

    def fetched(name, k):
        arrived(slot(name, k), load_sem(name, k))

    def again(k, work):
        pl.when(k >= 4)(work)

    def pass_on(k):
        arrived(near_far.at[k], r.recv_far.at[k])

        again(k, lambda: arrived(slot("pass", k), r.send_next.at[k - 4]))
        with_source(k, lambda source: fetch(source(far_of(k)), "pass", k))
        fetch(near_far.at[k], "far", k)
        fetched("pass", k)
        fetched("far", k)
        total = slot("pass", k)
        add(total, total, slot("far", k))
        remote(
            total, far_in.at[k], r.send_next.at[k], r.recv_next.at[k], (c, s, far_of(k))
        ).start()

    def plane_total(k):
        arrived(near_own.at[k], r.recv_own.at[k])
        arrived(far_in.at[k], r.recv_next.at[k])

        again(k, lambda: arrived(slot("own", k), r.send_z.at[k - 4]))
        with_source(k, lambda source: fetch(source(f), "own", k))
        fetch(near_own.at[k], "near", k)
        fetch(far_in.at[k], "last", k)
        for name in ("own", "near", "last"):
            fetched(name, k)
        own, send = slot("own", k), r.send_z.at[k]
        add(own, own, slot("near", k), slot("last", k))
        pltpu.make_async_copy(own, plane_sum.at[k], r.stored.at[k]).start()

        @pl.when(s == 0)
        def _():
            remote(own, from_left.at[k], send, r.recv_left.at[k], (c, 1, f)).start()

        @pl.when(s == 3)
        def _():
            remote(own, from_right.at[k], send, r.recv_right.at[k], (c, 2, f)).start()

        @pl.when(early)
        def _():
            remote(own, pair_sum.at[k], send, r.recv_pair.at[k], (c, 3 - s, f)).start()

    def plane_done(k):
        arrived(plane_sum.at[k], r.stored.at[k])

    def in_plane(t):
        @pl.when((t + AHEAD < CHUNKS) & (early | (t == 0) | (t > 3)))
        def _():
            begin(t + AHEAD)

        @pl.when(late & (t == 3))
        def _():
            for k in range(4, 7):
                begin(k)

        for lag, work in ((3, plane_done), (2, plane_total), (0, pass_on)):
            @pl.when((t >= lag) & (t < lag + CHUNKS))
            def _():
                work(t - lag)

    def relay_on(k):
        @pl.when(s == 1)
        def _():
            arrived(from_left.at[k], r.recv_left.at[k])
            remote(
                from_left.at[k], from_left.at[k], r.send_on.at[k], r.recv_left.at[k], (c, 2, f)
            ).start()

        @pl.when(s == 2)
        def _():
            arrived(from_right.at[k], r.recv_right.at[k])
            remote(
                from_right.at[k], from_right.at[k], r.send_on.at[k], r.recv_right.at[k], (c, 1, f)
            ).start()

    def relay_out(k):
        @pl.when(s == 1)
        def _():
            arrived(from_right.at[k], r.recv_right.at[k])
            remote(
                from_right.at[k], from_right.at[k], r.send_back.at[k], r.recv_right.at[k], (c, 0, f)
            ).start()

        @pl.when(s == 2)
        def _():
            arrived(from_left.at[k], r.recv_left.at[k])
            remote(
                from_left.at[k], from_left.at[k], r.send_back.at[k], r.recv_left.at[k], (c, 3, f)
            ).start()

    def everything(chunk):
        return chunk

    def place(k, owner, chunk):
        def put(pieces):
            for src, dst in pieces:

                @pl.when(c == owner)
                def _():
                    pltpu.make_async_copy(src(chunk), dst, r.keep.at[k]).start()

                @pl.when(c != owner)
                def _():
                    remote(src(chunk), dst, r.give.at[k], r.given.at[k], sibling).start()

        @pl.when(k < 4)
        def _():
            rows = pl.ds(c * 512 + (k // 2) * 256, 256)
            put([(everything, o_down.at[rows, pl.ds(lane((k % 2) * 512), 512)])])

        @pl.when((k >= 4) & (k < 12))
        def _():
            put([(everything, o_in.at[:, pl.ds(lane((k - 4) * 1024 + c * 512), 512)])])

        @pl.when(k == 12)
        def _():
            put([
                (
                    lambda chunk, part=part: chunk.at[pl.ds(part * 128, 128)],
                    o_out.at[pl.ds(c * 128, 128), pl.ds(part * 512, 512)],
                )
                for part in range(2)
            ])

        @pl.when(k > 12)
        def _():
            put([
                (
                    lambda chunk, part=part: chunk.at[:, pl.ds(part * 128, 128)],
                    o_qkv.at[:, pl.ds(lane((k - 13) * 1024 + part * 256 + c * 128), 128)],
                )
                for part in range(4)
            ])

    def placed(k, owner):
        @pl.when(c == owner)
        def _():
            arrived(plane_sum.at[k], r.keep.at[k])

        @pl.when(c != owner)
        def _():
            arrived(plane_sum.at[k], r.give.at[k])

    def pair_load(k):
        @pl.when(early)
        def _():
            arrived(pair_sum.at[k], r.recv_pair.at[k])

            @pl.when(k >= 4)
            def _():
                arrived(slot("pair", k), r.send_out.at[k - 4])
                placed(k - 4, 0)

            fetch(plane_sum.at[k], "pair", k)
            fetch(pair_sum.at[k], "other", k)

    def pair_send(k):
        @pl.when(early)
        def _():
            fetched("pair", k)
            fetched("other", k)
            total = slot("pair", k)
            add(total, total, slot("other", k))
            remote(total, pair_sum.at[k], r.send_out.at[k], r.recv_pair.at[k], late_plane).start()
            place(k, 0, total)

    def pair_take(k):
        @pl.when(late)
        def _():
            arrived(pair_sum.at[k], r.recv_pair.at[k])
            again(k, lambda: placed(k - 4, 0))
            fetch(pair_sum.at[k], "pair", k)
            fetched("pair", k)
            place(k, 0, slot("pair", k))

    def late_load(k):
        again(k, lambda: placed(k - 4, 1))

        @pl.when(early)
        def _():
            fetch(from_left.at[k], "late", k)
            fetch(from_right.at[k], "side", k)

        @pl.when(s == 0)
        def _():
            arrived(from_right.at[k], r.recv_right.at[k])
            fetch(from_right.at[k], "side", k)

        @pl.when(s == 3)
        def _():
            arrived(from_left.at[k], r.recv_left.at[k])
            fetch(from_left.at[k], "side", k)

        @pl.when(late)
        def _():
            fetch(plane_sum.at[k], "late", k)

    def late_place(k):
        fetched("late", k)
        fetched("side", k)
        total = slot("late", k)
        add(total, total, slot("side", k))
        place(k, 1, total)

    def between_planes(t):
        @pl.when(early)
        def _():
            for lag, work in ((-4, relay_on), (-2, relay_out)):
                @pl.when(t < lag + CHUNKS)
                def _():
                    work(t - lag)

        for lag, work in (
            (4, pair_load), (4, pair_send), (19, pair_take), (6 + 10 * layer, late_load),
            (6 + 10 * layer, late_place),
        ):
            @pl.when((t >= lag) & (t < lag + CHUNKS))
            def _():
                work(t - lag)

    def weight_grad(count, tile, width_of, pieces):
        def stage(n):
            return r.wd.at[pl.ds((n % 2) * 256, 256), pl.ds(0, width_of)]

        def work(n):
            @pl.when(n >= 2)
            def _():
                arrived(stage(n), r.staged.at[n % 2])

            left, right = tile(n)
            total = contract_rows(left(0), right(0)) + contract_rows(left(1), right(1))
            stage(n)[...] = low(total)
            for src, dst in pieces(n, stage(n)):
                pltpu.make_async_copy(src, dst, r.staged.at[n % 2]).start()

        every(count, work)
        for n in range(count - 2, count):
            arrived(stage(n), r.staged.at[n % 2])

    def grad_of_down():
        weight_grad(
            8,
            lambda n: (lambda side: r.inner[side, :, columns(n)], lambda side: r.grad_rows[side]),
            width,
            lambda n, src: [(src, g_down.at[pl.ds(n * 256, 256)])],
        )

    def grad_of_lift(ref, to):
        weight_grad(
            8,
            lambda n: (
                lambda side: r.mid[side, :, columns(n // 2)],
                lambda side: ref[side, :, pl.ds(lane((n % 2) * 1024), 1024)],
            ),
            1024,
            lambda n, src: [
                (src, to.at[pl.ds((n // 2) * 256, 256), pl.ds(lane((n % 2) * 1024), 1024)])
            ],
        )

    def grad_of_out():
        weight_grad(
            2,
            lambda n: (lambda side: r.att[side, :, columns(n)], lambda side: r.grad_rows[side]),
            width,
            lambda n, src: [
                (
                    src.at[pl.ds(owner * 128, 128), pl.ds(part * 512, 512)],
                    g_out.at[pl.ds(n * 512 + owner * 256 + part * 128, 128)],
                )
                for owner in range(2)
                for part in range(2)
            ],
        )

    def grad_of_qkv():
        weight_grad(
            12,
            lambda n: (
                lambda side: r.hid[side, :, columns(n // 3)],
                lambda side: r.mixed[side, :, pl.ds(lane((n % 3) * 512), 512)],
            ),
            512,
            lambda n, src: [
                (src, g_qkv.at[pl.ds((n // 3) * 256, 256), pl.ds(lane((n % 3) * 512), 512)])
            ],
        )

    fits = (place_col >= start_row) & (place_col <= place_row)
    r.bias[...] = jnp.where(fits, 0.0, MASKED)
    settle_relays()
    settle_spread()

    @pl.when(early)
    def _():
        relay_on(0)

    def second_back(b):
        rows = pl.ds(b * 64, 64)

        @pl.when(b % 2 == 0)
        def _():
            arrived(r.grad_in.at[rows_of(b // 2)], r.grad_recv.at[b // 2])

        start = r.hid[0, rows].astype(full)
        middle = unit(start + r.alpha_attn[...] * (unit(r.branch[rows]) - start))
        total = r.output[rows]
        change = unit(total) - middle
        grad = unit_back(middle + r.alpha_mlp[...] * change, r.grad_in[rows].astype(full))
        r.sum_alphas[1:2] += jnp.sum(grad * change, axis=0, keepdims=True)
        r.grad_rows[0, rows] = low(unit_back(total, r.alpha_mlp[...] * grad))
        r.middle[rows] = grad * (1.0 - r.alpha_mlp[...])
        share_rows(r.grad_rows, 1, b)

    every(8, second_back)

    for side in range(2):
        if side:
            shared(r.grad_rows, 1)

        def close_gate(n, side=side):
            at = pl.ds(lane(n * 512), 512)
            grad = last_dims(r.grad_rows[side], r.wd[pl.ds(n * 512, 512)])
            lift_up = r.up[side, :, at].astype(full)
            lift_gate = r.gate[side, :, at].astype(full)
            gating = lift_gate * r.scale_gate[:, at]
            sigmoid = jax.nn.sigmoid(gating)
            grad_up = grad * (gating * sigmoid)
            grad_gate = (
                grad * (lift_up * r.scale_up[:, at]) * sigmoid * (1.0 + gating * (1.0 - sigmoid))
            )
            r.sum_scales[0:1, at] += jnp.sum(grad_up * lift_up, axis=0, keepdims=True)
            r.sum_scales[1:2, at] += jnp.sum(grad_gate * lift_gate, axis=0, keepdims=True)
            r.up[side, :, at] = low(grad_up * r.scale_up[:, at])
            r.gate[side, :, at] = low(grad_gate * r.scale_gate[:, at])

        every(4, close_gate)
    grad_of_down()
    for k in range(AHEAD):
        begin(k)

    def relays(on, out):
        @pl.when(early)
        def _():
            for k in on:
                relay_on(k)
            for k in out:
                relay_out(k)

    relays((1, 2), (0,))

    @pl.when(early)
    def _():
        grad_of_lift(r.up, g_up)

    relays((3,), (1,))

    def lifted(side, n):
        rows = pl.ds(n * 256, 256)
        return last_dims(r.up[side], r.wu[rows]) + last_dims(r.gate[side], r.wg[rows])

    settle_sent(1)
    exchange(2, lifted, r.middle)
    in_plane(0)
    relays((4,), (2,))
    settle_shared(r.grad_rows, 1)

    def first_back(b):
        rows = pl.ds(b * 64, 64)
        start = r.hid[0, rows].astype(full)
        total = r.branch[rows]
        change = unit(total) - start
        grad = r.middle[rows] + r.got[rows].astype(full)
        grad = unit_back(start + r.alpha_attn[...] * change, grad)
        r.sum_alphas[0:1] += jnp.sum(grad * change, axis=0, keepdims=True)
        r.grad_rows[0, rows] = low(unit_back(total, r.alpha_attn[...] * grad))
        r.middle[rows] = grad * (1.0 - r.alpha_attn[...])
        share_rows(r.grad_rows, 2, b)

    every(8, first_back)

    shared(r.grad_rows, 2)

    marks = (
        lax.broadcasted_iota(jnp.int32, (8, 2 * HEAD), 1) // HEAD
        == lax.broadcasted_iota(jnp.int32, (8, 2 * HEAD), 0)
    ).astype(jnp.bfloat16)

    def attend_back(pair):
        @pl.when(pair % 2 == 0)
        def _():
            in_plane(1 + pair // 2)

        @pl.when(early & (pair % 2 == 0))
        def _():
            relay_on(5 + pair // 2)
            relay_out(3 + pair // 2)

        prepare(pair)
        at = lanes_of(pair, 0)
        heads = r.wo[pl.ds(pair * 128, 128)]
        merge(r.grads, *(low(last_dims(r.grad_rows[side], heads)) for side in range(2)))
        merge(r.raw, r.att[0, :, at], r.att[1, :, at])
        r.dk[...] = jnp.zeros_like(r.dk)
        r.dv[...] = jnp.zeros_like(r.dv)
        for q in range(4):
            at = slice(q * 256, (q + 1) * 256)
            upto = slice(0, (q + 1) * 256)
            deltas = row_sums(r.grads[at].astype(full) * r.raw[at].astype(full), marks)
            delta = jnp.concatenate([deltas[h : h + 1] for h in range(2)], axis=1)
            log_sum = jnp.concatenate([r.log_sums[pair, h : h + 1, at] for h in range(2)], axis=1)
            query, grad, key = of_heads(r.queries[at]), of_heads(r.grads[at]), r.keys[upto]
            mask = jnp.concatenate([r.bias[upto, at]] * 2, axis=1)
            weighted = jnp.exp(last_dims(key, query) + (mask - log_sum))
            grad_scores = low(
                weighted * (last_dims(r.values[upto, : 2 * HEAD], grad) - delta)
            )
            r.dv[upto] += dot(low(weighted), grad)
            r.dk[upto] += dot(grad_scores, query)
            to_queries = contract_rows(grad_scores, key)
            r.dq[at] = (
                head_lanes(0, full) * to_queries[:256] + head_lanes(1, full) * to_queries[256:]
            )

        scale = r.flat[pair, pl.ds(c, 1), :]
        scale_sum = 0.0
        for part, grad in enumerate((r.dq, r.dk)):
            normed, factor = normal(pair, part)
            found = grad[...] * SCORE_SCALE if part == 0 else grad[...]
            scale_sum = scale_sum + jnp.sum(found * normed, axis=0, keepdims=True)
            step = found * scale
            grad[...] = factor * (step - normed * sums_of_halves(normed * step))
        r.sum_qk[pl.ds(pair, 1)] = scale_sum
        for part, grad in enumerate((r.dq, r.dk, r.dv)):
            at = lanes_of(pair, part)
            for q in range(4):
                rows = slice(q * BLOCK, (q + 1) * BLOCK)
                r.mixed[0, rows, at] = low(grad[q * 256 : q * 256 + BLOCK])
                r.mixed[1, rows, at] = low(grad[q * 256 + BLOCK : (q + 1) * 256])

    every(4, attend_back)

    relays((7,), (5,))
    settle_sent(2)
    exchange(
        3, lambda side, n: last_dims(r.mixed[side], r.wq[pl.ds(n * 256, 256)]), r.middle,
    )

    for b in range(4):
        rows = rows_of(b)

        @pl.when(early)
        def _():
            arrived(r.result.at[rows], r.result_send.at[b])

        arrived(r.result.at[rows], r.owner_send.at[0, b])

    def finish(b):
        rows = rows_of(b)
        r.result[rows] = low(r.middle[rows] + r.got[rows].astype(full))

        @pl.when(late)
        def _():
            remote(
                r.result.at[rows], r.grad_in.at[rows], r.result_send.at[b], r.grad_recv.at[b],
                early_plane,
            ).start()

    every(4, finish)
    to_owners(1, r.result, o_grad)

    for b in range(4):
        arrived(r.flags.at[b], r.flag_recv.at[b])
    r.flags_full[...] = r.flags[...].astype(full)
    ones = jnp.ones((8, width), jnp.bfloat16)
    for b in range(4):
        squares = row_sums(r.branch[rows_of(b)] * r.branch[rows_of(b)], ones)[:1]
        r.sum_valid[...] += squares * r.flags_full[b, pl.ds(c, 1), :]

    for owner in range(4):
        r.terms[owner, pl.ds(c, 1), :] = r.sum_qk[owner : owner + 1]
        for n in range(2):
            for j in range(4):
                at = slice((owner % 2 * 2 + n) * 512 + j * 128, (owner % 2 * 2 + n) * 512 + (j + 1) * 128)
                scale = math.sqrt(width) if owner // 2 else 1.0
                r.terms[owner, pl.ds(2 + n * 8 + j + c * 4, 1), :] = (
                    r.sum_scales[owner // 2 : owner // 2 + 1, at] * scale
                )
        for j in range(4):
            at = slice(owner % 2 * 512 + j * 128, owner % 2 * 512 + (j + 1) * 128)
            r.terms[owner, 18 + j : 19 + j, :] = r.sum_alphas[owner // 2 : owner // 2 + 1, at]
        r.terms[owner, 22:23, :] = r.sum_valid[...]
    flow = Flow((r.v0, r.v1, r.v2, r.v3, r.v4, r.v5, r.v6, r.v7), r.vector)
    flow.begin(lambda to: r.terms.at[to])

    @pl.when(late)
    def _():
        grad_of_lift(r.up, g_up)

    in_plane(3)

    def step(t):
        @pl.when(t == 4)
        def _():
            grad_of_lift(r.gate, g_gate)

        @pl.when(t == 8)
        def _():
            grad_of_out()
            grad_of_qkv()

        between_planes(t)
        in_plane(t)
        for at, work in ((6, flow.pass_on), (8, flow.finish_plane), (12, flow.middle_planes)):
            pl.when(t == at)(work)

        @pl.when(t == 16 + 18 * layer)
        def _():
            flow.all_planes(o_vectors.at[c])

    every(CHUNKS + 19 - 4, lambda n: step(n + 4))

    def settle(k):
        chunk = plane_sum.at[k]
        for sem in (r.send_own, r.send_far, r.given):
            arrived(chunk, sem.at[k])

        @pl.when(early)
        def _():
            arrived(chunk, r.send_on.at[k])
            arrived(chunk, r.send_back.at[k])

        @pl.when(k >= CHUNKS - 4)
        def _():
            arrived(chunk, r.send_next.at[k])
            arrived(chunk, r.send_z.at[k])
            placed(k, 1)

        @pl.when(k >= CHUNKS - 4)
        def _():
            placed(k, 0)

        @pl.when(early & (k >= CHUNKS - 4))
        def _():
            arrived(chunk, r.send_out.at[k])

    every(CHUNKS, settle)
    flow.settle()
    settle_shared(r.mid, 0)
    settle_shared(r.grad_rows, 2)
    settle_sent(3)
    for b in range(4):
        rows = rows_of(b)
        arrived(r.hid.at[1, rows], r.oth_send.at[b])

        @pl.when(late)
        def _():
            arrived(r.result.at[rows], r.result_send.at[b])

        @pl.when(s != b)
        def _():
            arrived(o_row.at[rows], r.row_send.at[b])
            arrived(r.flags.at[b], r.flag_send.at[b])

        arrived(r.result.at[rows], r.owner_send.at[1, b])

    for array, to_ref in enumerate((o_hidden, o_grad)):
        for micro in range(2):
            for core in range(2):

                @pl.when(jnp.logical_not((c == layer) & (c == core) & (s // 2 == micro)))
                def _():
                    arrived(
                        to_ref.at[micro, pl.ds(core * BLOCK, BLOCK)],
                        r.owner_recv.at[array, micro, core],
                    )


def relay_all(w_qkv, w_out, w_in, w_down, vectors, valid, tokens, cotangent, ends):
    width = w_out.shape[1]
    units = w_down.shape[0] * 4
    half = units // 2

    def low_shape(*shape):
        return jax.ShapeDtypeStruct(shape, jnp.bfloat16)

    chunks = low_shape(CHUNKS, 256, 512)
    rows = low_shape(2, 2 * BLOCK, width)
    anywhere = pl.BlockSpec(memory_space=pl.ANY)
    scalars = pl.BlockSpec(memory_space=pltpu.SMEM)
    scratch = scratch_of(width, units, vectors.shape[0], valid.shape[1])
    out_shape = [
        low_shape(half // 2, width), low_shape(width // 4, 2 * units), low_shape(width // 4, width),
        low_shape(width // 4, 3 * width), jax.ShapeDtypeStruct((2, 24, 128), jnp.float32),
        rows, rows, low_shape(4 * BLOCK, width),
        low_shape(half, width), low_shape(width, half), low_shape(width, half),
        low_shape(width, width // 2), low_shape(width, 3 * width // 2),
    ] + [chunks] * 7
    return pl.pallas_call(
        functools.partial(relay_kernel, tuple(scratch)),
        out_shape=out_shape,
        in_specs=[anywhere] * 8 + [scalars],
        out_specs=[anywhere] * len(out_shape),
        scratch_shapes=list(scratch.values()),
        compiler_params=pltpu.CompilerParams(
            collective_id=0, has_side_effects=True, vmem_limit_bytes=62 * 2**20
        ),
    )(
        w_qkv, w_out, w_in, w_down, vectors, valid, tokens, cotangent, ends,
    )[:7]


def per_device(
    tokens, cotangent, lengths, valid_mask, w_qkv, w_out, w_in, w_down, qk_scale, mlp_scale, alphas
):
    c, s, f, _, _, layer = position()
    second = layer == 1
    micro = s // 2
    width = tokens.shape[3]
    group = tokens.shape[2]
    units = w_down.shape[1] * 4

    vectors = jnp.concatenate([qk_scale[0], mlp_scale[0], alphas[0]])
    vectors = jnp.pad(vectors, (0, 32 * 128 - vectors.shape[0])).reshape(32, 128)
    valid = low(jnp.pad(valid_mask[:, 0], ((0, 0), (0, 16 * 128 - group)))).reshape(2, 16, 128)
    ends = jnp.cumsum(pick(lengths, micro, 0)[0])[:-1]
    grad_down, grad_in_proj, grad_out, grad_qkv, vectors, hidden_out, grad_in = relay_all(
        w_qkv[0], w_out[0], w_in[0], w_down[0], vectors, valid, tokens[:, 0], cotangent[:, 0], ends
    )
    cut_qk, cut_mlp = qk_scale.shape[1], qk_scale.shape[1] + mlp_scale.shape[1]
    full = jnp.sum(vectors, axis=0).reshape(-1)
    cuts = (cut_qk, cut_mlp, cut_mlp + alphas.shape[1])
    grad_qk_scale = full[: cuts[0]][None]
    grad_mlp_scale = full[cuts[0] : cuts[1]][None]
    grad_alphas = full[cuts[1] : cuts[2]][None]
    token_count = tokens.shape[0] * lax.axis_size("fsdp") * 4 * group
    total = jnp.sum(full[cuts[2] : cuts[2] + 128], keepdims=True)
    rms_stats = jnp.sqrt(total / token_count + epsilon)
    as_float = [
        part.astype(jnp.float32)[None] for part in (grad_qkv, grad_out, grad_in_proj, grad_down)
    ]
    return (
        hidden_out[None, :, None], grad_in.astype(jnp.float32)[None, :, None], *as_float,
        grad_qk_scale, grad_mlp_scale, grad_alphas, rms_stats,
    )


def solution(mesh):
    placed = (
        P(None, "fsdp", "seq", None),
        P(None, "fsdp", "seq", None),
        P(None, "fsdp", None),
        P(None, "fsdp", "seq"),
        P("section", "fsdp", None),
        P("section", "fsdp", None),
        P("section", "fsdp", None),
        P("section", "fsdp", None),
        P("section", "fsdp"),
        P("section", "fsdp"),
        P("section", "fsdp"),
    )
    planes = mesh.shape["section"] == 2 and mesh.shape["seq"] == 4 and mesh.shape["fsdp"] == 4
    return jax.shard_map(
        per_device if planes else per_device_general,
        mesh=mesh,
        in_specs=placed,
        out_specs=(
            P("section", None, "fsdp", "seq", None),
            P("section", None, "fsdp", "seq", None),
            P("section", "fsdp", None),
            P("section", "fsdp", None),
            P("section", "fsdp", None),
            P("section", "fsdp", None),
            P("section", "fsdp"),
            P("section", "fsdp"),
            P("section", "fsdp"),
            P("section"),
        ),
        check_vma=False,
    )
```
